32 devices in a mesh: groups: 2 (over x), gx: 16 (over z, y, core).
Axes of the slice: x: 2, y: 2, z: 4, core: 2. Of those that a mesh axis runs over, the one named last changes fastest.
Arguments:
- point_feats: bfloat16 [16384, 64], P(('groups', 'gx')), parts along dimension 0, may hold values from -6 to 6
- pair_point: int32 [32, 16, 128], P(('groups', 'gx')), parts along dimension 0, may hold values from 0 to 511
- pair_cell: int32 [16, 32, 128], P(None, ('groups', 'gx')), parts along dimension 1, may hold values from 0 to 16383
- kernel: float32 [32, 16, 128], P(('groups', 'gx')), parts along dimension 0, may hold values from 0.1 to 1
- counts: int32 [32, 16], P(('groups', 'gx')), parts along dimension 0, may hold values from 1 to 128, as said below
- area: float32 [16384], P(('groups', 'gx')), parts along dimension 0, may hold values from 0.3 to 3
- normals: float32 [2, 16384], P(None, ('groups', 'gx')), parts along dimension 1, may hold values from -4 to 4
- targets: float32 [4], P('groups'), parts along dimension 0, may hold values from -4 to 4
- spec_weight: bfloat16 [1024, 64, 64], P('gx'), may hold values from -0.75 to 0.75
- skip_weight: bfloat16 [64, 64], replicated, may hold values from -0.75 to 0.75
- skip_bias: float32 [64], replicated, may hold values from -3 to 3
- head_weight: bfloat16 [64, 64], replicated, may hold values from -0.75 to 0.75
- head_bias: float32 [64], replicated, may hold values from -3 to 3
- out_weight: float32 [64], replicated, may hold values from -0.75 to 0.75
Outputs:
- pressure: float32 [16384], P(('groups', 'gx')), parts along dimension 0
- forces: float32 [4], P('groups'), parts along dimension 0
- spec_grad: float32 [2048, 64, 64], P(('groups', 'gx')), parts along dimension 0
- skip_grad: float32 [128, 64], P('groups'), parts along dimension 0
- out_grad: float32 [128], P('groups'), parts along dimension 0
The draws below stay inside these ranges and needn't reach their ends.
There are 2 independent parts, one for each index of `groups`. The reference program is written for one: setup_inputs(seed, part) draws one part's arguments, and reference() takes and returns one part's arrays. A program takes and returns all parts, laid end to end along the dimension named above; an argument that names none is the same for every part. Nothing has to cross between parts.
Inputs may be any that keep to these rules, and one draw needn't show every extreme that they name: counts[s, d] valid slots lead each block; some block of every draw is full. `pair_cell`: cells of the destination slab, numbered x-plane, then y, then z.
All inputs are finite; a program needn't handle non-finite values.
Results may differ from the reference program's by a relative error of at most 0.0055.
The reference program's roundings to bfloat16 on the way count: a program that leaves them out, or rounds other values in their place, can miss the bound.
Values may be sent and summed in bfloat16 or wider, within the bound.
No kernel may reach another device: no remote copies, remote signals or barrier semaphores. Data moves between devices by JAX's collectives and lax.ppermute only.
A program may use at most 128 MiB of HBM per device.

```python
import math
import jax
import jax.numpy as jnp
from jax import lax

C = 64
GX = 128
GY = 128
MODES = 32
PD = 512
BP = 128
NMODE = 1024
XL = 8
SZ = 16
NPTS = 8192
N_GX = 16


def draw_counts(key, part):
    key = jax.random.fold_in(key, 7)
    load_key, base_key, pick_key = jax.random.split(key, 3)
    loads = jax.random.randint(load_key, (N_GX, 1), 1, 4)
    base_counts = jax.random.randint(base_key, (N_GX, N_GX), BP // 2, BP + 1)
    filled = jnp.maximum(loads * base_counts // 3, 1)
    chosen = jax.random.randint(pick_key, (2,), 0, N_GX)
    return filled.at[chosen[0], chosen[1]].set(BP).astype(jnp.int32)


def with_ends(values, key, least, top_value):
    longest = values.shape.index(max(values.shape))
    spots = []
    for shift in (0, 1):
        where = [jax.random.randint(jax.random.fold_in(key, axis), (), 0, length) for axis, length in enumerate(values.shape)]
        where[longest] = (where[longest] + shift) % values.shape[longest]
        spots.append(tuple(where))
    return values.at[spots[0]].set(least).at[spots[1]].set(top_value)


def steps_of(rng, extent, cuts, low, high):
    loudness, own = 1.0, jax.random.fold_in(rng, 6)
    for dim, shards_of in cuts:
        steps = jnp.exp(jax.random.uniform(jax.random.fold_in(own, dim), (shards_of,), jnp.float32, low / len(cuts), high / len(cuts)))
        loudness = loudness * jnp.repeat(steps, extent[dim] // shards_of).reshape([-1 if axis == dim else 1 for axis in range(len(extent))])
    return loudness


def scatter_about(key, dims, spread, limit, pieces=(), kind=jnp.bfloat16):
    values = spread * jax.random.normal(key, dims, jnp.float32)
    if pieces:
        values = values * steps_of(key, dims, pieces, -0.22, 0.18)
    return jnp.clip(values, -limit, limit).astype(kind)


def setup_inputs(seed: int = 0, part: int = 0) -> dict:
    keys = jax.random.split(jax.random.key(seed), 15)
    part_keys = jax.random.split(jax.random.fold_in(keys[14], part), 15)
    return {
        "point_feats": scatter_about(part_keys[0], (NPTS, C), 1.0, 6.0, ((0, 16),)),
        "pair_point": with_ends(jax.random.randint(part_keys[1], (N_GX, N_GX, BP), 0, PD), jax.random.fold_in(part_keys[1], 1), 0, PD - 1).astype(jnp.int32),
        "pair_cell": with_ends(jax.random.randint(part_keys[2], (N_GX, N_GX, BP), 0, XL * GY * SZ), jax.random.fold_in(part_keys[2], 1), 0, (XL * GY * SZ) - 1).astype(jnp.int32),
        "kernel": jnp.clip(jnp.exp(math.log(1.0) - 2.3025851 * jax.random.uniform(part_keys[3], (N_GX, N_GX, BP), jnp.float32) ** steps_of(part_keys[3], (N_GX, N_GX, BP), ((0, 16),), -0.2, 0.2)), 0.1, 1.0),
        "counts": draw_counts(jax.random.fold_in(jax.random.fold_in(keys[14], part), 71), part),
        "area": jnp.clip(jnp.exp(math.log(3.0) - 2.3025851 * jax.random.uniform(part_keys[5], (NPTS,), jnp.float32) ** steps_of(part_keys[5], (NPTS,), ((0, 16),), -0.2, 0.2)), 0.3, 3.0),
        "normals": scatter_about(part_keys[6], (2, NPTS), 1.0, 4.0, ((1, 16),), jnp.float32),
        "targets": scatter_about(part_keys[7], (2,), 1.0, 4.0, (), jnp.float32),
        "spec_weight": scatter_about(keys[8], (NMODE, C, C), C ** -0.5, 0.75, ((0, 16),)),
        "skip_weight": scatter_about(keys[9], (C, C), C ** -0.5, 0.75),
        "skip_bias": scatter_about(keys[10], (C,), 0.5, 3.0, (), jnp.float32),
        "head_weight": scatter_about(keys[11], (C, C), C ** -0.5, 0.75),
        "head_bias": scatter_about(keys[12], (C,), 0.5, 3.0, (), jnp.float32),
        "out_weight": scatter_about(keys[13], (C,), C ** -0.5, 0.75, (), jnp.float32),
    }


def fourier_rows(length, number):
    places = jnp.arange(length, dtype=jnp.float32)
    order = jnp.arange(number)
    half = number // 2
    freqs = jnp.where(order < half, order, order - half + 1).astype(jnp.float32)
    angles = 2.0 * math.pi / length * freqs[:, None] * places[None, :]
    table = jnp.where((order < half)[:, None], jnp.cos(angles), jnp.sin(angles))
    return (table * math.sqrt(2.0 / length)).astype(jnp.bfloat16)

def gelu_value(values):
    return 0.5 * values * (1.0 + lax.erf(values * (1.0 / math.sqrt(2.0))))

def gelu_slope(values):
    return 0.5 * (1.0 + lax.erf(values * (1.0 / math.sqrt(2.0)))) + values * jnp.exp(-0.5 * values * values) * (1.0 / math.sqrt(2.0 * math.pi))

def reference(point_feats, pair_point, pair_cell, kernel, counts, area, normals, targets, spec_weight, skip_weight, skip_bias, head_weight, head_bias, out_weight):
    width = point_feats.shape[1]
    slab_cells = XL * GY * SZ
    total_cells = GX * GY * SZ
    valid_mask = jnp.arange(BP)[None, None, :] < counts[:, :, None]
    pair_weight = jnp.where(valid_mask, kernel, jnp.float32(0.0))
    source_ids = (jnp.arange(N_GX)[:, None, None] * PD + pair_point).astype(jnp.int32)
    target_ids = (jnp.arange(N_GX)[None, :, None] * slab_cells + pair_cell).astype(jnp.int32)
    sender_weight = pair_weight * area[source_ids]
    contrib = (sender_weight[..., None] * point_feats[source_ids].astype(jnp.float32)).astype(jnp.bfloat16)
    latent = jax.ops.segment_sum(contrib.reshape(-1, width).astype(jnp.float32), target_ids.reshape(-1), num_segments=total_cells).astype(jnp.bfloat16)
    col_table = fourier_rows(GY, MODES).astype(jnp.float32)
    row_table = fourier_rows(GX, MODES).astype(jnp.float32)
    volume = latent.reshape(GX, GY, SZ * width).astype(jnp.float32)
    along_y = jnp.einsum('by,xyk->xbk', col_table, volume).astype(jnp.bfloat16)
    spectrum = jnp.einsum('ax,xbk->abk', row_table, along_y.astype(jnp.float32)).astype(jnp.bfloat16)
    spec_flat = spectrum.reshape(NMODE, SZ, width).astype(jnp.float32)
    mixed = jnp.einsum('mzc,mcd->mzd', spec_flat, spec_weight.astype(jnp.float32)).astype(jnp.bfloat16)
    back_x = jnp.einsum('ax,abk->xbk', row_table, mixed.reshape(MODES, MODES, SZ * width).astype(jnp.float32)).astype(jnp.bfloat16)
    spatial = jnp.einsum('by,xbk->xyk', col_table, back_x.astype(jnp.float32)).reshape(total_cells, width)
    pre = spatial + jnp.dot(latent, skip_weight, preferred_element_type=jnp.float32) + skip_bias
    features = gelu_value(pre).astype(jnp.bfloat16)
    gathered = features[target_ids].astype(jnp.float32)
    point_latent = jax.ops.segment_sum((pair_weight[..., None] * gathered).reshape(-1, width), source_ids.reshape(-1), num_segments=NPTS)
    head_matrix = head_weight.astype(jnp.float32)
    head_pre = jnp.dot(point_latent, head_matrix, precision=lax.Precision.HIGHEST) + head_bias
    head = gelu_value(head_pre)
    pressure = jnp.dot(head, out_weight, precision=lax.Precision.HIGHEST)
    scale = 1.0 / math.sqrt(NPTS)
    weighted = pressure * area
    forces = scale * jnp.stack([jnp.sum(weighted * normals[0]), jnp.sum(weighted * normals[1])])
    misfit = forces - targets
    point_grad = 2.0 * scale * (misfit[0] * normals[0] + misfit[1] * normals[1]) * area
    out_grad = jnp.dot(point_grad, head, precision=lax.Precision.HIGHEST)
    head_grad = point_grad[:, None] * out_weight[None, :] * gelu_slope(head_pre)
    latent_grad = jnp.dot(head_grad, head_matrix.T, precision=lax.Precision.HIGHEST).astype(jnp.bfloat16)
    grad_pairs = (pair_weight[..., None] * latent_grad[source_ids].astype(jnp.float32)).astype(jnp.bfloat16)
    cell_grad = jax.ops.segment_sum(grad_pairs.reshape(-1, width).astype(jnp.float32), target_ids.reshape(-1), num_segments=total_cells)
    pre_grad = (cell_grad * gelu_slope(pre)).astype(jnp.bfloat16)
    skip_grad = jnp.dot(latent.T, pre_grad, preferred_element_type=jnp.float32)
    grad_y = jnp.einsum('by,xyk->xbk', col_table, pre_grad.reshape(GX, GY, SZ * width).astype(jnp.float32)).astype(jnp.bfloat16)
    grad_spec = jnp.einsum('ax,xbk->abk', row_table, grad_y.astype(jnp.float32)).astype(jnp.bfloat16)
    spec_grad = jnp.einsum('mzc,mzd->mcd', spec_flat, grad_spec.reshape(NMODE, SZ, width).astype(jnp.float32))
    return (pressure, forces, spec_grad, skip_grad, out_grad)
```

```python
import functools
import math

import jax
import jax.numpy as jnp
import ml_dtypes
import numpy as np
from jax import lax
from jax.experimental import pallas as pl
from jax.experimental.pallas import tpu as pltpu
from jax.sharding import PartitionSpec as P

GX = 128
GY = 128
MODES = 32
ZL = 1
NMODE = 1024


def fourier_rows(length, number):
    places = jnp.arange(length, dtype=jnp.float32)
    order = jnp.arange(number)
    half = number // 2
    freqs = jnp.where(order < half, order, order - half + 1).astype(jnp.float32)
    angles = 2.0 * math.pi / length * freqs[:, None] * places[None, :]
    table = jnp.where((order < half)[:, None], jnp.cos(angles), jnp.sin(angles))
    return (table * math.sqrt(2.0 / length)).astype(jnp.bfloat16)


def gelu_value(values):
    return 0.5 * values * (1.0 + lax.erf(values * (1.0 / math.sqrt(2.0))))


def gelu_slope(values):
    return 0.5 * (1.0 + lax.erf(values * (1.0 / math.sqrt(2.0)))) + values * jnp.exp(
        -0.5 * values * values
    ) * (1.0 / math.sqrt(2.0 * math.pi))


def general_step(
    point_feats,
    pair_point,
    pair_cell,
    kernel,
    counts,
    area,
    normals,
    targets,
    spec_weight,
    skip_weight,
    skip_bias,
    head_weight,
    head_bias,
    out_weight,
):
    devices = lax.axis_size("gx")
    local_points, width = point_feats.shape
    block_slots = pair_point.shape[2]
    row_count = GX // devices
    depth = ZL * devices
    slab_cells = row_count * GY * depth
    valid_mask = jnp.arange(block_slots)[None, :] < counts[0][:, None]
    point_rows = pair_point[0]
    pair_weight = jnp.where(valid_mask, kernel[0], jnp.float32(0.0))
    sender_weight = pair_weight * area[point_rows]
    contrib = (sender_weight[..., None] * point_feats[point_rows].astype(jnp.float32)).astype(
        jnp.bfloat16
    )
    arrived = lax.all_to_all(contrib, "gx", split_axis=0, concat_axis=0, tiled=True)
    cell_rows = pair_cell[:, 0, :].reshape(-1)
    latent = jax.ops.segment_sum(
        arrived.reshape(-1, width).astype(jnp.float32), cell_rows, num_segments=slab_cells
    ).astype(jnp.bfloat16)
    col_table = fourier_rows(GY, MODES)
    row_table = fourier_rows(GX, MODES)
    volume = latent.reshape(row_count, GY, depth * width)
    along_y = jnp.einsum(
        "by,xyk->xbk", col_table, volume, preferred_element_type=jnp.float32
    ).astype(jnp.bfloat16)
    columns = lax.all_to_all(along_y, "gx", split_axis=2, concat_axis=0, tiled=True)
    spectrum = jnp.einsum(
        "ax,xbk->abk", row_table, columns, preferred_element_type=jnp.float32
    ).astype(jnp.bfloat16)
    mode_rows = lax.all_to_all(
        spectrum.reshape(NMODE, ZL * width), "gx", split_axis=0, concat_axis=1, tiled=True
    )
    own_modes = mode_rows.shape[0]
    mixed_rows = jnp.einsum(
        "mzc,mcd->mzd",
        mode_rows.reshape(own_modes, depth, width),
        spec_weight,
        preferred_element_type=jnp.float32,
    ).astype(jnp.bfloat16)
    mixed = lax.all_to_all(
        mixed_rows.reshape(own_modes, depth * width), "gx", split_axis=1, concat_axis=0, tiled=True
    )
    back_x = jnp.einsum(
        "ax,abk->xbk",
        row_table,
        mixed.reshape(MODES, MODES, ZL * width),
        preferred_element_type=jnp.float32,
    ).astype(jnp.bfloat16)
    slabs = lax.all_to_all(back_x, "gx", split_axis=0, concat_axis=2, tiled=True)
    spatial = jnp.einsum(
        "by,xbk->xyk", col_table, slabs, preferred_element_type=jnp.float32
    ).reshape(slab_cells, width)
    pre = spatial + jnp.dot(latent, skip_weight, preferred_element_type=jnp.float32) + skip_bias
    features = gelu_value(pre).astype(jnp.bfloat16)
    picked = features[cell_rows].reshape(devices, block_slots, width)
    returned = lax.all_to_all(picked, "gx", split_axis=0, concat_axis=0, tiled=True)
    point_latent = jax.ops.segment_sum(
        (pair_weight[..., None] * returned.astype(jnp.float32)).reshape(-1, width),
        point_rows.reshape(-1),
        num_segments=local_points,
    )
    head_matrix = head_weight.astype(jnp.float32)
    head_pre = jnp.dot(point_latent, head_matrix, precision=lax.Precision.HIGHEST) + head_bias
    head = gelu_value(head_pre)
    pressure = jnp.dot(head, out_weight, precision=lax.Precision.HIGHEST)
    weighted = pressure * area
    scale = 1.0 / math.sqrt(local_points * devices)
    totals = lax.psum(
        jnp.stack([jnp.sum(weighted * normals[0]), jnp.sum(weighted * normals[1])]), "gx"
    )
    forces = scale * totals
    misfit = forces - targets
    point_grad = 2.0 * scale * (misfit[0] * normals[0] + misfit[1] * normals[1]) * area
    out_part = jnp.dot(point_grad, head, precision=lax.Precision.HIGHEST)
    head_grad = point_grad[:, None] * out_weight[None, :] * gelu_slope(head_pre)
    latent_grad = jnp.dot(head_grad, head_matrix.T, precision=lax.Precision.HIGHEST).astype(
        jnp.bfloat16
    )
    grad_pairs = (pair_weight[..., None] * latent_grad[point_rows].astype(jnp.float32)).astype(
        jnp.bfloat16
    )
    grad_arrived = lax.all_to_all(grad_pairs, "gx", split_axis=0, concat_axis=0, tiled=True)
    cell_grad = jax.ops.segment_sum(
        grad_arrived.reshape(-1, width).astype(jnp.float32), cell_rows, num_segments=slab_cells
    )
    pre_grad = (cell_grad * gelu_slope(pre)).astype(jnp.bfloat16)
    skip_part = jnp.dot(latent.T, pre_grad, preferred_element_type=jnp.float32)
    grad_y = jnp.einsum(
        "by,xyk->xbk",
        col_table,
        pre_grad.reshape(row_count, GY, depth * width),
        preferred_element_type=jnp.float32,
    ).astype(jnp.bfloat16)
    grad_columns = lax.all_to_all(grad_y, "gx", split_axis=2, concat_axis=0, tiled=True)
    grad_spec = jnp.einsum(
        "ax,xbk->abk", row_table, grad_columns, preferred_element_type=jnp.float32
    ).astype(jnp.bfloat16)
    grad_rows = lax.all_to_all(
        grad_spec.reshape(NMODE, ZL * width), "gx", split_axis=0, concat_axis=1, tiled=True
    )
    own_modes = grad_rows.shape[0]
    spec_grad = jnp.einsum(
        "mzc,mzd->mcd",
        mode_rows.reshape(own_modes, depth, width),
        grad_rows.reshape(own_modes, depth, width),
        preferred_element_type=jnp.float32,
    )
    out_grad, skip_grad = lax.psum((out_part, skip_part), "gx")
    return (pressure, forces, spec_grad, skip_grad, out_grad)


F32 = jnp.float32
BF16 = jnp.bfloat16
LANES = 128
WIDTH = 64


def host_rows(length, number):
    places = np.arange(length, dtype=np.float32)
    order = np.arange(number)
    half = number // 2
    freqs = np.where(order < half, order, order - half + 1).astype(np.float32)
    angles = np.float32(2.0 * math.pi / length) * freqs[:, None] * places[None, :]
    table = np.where((order < half)[:, None], np.cos(angles), np.sin(angles))
    table = table.astype(np.float32) * np.float32(math.sqrt(2.0 / length))
    return table.astype(ml_dtypes.bfloat16)


def three_parts(values):
    first = values.astype(BF16)
    rest = values - first.astype(F32)
    second = rest.astype(BF16)
    third = (rest - second.astype(F32)).astype(BF16)
    return first, second, third


def mm(left, right):
    return jnp.dot(left, right, preferred_element_type=F32)


def mm_nt(left, right):
    return lax.dot_general(left, right, (((1,), (1,)), ((), ())), preferred_element_type=F32)


def mm_tn(left, right):
    return lax.dot_general(left, right, (((0,), (0,)), ((), ())), preferred_element_type=F32)


def two_rows(ref, pair):
    return jnp.concatenate([ref[2 * pair : 2 * pair + 1, :], ref[2 * pair + 1 : 2 * pair + 2, :]], axis=1)


def source_kernel(group_ref, count_ref, point_ref, kern_ref, area_ref, feat_ref, weight_ref, msg_ref, pw_ref):
    devices = point_ref.shape[0]
    points = feat_ref.shape[1]
    low = MODES // devices
    first, second, third = three_parts(area_ref[...])
    place = lax.broadcasted_iota(jnp.int32, (16, points), 0)
    extra = jnp.where(
        place == 0,
        first.astype(F32),
        jnp.where(place == 1, second.astype(F32), jnp.where(place == 2, third.astype(F32), 0.0)),
    ).astype(BF16)
    table = jnp.concatenate([feat_ref[...], extra], axis=0)
    rows = lax.broadcasted_iota(jnp.int32, (points, 2 * LANES), 0)
    lane = lax.broadcasted_iota(jnp.int32, (1, LANES), 1)
    offset = group_ref[0] * MODES
    for pair in range(devices // 2):
        hot = jnp.where(rows == two_rows(point_ref, pair), 1.0, 0.0).astype(BF16)
        got = mm(table, hot)
        spread = got[WIDTH : WIDTH + 1] + got[WIDTH + 1 : WIDTH + 2] + got[WIDTH + 2 : WIDTH + 3]
        for half in range(2):
            dest = 2 * pair + half
            cut = slice(half * LANES, (half + 1) * LANES)
            weight = jnp.where(lane < count_ref[0, dest], kern_ref[dest : dest + 1, :], 0.0)
            pw_ref[dest : dest + 1, :] = weight
            msg_ref[dest, 0:WIDTH, :] = ((weight * spread[:, cut]) * got[0:WIDTH, cut]).astype(BF16)
            msg_ref[dest, WIDTH : 2 * WIDTH, :] = jnp.concatenate(
                [weight_ref[offset + low * dest], weight_ref[offset + low * dest + 1]], axis=1
            )


def place_kernel(depth, cell_ref, by_ref, col_ref, lp_ref, zr_ref):
    devices = cell_ref.shape[0]
    zbits = depth.bit_length() - 1
    rows = by_ref.shape[0]
    slab = rows // MODES
    yrow = lax.broadcasted_iota(jnp.int32, (GY, LANES), 0)
    xrow = jnp.bitwise_and(lax.broadcasted_iota(jnp.int32, (rows, LANES), 0), slab - 1)
    up = lax.broadcasted_iota(jnp.int32, (LANES, LANES), 0) < lax.broadcasted_iota(
        jnp.int32, (LANES, LANES), 1
    )
    for block in range(devices):
        cells = cell_ref[block : block + 1, :]
        cut = slice(block * LANES, (block + 1) * LANES)
        col_ref[cut, :] = jnp.broadcast_to(cells.astype(F32), (LANES, LANES)).T
        ypos = jnp.bitwise_and(jnp.right_shift(cells, zbits), GY - 1)
        xpos = jnp.right_shift(cells, zbits + GY.bit_length() - 1)
        hot = jnp.where(yrow == ypos, 1.0, 0.0).astype(BF16)
        lp_ref[:, cut] = jnp.where(xrow == xpos, mm(by_ref[...], hot), 0.0).astype(BF16)
    for block in range(devices):
        cells = cell_ref[block : block + 1, :]
        row = cells.astype(F32)
        cut = slice(block * LANES, (block + 1) * LANES)
        same = jnp.where(jnp.logical_and(col_ref[cut, :] == row, up), 1.0, 0.0)
        seen = jnp.max(same, axis=0, keepdims=True)
        if block:
            before = jnp.where(col_ref[0 : block * LANES, :] == row, 1.0, 0.0)
            seen = jnp.maximum(seen, jnp.max(before, axis=0, keepdims=True))
        zr_ref[block : block + 1, :] = jnp.where(
            seen > 0.0, -1, jnp.bitwise_and(cells, depth - 1)
        )


def equal_cells(col_ref, cell_ref, same_ref, pair):
    for half in range(2):
        row = cell_ref[2 * pair + half : 2 * pair + half + 1, :].astype(F32)
        same_ref[:, half * LANES : (half + 1) * LANES] = jnp.where(
            col_ref[...] == row, 1.0, 0.0
        ).astype(BF16)


def spread_depth(values, zpos, rp_ref, pair):
    cut = slice(pair * 2 * LANES, (pair + 1) * 2 * LANES)
    for level in range(rp_ref.shape[0] // WIDTH):
        rp_ref[level * WIDTH : (level + 1) * WIDTH, cut] = jnp.where(
            zpos == level, values, 0.0
        ).astype(BF16)


def slab_rows(lp_ref, rp_ref, msg_ref):
    devices = msg_ref.shape[0]
    step = lp_ref.shape[0] // devices
    for quad in range(rp_ref.shape[0] // (4 * WIDTH)):
        out = mm_nt(lp_ref[...], rp_ref[quad * 4 * WIDTH : (quad + 1) * 4 * WIDTH, :]).astype(BF16)
        for half in range(2):
            level = 2 * quad + half
            for dest in range(devices):
                msg_ref[dest, level * step : (level + 1) * step, :] = out[
                    dest * step : (dest + 1) * step, half * LANES : (half + 1) * LANES
                ]


def cell_kernel(rx_ref, cell_ref, zr_ref, col_ref, lp_ref, msg_ref, lat_ref, xs_ref, same_a, same_b, rp_ref):
    devices = rx_ref.shape[0]
    for block in range(devices):
        xs_ref[:, block * LANES : (block + 1) * LANES] = rx_ref[block, 0:WIDTH, :]
    for pair in range(devices // 2):
        same_ref = (same_a, same_b)[pair % 2]
        equal_cells(col_ref, cell_ref, same_ref, pair)
        latent = mm(xs_ref[...], same_ref[...])
        lat_ref[:, pair * 2 * LANES : (pair + 1) * 2 * LANES] = latent.astype(BF16)
        spread_depth(latent, two_rows(zr_ref, pair), rp_ref, pair)
    slab_rows(lp_ref, rp_ref, msg_ref)


def to_modes(rx_ref, table_ref, sp_ref):
    levels = sp_ref.shape[0] // table_ref.shape[0]
    step = table_ref.shape[1] // rx_ref.shape[0]
    for level in range(levels):
        block = rx_ref[:, level * step : (level + 1) * step, :].reshape(table_ref.shape[1], LANES)
        coeffs = mm(table_ref[...], block).astype(BF16).astype(F32)
        sp_ref[pl.ds(level, table_ref.shape[0], stride=levels), :] = coeffs


def swap_halves(values):
    return pltpu.roll(values, WIDTH, 1)


def mode_kernel(group_ref, rx_ref, own_ref, other_ref, table_ref, back_ref, msg_ref, spec_ref, sp_ref, mx_ref):
    devices = rx_ref.shape[0]
    own_rows = spec_ref.shape[1]
    modes = table_ref.shape[0]
    levels = sp_ref.shape[0] // modes
    step = back_ref.shape[0] // devices
    to_modes(rx_ref, table_ref, sp_ref)
    for dest in range(devices):
        spec_ref[dest] = sp_ref[dest * own_rows : (dest + 1) * own_rows, :].astype(BF16)
    left = lax.broadcasted_iota(jnp.int32, (levels, LANES), 1) < WIDTH
    for order in range(MODES):
        source, which = order // 2, order % 2
        mine = jnp.full((WIDTH, LANES), group_ref[0], jnp.int32) == which
        weight = jnp.where(
            mine,
            own_ref[source, WIDTH : 2 * WIDTH, :].astype(F32),
            other_ref[source].astype(F32),
        ).astype(BF16)
        at = order * 2 * levels
        even = sp_ref[at : at + levels, :]
        odd = sp_ref[at + levels : at + 2 * levels, :]
        rows = jnp.concatenate([even, swap_halves(even), odd, swap_halves(odd)], axis=0)
        out = mm(rows[:, 0:WIDTH].astype(BF16), weight)
        mx_ref[at : at + levels, :] = jnp.where(
            left, out[0:levels], swap_halves(out[levels : 2 * levels])
        )
        mx_ref[at + levels : at + 2 * levels, :] = jnp.where(
            left, swap_halves(out[2 * levels : 3 * levels]), out[3 * levels : 4 * levels]
        )
    for level in range(levels):
        mixed = mx_ref[pl.ds(level, modes, stride=levels), :].astype(BF16)
        out = mm(back_ref[...], mixed).astype(BF16)
        for dest in range(devices):
            msg_ref[dest, level * step : (level + 1) * step, :] = out[dest * step : (dest + 1) * step]


def pre_kernel(depth, rx_ref, lp_ref, lat_ref, cell_ref, skip_ref, bias_ref, msg_ref, pre_ref, rt_ref):
    devices = rx_ref.shape[0]
    rows = lp_ref.shape[0]
    step = rows // devices
    for level in range(rt_ref.shape[0] // LANES):
        block = rx_ref[:, level * step : (level + 1) * step, :].reshape(rows, LANES)
        rt_ref[level * LANES : (level + 1) * LANES, :] = block.T
    for pair in range(devices // 2):
        cut = slice(pair * 2 * LANES, (pair + 1) * 2 * LANES)
        zpos = jnp.bitwise_and(two_rows(cell_ref, pair), depth - 1)
        field = mm(rt_ref[...], lp_ref[:, cut])
        total = jnp.where(zpos == 0, field[0:WIDTH], 0.0)
        for level in range(1, depth):
            total += jnp.where(zpos == level, field[level * WIDTH : (level + 1) * WIDTH], 0.0)
        pre = total + mm_tn(skip_ref[...], lat_ref[:, cut]) + bias_ref[...]
        pre_ref[:, cut] = pre
        feats = gelu_value(pre).astype(BF16)
        for half in range(2):
            msg_ref[2 * pair + half] = feats[:, half * LANES : (half + 1) * LANES]


def slope_kernel(pre_ref, slope_ref):
    slope_ref[...] = gelu_slope(pre_ref[...])


def head_kernel(rx_ref, point_ref, pw_ref, head_ref, bias_ref, out_ref, area_ref, normal_ref, pres_ref, part_ref, hp_ref, value_ref, hot_ref):
    devices = rx_ref.shape[0]
    points = area_ref.shape[1]
    rows = lax.broadcasted_iota(jnp.int32, (points, LANES), 0)
    for block in range(devices):
        cut = slice(block * LANES, (block + 1) * LANES)
        parts = three_parts(pw_ref[block : block + 1, :] * rx_ref[block].astype(F32))
        for index, part in enumerate(parts):
            value_ref[index * WIDTH : (index + 1) * WIDTH, cut] = part
        hot_ref[:, cut] = jnp.where(rows == point_ref[block : block + 1, :], 1.0, 0.0).astype(BF16)
    sums = mm_nt(value_ref[...], hot_ref[...])
    latent = sums[0:WIDTH] + sums[WIDTH : 2 * WIDTH] + sums[2 * WIDTH : 3 * WIDTH]
    first, second, third = three_parts(latent)
    weight = head_ref[...]
    head_pre = mm_tn(weight, first) + mm_tn(weight, second) + mm_tn(weight, third) + bias_ref[...]
    hp_ref[...] = head_pre
    pressure = jnp.sum(gelu_value(head_pre) * out_ref[...], axis=0, keepdims=True)
    pres_ref[...] = pressure
    weighted = pressure * area_ref[...]
    drag = jnp.sum(weighted * normal_ref[0:1, :], axis=1, keepdims=True)
    lift = jnp.sum(weighted * normal_ref[1:2, :], axis=1, keepdims=True)
    lane = lax.broadcasted_iota(jnp.int32, (1, LANES), 1)
    row = jnp.where(lane == 0, drag, jnp.where(lane == 1, lift, 0.0))
    for dest in range(devices):
        part_ref[dest] = row


def pair_kernel(hp_ref, point_ref, head_ref, out_ref, area_ref, normal_ref, up_ref, na_ref, head_out):
    devices = point_ref.shape[0]
    points = area_ref.shape[1]
    head_pre = hp_ref[...]
    head_out[...] = gelu_value(head_pre)
    base = out_ref[...] * gelu_slope(head_pre)
    first, second, third = three_parts(base)
    weight = head_ref[...]
    grad = mm(weight, first) + mm(weight, second) + mm(weight, third)
    parts = three_parts(grad)
    place = lax.broadcasted_iota(jnp.int32, (16, points), 0)
    extra = jnp.zeros((16, points), F32)
    for which in range(2):
        scaled = three_parts(normal_ref[which : which + 1, :] * area_ref[...])
        for index, part in enumerate(scaled):
            extra = jnp.where(place == 3 * which + index, part.astype(F32), extra)
    table = jnp.concatenate(list(parts) + [extra.astype(BF16)], axis=0)
    rows = lax.broadcasted_iota(jnp.int32, (points, 2 * LANES), 0)
    for pair in range(devices // 2):
        hot = jnp.where(rows == two_rows(point_ref, pair), 1.0, 0.0).astype(BF16)
        got = mm(table, hot)
        up_ref[:, pair * 2 * LANES : (pair + 1) * 2 * LANES] = (
            got[0:WIDTH] + got[WIDTH : 2 * WIDTH] + got[2 * WIDTH : 3 * WIDTH]
        )
        tail = got[3 * WIDTH : 3 * WIDTH + 16]
        for which in range(2):
            at = 3 * which
            value = tail[at : at + 1] + tail[at + 1 : at + 2] + tail[at + 2 : at + 3]
            for half in range(2):
                na_ref[which, 2 * pair + half : 2 * pair + half + 1, :] = value[
                    :, half * LANES : (half + 1) * LANES
                ]


def grad_kernel(scale, target_ref, part_ref, up_ref, na_ref, pw_ref, head_ref, area_ref, normal_ref, msg_ref, force_ref, outp_ref):
    devices = part_ref.shape[0]
    totals = part_ref[0]
    for source in range(1, devices):
        totals += part_ref[source]
    forces = scale * totals
    force_ref[...] = forces
    drag = forces[:, 0:1] - target_ref[0]
    lift = forces[:, 1:2] - target_ref[1]
    twice = 2.0 * scale
    for dest in range(devices):
        along = twice * (drag * na_ref[0, dest : dest + 1, :] + lift * na_ref[1, dest : dest + 1, :])
        grad = (along * up_ref[:, dest * LANES : (dest + 1) * LANES]).astype(BF16).astype(F32)
        msg_ref[dest] = (pw_ref[dest : dest + 1, :] * grad).astype(BF16)
    point_grad = twice * (drag * normal_ref[0:1, :] + lift * normal_ref[1:2, :]) * area_ref[...]
    spread = jnp.broadcast_to(point_grad, (8, point_grad.shape[1]))
    found = lax.dot_general(
        spread,
        head_ref[...],
        (((1,), (1,)), ((), ())),
        precision=lax.Precision.HIGHEST,
        preferred_element_type=F32,
    )
    outp_ref[...] = jnp.where(lax.broadcasted_iota(jnp.int32, found.shape, 0) == 0, found, 0.0)


def fold_rows(values):
    first, second, third = three_parts(values)
    upper = jnp.concatenate([first.astype(F32), second.astype(F32)], axis=1)
    lower = jnp.concatenate([third.astype(F32), jnp.zeros_like(values)], axis=1)
    return upper, lower


def back_kernel(rx_ref, cell_ref, zr_ref, col_ref, lp_ref, lat_ref, slope_ref, outp_ref, msg_ref, xs_ref, pg_ref, same_a, same_b, rp_ref):
    devices = rx_ref.shape[0]
    main = lp_ref.shape[0] // devices * (rp_ref.shape[0] // LANES)
    for block in range(devices):
        xs_ref[:, block * LANES : (block + 1) * LANES] = rx_ref[block]
    for pair in range(devices // 2):
        cut = slice(pair * 2 * LANES, (pair + 1) * 2 * LANES)
        same_ref = (same_a, same_b)[pair % 2]
        equal_cells(col_ref, cell_ref, same_ref, pair)
        grad = mm(xs_ref[...], same_ref[...]) * slope_ref[:, cut]
        zpos = two_rows(zr_ref, pair)
        pg_ref[:, cut] = jnp.where(zpos >= 0, grad, 0.0).astype(BF16)
        spread_depth(grad, zpos, rp_ref, pair)
    slab_rows(lp_ref, rp_ref, msg_ref)
    skip = mm_nt(lat_ref[...], pg_ref[...])
    upper, lower = fold_rows(jnp.concatenate([skip, outp_ref[...]], axis=0))
    blocks = upper.shape[0] // 8
    for dest in range(devices):
        if dest < blocks:
            cut = slice(8 * dest, 8 * dest + 8)
            rows = jnp.concatenate([upper[cut], lower[cut]], axis=0)
        else:
            rows = jnp.zeros((16, LANES), F32)
        msg_ref[dest, main : main + 16, :] = rows.astype(BF16)


def spec_kernel(rx_ref, table_ref, spec_ref, msg_ref, sp_ref):
    devices = rx_ref.shape[0]
    own_rows = spec_ref.shape[1]
    main = rx_ref.shape[1] - 16
    to_modes(rx_ref, table_ref, sp_ref)
    total = rx_ref[0, main : main + 16, :].astype(F32)
    for source in range(1, devices):
        total += rx_ref[source, main : main + 16, :].astype(F32)
    upper, lower = total[0:8], total[8:16]
    left = lax.broadcasted_iota(jnp.int32, (8, LANES), 1) < WIDTH
    value = jnp.where(left, upper + swap_halves(upper) + lower, 0.0)
    first, second, third = three_parts(value)
    upper = first.astype(F32) + swap_halves(second.astype(F32))
    rows = jnp.concatenate([upper, third.astype(F32)], axis=0).astype(BF16)
    for dest in range(devices):
        msg_ref[dest, 0:own_rows, :] = spec_ref[dest]
        msg_ref[dest, own_rows : 2 * own_rows, :] = sp_ref[
            dest * own_rows : (dest + 1) * own_rows, :
        ].astype(BF16)
        msg_ref[dest, 2 * own_rows : 2 * own_rows + 16, :] = rows


def final_kernel(rx_ref, spec_ref, skip_ref, out_ref):
    devices = rx_ref.shape[0]
    own_rows = (rx_ref.shape[1] - 16) // 2
    for source in range(devices):
        for which in range(own_rows // 16):
            at = which * 16
            coeffs = rx_ref[source, at : at + 16, :].astype(F32)
            grads = rx_ref[source, own_rows + at : own_rows + at + 16, :].astype(F32)
            for low in range(2):
                cut = slice(8 * low, 8 * low + 8)
                left, right = coeffs[cut], grads[cut]
                left = jnp.concatenate([left, swap_halves(left)], axis=0)[:, 0:WIDTH]
                right = jnp.concatenate([right, swap_halves(right)], axis=0)[:, 0:WIDTH]
                spec_ref[which * MODES + 2 * source + low] = mm_tn(
                    left.astype(BF16), right.astype(BF16)
                )
    for source in range(WIDTH // 8 + 1):
        rows = rx_ref[source, 2 * own_rows : 2 * own_rows + 16, :].astype(F32)
        value = (rows[0:8] + swap_halves(rows[0:8]) + rows[8:16])[:, 0:WIDTH]
        if source < WIDTH // 8:
            skip_ref[8 * source : 8 * source + 8, :] = value
        else:
            out_ref[...] = value


def run(kernel, outs, ins, flops, scratch=(), smem=0):
    vmem = pl.BlockSpec(memory_space=pltpu.VMEM)
    moved = sum(math.prod(a.shape) * a.dtype.itemsize for a in list(ins) + list(outs))
    return pl.pallas_call(
        kernel,
        out_shape=tuple(outs),
        in_specs=[pl.BlockSpec(memory_space=pltpu.SMEM)] * smem + [vmem] * (len(ins) - smem),
        out_specs=tuple([vmem] * len(outs)),
        scratch_shapes=list(scratch),
        compiler_params=pltpu.CompilerParams(vmem_limit_bytes=48 * 1024 * 1024),
        cost_estimate=pl.CostEstimate(flops=flops, bytes_accessed=moved, transcendentals=0),
    )(*ins)


def slab_step(
    point_feats,
    pair_point,
    pair_cell,
    kernel,
    counts,
    area,
    normals,
    targets,
    spec_weight,
    skip_weight,
    skip_bias,
    head_weight,
    head_bias,
    out_weight,
):
    n = lax.axis_size("gx")
    points = point_feats.shape[0]
    slots = n * LANES
    slab = GX // n
    low = MODES // n
    depth = ZL * n
    levels = depth * WIDTH // LANES
    rows = MODES * slab
    main = levels * slab * low
    own_rows = low * low * levels
    shape = jax.ShapeDtypeStruct

    by = host_rows(GY, MODES)
    bx = host_rows(GX, MODES)
    by_rows = jnp.asarray(np.repeat(by, slab, axis=0))
    table = np.zeros((MODES, low, n, low, slab), ml_dtypes.bfloat16)
    for index in range(low):
        table[:, index, :, index, :] = bx.reshape(MODES, n, slab)
    table = table.reshape(MODES * low, rows)
    back = jnp.asarray(np.ascontiguousarray(table.T))
    table = jnp.asarray(table)

    def exchange(message):
        return lax.all_to_all(message, "gx", split_axis=0, concat_axis=0, tiled=True)

    group = lax.axis_index("groups").astype(jnp.int32).reshape(1)
    point_rows = pair_point[0]
    cells = pair_cell[:, 0, :]
    area_row = area.reshape(1, points)
    msg, pw = run(
        source_kernel,
        [shape((n, 2 * WIDTH, LANES), BF16), shape((n, LANES), F32)],
        [group, counts, point_rows, kernel[0], area_row, point_feats.T, spec_weight],
        2 * 80 * points * slots,
        smem=2,
    )
    rx = exchange(msg)
    col, lp, zr = run(
        functools.partial(place_kernel, depth),
        [shape((slots, LANES), F32), shape((rows, slots), BF16), shape((n, LANES), jnp.int32)],
        [cells, by_rows],
        2 * rows * LANES * slots,
    )
    other = lax.ppermute(rx[:, WIDTH : 2 * WIDTH, :], "groups", [(0, 1), (1, 0)])
    sum_scratch = [
        pltpu.VMEM((slots, 2 * LANES), BF16),
        pltpu.VMEM((slots, 2 * LANES), BF16),
        pltpu.VMEM((depth * WIDTH, slots), BF16),
    ]
    big = 2 * WIDTH * slots * slots + 2 * rows * slots * depth * WIDTH
    msg, lat = run(
        cell_kernel,
        [shape((n, main, LANES), BF16), shape((WIDTH, slots), BF16)],
        [rx, cells, zr, col, lp],
        big,
        scratch=[pltpu.VMEM((WIDTH, slots), BF16)] + sum_scratch,
    )
    columns = exchange(msg)
    msg, spec = run(
        mode_kernel,
        [shape((n, main, LANES), BF16), shape((n, own_rows, LANES), BF16)],
        [group, columns, rx, other, table, back],
        4 * MODES * low * rows * depth * WIDTH,
        scratch=[pltpu.VMEM((MODES * low * levels, LANES), F32)] * 2,
        smem=1,
    )
    slabs = exchange(msg)
    msg, pre = run(
        functools.partial(pre_kernel, depth),
        [shape((n, WIDTH, LANES), BF16), shape((WIDTH, slots), F32)],
        [slabs, lp, lat, cells, skip_weight, skip_bias.reshape(WIDTH, 1)],
        2 * rows * slots * depth * WIDTH,
        scratch=[pltpu.VMEM((depth * WIDTH, rows), BF16)],
    )
    returned = exchange(msg)
    (slope,) = run(slope_kernel, [shape(pre.shape, F32)], [pre], 100 * WIDTH * slots)
    out_col = out_weight.reshape(WIDTH, 1)
    pressure, part, head_pre = run(
        head_kernel,
        [shape((1, points), F32), shape((n, 1, LANES), F32), shape((WIDTH, points), F32)],
        [returned, point_rows, pw, head_weight, head_bias.reshape(WIDTH, 1), out_col, area_row, normals],
        2 * 3 * WIDTH * points * slots,
        scratch=[pltpu.VMEM((3 * WIDTH, slots), BF16), pltpu.VMEM((points, slots), BF16)],
    )
    parts = exchange(part)
    up, na, head = run(
        pair_kernel,
        [shape((WIDTH, slots), F32), shape((2, n, LANES), F32), shape((WIDTH, points), F32)],
        [head_pre, point_rows, head_weight, out_col, area_row, normals],
        2 * 208 * points * slots,
    )
    scale = 1.0 / math.sqrt(points * n)
    msg, forces, outp = run(
        functools.partial(grad_kernel, scale),
        [shape((n, WIDTH, LANES), BF16), shape((1, LANES), F32), shape((8, WIDTH), F32)],
        [targets, parts, up, na, pw, head, area_row, normals],
        10 * WIDTH * slots,
        smem=1,
    )
    grads = exchange(msg)
    (msg,) = run(
        back_kernel,
        [shape((n, main + 16, LANES), BF16)],
        [grads, cells, zr, col, lp, lat, slope, outp],
        big,
        scratch=[pltpu.VMEM((WIDTH, slots), BF16)] * 2 + sum_scratch,
    )
    grad_columns = exchange(msg)
    (msg,) = run(
        spec_kernel,
        [shape((n, 2 * own_rows + 16, LANES), BF16)],
        [grad_columns, table, spec],
        2 * MODES * low * rows * depth * WIDTH,
        scratch=[pltpu.VMEM((MODES * low * levels, LANES), F32)],
    )
    finals = exchange(msg)
    spec_grad, skip_grad, out_grad = run(
        final_kernel,
        [
            shape((spec_weight.shape[0], WIDTH, WIDTH), F32),
            shape((WIDTH, WIDTH), F32),
            shape((8, WIDTH), F32),
        ],
        [finals],
        2 * NMODE * WIDTH * WIDTH * depth // n,
    )
    return (pressure.reshape(points), forces[0, 0:2], spec_grad, skip_grad, out_grad[0])


def solution(mesh):
    fits = mesh.shape["gx"] == 16 and mesh.shape["groups"] == 2
    per_device = slab_step if fits else general_step
    in_specs = (
        P(("groups", "gx"), None),
        P(("groups", "gx"), None, None),
        P(None, ("groups", "gx"), None),
        P(("groups", "gx"), None, None),
        P(("groups", "gx"), None),
        P(("groups", "gx")),
        P(None, ("groups", "gx")),
        P("groups"),
        P("gx", None, None),
        P(),
        P(),
        P(),
        P(),
        P(),
    )
    out_specs = (
        P(("groups", "gx")),
        P("groups"),
        P(("groups", "gx"), None, None),
        P("groups", None),
        P("groups"),
    )
    return jax.shard_map(
        per_device, mesh=mesh, in_specs=in_specs, out_specs=out_specs, check_vma=False
    )
```

```python
import functools
import math

import jax
import jax.numpy as jnp
import ml_dtypes
import numpy as np
from jax import lax
from jax.experimental import pallas as pl
from jax.experimental.pallas import tpu as pltpu
from jax.sharding import PartitionSpec as P

GX = 128
GY = 128
MODES = 32
ZL = 1
NMODE = 1024


def fourier_rows(length, number):
    places = jnp.arange(length, dtype=jnp.float32)
    order = jnp.arange(number)
    half = number // 2
    freqs = jnp.where(order < half, order, order - half + 1).astype(jnp.float32)
    angles = 2.0 * math.pi / length * freqs[:, None] * places[None, :]
    table = jnp.where((order < half)[:, None], jnp.cos(angles), jnp.sin(angles))
    return (table * math.sqrt(2.0 / length)).astype(jnp.bfloat16)


def gelu_value(values):
    return 0.5 * values * (1.0 + lax.erf(values * (1.0 / math.sqrt(2.0))))


def gelu_slope(values):
    return 0.5 * (1.0 + lax.erf(values * (1.0 / math.sqrt(2.0)))) + values * jnp.exp(
        -0.5 * values * values
    ) * (1.0 / math.sqrt(2.0 * math.pi))


def general_step(
    point_feats,
    pair_point,
    pair_cell,
    kernel,
    counts,
    area,
    normals,
    targets,
    spec_weight,
    skip_weight,
    skip_bias,
    head_weight,
    head_bias,
    out_weight,
):
    devices = lax.axis_size("gx")
    local_points, width = point_feats.shape
    block_slots = pair_point.shape[2]
    row_count = GX // devices
    depth = ZL * devices
    slab_cells = row_count * GY * depth
    valid_mask = jnp.arange(block_slots)[None, :] < counts[0][:, None]
    point_rows = pair_point[0]
    pair_weight = jnp.where(valid_mask, kernel[0], jnp.float32(0.0))
    sender_weight = pair_weight * area[point_rows]
    contrib = (sender_weight[..., None] * point_feats[point_rows].astype(jnp.float32)).astype(
        jnp.bfloat16
    )
    arrived = lax.all_to_all(contrib, "gx", split_axis=0, concat_axis=0, tiled=True)
    cell_rows = pair_cell[:, 0, :].reshape(-1)
    latent = jax.ops.segment_sum(
        arrived.reshape(-1, width).astype(jnp.float32), cell_rows, num_segments=slab_cells
    ).astype(jnp.bfloat16)
    col_table = fourier_rows(GY, MODES)
    row_table = fourier_rows(GX, MODES)
    volume = latent.reshape(row_count, GY, depth * width)
    along_y = jnp.einsum(
        "by,xyk->xbk", col_table, volume, preferred_element_type=jnp.float32
    ).astype(jnp.bfloat16)
    columns = lax.all_to_all(along_y, "gx", split_axis=2, concat_axis=0, tiled=True)
    spectrum = jnp.einsum(
        "ax,xbk->abk", row_table, columns, preferred_element_type=jnp.float32
    ).astype(jnp.bfloat16)
    mode_rows = lax.all_to_all(
        spectrum.reshape(NMODE, ZL * width), "gx", split_axis=0, concat_axis=1, tiled=True
    )
    own_modes = mode_rows.shape[0]
    mixed_rows = jnp.einsum(
        "mzc,mcd->mzd",
        mode_rows.reshape(own_modes, depth, width),
        spec_weight,
        preferred_element_type=jnp.float32,
    ).astype(jnp.bfloat16)
    mixed = lax.all_to_all(
        mixed_rows.reshape(own_modes, depth * width), "gx", split_axis=1, concat_axis=0, tiled=True
    )
    back_x = jnp.einsum(
        "ax,abk->xbk",
        row_table,
        mixed.reshape(MODES, MODES, ZL * width),
        preferred_element_type=jnp.float32,
    ).astype(jnp.bfloat16)
    slabs = lax.all_to_all(back_x, "gx", split_axis=0, concat_axis=2, tiled=True)
    spatial = jnp.einsum(
        "by,xbk->xyk", col_table, slabs, preferred_element_type=jnp.float32
    ).reshape(slab_cells, width)
    pre = spatial + jnp.dot(latent, skip_weight, preferred_element_type=jnp.float32) + skip_bias
    features = gelu_value(pre).astype(jnp.bfloat16)
    picked = features[cell_rows].reshape(devices, block_slots, width)
    returned = lax.all_to_all(picked, "gx", split_axis=0, concat_axis=0, tiled=True)
    point_latent = jax.ops.segment_sum(
        (pair_weight[..., None] * returned.astype(jnp.float32)).reshape(-1, width),
        point_rows.reshape(-1),
        num_segments=local_points,
    )
    head_matrix = head_weight.astype(jnp.float32)
    head_pre = jnp.dot(point_latent, head_matrix, precision=lax.Precision.HIGHEST) + head_bias
    head = gelu_value(head_pre)
    pressure = jnp.dot(head, out_weight, precision=lax.Precision.HIGHEST)
    weighted = pressure * area
    scale = 1.0 / math.sqrt(local_points * devices)
    totals = lax.psum(
        jnp.stack([jnp.sum(weighted * normals[0]), jnp.sum(weighted * normals[1])]), "gx"
    )
    forces = scale * totals
    misfit = forces - targets
    point_grad = 2.0 * scale * (misfit[0] * normals[0] + misfit[1] * normals[1]) * area
    out_part = jnp.dot(point_grad, head, precision=lax.Precision.HIGHEST)
    head_grad = point_grad[:, None] * out_weight[None, :] * gelu_slope(head_pre)
    latent_grad = jnp.dot(head_grad, head_matrix.T, precision=lax.Precision.HIGHEST).astype(
        jnp.bfloat16
    )
    grad_pairs = (pair_weight[..., None] * latent_grad[point_rows].astype(jnp.float32)).astype(
        jnp.bfloat16
    )
    grad_arrived = lax.all_to_all(grad_pairs, "gx", split_axis=0, concat_axis=0, tiled=True)
    cell_grad = jax.ops.segment_sum(
        grad_arrived.reshape(-1, width).astype(jnp.float32), cell_rows, num_segments=slab_cells
    )
    pre_grad = (cell_grad * gelu_slope(pre)).astype(jnp.bfloat16)
    skip_part = jnp.dot(latent.T, pre_grad, preferred_element_type=jnp.float32)
    grad_y = jnp.einsum(
        "by,xyk->xbk",
        col_table,
        pre_grad.reshape(row_count, GY, depth * width),
        preferred_element_type=jnp.float32,
    ).astype(jnp.bfloat16)
    grad_columns = lax.all_to_all(grad_y, "gx", split_axis=2, concat_axis=0, tiled=True)
    grad_spec = jnp.einsum(
        "ax,xbk->abk", row_table, grad_columns, preferred_element_type=jnp.float32
    ).astype(jnp.bfloat16)
    grad_rows = lax.all_to_all(
        grad_spec.reshape(NMODE, ZL * width), "gx", split_axis=0, concat_axis=1, tiled=True
    )
    own_modes = grad_rows.shape[0]
    spec_grad = jnp.einsum(
        "mzc,mzd->mcd",
        mode_rows.reshape(own_modes, depth, width),
        grad_rows.reshape(own_modes, depth, width),
        preferred_element_type=jnp.float32,
    )
    out_grad, skip_grad = lax.psum((out_part, skip_part), "gx")
    return (pressure, forces, spec_grad, skip_grad, out_grad)


F32 = jnp.float32
BF16 = jnp.bfloat16
LANES = 128
WIDTH = 64


def host_rows(length, number):
    places = np.arange(length, dtype=np.float32)
    order = np.arange(number)
    half = number // 2
    freqs = np.where(order < half, order, order - half + 1).astype(np.float32)
    angles = np.float32(2.0 * math.pi / length) * freqs[:, None] * places[None, :]
    table = np.where((order < half)[:, None], np.cos(angles), np.sin(angles))
    table = table.astype(np.float32) * np.float32(math.sqrt(2.0 / length))
    return table.astype(ml_dtypes.bfloat16)


def three_parts(values):
    first = values.astype(BF16)
    rest = values - first.astype(F32)
    second = rest.astype(BF16)
    third = (rest - second.astype(F32)).astype(BF16)
    return first, second, third


def mm(left, right):
    return jnp.dot(left, right, preferred_element_type=F32)


def mm_nt(left, right):
    return lax.dot_general(left, right, (((1,), (1,)), ((), ())), preferred_element_type=F32)


def mm_tn(left, right):
    return lax.dot_general(left, right, (((0,), (0,)), ((), ())), preferred_element_type=F32)


def two_rows(ref, pair):
    return jnp.concatenate([ref[2 * pair : 2 * pair + 1, :], ref[2 * pair + 1 : 2 * pair + 2, :]], axis=1)


def source_kernel(group_ref, count_hbm, point_hbm, kern_hbm, area_hbm, feat_hbm, weight_hbm, msg_ref, pw_ref, count_ref, point_ref, kern_ref, area_ref, feat_ref, weight_ref, sems):
    devices, points = point_ref.shape[0], feat_ref.shape[1]
    low = MODES // devices
    pieces = (
        (point_hbm, point_ref),
        (area_hbm, area_ref),
        (feat_hbm, feat_ref),
        (kern_hbm, kern_ref),
        (count_hbm, count_ref),
        (weight_hbm.at[pl.ds(group_ref[0] * MODES, MODES)], weight_ref),
    )
    copies = [
        pltpu.make_async_copy(source, place, sems.at[index])
        for index, (source, place) in enumerate(pieces)
    ]
    for copy in copies:
        copy.start()
    for copy in copies[:-1]:
        copy.wait()
    first, second, third = three_parts(area_ref[...])
    place = lax.broadcasted_iota(jnp.int32, (16, points), 0)
    extra = jnp.where(
        place == 0,
        first.astype(F32),
        jnp.where(place == 1, second.astype(F32), jnp.where(place == 2, third.astype(F32), 0.0)),
    ).astype(BF16)
    table = jnp.concatenate([feat_ref[...], extra], axis=0)
    rows = lax.broadcasted_iota(jnp.int32, (points, 2 * LANES), 0)
    lane = lax.broadcasted_iota(jnp.int32, (1, LANES), 1)
    for pair in range(devices // 2):
        hot = jnp.where(rows == two_rows(point_ref, pair), 1.0, 0.0).astype(BF16)
        got = mm(table, hot)
        spread = got[WIDTH : WIDTH + 1] + got[WIDTH + 1 : WIDTH + 2] + got[WIDTH + 2 : WIDTH + 3]
        for half in range(2):
            dest = 2 * pair + half
            cut = slice(half * LANES, (half + 1) * LANES)
            valid = lane < count_ref[0:1, dest : dest + 1]
            weight = jnp.where(valid, kern_ref[dest : dest + 1, :], 0.0)
            pw_ref[dest : dest + 1, :] = weight
            msg_ref[dest, 0:WIDTH, :] = ((weight * spread[:, cut]) * got[0:WIDTH, cut]).astype(BF16)
    copies[-1].wait()
    for dest in range(devices):
        msg_ref[dest, WIDTH : 2 * WIDTH, :] = jnp.concatenate(
            [weight_ref[low * dest], weight_ref[low * dest + 1]], axis=1
        )


def place_kernel(depth, cell_ref, by_ref, same_ref, lp_ref, zr_ref, col_ref):
    devices = cell_ref.shape[0]
    zbits = depth.bit_length() - 1
    rows = by_ref.shape[0]
    slab = rows // MODES
    yrow = lax.broadcasted_iota(jnp.int32, (GY, LANES), 0)
    xrow = jnp.bitwise_and(lax.broadcasted_iota(jnp.int32, (rows, LANES), 0), slab - 1)
    up = lax.broadcasted_iota(jnp.int32, (LANES, LANES), 0) < lax.broadcasted_iota(
        jnp.int32, (LANES, LANES), 1
    )
    for block in range(devices):
        cells = cell_ref[block : block + 1, :]
        cut = slice(block * LANES, (block + 1) * LANES)
        col_ref[cut, :] = jnp.broadcast_to(cells.astype(F32), (LANES, LANES)).T
        ypos = jnp.bitwise_and(jnp.right_shift(cells, zbits), GY - 1)
        xpos = jnp.right_shift(cells, zbits + GY.bit_length() - 1)
        hot = jnp.where(yrow == ypos, 1.0, 0.0).astype(BF16)
        lp_ref[:, cut] = jnp.where(xrow == xpos, mm(by_ref[...], hot), 0.0).astype(BF16)
    for block in range(devices):
        cells = cell_ref[block : block + 1, :]
        row = cells.astype(F32)
        cut = slice(block * LANES, (block + 1) * LANES)
        same = jnp.where(jnp.logical_and(col_ref[cut, :] == row, up), 1.0, 0.0)
        seen = jnp.max(same, axis=0, keepdims=True)
        if block:
            before = jnp.where(col_ref[0 : block * LANES, :] == row, 1.0, 0.0)
            seen = jnp.maximum(seen, jnp.max(before, axis=0, keepdims=True))
        zr_ref[block : block + 1, :] = jnp.where(
            seen > 0.0, -1, jnp.bitwise_and(cells, depth - 1)
        )
    equal_cells(cell_ref, col_ref, same_ref)


def equal_cells(cell_ref, col_ref, same_ref):
    for block in range(cell_ref.shape[0]):
        row = cell_ref[block : block + 1, :].astype(F32)
        same_ref[:, block * LANES : (block + 1) * LANES] = jnp.where(
            col_ref[...] == row, 1.0, 0.0
        ).astype(BF16)


def same_kernel(cell_ref, after_ref, same_ref, col_ref):
    for block in range(cell_ref.shape[0]):
        row = cell_ref[block : block + 1, :].astype(F32)
        cut = slice(block * LANES, (block + 1) * LANES)
        col_ref[cut, :] = jnp.broadcast_to(row, (LANES, LANES)).T
    equal_cells(cell_ref, col_ref, same_ref)


def spread_depth(values, zpos, rp_ref, pair):
    cut = slice(pair * 2 * LANES, (pair + 1) * 2 * LANES)
    for level in range(rp_ref.shape[0] // WIDTH):
        rp_ref[level * WIDTH : (level + 1) * WIDTH, cut] = jnp.where(
            zpos == level, values, 0.0
        ).astype(BF16)


def slab_rows(lp_ref, rp_ref, msg_ref):
    devices = msg_ref.shape[0]
    step = lp_ref.shape[0] // devices
    for quad in range(rp_ref.shape[0] // (4 * WIDTH)):
        out = mm_nt(lp_ref[...], rp_ref[quad * 4 * WIDTH : (quad + 1) * 4 * WIDTH, :]).astype(BF16)
        for half in range(2):
            level = 2 * quad + half
            for dest in range(devices):
                msg_ref[dest, level * step : (level + 1) * step, :] = out[
                    dest * step : (dest + 1) * step, half * LANES : (half + 1) * LANES
                ]


def cell_kernel(rx_ref, same_ref, zr_ref, lp_ref, msg_ref, lat_ref, xs_ref, rp_ref):
    devices = rx_ref.shape[0]
    for block in range(devices):
        xs_ref[:, block * LANES : (block + 1) * LANES] = rx_ref[block, 0:WIDTH, :]
    for pair in range(devices // 2):
        cut = slice(pair * 2 * LANES, (pair + 1) * 2 * LANES)
        latent = mm(xs_ref[...], same_ref[:, cut])
        lat_ref[:, cut] = latent.astype(BF16)
        spread_depth(latent, two_rows(zr_ref, pair), rp_ref, pair)
    slab_rows(lp_ref, rp_ref, msg_ref)


def to_modes(rx_ref, table_ref, sp_ref):
    levels = sp_ref.shape[0] // table_ref.shape[0]
    step = table_ref.shape[1] // rx_ref.shape[0]
    for level in range(levels):
        block = rx_ref[:, level * step : (level + 1) * step, :].reshape(table_ref.shape[1], LANES)
        coeffs = mm(table_ref[...], block).astype(BF16).astype(F32)
        sp_ref[pl.ds(level, table_ref.shape[0], stride=levels), :] = coeffs


def swap_halves(values):
    return pltpu.roll(values, WIDTH, 1)


def mode_kernel(group_ref, rx_ref, own_ref, other_ref, table_ref, back_ref, msg_ref, spec_ref, sp_ref, mx_ref):
    devices = rx_ref.shape[0]
    own_rows = spec_ref.shape[1]
    modes = table_ref.shape[0]
    levels = sp_ref.shape[0] // modes
    step = back_ref.shape[0] // devices
    to_modes(rx_ref, table_ref, sp_ref)
    for dest in range(devices):
        spec_ref[dest] = sp_ref[dest * own_rows : (dest + 1) * own_rows, :].astype(BF16)
    left = lax.broadcasted_iota(jnp.int32, (levels, LANES), 1) < WIDTH
    for order in range(MODES):
        source, which = order // 2, order % 2
        mine = jnp.full((WIDTH, LANES), group_ref[0], jnp.int32) == which
        weight = jnp.where(
            mine,
            own_ref[source, WIDTH : 2 * WIDTH, :].astype(F32),
            other_ref[source].astype(F32),
        ).astype(BF16)
        at = order * 2 * levels
        even = sp_ref[at : at + levels, :]
        odd = sp_ref[at + levels : at + 2 * levels, :]
        rows = jnp.concatenate([even, swap_halves(even), odd, swap_halves(odd)], axis=0)
        out = mm(rows[:, 0:WIDTH].astype(BF16), weight)
        mx_ref[at : at + levels, :] = jnp.where(
            left, out[0:levels], swap_halves(out[levels : 2 * levels])
        )
        mx_ref[at + levels : at + 2 * levels, :] = jnp.where(
            left, swap_halves(out[2 * levels : 3 * levels]), out[3 * levels : 4 * levels]
        )
    for level in range(levels):
        mixed = mx_ref[pl.ds(level, modes, stride=levels), :].astype(BF16)
        out = mm(back_ref[...], mixed).astype(BF16)
        for dest in range(devices):
            msg_ref[dest, level * step : (level + 1) * step, :] = out[dest * step : (dest + 1) * step]


def pre_kernel(depth, rx_ref, lp_ref, lat_ref, cell_ref, skip_ref, bias_ref, msg_ref, pre_ref, rt_ref):
    devices = rx_ref.shape[0]
    rows = lp_ref.shape[0]
    step = rows // devices
    for level in range(rt_ref.shape[0] // LANES):
        block = rx_ref[:, level * step : (level + 1) * step, :].reshape(rows, LANES)
        rt_ref[level * LANES : (level + 1) * LANES, :] = block.T
    for pair in range(devices // 2):
        cut = slice(pair * 2 * LANES, (pair + 1) * 2 * LANES)
        zpos = jnp.bitwise_and(two_rows(cell_ref, pair), depth - 1)
        field = mm(rt_ref[...], lp_ref[:, cut])
        total = jnp.where(zpos == 0, field[0:WIDTH], 0.0)
        for level in range(1, depth):
            total += jnp.where(zpos == level, field[level * WIDTH : (level + 1) * WIDTH], 0.0)
        pre = total + mm_tn(skip_ref[...], lat_ref[:, cut]) + bias_ref[...]
        pre_ref[:, cut] = pre
        feats = gelu_value(pre).astype(BF16)
        for half in range(2):
            msg_ref[2 * pair + half] = feats[:, half * LANES : (half + 1) * LANES]


def slope_kernel(pre_ref, slope_ref):
    slope_ref[...] = gelu_slope(pre_ref[...])


def head_kernel(rx_ref, point_ref, pw_ref, head_ref, bias_ref, out_ref, area_ref, normal_ref, pres_ref, msg_ref, value_ref, hot_ref):
    devices = rx_ref.shape[0]
    points = area_ref.shape[1]
    rows = lax.broadcasted_iota(jnp.int32, (points, LANES), 0)
    for block in range(devices):
        cut = slice(block * LANES, (block + 1) * LANES)
        parts = three_parts(pw_ref[block : block + 1, :] * rx_ref[block].astype(F32))
        for index, part in enumerate(parts):
            value_ref[index * WIDTH : (index + 1) * WIDTH, cut] = part
        hot_ref[:, cut] = jnp.where(rows == point_ref[block : block + 1, :], 1.0, 0.0).astype(BF16)
    sums = mm_nt(value_ref[...], hot_ref[...])
    latent = sums[0:WIDTH] + sums[WIDTH : 2 * WIDTH] + sums[2 * WIDTH : 3 * WIDTH]
    first, second, third = three_parts(latent)
    weight = head_ref[...]
    head_pre = mm_tn(weight, first) + mm_tn(weight, second) + mm_tn(weight, third) + bias_ref[...]
    head = gelu_value(head_pre)
    pressure = jnp.sum(head * out_ref[...], axis=0, keepdims=True)
    pres_ref[...] = pressure
    along = [normal_ref[which : which + 1, :] * area_ref[...] for which in range(2)]
    first, second, third = three_parts(out_ref[...] * gelu_slope(head_pre))
    grad = mm(weight, first) + mm(weight, second) + mm(weight, third)
    place = lax.broadcasted_iota(jnp.int32, (16, points), 0)
    extra = jnp.zeros((16, points), F32)
    for which in range(2):
        for index, part in enumerate(three_parts(along[which])):
            extra = jnp.where(place == 3 + 3 * which + index, part.astype(F32), extra)
    upper = grad.astype(BF16)
    lower = (grad - upper.astype(F32)).astype(BF16)
    table = jnp.concatenate([upper, lower, extra.astype(BF16)], axis=0)
    lane = lax.broadcasted_iota(jnp.int32, (1, LANES), 1)
    partial = []
    for which in range(2):
        force = jnp.sum(pressure * area_ref[...] * normal_ref[which : which + 1, :], axis=1, keepdims=True)
        partial.append(force)
    force_row = jnp.where(lane == 0, partial[0], jnp.where(lane == 1, partial[1], 0.0))
    out_rows = lax.dot_general(
        jnp.concatenate([along[0], along[1], jnp.zeros((6, points), F32)], axis=0),
        head,
        (((1,), (1,)), ((), ())),
        precision=lax.Precision.HIGHEST,
        preferred_element_type=F32,
    )
    out_row = jnp.concatenate([out_rows[0:1], out_rows[1:2]], axis=1)
    place = lax.broadcasted_iota(jnp.int32, (16, LANES), 0)
    common = jnp.zeros((16, LANES), F32)
    for index, part in enumerate(three_parts(out_row)):
        common = jnp.where(place == 9 + index, part.astype(F32), common)
    for index, part in enumerate(three_parts(force_row)):
        common = jnp.where(place == 12 + index, part.astype(F32), common)
    for block in range(devices):
        cut = slice(block * LANES, (block + 1) * LANES)
        got = mm(table, hot_ref[:, cut])
        msg_ref[block, 0 : 2 * WIDTH, :] = got[0 : 2 * WIDTH].astype(BF16)
        tail = got[2 * WIDTH : 2 * WIDTH + 16] + common
        for index, part in enumerate(three_parts(pw_ref[block : block + 1, :])):
            tail = jnp.where(place == index, part.astype(F32), tail)
        msg_ref[block, 2 * WIDTH : 2 * WIDTH + 16, :] = tail.astype(BF16)


def fold_rows(values):
    first, second, third = three_parts(values)
    upper = jnp.concatenate([first.astype(F32), second.astype(F32)], axis=1)
    lower = jnp.concatenate([third.astype(F32), jnp.zeros_like(values)], axis=1)
    return upper, lower


def back_kernel(scale, rx_ref, target_ref, same_ref, zr_ref, lp_ref, lat_ref, slope_ref, msg_ref, force_ref, outg_ref, xs_ref, pg_ref, rp_ref):
    devices = rx_ref.shape[0]
    main = lp_ref.shape[0] // devices * (rp_ref.shape[0] // LANES)
    extra = slice(2 * WIDTH, 2 * WIDTH + 16)
    total = rx_ref[0, extra, :].astype(F32)
    for block in range(1, devices):
        total += rx_ref[block, extra, :].astype(F32)
    forces = scale * (total[12:13] + total[13:14] + total[14:15])
    force_ref[...] = forces[:, 0:2]
    misfit = forces[:, 0:2] - target_ref[...]
    drag, lift = misfit[:, 0:1], misfit[:, 1:2]
    twice = 2.0 * scale
    out_row = total[9:10] + total[10:11] + total[11:12]
    outg_ref[...] = twice * (drag * out_row[:, 0:WIDTH] + lift * out_row[:, WIDTH : 2 * WIDTH])
    for block in range(devices):
        tail = rx_ref[block, extra, :].astype(F32)
        weight, first, second = (
            tail[at : at + 1] + tail[at + 1 : at + 2] + tail[at + 2 : at + 3] for at in (0, 3, 6)
        )
        grad = rx_ref[block, 0:WIDTH, :].astype(F32) + rx_ref[block, WIDTH : 2 * WIDTH, :].astype(F32)
        along = twice * (drag * first + lift * second)
        grad = (along * grad).astype(BF16).astype(F32)
        xs_ref[:, block * LANES : (block + 1) * LANES] = (weight * grad).astype(BF16)
    for pair in range(devices // 2):
        cut = slice(pair * 2 * LANES, (pair + 1) * 2 * LANES)
        grad = mm(xs_ref[...], same_ref[:, cut]) * slope_ref[:, cut]
        zpos = two_rows(zr_ref, pair)
        pg_ref[:, cut] = jnp.where(zpos >= 0, grad, 0.0).astype(BF16)
        spread_depth(grad, zpos, rp_ref, pair)
    slab_rows(lp_ref, rp_ref, msg_ref)
    upper, lower = fold_rows(mm_nt(lat_ref[...], pg_ref[...]))
    blocks = upper.shape[0] // 8
    for dest in range(devices):
        if dest < blocks:
            cut = slice(8 * dest, 8 * dest + 8)
            rows = jnp.concatenate([upper[cut], lower[cut]], axis=0)
        else:
            rows = jnp.zeros((16, LANES), F32)
        msg_ref[dest, main : main + 16, :] = rows.astype(BF16)


def spec_kernel(rx_ref, table_ref, spec_ref, msg_ref, sp_ref):
    devices = rx_ref.shape[0]
    own_rows = spec_ref.shape[1]
    main = rx_ref.shape[1] - 16
    to_modes(rx_ref, table_ref, sp_ref)
    total = rx_ref[0, main : main + 16, :].astype(F32)
    for source in range(1, devices):
        total += rx_ref[source, main : main + 16, :].astype(F32)
    upper, lower = total[0:8], total[8:16]
    left = lax.broadcasted_iota(jnp.int32, (8, LANES), 1) < WIDTH
    value = jnp.where(left, upper + swap_halves(upper) + lower, 0.0)
    first, second, third = three_parts(value)
    upper = first.astype(F32) + swap_halves(second.astype(F32))
    rows = jnp.concatenate([upper, third.astype(F32)], axis=0).astype(BF16)
    for dest in range(devices):
        msg_ref[dest, 0:own_rows, :] = spec_ref[dest]
        msg_ref[dest, own_rows : 2 * own_rows, :] = sp_ref[
            dest * own_rows : (dest + 1) * own_rows, :
        ].astype(BF16)
        msg_ref[dest, 2 * own_rows : 2 * own_rows + 16, :] = rows


def final_kernel(rx_ref, spec_ref, skip_ref):
    devices = rx_ref.shape[0]
    own_rows = (rx_ref.shape[1] - 16) // 2
    for source in range(devices):
        for which in range(own_rows // 16):
            at = which * 16
            coeffs = rx_ref[source, at : at + 16, :].astype(F32)
            grads = rx_ref[source, own_rows + at : own_rows + at + 16, :].astype(F32)
            for low in range(2):
                cut = slice(8 * low, 8 * low + 8)
                left, right = coeffs[cut], grads[cut]
                left = jnp.concatenate([left, swap_halves(left)], axis=0)[:, 0:WIDTH]
                right = jnp.concatenate([right, swap_halves(right)], axis=0)[:, 0:WIDTH]
                spec_ref[which * MODES + 2 * source + low] = mm_tn(
                    left.astype(BF16), right.astype(BF16)
                )
    for source in range(WIDTH // 8):
        rows = rx_ref[source, 2 * own_rows : 2 * own_rows + 16, :].astype(F32)
        value = (rows[0:8] + swap_halves(rows[0:8]) + rows[8:16])[:, 0:WIDTH]
        skip_ref[8 * source : 8 * source + 8, :] = value


def run(kernel, outs, ins, flops, scratch=(), smem=0, hbm=False, grant=16):
    vmem = pl.BlockSpec(memory_space=pltpu.VMEM)
    rest = pl.BlockSpec(memory_space=pltpu.HBM) if hbm else vmem
    moved = sum(math.prod(a.shape) * a.dtype.itemsize for a in list(ins) + list(outs))
    return pl.pallas_call(
        kernel,
        out_shape=tuple(outs),
        in_specs=[pl.BlockSpec(memory_space=pltpu.SMEM)] * smem + [rest] * (len(ins) - smem),
        out_specs=tuple([vmem] * len(outs)),
        scratch_shapes=list(scratch),
        compiler_params=pltpu.CompilerParams(vmem_limit_bytes=grant * 1024 * 1024),
        cost_estimate=pl.CostEstimate(flops=flops, bytes_accessed=moved, transcendentals=0),
    )(*ins)


def slab_step(
    point_feats,
    pair_point,
    pair_cell,
    kernel,
    counts,
    area,
    normals,
    targets,
    spec_weight,
    skip_weight,
    skip_bias,
    head_weight,
    head_bias,
    out_weight,
):
    n = lax.axis_size("gx")
    points = point_feats.shape[0]
    slots = n * LANES
    slab = GX // n
    low = MODES // n
    depth = ZL * n
    levels = depth * WIDTH // LANES
    rows = MODES * slab
    main = levels * slab * low
    own_rows = low * low * levels
    shape = jax.ShapeDtypeStruct

    by = host_rows(GY, MODES)
    bx = host_rows(GX, MODES)
    by_rows = jnp.asarray(np.repeat(by, slab, axis=0))
    table = np.zeros((MODES, low, n, low, slab), ml_dtypes.bfloat16)
    for index in range(low):
        table[:, index, :, index, :] = bx.reshape(MODES, n, slab)
    table = table.reshape(MODES * low, rows)
    back = jnp.asarray(np.ascontiguousarray(table.T))
    table = jnp.asarray(table)

    def exchange(message):
        return lax.all_to_all(message, "gx", split_axis=0, concat_axis=0, tiled=True)

    group = lax.axis_index("groups").astype(jnp.int32).reshape(1)
    point_rows = pair_point[0]
    cells = pair_cell[:, 0, :]
    area_row = area.reshape(1, points)
    msg, pw = run(
        source_kernel,
        [shape((n, 2 * WIDTH, LANES), BF16), shape((n, LANES), F32)],
        [group, counts, point_rows, kernel[0], area_row, point_feats.T, spec_weight],
        2 * 80 * points * slots,
        scratch=[
            pltpu.VMEM((1, n), jnp.int32),
            pltpu.VMEM((n, LANES), jnp.int32),
            pltpu.VMEM((n, LANES), F32),
            pltpu.VMEM((1, points), F32),
            pltpu.VMEM((WIDTH, points), BF16),
            pltpu.VMEM((MODES, WIDTH, WIDTH), BF16),
            pltpu.SemaphoreType.DMA((6,)),
        ],
        smem=1,
        hbm=True,
    )
    rx = exchange(msg)
    columns_scratch = pltpu.VMEM((slots, LANES), F32)
    same, lp, zr = run(
        functools.partial(place_kernel, depth),
        [shape((slots, slots), BF16), shape((rows, slots), BF16), shape((n, LANES), jnp.int32)],
        [cells, by_rows],
        2 * rows * LANES * slots,
        scratch=[columns_scratch],
    )
    other = lax.ppermute(rx[:, WIDTH : 2 * WIDTH, :], "groups", [(0, 1), (1, 0)])
    pair_rows = pltpu.VMEM((WIDTH, slots), BF16)
    deep_rows = pltpu.VMEM((depth * WIDTH, slots), BF16)
    big = 2 * WIDTH * slots * slots + 2 * rows * slots * depth * WIDTH
    msg, lat = run(
        cell_kernel,
        [shape((n, main, LANES), BF16), shape((WIDTH, slots), BF16)],
        [rx, same, zr, lp],
        big,
        scratch=[pair_rows, deep_rows],
    )
    columns = exchange(msg)
    msg, spec = run(
        mode_kernel,
        [shape((n, main, LANES), BF16), shape((n, own_rows, LANES), BF16)],
        [group, columns, rx, other, table, back],
        4 * MODES * low * rows * depth * WIDTH,
        scratch=[pltpu.VMEM((MODES * low * levels, LANES), F32)] * 2,
        smem=1,
    )
    slabs = exchange(msg)
    msg, pre = run(
        functools.partial(pre_kernel, depth),
        [shape((n, WIDTH, LANES), BF16), shape((WIDTH, slots), F32)],
        [slabs, lp, lat, cells, skip_weight, skip_bias.reshape(WIDTH, 1)],
        2 * rows * slots * depth * WIDTH,
        scratch=[pltpu.VMEM((depth * WIDTH, rows), BF16)],
    )
    returned = exchange(msg)
    (slope,) = run(slope_kernel, [shape(pre.shape, F32)], [pre], 100 * WIDTH * slots)
    out_col = out_weight.reshape(WIDTH, 1)
    pressure, msg = run(
        head_kernel,
        [shape((1, points), F32), shape((n, 2 * WIDTH + 16, LANES), BF16)],
        [returned, point_rows, pw, head_weight, head_bias.reshape(WIDTH, 1), out_col, area_row, normals],
        2 * 3 * WIDTH * points * slots,
        scratch=[pltpu.VMEM((3 * WIDTH, slots), BF16), pltpu.VMEM((points, slots), BF16)],
    )
    grads = exchange(msg)
    (same,) = run(
        same_kernel,
        [shape((slots, slots), BF16)],
        [cells, pressure],
        2 * slots * slots,
        scratch=[columns_scratch],
    )
    scale = 1.0 / math.sqrt(points * n)
    msg, forces, out_grad = run(
        functools.partial(back_kernel, scale),
        [shape((n, main + 16, LANES), BF16), shape((1, 2), F32), shape((1, WIDTH), F32)],
        [grads, targets.reshape(1, 2), same, zr, lp, lat, slope],
        big,
        scratch=[pair_rows, pair_rows, deep_rows],
    )
    grad_columns = exchange(msg)
    (msg,) = run(
        spec_kernel,
        [shape((n, 2 * own_rows + 16, LANES), BF16)],
        [grad_columns, table, spec],
        2 * MODES * low * rows * depth * WIDTH,
        scratch=[pltpu.VMEM((MODES * low * levels, LANES), F32)],
    )
    finals = exchange(msg)
    spec_grad, skip_grad = run(
        final_kernel,
        [shape((spec_weight.shape[0], WIDTH, WIDTH), F32), shape((WIDTH, WIDTH), F32)],
        [finals],
        2 * NMODE * WIDTH * WIDTH * depth // n,
    )
    return (pressure.reshape(points), forces.reshape(2), spec_grad, skip_grad, out_grad.reshape(WIDTH))


def solution(mesh):
    fits = mesh.shape["gx"] == 16 and mesh.shape["groups"] == 2
    per_device = slab_step if fits else general_step
    in_specs = (
        P(("groups", "gx"), None),
        P(("groups", "gx"), None, None),
        P(None, ("groups", "gx"), None),
        P(("groups", "gx"), None, None),
        P(("groups", "gx"), None),
        P(("groups", "gx")),
        P(None, ("groups", "gx")),
        P("groups"),
        P("gx", None, None),
        P(),
        P(),
        P(),
        P(),
        P(),
    )
    out_specs = (
        P(("groups", "gx")),
        P("groups"),
        P(("groups", "gx"), None, None),
        P("groups", None),
        P("groups"),
    )
    return jax.shard_map(
        per_device, mesh=mesh, in_specs=in_specs, out_specs=out_specs, check_vma=False
    )
```

```python
import functools
import math

import jax
import jax.numpy as jnp
import ml_dtypes
import numpy as np
from jax import lax
from jax.experimental import pallas as pl
from jax.experimental.pallas import tpu as pltpu
from jax.sharding import PartitionSpec as P

GX = 128
GY = 128
MODES = 32
ZL = 1
NMODE = 1024


def fourier_rows(length, number):
    places = jnp.arange(length, dtype=jnp.float32)
    order = jnp.arange(number)
    half = number // 2
    freqs = jnp.where(order < half, order, order - half + 1).astype(jnp.float32)
    angles = 2.0 * math.pi / length * freqs[:, None] * places[None, :]
    table = jnp.where((order < half)[:, None], jnp.cos(angles), jnp.sin(angles))
    return (table * math.sqrt(2.0 / length)).astype(jnp.bfloat16)


def gelu_value(values):
    return 0.5 * values * (1.0 + lax.erf(values * (1.0 / math.sqrt(2.0))))


def gelu_slope(values):
    return 0.5 * (1.0 + lax.erf(values * (1.0 / math.sqrt(2.0)))) + values * jnp.exp(
        -0.5 * values * values
    ) * (1.0 / math.sqrt(2.0 * math.pi))


def general_step(
    point_feats,
    pair_point,
    pair_cell,
    kernel,
    counts,
    area,
    normals,
    targets,
    spec_weight,
    skip_weight,
    skip_bias,
    head_weight,
    head_bias,
    out_weight,
):
    devices = lax.axis_size("gx")
    local_points, width = point_feats.shape
    block_slots = pair_point.shape[2]
    row_count = GX // devices
    depth = ZL * devices
    slab_cells = row_count * GY * depth
    valid_mask = jnp.arange(block_slots)[None, :] < counts[0][:, None]
    point_rows = pair_point[0]
    pair_weight = jnp.where(valid_mask, kernel[0], jnp.float32(0.0))
    sender_weight = pair_weight * area[point_rows]
    contrib = (sender_weight[..., None] * point_feats[point_rows].astype(jnp.float32)).astype(
        jnp.bfloat16
    )
    arrived = lax.all_to_all(contrib, "gx", split_axis=0, concat_axis=0, tiled=True)
    cell_rows = pair_cell[:, 0, :].reshape(-1)
    latent = jax.ops.segment_sum(
        arrived.reshape(-1, width).astype(jnp.float32), cell_rows, num_segments=slab_cells
    ).astype(jnp.bfloat16)
    col_table = fourier_rows(GY, MODES)
    row_table = fourier_rows(GX, MODES)
    volume = latent.reshape(row_count, GY, depth * width)
    along_y = jnp.einsum(
        "by,xyk->xbk", col_table, volume, preferred_element_type=jnp.float32
    ).astype(jnp.bfloat16)
    columns = lax.all_to_all(along_y, "gx", split_axis=2, concat_axis=0, tiled=True)
    spectrum = jnp.einsum(
        "ax,xbk->abk", row_table, columns, preferred_element_type=jnp.float32
    ).astype(jnp.bfloat16)
    mode_rows = lax.all_to_all(
        spectrum.reshape(NMODE, ZL * width), "gx", split_axis=0, concat_axis=1, tiled=True
    )
    own_modes = mode_rows.shape[0]
    mixed_rows = jnp.einsum(
        "mzc,mcd->mzd",
        mode_rows.reshape(own_modes, depth, width),
        spec_weight,
        preferred_element_type=jnp.float32,
    ).astype(jnp.bfloat16)
    mixed = lax.all_to_all(
        mixed_rows.reshape(own_modes, depth * width), "gx", split_axis=1, concat_axis=0, tiled=True
    )
    back_x = jnp.einsum(
        "ax,abk->xbk",
        row_table,
        mixed.reshape(MODES, MODES, ZL * width),
        preferred_element_type=jnp.float32,
    ).astype(jnp.bfloat16)
    slabs = lax.all_to_all(back_x, "gx", split_axis=0, concat_axis=2, tiled=True)
    spatial = jnp.einsum(
        "by,xbk->xyk", col_table, slabs, preferred_element_type=jnp.float32
    ).reshape(slab_cells, width)
    pre = spatial + jnp.dot(latent, skip_weight, preferred_element_type=jnp.float32) + skip_bias
    features = gelu_value(pre).astype(jnp.bfloat16)
    picked = features[cell_rows].reshape(devices, block_slots, width)
    returned = lax.all_to_all(picked, "gx", split_axis=0, concat_axis=0, tiled=True)
    point_latent = jax.ops.segment_sum(
        (pair_weight[..., None] * returned.astype(jnp.float32)).reshape(-1, width),
        point_rows.reshape(-1),
        num_segments=local_points,
    )
    head_matrix = head_weight.astype(jnp.float32)
    head_pre = jnp.dot(point_latent, head_matrix, precision=lax.Precision.HIGHEST) + head_bias
    head = gelu_value(head_pre)
    pressure = jnp.dot(head, out_weight, precision=lax.Precision.HIGHEST)
    weighted = pressure * area
    scale = 1.0 / math.sqrt(local_points * devices)
    totals = lax.psum(
        jnp.stack([jnp.sum(weighted * normals[0]), jnp.sum(weighted * normals[1])]), "gx"
    )
    forces = scale * totals
    misfit = forces - targets
    point_grad = 2.0 * scale * (misfit[0] * normals[0] + misfit[1] * normals[1]) * area
    out_part = jnp.dot(point_grad, head, precision=lax.Precision.HIGHEST)
    head_grad = point_grad[:, None] * out_weight[None, :] * gelu_slope(head_pre)
    latent_grad = jnp.dot(head_grad, head_matrix.T, precision=lax.Precision.HIGHEST).astype(
        jnp.bfloat16
    )
    grad_pairs = (pair_weight[..., None] * latent_grad[point_rows].astype(jnp.float32)).astype(
        jnp.bfloat16
    )
    grad_arrived = lax.all_to_all(grad_pairs, "gx", split_axis=0, concat_axis=0, tiled=True)
    cell_grad = jax.ops.segment_sum(
        grad_arrived.reshape(-1, width).astype(jnp.float32), cell_rows, num_segments=slab_cells
    )
    pre_grad = (cell_grad * gelu_slope(pre)).astype(jnp.bfloat16)
    skip_part = jnp.dot(latent.T, pre_grad, preferred_element_type=jnp.float32)
    grad_y = jnp.einsum(
        "by,xyk->xbk",
        col_table,
        pre_grad.reshape(row_count, GY, depth * width),
        preferred_element_type=jnp.float32,
    ).astype(jnp.bfloat16)
    grad_columns = lax.all_to_all(grad_y, "gx", split_axis=2, concat_axis=0, tiled=True)
    grad_spec = jnp.einsum(
        "ax,xbk->abk", row_table, grad_columns, preferred_element_type=jnp.float32
    ).astype(jnp.bfloat16)
    grad_rows = lax.all_to_all(
        grad_spec.reshape(NMODE, ZL * width), "gx", split_axis=0, concat_axis=1, tiled=True
    )
    own_modes = grad_rows.shape[0]
    spec_grad = jnp.einsum(
        "mzc,mzd->mcd",
        mode_rows.reshape(own_modes, depth, width),
        grad_rows.reshape(own_modes, depth, width),
        preferred_element_type=jnp.float32,
    )
    out_grad, skip_grad = lax.psum((out_part, skip_part), "gx")
    return (pressure, forces, spec_grad, skip_grad, out_grad)


F32 = jnp.float32
BF16 = jnp.bfloat16
LANES = 128
WIDTH = 64


def host_rows(length, number):
    places = np.arange(length, dtype=np.float32)
    order = np.arange(number)
    half = number // 2
    freqs = np.where(order < half, order, order - half + 1).astype(np.float32)
    angles = np.float32(2.0 * math.pi / length) * freqs[:, None] * places[None, :]
    table = np.where((order < half)[:, None], np.cos(angles), np.sin(angles))
    table = table.astype(np.float32) * np.float32(math.sqrt(2.0 / length))
    return table.astype(ml_dtypes.bfloat16)


def three_parts(values):
    first = values.astype(BF16)
    rest = values - first.astype(F32)
    second = rest.astype(BF16)
    third = (rest - second.astype(F32)).astype(BF16)
    return first, second, third


def mm(left, right):
    return jnp.dot(left, right, preferred_element_type=F32)


def mm_nt(left, right):
    return lax.dot_general(left, right, (((1,), (1,)), ((), ())), preferred_element_type=F32)


def mm_tn(left, right):
    return lax.dot_general(left, right, (((0,), (0,)), ((), ())), preferred_element_type=F32)


def two_rows(ref, pair):
    return jnp.concatenate([ref[2 * pair : 2 * pair + 1, :], ref[2 * pair + 1 : 2 * pair + 2, :]], axis=1)


def source_kernel(group_ref, count_hbm, point_hbm, kern_hbm, area_hbm, feat_hbm, weight_hbm, msg_ref, pw_ref, count_ref, point_ref, kern_ref, area_ref, feat_ref, weight_ref, sems):
    devices, points = point_ref.shape[0], feat_ref.shape[1]
    low = MODES // devices
    pieces = (
        (point_hbm, point_ref),
        (area_hbm, area_ref),
        (feat_hbm, feat_ref),
        (kern_hbm, kern_ref),
        (count_hbm, count_ref),
        (weight_hbm.at[pl.ds(group_ref[0] * MODES, MODES)], weight_ref),
    )
    copies = [
        pltpu.make_async_copy(source, place, sems.at[index])
        for index, (source, place) in enumerate(pieces)
    ]
    for copy in copies:
        copy.start()
    for copy in copies[:-1]:
        copy.wait()
    first, second, third = three_parts(area_ref[...])
    place = lax.broadcasted_iota(jnp.int32, (16, points), 0)
    extra = jnp.where(
        place == 0,
        first.astype(F32),
        jnp.where(place == 1, second.astype(F32), jnp.where(place == 2, third.astype(F32), 0.0)),
    ).astype(BF16)
    table = jnp.concatenate([feat_ref[...], extra], axis=0)
    rows = lax.broadcasted_iota(jnp.int32, (points, 2 * LANES), 0)
    lane = lax.broadcasted_iota(jnp.int32, (1, LANES), 1)
    for pair in range(devices // 2):
        hot = jnp.where(rows == two_rows(point_ref, pair), 1.0, 0.0).astype(BF16)
        got = mm(table, hot)
        spread = got[WIDTH : WIDTH + 1] + got[WIDTH + 1 : WIDTH + 2] + got[WIDTH + 2 : WIDTH + 3]
        for half in range(2):
            dest = 2 * pair + half
            cut = slice(half * LANES, (half + 1) * LANES)
            valid = lane < count_ref[0:1, dest : dest + 1]
            weight = jnp.where(valid, kern_ref[dest : dest + 1, :], 0.0)
            pw_ref[dest : dest + 1, :] = weight
            msg_ref[dest, 0:WIDTH, :] = ((weight * spread[:, cut]) * got[0:WIDTH, cut]).astype(BF16)
    copies[-1].wait()
    for dest in range(devices):
        msg_ref[dest, WIDTH : 2 * WIDTH, :] = jnp.concatenate(
            [weight_ref[low * dest], weight_ref[low * dest + 1]], axis=1
        )


def place_kernel(depth, cell_ref, by_ref, same_hbm, lp_ref, zr_ref, same_ref, col_ref, sems):
    devices = cell_ref.shape[0]
    zbits = depth.bit_length() - 1
    rows = by_ref.shape[0]
    slab = rows // MODES
    yrow = lax.broadcasted_iota(jnp.int32, (GY, LANES), 0)
    xrow = jnp.bitwise_and(lax.broadcasted_iota(jnp.int32, (rows, LANES), 0), slab - 1)
    up = lax.broadcasted_iota(jnp.int32, (LANES, LANES), 0) < lax.broadcasted_iota(
        jnp.int32, (LANES, LANES), 1
    )
    for block in range(devices):
        cells = cell_ref[block : block + 1, :]
        cut = slice(block * LANES, (block + 1) * LANES)
        col_ref[cut, :] = jnp.broadcast_to(cells.astype(F32), (LANES, LANES)).T
        ypos = jnp.bitwise_and(jnp.right_shift(cells, zbits), GY - 1)
        xpos = jnp.right_shift(cells, zbits + GY.bit_length() - 1)
        hot = jnp.where(yrow == ypos, 1.0, 0.0).astype(BF16)
        lp_ref[:, cut] = jnp.where(xrow == xpos, mm(by_ref[...], hot), 0.0).astype(BF16)
    for block in range(devices):
        cells = cell_ref[block : block + 1, :]
        row = cells.astype(F32)
        cut = slice(block * LANES, (block + 1) * LANES)
        same = jnp.where(jnp.logical_and(col_ref[cut, :] == row, up), 1.0, 0.0)
        seen = jnp.max(same, axis=0, keepdims=True)
        if block:
            before = jnp.where(col_ref[0 : block * LANES, :] == row, 1.0, 0.0)
            seen = jnp.maximum(seen, jnp.max(before, axis=0, keepdims=True))
        zr_ref[block : block + 1, :] = jnp.where(
            seen > 0.0, -1, jnp.bitwise_and(cells, depth - 1)
        )
    copies = []
    for pair in range(devices // 2):
        for half in range(2):
            row = cell_ref[2 * pair + half : 2 * pair + half + 1, :].astype(F32)
            same_ref[pair, :, half * LANES : (half + 1) * LANES] = jnp.where(
                col_ref[...] == row, 1.0, 0.0
            ).astype(BF16)
        copies.append(pltpu.make_async_copy(same_ref.at[pair], same_hbm.at[pair], sems.at[pair]))
        copies[-1].start()
    for copy in copies:
        copy.wait()


def fetch_blocks(source, place, sems):
    copies = [
        pltpu.make_async_copy(source.at[block], place.at[block], sems.at[block])
        for block in range(source.shape[0])
    ]
    for copy in copies:
        copy.start()
    return copies


def spread_depth(values, zpos, rp_ref, pair):
    cut = slice(pair * 2 * LANES, (pair + 1) * 2 * LANES)
    for level in range(rp_ref.shape[0] // WIDTH):
        rp_ref[level * WIDTH : (level + 1) * WIDTH, cut] = jnp.where(
            zpos == level, values, 0.0
        ).astype(BF16)


def slab_rows(lp_ref, rp_ref, msg_ref):
    devices = msg_ref.shape[0]
    step = lp_ref.shape[0] // devices
    for quad in range(rp_ref.shape[0] // (4 * WIDTH)):
        out = mm_nt(lp_ref[...], rp_ref[quad * 4 * WIDTH : (quad + 1) * 4 * WIDTH, :]).astype(BF16)
        for half in range(2):
            level = 2 * quad + half
            for dest in range(devices):
                msg_ref[dest, level * step : (level + 1) * step, :] = out[
                    dest * step : (dest + 1) * step, half * LANES : (half + 1) * LANES
                ]


def cell_kernel(same_hbm, rx_ref, zr_ref, lp_ref, msg_ref, lat_ref, same_ref, sems, xs_ref, rp_ref):
    devices = rx_ref.shape[0]
    copies = fetch_blocks(same_hbm, same_ref, sems)
    for block in range(devices):
        xs_ref[:, block * LANES : (block + 1) * LANES] = rx_ref[block, 0:WIDTH, :]
    for pair in range(devices // 2):
        cut = slice(pair * 2 * LANES, (pair + 1) * 2 * LANES)
        copies[pair].wait()
        latent = mm(xs_ref[...], same_ref[pair])
        lat_ref[:, cut] = latent.astype(BF16)
        spread_depth(latent, two_rows(zr_ref, pair), rp_ref, pair)
    slab_rows(lp_ref, rp_ref, msg_ref)


def to_modes(rx_ref, table, sp_ref):
    levels = sp_ref.shape[0] // table.shape[0]
    step = table.shape[1] // rx_ref.shape[0]
    for level in range(levels):
        block = rx_ref[:, level * step : (level + 1) * step, :].reshape(table.shape[1], LANES)
        coeffs = mm(table, block).astype(BF16).astype(F32)
        sp_ref[pl.ds(level, table.shape[0], stride=levels), :] = coeffs


def swap_halves(values):
    return pltpu.roll(values, WIDTH, 1)


def mode_kernel(group_ref, rx_ref, own_ref, other_ref, table_ref, back_ref, msg_ref, spec_ref, sp_ref, mx_ref):
    devices = rx_ref.shape[0]
    own_rows = spec_ref.shape[1]
    modes = table_ref.shape[0]
    levels = sp_ref.shape[0] // modes
    step = back_ref.shape[0] // devices
    to_modes(rx_ref, table_ref[...], sp_ref)
    for dest in range(devices):
        spec_ref[dest] = sp_ref[dest * own_rows : (dest + 1) * own_rows, :].astype(BF16)
    left = lax.broadcasted_iota(jnp.int32, (levels, LANES), 1) < WIDTH
    for order in range(MODES):
        source, which = order // 2, order % 2
        mine = jnp.full((WIDTH, LANES), group_ref[0], jnp.int32) == which
        weight = jnp.where(
            mine,
            own_ref[source, WIDTH : 2 * WIDTH, :].astype(F32),
            other_ref[source].astype(F32),
        ).astype(BF16)
        at = order * 2 * levels
        even = sp_ref[at : at + levels, :]
        odd = sp_ref[at + levels : at + 2 * levels, :]
        rows = jnp.concatenate([even, swap_halves(even), odd, swap_halves(odd)], axis=0)
        out = mm(rows[:, 0:WIDTH].astype(BF16), weight)
        mx_ref[at : at + levels, :] = jnp.where(
            left, out[0:levels], swap_halves(out[levels : 2 * levels])
        )
        mx_ref[at + levels : at + 2 * levels, :] = jnp.where(
            left, swap_halves(out[2 * levels : 3 * levels]), out[3 * levels : 4 * levels]
        )
    for level in range(levels):
        mixed = mx_ref[pl.ds(level, modes, stride=levels), :].astype(BF16)
        out = mm(back_ref[...], mixed).astype(BF16)
        for dest in range(devices):
            msg_ref[dest, level * step : (level + 1) * step, :] = out[dest * step : (dest + 1) * step]


def pre_kernel(depth, rx_ref, lp_ref, lat_ref, cell_ref, skip_ref, bias_ref, msg_ref, pre_ref, rt_ref):
    devices = rx_ref.shape[0]
    rows = lp_ref.shape[0]
    step = rows // devices
    for level in range(rt_ref.shape[0] // LANES):
        block = rx_ref[:, level * step : (level + 1) * step, :].reshape(rows, LANES)
        rt_ref[level * LANES : (level + 1) * LANES, :] = block.T
    for pair in range(devices // 2):
        cut = slice(pair * 2 * LANES, (pair + 1) * 2 * LANES)
        zpos = jnp.bitwise_and(two_rows(cell_ref, pair), depth - 1)
        field = mm(rt_ref[...], lp_ref[:, cut])
        total = jnp.where(zpos == 0, field[0:WIDTH], 0.0)
        for level in range(1, depth):
            total += jnp.where(zpos == level, field[level * WIDTH : (level + 1) * WIDTH], 0.0)
        pre = total + mm_tn(skip_ref[...], lat_ref[:, cut]) + bias_ref[...]
        pre_ref[:, cut] = pre
        feats = gelu_value(pre).astype(BF16)
        for half in range(2):
            msg_ref[2 * pair + half] = feats[:, half * LANES : (half + 1) * LANES]


def slope_kernel(pre_ref, slope_ref):
    slope_ref[...] = gelu_slope(pre_ref[...])


def head_kernel(rx_ref, point_ref, pw_ref, head_ref, bias_ref, out_ref, area_ref, normal_ref, pres_ref, msg_ref, value_ref, hot_ref):
    devices = rx_ref.shape[0]
    points = area_ref.shape[1]
    rows = lax.broadcasted_iota(jnp.int32, (points, LANES), 0)
    for block in range(devices):
        cut = slice(block * LANES, (block + 1) * LANES)
        parts = three_parts(pw_ref[block : block + 1, :] * rx_ref[block].astype(F32))
        for index, part in enumerate(parts):
            value_ref[index * WIDTH : (index + 1) * WIDTH, cut] = part
        hot_ref[:, cut] = jnp.where(rows == point_ref[block : block + 1, :], 1.0, 0.0).astype(BF16)
    sums = mm_nt(value_ref[...], hot_ref[...])
    latent = sums[0:WIDTH] + sums[WIDTH : 2 * WIDTH] + sums[2 * WIDTH : 3 * WIDTH]
    first, second, third = three_parts(latent)
    weight = head_ref[...]
    head_pre = mm_tn(weight, first) + mm_tn(weight, second) + mm_tn(weight, third) + bias_ref[...]
    head = gelu_value(head_pre)
    pressure = jnp.sum(head * out_ref[...], axis=0, keepdims=True)
    pres_ref[...] = pressure
    along = [normal_ref[which : which + 1, :] * area_ref[...] for which in range(2)]
    first, second, third = three_parts(out_ref[...] * gelu_slope(head_pre))
    grad = mm(weight, first) + mm(weight, second) + mm(weight, third)
    place = lax.broadcasted_iota(jnp.int32, (16, points), 0)
    extra = jnp.zeros((16, points), F32)
    for which in range(2):
        for index, part in enumerate(three_parts(along[which])):
            extra = jnp.where(place == 3 + 3 * which + index, part.astype(F32), extra)
    upper = grad.astype(BF16)
    lower = (grad - upper.astype(F32)).astype(BF16)
    table = jnp.concatenate([upper, lower, extra.astype(BF16)], axis=0)
    lane = lax.broadcasted_iota(jnp.int32, (1, LANES), 1)
    partial = []
    for which in range(2):
        force = jnp.sum(pressure * area_ref[...] * normal_ref[which : which + 1, :], axis=1, keepdims=True)
        partial.append(force)
    force_row = jnp.where(lane == 0, partial[0], jnp.where(lane == 1, partial[1], 0.0))
    out_rows = lax.dot_general(
        jnp.concatenate([along[0], along[1], jnp.zeros((6, points), F32)], axis=0),
        head,
        (((1,), (1,)), ((), ())),
        precision=lax.Precision.HIGHEST,
        preferred_element_type=F32,
    )
    out_row = jnp.concatenate([out_rows[0:1], out_rows[1:2]], axis=1)
    place = lax.broadcasted_iota(jnp.int32, (16, LANES), 0)
    common = jnp.zeros((16, LANES), F32)
    for index, part in enumerate(three_parts(out_row)):
        common = jnp.where(place == 9 + index, part.astype(F32), common)
    for index, part in enumerate(three_parts(force_row)):
        common = jnp.where(place == 12 + index, part.astype(F32), common)
    for block in range(devices):
        cut = slice(block * LANES, (block + 1) * LANES)
        got = mm(table, hot_ref[:, cut])
        msg_ref[block, 0 : 2 * WIDTH, :] = got[0 : 2 * WIDTH].astype(BF16)
        tail = got[2 * WIDTH : 2 * WIDTH + 16] + common
        for index, part in enumerate(three_parts(pw_ref[block : block + 1, :])):
            tail = jnp.where(place == index, part.astype(F32), tail)
        msg_ref[block, 2 * WIDTH : 2 * WIDTH + 16, :] = tail.astype(BF16)


def fold_rows(values):
    first, second, third = three_parts(values)
    upper = jnp.concatenate([first.astype(F32), second.astype(F32)], axis=1)
    lower = jnp.concatenate([third.astype(F32), jnp.zeros_like(values)], axis=1)
    return upper, lower


def back_kernel(scale, same_hbm, rx_ref, target_ref, zr_ref, lp_ref, lat_ref, slope_ref, msg_ref, force_ref, outg_ref, same_ref, sems, xs_ref, pg_ref, rp_ref):
    devices = rx_ref.shape[0]
    main = msg_ref.shape[1] - 16
    copies = fetch_blocks(same_hbm, same_ref, sems)
    extra = slice(2 * WIDTH, 2 * WIDTH + 16)
    total = rx_ref[0, extra, :].astype(F32)
    for block in range(1, devices):
        total += rx_ref[block, extra, :].astype(F32)
    forces = scale * (total[12:13] + total[13:14] + total[14:15])
    force_ref[...] = forces[:, 0:2]
    misfit = forces[:, 0:2] - target_ref[...]
    drag, lift = misfit[:, 0:1], misfit[:, 1:2]
    twice = 2.0 * scale
    out_row = total[9:10] + total[10:11] + total[11:12]
    outg_ref[...] = twice * (drag * out_row[:, 0:WIDTH] + lift * out_row[:, WIDTH : 2 * WIDTH])
    for block in range(devices):
        tail = rx_ref[block, extra, :].astype(F32)
        weight, first, second = (
            tail[at : at + 1] + tail[at + 1 : at + 2] + tail[at + 2 : at + 3] for at in (0, 3, 6)
        )
        grad = rx_ref[block, 0:WIDTH, :].astype(F32) + rx_ref[block, WIDTH : 2 * WIDTH, :].astype(F32)
        along = twice * (drag * first + lift * second)
        grad = (along * grad).astype(BF16).astype(F32)
        xs_ref[:, block * LANES : (block + 1) * LANES] = (weight * grad).astype(BF16)
    for pair in range(devices // 2):
        cut = slice(pair * 2 * LANES, (pair + 1) * 2 * LANES)
        copies[pair].wait()
        grad = mm(xs_ref[...], same_ref[pair]) * slope_ref[:, cut]
        zpos = two_rows(zr_ref, pair)
        pg_ref[:, cut] = jnp.where(zpos >= 0, grad, 0.0).astype(BF16)
        spread_depth(grad, zpos, rp_ref, pair)
    slab_rows(lp_ref, rp_ref, msg_ref)
    upper, lower = fold_rows(mm_nt(lat_ref[...], pg_ref[...]))
    for dest in range(msg_ref.shape[0]):
        cut = slice(8 * dest, 8 * dest + 8)
        rows = jnp.concatenate([upper[cut], lower[cut]], axis=0)
        msg_ref[dest, main : main + 16, :] = rows.astype(BF16)


def spec_kernel(half_ref, rx_ref, table_ref, spec_ref, msg_ref, sp_ref):
    peers = rx_ref.shape[0]
    devices, own_rows = spec_ref.shape[0], spec_ref.shape[1]
    part_rows = sp_ref.shape[0] // devices
    main = rx_ref.shape[1] - 16
    to_modes(rx_ref, table_ref[half_ref[0]], sp_ref)
    total = rx_ref[0, main : main + 16, :].astype(F32)
    for source in range(1, peers):
        total += rx_ref[source, main : main + 16, :].astype(F32)
    upper, lower = total[0:8], total[8:16]
    left = lax.broadcasted_iota(jnp.int32, (8, LANES), 1) < WIDTH
    value = jnp.where(left, upper + swap_halves(upper) + lower, 0.0)
    first, second, third = three_parts(value)
    upper = first.astype(F32) + swap_halves(second.astype(F32))
    rows = jnp.concatenate([upper, third.astype(F32)], axis=0).astype(BF16)
    for dest in range(devices):
        msg_ref[dest, 0:own_rows, :] = spec_ref[dest]
        msg_ref[dest, own_rows : own_rows + part_rows, :] = sp_ref[
            dest * part_rows : (dest + 1) * part_rows, :
        ].astype(BF16)
        msg_ref[dest, own_rows + part_rows : own_rows + part_rows + 16, :] = rows


def both_halves(values):
    return jnp.concatenate([values, swap_halves(values)], axis=0)[:, 0:WIDTH]


def final_kernel(peers, rx_ref, spec_ref, skip_ref):
    devices = rx_ref.shape[0]
    low = MODES // devices
    high = MODES // peers
    owned = spec_ref.shape[0] // MODES
    part_rows = owned * high * 8
    own_rows = rx_ref.shape[1] - 16 - part_rows
    for source in range(devices):
        for which in range(owned):
            at = which * 8 * low
            coeffs = rx_ref[source, at : at + 8 * low, :].astype(F32)
            peer, inner = divmod(low * source, high)
            at = own_rows + (which * high + inner) * 8
            grads = [
                rx_ref[peer + shift, at : at + 8 * low, :].astype(F32)
                for shift in range(0, devices, peers)
            ]
            for index in range(low):
                cut = slice(8 * index, 8 * index + 8)
                left = both_halves(coeffs[cut])
                left = jnp.concatenate([left] * len(grads), axis=0)
                right = jnp.concatenate([both_halves(part[cut]) for part in grads], axis=0)
                spec_ref[which * MODES + low * source + index] = mm_tn(
                    left.astype(BF16), right.astype(BF16)
                )
    at = own_rows + part_rows
    for peer in range(peers):
        rows = rx_ref[peer, at : at + 16, :].astype(F32)
        for shift in range(peers, devices, peers):
            rows += rx_ref[peer + shift, at : at + 16, :].astype(F32)
        value = (rows[0:8] + swap_halves(rows[0:8]) + rows[8:16])[:, 0:WIDTH]
        skip_ref[8 * peer : 8 * peer + 8, :] = value


def run(kernel, outs, ins, flops, scratch=(), smem=0, hbm=0, hbm_outs=0, grant=16):
    vmem = pl.BlockSpec(memory_space=pltpu.VMEM)
    far = pl.BlockSpec(memory_space=pltpu.HBM)
    scalar = pl.BlockSpec(memory_space=pltpu.SMEM)
    moved = sum(math.prod(a.shape) * a.dtype.itemsize for a in list(ins) + list(outs))
    return pl.pallas_call(
        kernel,
        out_shape=tuple(outs),
        in_specs=[scalar] * smem + [far] * hbm + [vmem] * (len(ins) - smem - hbm),
        out_specs=tuple([far] * hbm_outs + [vmem] * (len(outs) - hbm_outs)),
        scratch_shapes=list(scratch),
        compiler_params=pltpu.CompilerParams(vmem_limit_bytes=grant * 1024 * 1024),
        cost_estimate=pl.CostEstimate(flops=flops, bytes_accessed=moved, transcendentals=0),
    )(*ins)


def slab_step(
    point_feats,
    pair_point,
    pair_cell,
    kernel,
    counts,
    area,
    normals,
    targets,
    spec_weight,
    skip_weight,
    skip_bias,
    head_weight,
    head_bias,
    out_weight,
):
    n = lax.axis_size("gx")
    points = point_feats.shape[0]
    slots = n * LANES
    slab = GX // n
    low = MODES // n
    depth = ZL * n
    levels = depth * WIDTH // LANES
    rows = MODES * slab
    main = levels * slab * low
    own_rows = low * low * levels
    shape = jax.ShapeDtypeStruct

    by = host_rows(GY, MODES)
    bx = host_rows(GX, MODES)
    by_rows = jnp.asarray(np.repeat(by, slab, axis=0))
    table = np.zeros((MODES, low, n, low, slab), ml_dtypes.bfloat16)
    for index in range(low):
        table[:, index, :, index, :] = bx.reshape(MODES, n, slab)
    table = table.reshape(MODES * low, rows)
    back = jnp.asarray(np.ascontiguousarray(table.T))
    table = jnp.asarray(table)
    peers = 8
    halves = n // peers
    high = MODES // peers
    part_table = np.zeros((halves, MODES, high, peers, high, slab), ml_dtypes.bfloat16)
    for index in range(high):
        part_table[:, :, index, :, index, :] = np.moveaxis(
            bx.reshape(MODES, halves, peers, slab), 1, 0
        )
    part_table = jnp.asarray(part_table.reshape(halves, MODES * high, rows))
    near = [[half * peers + peer for peer in range(peers)] for half in range(halves)]
    half = (lax.axis_index("gx") // peers).astype(jnp.int32).reshape(1)

    def exchange(message):
        return lax.all_to_all(message, "gx", split_axis=0, concat_axis=0, tiled=True)

    group = lax.axis_index("groups").astype(jnp.int32).reshape(1)
    point_rows = pair_point[0]
    cells = pair_cell[:, 0, :]
    area_row = area.reshape(1, points)
    msg, pw = run(
        source_kernel,
        [shape((n, 2 * WIDTH, LANES), BF16), shape((n, LANES), F32)],
        [group, counts, point_rows, kernel[0], area_row, point_feats.T, spec_weight],
        2 * 80 * points * slots,
        scratch=[
            pltpu.VMEM((1, n), jnp.int32),
            pltpu.VMEM((n, LANES), jnp.int32),
            pltpu.VMEM((n, LANES), F32),
            pltpu.VMEM((1, points), F32),
            pltpu.VMEM((WIDTH, points), BF16),
            pltpu.VMEM((MODES, WIDTH, WIDTH), BF16),
            pltpu.SemaphoreType.DMA((6,)),
        ],
        smem=1,
        hbm=6,
        grant=60,
    )
    rx = exchange(msg)
    same_shape = (n // 2, slots, 2 * LANES)
    same_scratch = [pltpu.VMEM(same_shape, BF16), pltpu.SemaphoreType.DMA((n // 2,))]
    same, lp, zr = run(
        functools.partial(place_kernel, depth),
        [shape(same_shape, BF16), shape((rows, slots), BF16), shape((n, LANES), jnp.int32)],
        [cells, by_rows],
        2 * rows * LANES * slots,
        scratch=[
            pltpu.VMEM(same_shape, BF16),
            pltpu.VMEM((slots, LANES), F32),
            pltpu.SemaphoreType.DMA((n // 2,)),
        ],
        hbm_outs=1,
        grant=24,
    )
    other = lax.ppermute(rx[:, WIDTH : 2 * WIDTH, :], "groups", [(0, 1), (1, 0)])
    pair_rows = pltpu.VMEM((WIDTH, slots), BF16)
    deep_rows = pltpu.VMEM((depth * WIDTH, slots), BF16)
    big = 2 * WIDTH * slots * slots + 2 * rows * slots * depth * WIDTH
    msg, lat = run(
        cell_kernel,
        [shape((n, main, LANES), BF16), shape((WIDTH, slots), BF16)],
        [same, rx, zr, lp],
        big,
        scratch=same_scratch + [pair_rows, deep_rows],
        hbm=1,
        grant=56,
    )
    columns = exchange(msg)
    msg, spec = run(
        mode_kernel,
        [shape((n, main, LANES), BF16), shape((n, own_rows, LANES), BF16)],
        [group, columns, rx, other, table, back],
        4 * MODES * low * rows * depth * WIDTH,
        scratch=[pltpu.VMEM((MODES * low * levels, LANES), F32)] * 2,
        smem=1,
    )
    slabs = exchange(msg)
    msg, pre = run(
        functools.partial(pre_kernel, depth),
        [shape((n, WIDTH, LANES), BF16), shape((WIDTH, slots), F32)],
        [slabs, lp, lat, cells, skip_weight, skip_bias.reshape(WIDTH, 1)],
        2 * rows * slots * depth * WIDTH,
        scratch=[pltpu.VMEM((depth * WIDTH, rows), BF16)],
    )
    returned = exchange(msg)
    (slope,) = run(slope_kernel, [shape(pre.shape, F32)], [pre], 100 * WIDTH * slots)
    out_col = out_weight.reshape(WIDTH, 1)
    pressure, msg = run(
        head_kernel,
        [shape((1, points), F32), shape((n, 2 * WIDTH + 16, LANES), BF16)],
        [returned, point_rows, pw, head_weight, head_bias.reshape(WIDTH, 1), out_col, area_row, normals],
        2 * 3 * WIDTH * points * slots,
        scratch=[pltpu.VMEM((3 * WIDTH, slots), BF16), pltpu.VMEM((points, slots), BF16)],
    )
    grads = exchange(msg)
    scale = 1.0 / math.sqrt(points * n)
    msg, forces, out_grad = run(
        functools.partial(back_kernel, scale),
        [
            shape((peers, halves * main + 16, LANES), BF16),
            shape((1, 2), F32),
            shape((1, WIDTH), F32),
        ],
        [same, grads, targets.reshape(1, 2), zr, lp, lat, slope],
        big,
        scratch=same_scratch + [pair_rows, pair_rows, deep_rows],
        hbm=1,
        grant=56,
    )
    grad_columns = lax.all_to_all(
        msg, "gx", split_axis=0, concat_axis=0, tiled=True, axis_index_groups=near
    )
    part_rows = MODES * high * levels // n
    (msg,) = run(
        spec_kernel,
        [shape((n, own_rows + part_rows + 16, LANES), BF16)],
        [half, grad_columns, part_table, spec],
        2 * MODES * high * rows * depth * WIDTH,
        scratch=[pltpu.VMEM((MODES * high * levels, LANES), F32)],
        smem=1,
    )
    finals = exchange(msg)
    spec_grad, skip_grad = run(
        functools.partial(final_kernel, peers),
        [shape((spec_weight.shape[0], WIDTH, WIDTH), F32), shape((WIDTH, WIDTH), F32)],
        [finals],
        2 * NMODE * WIDTH * WIDTH * depth // n,
    )
    return (pressure.reshape(points), forces.reshape(2), spec_grad, skip_grad, out_grad.reshape(WIDTH))


def solution(mesh):
    fits = mesh.shape["gx"] == 16 and mesh.shape["groups"] == 2
    per_device = slab_step if fits else general_step
    in_specs = (
        P(("groups", "gx"), None),
        P(("groups", "gx"), None, None),
        P(None, ("groups", "gx"), None),
        P(("groups", "gx"), None, None),
        P(("groups", "gx"), None),
        P(("groups", "gx")),
        P(None, ("groups", "gx")),
        P("groups"),
        P("gx", None, None),
        P(),
        P(),
        P(),
        P(),
        P(),
    )
    out_specs = (
        P(("groups", "gx")),
        P("groups"),
        P(("groups", "gx"), None, None),
        P("groups", None),
        P("groups"),
    )
    return jax.shard_map(
        per_device, mesh=mesh, in_specs=in_specs, out_specs=out_specs, check_vma=False
    )
```

```python
import functools
import math

import jax
import jax.numpy as jnp
import ml_dtypes
import numpy as np
from jax import lax
from jax.experimental import pallas as pl
from jax.experimental.pallas import tpu as pltpu
from jax.sharding import PartitionSpec as P

GX = 128
GY = 128
MODES = 32
ZL = 1
NMODE = 1024


def fourier_rows(length, number):
    places = jnp.arange(length, dtype=jnp.float32)
    order = jnp.arange(number)
    half = number // 2
    freqs = jnp.where(order < half, order, order - half + 1).astype(jnp.float32)
    angles = 2.0 * math.pi / length * freqs[:, None] * places[None, :]
    table = jnp.where((order < half)[:, None], jnp.cos(angles), jnp.sin(angles))
    return (table * math.sqrt(2.0 / length)).astype(jnp.bfloat16)


def gelu_value(values):
    return 0.5 * values * (1.0 + lax.erf(values * (1.0 / math.sqrt(2.0))))


def gelu_slope(values):
    return 0.5 * (1.0 + lax.erf(values * (1.0 / math.sqrt(2.0)))) + values * jnp.exp(
        -0.5 * values * values
    ) * (1.0 / math.sqrt(2.0 * math.pi))


def general_step(
    point_feats,
    pair_point,
    pair_cell,
    kernel,
    counts,
    area,
    normals,
    targets,
    spec_weight,
    skip_weight,
    skip_bias,
    head_weight,
    head_bias,
    out_weight,
):
    devices = lax.axis_size("gx")
    local_points, width = point_feats.shape
    block_slots = pair_point.shape[2]
    row_count = GX // devices
    depth = ZL * devices
    slab_cells = row_count * GY * depth
    valid_mask = jnp.arange(block_slots)[None, :] < counts[0][:, None]
    point_rows = pair_point[0]
    pair_weight = jnp.where(valid_mask, kernel[0], jnp.float32(0.0))
    sender_weight = pair_weight * area[point_rows]
    contrib = (sender_weight[..., None] * point_feats[point_rows].astype(jnp.float32)).astype(
        jnp.bfloat16
    )
    arrived = lax.all_to_all(contrib, "gx", split_axis=0, concat_axis=0, tiled=True)
    cell_rows = pair_cell[:, 0, :].reshape(-1)
    latent = jax.ops.segment_sum(
        arrived.reshape(-1, width).astype(jnp.float32), cell_rows, num_segments=slab_cells
    ).astype(jnp.bfloat16)
    col_table = fourier_rows(GY, MODES)
    row_table = fourier_rows(GX, MODES)
    volume = latent.reshape(row_count, GY, depth * width)
    along_y = jnp.einsum(
        "by,xyk->xbk", col_table, volume, preferred_element_type=jnp.float32
    ).astype(jnp.bfloat16)
    columns = lax.all_to_all(along_y, "gx", split_axis=2, concat_axis=0, tiled=True)
    spectrum = jnp.einsum(
        "ax,xbk->abk", row_table, columns, preferred_element_type=jnp.float32
    ).astype(jnp.bfloat16)
    mode_rows = lax.all_to_all(
        spectrum.reshape(NMODE, ZL * width), "gx", split_axis=0, concat_axis=1, tiled=True
    )
    own_modes = mode_rows.shape[0]
    mixed_rows = jnp.einsum(
        "mzc,mcd->mzd",
        mode_rows.reshape(own_modes, depth, width),
        spec_weight,
        preferred_element_type=jnp.float32,
    ).astype(jnp.bfloat16)
    mixed = lax.all_to_all(
        mixed_rows.reshape(own_modes, depth * width), "gx", split_axis=1, concat_axis=0, tiled=True
    )
    back_x = jnp.einsum(
        "ax,abk->xbk",
        row_table,
        mixed.reshape(MODES, MODES, ZL * width),
        preferred_element_type=jnp.float32,
    ).astype(jnp.bfloat16)
    slabs = lax.all_to_all(back_x, "gx", split_axis=0, concat_axis=2, tiled=True)
    spatial = jnp.einsum(
        "by,xbk->xyk", col_table, slabs, preferred_element_type=jnp.float32
    ).reshape(slab_cells, width)
    pre = spatial + jnp.dot(latent, skip_weight, preferred_element_type=jnp.float32) + skip_bias
    features = gelu_value(pre).astype(jnp.bfloat16)
    picked = features[cell_rows].reshape(devices, block_slots, width)
    returned = lax.all_to_all(picked, "gx", split_axis=0, concat_axis=0, tiled=True)
    point_latent = jax.ops.segment_sum(
        (pair_weight[..., None] * returned.astype(jnp.float32)).reshape(-1, width),
        point_rows.reshape(-1),
        num_segments=local_points,
    )
    head_matrix = head_weight.astype(jnp.float32)
    head_pre = jnp.dot(point_latent, head_matrix, precision=lax.Precision.HIGHEST) + head_bias
    head = gelu_value(head_pre)
    pressure = jnp.dot(head, out_weight, precision=lax.Precision.HIGHEST)
    weighted = pressure * area
    scale = 1.0 / math.sqrt(local_points * devices)
    totals = lax.psum(
        jnp.stack([jnp.sum(weighted * normals[0]), jnp.sum(weighted * normals[1])]), "gx"
    )
    forces = scale * totals
    misfit = forces - targets
    point_grad = 2.0 * scale * (misfit[0] * normals[0] + misfit[1] * normals[1]) * area
    out_part = jnp.dot(point_grad, head, precision=lax.Precision.HIGHEST)
    head_grad = point_grad[:, None] * out_weight[None, :] * gelu_slope(head_pre)
    latent_grad = jnp.dot(head_grad, head_matrix.T, precision=lax.Precision.HIGHEST).astype(
        jnp.bfloat16
    )
    grad_pairs = (pair_weight[..., None] * latent_grad[point_rows].astype(jnp.float32)).astype(
        jnp.bfloat16
    )
    grad_arrived = lax.all_to_all(grad_pairs, "gx", split_axis=0, concat_axis=0, tiled=True)
    cell_grad = jax.ops.segment_sum(
        grad_arrived.reshape(-1, width).astype(jnp.float32), cell_rows, num_segments=slab_cells
    )
    pre_grad = (cell_grad * gelu_slope(pre)).astype(jnp.bfloat16)
    skip_part = jnp.dot(latent.T, pre_grad, preferred_element_type=jnp.float32)
    grad_y = jnp.einsum(
        "by,xyk->xbk",
        col_table,
        pre_grad.reshape(row_count, GY, depth * width),
        preferred_element_type=jnp.float32,
    ).astype(jnp.bfloat16)
    grad_columns = lax.all_to_all(grad_y, "gx", split_axis=2, concat_axis=0, tiled=True)
    grad_spec = jnp.einsum(
        "ax,xbk->abk", row_table, grad_columns, preferred_element_type=jnp.float32
    ).astype(jnp.bfloat16)
    grad_rows = lax.all_to_all(
        grad_spec.reshape(NMODE, ZL * width), "gx", split_axis=0, concat_axis=1, tiled=True
    )
    own_modes = grad_rows.shape[0]
    spec_grad = jnp.einsum(
        "mzc,mzd->mcd",
        mode_rows.reshape(own_modes, depth, width),
        grad_rows.reshape(own_modes, depth, width),
        preferred_element_type=jnp.float32,
    )
    out_grad, skip_grad = lax.psum((out_part, skip_part), "gx")
    return (pressure, forces, spec_grad, skip_grad, out_grad)


F32 = jnp.float32
BF16 = jnp.bfloat16
LANES = 128
WIDTH = 64


def host_rows(length, number):
    places = np.arange(length, dtype=np.float32)
    order = np.arange(number)
    half = number // 2
    freqs = np.where(order < half, order, order - half + 1).astype(np.float32)
    angles = np.float32(2.0 * math.pi / length) * freqs[:, None] * places[None, :]
    table = np.where((order < half)[:, None], np.cos(angles), np.sin(angles))
    table = table.astype(np.float32) * np.float32(math.sqrt(2.0 / length))
    return table.astype(ml_dtypes.bfloat16)


def three_parts(values):
    first = values.astype(BF16)
    rest = values - first.astype(F32)
    second = rest.astype(BF16)
    third = (rest - second.astype(F32)).astype(BF16)
    return first, second, third


def mm(left, right):
    return jnp.dot(left, right, preferred_element_type=F32)


def mm_nt(left, right):
    return lax.dot_general(left, right, (((1,), (1,)), ((), ())), preferred_element_type=F32)


def mm_tn(left, right):
    return lax.dot_general(left, right, (((0,), (0,)), ((), ())), preferred_element_type=F32)


def two_rows(ref, pair):
    return jnp.concatenate([ref[2 * pair : 2 * pair + 1, :], ref[2 * pair + 1 : 2 * pair + 2, :]], axis=1)


def source_kernel(group_ref, count_hbm, point_hbm, kern_hbm, area_hbm, feat_hbm, weight_hbm, msg_ref, pw_ref, count_ref, point_ref, kern_ref, area_ref, feat_ref, weight_ref, sems):
    devices, points = point_ref.shape[0], feat_ref.shape[1]
    low = MODES // devices
    pieces = (
        (point_hbm, point_ref),
        (area_hbm, area_ref),
        (feat_hbm, feat_ref),
        (kern_hbm, kern_ref),
        (count_hbm, count_ref),
        (weight_hbm.at[pl.ds(group_ref[0] * MODES, MODES)], weight_ref),
    )
    copies = [
        pltpu.make_async_copy(source, place, sems.at[index])
        for index, (source, place) in enumerate(pieces)
    ]
    for copy in copies:
        copy.start()
    for copy in copies[:-1]:
        copy.wait()
    first, second, third = three_parts(area_ref[...])
    place = lax.broadcasted_iota(jnp.int32, (16, points), 0)
    extra = jnp.where(
        place == 0,
        first.astype(F32),
        jnp.where(place == 1, second.astype(F32), jnp.where(place == 2, third.astype(F32), 0.0)),
    ).astype(BF16)
    table = jnp.concatenate([feat_ref[...], extra], axis=0)
    rows = lax.broadcasted_iota(jnp.int32, (points, 2 * LANES), 0)
    lane = lax.broadcasted_iota(jnp.int32, (1, LANES), 1)
    for pair in range(devices // 2):
        hot = jnp.where(rows == two_rows(point_ref, pair), 1.0, 0.0).astype(BF16)
        got = mm(table, hot)
        spread = got[WIDTH : WIDTH + 1] + got[WIDTH + 1 : WIDTH + 2] + got[WIDTH + 2 : WIDTH + 3]
        for half in range(2):
            dest = 2 * pair + half
            cut = slice(half * LANES, (half + 1) * LANES)
            valid = lane < count_ref[0:1, dest : dest + 1]
            weight = jnp.where(valid, kern_ref[dest : dest + 1, :], 0.0)
            pw_ref[dest : dest + 1, :] = weight
            msg_ref[dest, 0:WIDTH, :] = ((weight * spread[:, cut]) * got[0:WIDTH, cut]).astype(BF16)
    copies[-1].wait()
    for dest in range(devices):
        msg_ref[dest, WIDTH : 2 * WIDTH, :] = jnp.concatenate(
            [weight_ref[low * dest], weight_ref[low * dest + 1]], axis=1
        )


def columns_of(row):
    return jnp.broadcast_to(row, (LANES, LANES)).T


def pick_rows(rank_ref, pick_ref):
    rows = lax.broadcasted_iota(jnp.int32, (pick_ref.shape[0], LANES), 0)
    for block in range(rank_ref.shape[0]):
        pick_ref[:, block * LANES : (block + 1) * LANES] = jnp.where(
            rows == rank_ref[block : block + 1, :], 1.0, 0.0
        ).astype(BF16)


def place_kernel(depth, cell_ref, by_ref, lp_ref, zr_ref, rank_ref, same_ref, col_ref, flag_ref, pick_ref, part_ref):
    devices = cell_ref.shape[0]
    shared = same_ref.shape[0]
    zbits = depth.bit_length() - 1
    rows = by_ref.shape[0]
    slab = rows // MODES
    yrow = lax.broadcasted_iota(jnp.int32, (GY, LANES), 0)
    xrow = jnp.bitwise_and(lax.broadcasted_iota(jnp.int32, (rows, LANES), 0), slab - 1)
    down = lax.broadcasted_iota(jnp.int32, (LANES, LANES), 0)
    along = lax.broadcasted_iota(jnp.int32, (LANES, LANES), 1)
    place = lax.broadcasted_iota(jnp.int32, (16, LANES), 0)
    for block in range(devices):
        cells = cell_ref[block : block + 1, :]
        cut = slice(block * LANES, (block + 1) * LANES)
        col_ref[cut, :] = columns_of(cells.astype(F32))
        ypos = jnp.bitwise_and(jnp.right_shift(cells, zbits), GY - 1)
        xpos = jnp.right_shift(cells, zbits + GY.bit_length() - 1)
        hot = jnp.where(yrow == ypos, 1.0, 0.0).astype(BF16)
        lp_ref[:, cut] = jnp.where(xrow == xpos, mm(by_ref[...], hot), 0.0).astype(BF16)
        high = jnp.right_shift(cells, 7).astype(F32)
        low = jnp.bitwise_and(cells, 127).astype(F32)
        part_ref[:, cut] = jnp.where(place == 0, high, jnp.where(place == 1, low, 0.0)).astype(BF16)
    for block in range(devices):
        cells = cell_ref[block : block + 1, :]
        row = cells.astype(F32)
        cut = slice(block * LANES, (block + 1) * LANES)
        same = jnp.where(col_ref[cut, :] == row, 1.0, 0.0)
        before = jnp.sum(jnp.where(down < along, same, 0.0), axis=0, keepdims=True)
        count = jnp.sum(same, axis=0, keepdims=True)
        if block:
            early = jnp.where(col_ref[0 : block * LANES, :] == row, 1.0, 0.0)
            early = jnp.sum(early, axis=0, keepdims=True)
            before += early
            count += early
        if block < devices - 1:
            late = jnp.where(col_ref[(block + 1) * LANES :, :] == row, 1.0, 0.0)
            count += jnp.sum(late, axis=0, keepdims=True)
        zr_ref[block : block + 1, :] = jnp.where(
            before > 0.0, -1, jnp.bitwise_and(cells, depth - 1)
        )
        flag_ref[block : block + 1, :] = jnp.where(count > 1.0, 1.0, 0.0)
    flags = flag_ref[...]
    marks = flags.astype(BF16)
    inside = mm(marks, jnp.where(down <= along, 1.0, 0.0).astype(BF16))
    above = jnp.where(down < along, 1.0, 0.0)[:, 0:devices][0:devices]
    ahead = jnp.sum(mm_tn(above.astype(BF16), marks), axis=1, keepdims=True)
    rank_ref[...] = jnp.where(flags > 0.0, (inside + ahead - flags).astype(jnp.int32), -1)
    pick_rows(rank_ref, pick_ref)
    found = mm_nt(part_ref[...], pick_ref[...])
    found = found[0:1] * 128.0 + found[1:2]
    for block in range(shared // LANES):
        column = columns_of(found[:, block * LANES : (block + 1) * LANES])
        same_ref[block * LANES : (block + 1) * LANES, :] = jnp.where(
            jnp.concatenate([column] * (shared // LANES), axis=1) == found, 1.0, 0.0
        ).astype(BF16)


def sum_cells(xs_ref, cell_ref, rank_ref, same_ref, sums_ref, pick_ref, full_ref, col_ref):
    devices = cell_ref.shape[0]
    shared = same_ref.shape[0]
    few = jnp.max(rank_ref[...]) < shared

    @pl.when(few)
    def _():
        pick_rows(rank_ref, pick_ref)
        picked = mm_nt(xs_ref[...], pick_ref[...]).astype(BF16)
        parts = jnp.concatenate(three_parts(mm(picked, same_ref[...])), axis=0)
        for pair in range(devices // 2):
            span = slice(pair * 2 * LANES, (pair + 1) * 2 * LANES)
            got = mm(parts, pick_ref[:, span])
            got = got[0:WIDTH] + got[WIDTH : 2 * WIDTH] + got[2 * WIDTH : 3 * WIDTH]
            alone = two_rows(rank_ref, pair) < 0
            sums_ref[:, span] = jnp.where(alone, xs_ref[:, span].astype(F32), got)

    @pl.when(jnp.logical_not(few))
    def _():
        for block in range(devices):
            col_ref[block * LANES : (block + 1) * LANES, :] = columns_of(
                cell_ref[block : block + 1, :].astype(F32)
            )
        for block in range(devices):
            row = cell_ref[block : block + 1, :].astype(F32)
            full_ref[...] = jnp.where(col_ref[...] == row, 1.0, 0.0).astype(BF16)
            sums_ref[:, block * LANES : (block + 1) * LANES] = mm(xs_ref[...], full_ref[...])


def spread_depth(values, zpos, rp_ref, pair):
    cut = slice(pair * 2 * LANES, (pair + 1) * 2 * LANES)
    for level in range(rp_ref.shape[0] // WIDTH):
        rp_ref[level * WIDTH : (level + 1) * WIDTH, cut] = jnp.where(
            zpos == level, values, 0.0
        ).astype(BF16)


def slab_rows(lp_ref, rp_ref, msg_ref):
    devices = msg_ref.shape[0]
    step = lp_ref.shape[0] // devices
    for quad in range(rp_ref.shape[0] // (4 * WIDTH)):
        out = mm_nt(lp_ref[...], rp_ref[quad * 4 * WIDTH : (quad + 1) * 4 * WIDTH, :]).astype(BF16)
        for half in range(2):
            level = 2 * quad + half
            for dest in range(devices):
                msg_ref[dest, level * step : (level + 1) * step, :] = out[
                    dest * step : (dest + 1) * step, half * LANES : (half + 1) * LANES
                ]


def cell_kernel(rx_ref, cell_ref, rank_ref, same_ref, zr_ref, lp_ref, msg_ref, lat_ref, sums_ref, pick_ref, full_ref, col_ref, xs_ref, rp_ref):
    devices = rx_ref.shape[0]
    for block in range(devices):
        xs_ref[:, block * LANES : (block + 1) * LANES] = rx_ref[block, 0:WIDTH, :]
    sum_cells(xs_ref, cell_ref, rank_ref, same_ref, sums_ref, pick_ref, full_ref, col_ref)
    for pair in range(devices // 2):
        cut = slice(pair * 2 * LANES, (pair + 1) * 2 * LANES)
        latent = sums_ref[:, cut]
        lat_ref[:, cut] = latent.astype(BF16)
        spread_depth(latent, two_rows(zr_ref, pair), rp_ref, pair)
    slab_rows(lp_ref, rp_ref, msg_ref)


def to_modes(rx_ref, table, sp_ref):
    levels = sp_ref.shape[0] // table.shape[0]
    step = table.shape[1] // rx_ref.shape[0]
    for level in range(levels):
        block = rx_ref[:, level * step : (level + 1) * step, :].reshape(table.shape[1], LANES)
        coeffs = mm(table, block).astype(BF16).astype(F32)
        sp_ref[pl.ds(level, table.shape[0], stride=levels), :] = coeffs


def swap_halves(values):
    return pltpu.roll(values, WIDTH, 1)


def mode_kernel(group_ref, rx_ref, own_ref, other_ref, table_ref, back_ref, msg_ref, spec_ref, sp_ref, mx_ref):
    devices = rx_ref.shape[0]
    own_rows = spec_ref.shape[1]
    modes = table_ref.shape[0]
    levels = sp_ref.shape[0] // modes
    step = back_ref.shape[0] // devices
    to_modes(rx_ref, table_ref[...], sp_ref)
    for dest in range(devices):
        spec_ref[dest] = sp_ref[dest * own_rows : (dest + 1) * own_rows, :].astype(BF16)
    left = lax.broadcasted_iota(jnp.int32, (levels, LANES), 1) < WIDTH
    for order in range(MODES):
        source, which = order // 2, order % 2
        mine = jnp.full((WIDTH, LANES), group_ref[0], jnp.int32) == which
        weight = jnp.where(
            mine,
            own_ref[source].astype(F32),
            other_ref[source].astype(F32),
        ).astype(BF16)
        at = order * 2 * levels
        even = sp_ref[at : at + levels, :]
        odd = sp_ref[at + levels : at + 2 * levels, :]
        rows = jnp.concatenate([even, swap_halves(even), odd, swap_halves(odd)], axis=0)
        out = mm(rows[:, 0:WIDTH].astype(BF16), weight)
        mx_ref[at : at + levels, :] = jnp.where(
            left, out[0:levels], swap_halves(out[levels : 2 * levels])
        )
        mx_ref[at + levels : at + 2 * levels, :] = jnp.where(
            left, swap_halves(out[2 * levels : 3 * levels]), out[3 * levels : 4 * levels]
        )
    for level in range(levels):
        mixed = mx_ref[pl.ds(level, modes, stride=levels), :].astype(BF16)
        out = mm(back_ref[...], mixed).astype(BF16)
        for dest in range(devices):
            msg_ref[dest, level * step : (level + 1) * step, :] = out[dest * step : (dest + 1) * step]


def pre_kernel(depth, rx_ref, lp_ref, lat_ref, cell_ref, skip_ref, bias_ref, msg_ref, pre_ref, rt_ref):
    devices = rx_ref.shape[0]
    rows = lp_ref.shape[0]
    step = rows // devices
    for level in range(rt_ref.shape[0] // LANES):
        block = rx_ref[:, level * step : (level + 1) * step, :].reshape(rows, LANES)
        rt_ref[level * LANES : (level + 1) * LANES, :] = block.T
    for pair in range(devices // 2):
        cut = slice(pair * 2 * LANES, (pair + 1) * 2 * LANES)
        zpos = jnp.bitwise_and(two_rows(cell_ref, pair), depth - 1)
        field = mm(rt_ref[...], lp_ref[:, cut])
        total = jnp.where(zpos == 0, field[0:WIDTH], 0.0)
        for level in range(1, depth):
            total += jnp.where(zpos == level, field[level * WIDTH : (level + 1) * WIDTH], 0.0)
        pre = total + mm_tn(skip_ref[...], lat_ref[:, cut]) + bias_ref[...]
        pre_ref[:, cut] = pre
        feats = gelu_value(pre).astype(BF16)
        for half in range(2):
            msg_ref[2 * pair + half] = feats[:, half * LANES : (half + 1) * LANES]


def slope_kernel(pre_ref, slope_ref):
    slope_ref[...] = gelu_slope(pre_ref[...])


def head_kernel(rx_ref, point_ref, pw_ref, head_ref, bias_ref, out_ref, area_ref, normal_ref, pres_ref, msg_ref, value_ref, hot_ref):
    devices = rx_ref.shape[0]
    points = area_ref.shape[1]
    rows = lax.broadcasted_iota(jnp.int32, (points, LANES), 0)
    for block in range(devices):
        cut = slice(block * LANES, (block + 1) * LANES)
        parts = three_parts(pw_ref[block : block + 1, :] * rx_ref[block].astype(F32))
        for index, part in enumerate(parts):
            value_ref[index * WIDTH : (index + 1) * WIDTH, cut] = part
        hot_ref[:, cut] = jnp.where(rows == point_ref[block : block + 1, :], 1.0, 0.0).astype(BF16)
    sums = mm_nt(value_ref[...], hot_ref[...])
    latent = sums[0:WIDTH] + sums[WIDTH : 2 * WIDTH] + sums[2 * WIDTH : 3 * WIDTH]
    first, second, third = three_parts(latent)
    weight = head_ref[...]
    head_pre = mm_tn(weight, first) + mm_tn(weight, second) + mm_tn(weight, third) + bias_ref[...]
    head = gelu_value(head_pre)
    pressure = jnp.sum(head * out_ref[...], axis=0, keepdims=True)
    pres_ref[...] = pressure
    along = [normal_ref[which : which + 1, :] * area_ref[...] for which in range(2)]
    first, second, third = three_parts(out_ref[...] * gelu_slope(head_pre))
    grad = mm(weight, first) + mm(weight, second) + mm(weight, third)
    place = lax.broadcasted_iota(jnp.int32, (16, points), 0)
    extra = jnp.zeros((16, points), F32)
    for which in range(2):
        for index, part in enumerate(three_parts(along[which])):
            extra = jnp.where(place == 3 + 3 * which + index, part.astype(F32), extra)
    upper = grad.astype(BF16)
    lower = (grad - upper.astype(F32)).astype(BF16)
    table = jnp.concatenate([upper, lower, extra.astype(BF16)], axis=0)
    lane = lax.broadcasted_iota(jnp.int32, (1, LANES), 1)
    partial = []
    for which in range(2):
        force = jnp.sum(pressure * area_ref[...] * normal_ref[which : which + 1, :], axis=1, keepdims=True)
        partial.append(force)
    force_row = jnp.where(lane == 0, partial[0], jnp.where(lane == 1, partial[1], 0.0))
    out_rows = lax.dot_general(
        jnp.concatenate([along[0], along[1], jnp.zeros((6, points), F32)], axis=0),
        head,
        (((1,), (1,)), ((), ())),
        precision=lax.Precision.HIGHEST,
        preferred_element_type=F32,
    )
    out_row = jnp.concatenate([out_rows[0:1], out_rows[1:2]], axis=1)
    place = lax.broadcasted_iota(jnp.int32, (16, LANES), 0)
    common = jnp.zeros((16, LANES), F32)
    for index, part in enumerate(three_parts(out_row)):
        common = jnp.where(place == 9 + index, part.astype(F32), common)
    for index, part in enumerate(three_parts(force_row)):
        common = jnp.where(place == 12 + index, part.astype(F32), common)
    for block in range(devices):
        cut = slice(block * LANES, (block + 1) * LANES)
        got = mm(table, hot_ref[:, cut])
        msg_ref[block, 0 : 2 * WIDTH, :] = got[0 : 2 * WIDTH].astype(BF16)
        tail = got[2 * WIDTH : 2 * WIDTH + 16] + common
        for index, part in enumerate(three_parts(pw_ref[block : block + 1, :])):
            tail = jnp.where(place == index, part.astype(F32), tail)
        msg_ref[block, 2 * WIDTH : 2 * WIDTH + 16, :] = tail.astype(BF16)


def fold_rows(values):
    first, second, third = three_parts(values)
    upper = jnp.concatenate([first.astype(F32), second.astype(F32)], axis=1)
    lower = jnp.concatenate([third.astype(F32), jnp.zeros_like(values)], axis=1)
    return upper, lower


def back_kernel(scale, rx_ref, target_ref, cell_ref, rank_ref, same_ref, zr_ref, lp_ref, lat_ref, slope_ref, msg_ref, force_ref, outg_ref, sums_ref, pick_ref, full_ref, col_ref, xs_ref, pg_ref, rp_ref):
    devices = rx_ref.shape[0]
    main = msg_ref.shape[1] - 16
    extra = slice(2 * WIDTH, 2 * WIDTH + 16)
    total = rx_ref[0, extra, :].astype(F32)
    for block in range(1, devices):
        total += rx_ref[block, extra, :].astype(F32)
    forces = scale * (total[12:13] + total[13:14] + total[14:15])
    force_ref[...] = forces[:, 0:2]
    misfit = forces[:, 0:2] - target_ref[...]
    drag, lift = misfit[:, 0:1], misfit[:, 1:2]
    twice = 2.0 * scale
    out_row = total[9:10] + total[10:11] + total[11:12]
    outg_ref[...] = twice * (drag * out_row[:, 0:WIDTH] + lift * out_row[:, WIDTH : 2 * WIDTH])
    for block in range(devices):
        tail = rx_ref[block, extra, :].astype(F32)
        weight, first, second = (
            tail[at : at + 1] + tail[at + 1 : at + 2] + tail[at + 2 : at + 3] for at in (0, 3, 6)
        )
        grad = rx_ref[block, 0:WIDTH, :].astype(F32) + rx_ref[block, WIDTH : 2 * WIDTH, :].astype(F32)
        along = twice * (drag * first + lift * second)
        grad = (along * grad).astype(BF16).astype(F32)
        xs_ref[:, block * LANES : (block + 1) * LANES] = (weight * grad).astype(BF16)
    sum_cells(xs_ref, cell_ref, rank_ref, same_ref, sums_ref, pick_ref, full_ref, col_ref)
    for pair in range(devices // 2):
        cut = slice(pair * 2 * LANES, (pair + 1) * 2 * LANES)
        grad = sums_ref[:, cut] * slope_ref[:, cut]
        zpos = two_rows(zr_ref, pair)
        pg_ref[:, cut] = jnp.where(zpos >= 0, grad, 0.0).astype(BF16)
        spread_depth(grad, zpos, rp_ref, pair)
    slab_rows(lp_ref, rp_ref, msg_ref)
    upper, lower = fold_rows(mm_nt(lat_ref[...], pg_ref[...]))
    for dest in range(msg_ref.shape[0]):
        cut = slice(8 * dest, 8 * dest + 8)
        rows = jnp.concatenate([upper[cut], lower[cut]], axis=0)
        msg_ref[dest, main : main + 16, :] = rows.astype(BF16)


def spec_kernel(half_ref, rx_ref, table_ref, spec_ref, msg_ref, sp_ref):
    peers = rx_ref.shape[0]
    devices, own_rows = spec_ref.shape[0], spec_ref.shape[1]
    part_rows = sp_ref.shape[0] // devices
    main = rx_ref.shape[1] - 16
    to_modes(rx_ref, table_ref[half_ref[0]], sp_ref)
    total = rx_ref[0, main : main + 16, :].astype(F32)
    for source in range(1, peers):
        total += rx_ref[source, main : main + 16, :].astype(F32)
    upper, lower = total[0:8], total[8:16]
    left = lax.broadcasted_iota(jnp.int32, (8, LANES), 1) < WIDTH
    value = jnp.where(left, upper + swap_halves(upper) + lower, 0.0)
    first, second, third = three_parts(value)
    upper = first.astype(F32) + swap_halves(second.astype(F32))
    rows = jnp.concatenate([upper, third.astype(F32)], axis=0).astype(BF16)
    for dest in range(devices):
        msg_ref[dest, 0:own_rows, :] = spec_ref[dest]
        msg_ref[dest, own_rows : own_rows + part_rows, :] = sp_ref[
            dest * part_rows : (dest + 1) * part_rows, :
        ].astype(BF16)
        msg_ref[dest, own_rows + part_rows : own_rows + part_rows + 16, :] = rows


def both_halves(values):
    return jnp.concatenate([values, swap_halves(values)], axis=0)[:, 0:WIDTH]


def final_kernel(peers, rx_ref, spec_hbm, skip_ref, spec_ref, sems):
    devices = rx_ref.shape[0]
    low = MODES // devices
    high = MODES // peers
    owned = spec_ref.shape[0] // MODES
    part_rows = owned * high * 8
    own_rows = rx_ref.shape[1] - 16 - part_rows
    copies = []
    for which in range(owned):
        for source in range(devices):
            at = which * 8 * low
            coeffs = rx_ref[source, at : at + 8 * low, :].astype(F32)
            peer, inner = divmod(low * source, high)
            at = own_rows + (which * high + inner) * 8
            grads = [
                rx_ref[peer + shift, at : at + 8 * low, :].astype(F32)
                for shift in range(0, devices, peers)
            ]
            for index in range(low):
                cut = slice(8 * index, 8 * index + 8)
                left = both_halves(coeffs[cut])
                left = jnp.concatenate([left] * len(grads), axis=0)
                right = jnp.concatenate([both_halves(part[cut]) for part in grads], axis=0)
                spec_ref[which * MODES + low * source + index] = mm_tn(
                    left.astype(BF16), right.astype(BF16)
                )
            done = which * MODES + low * (source + 1)
            if done % 16 == 0:
                span = pl.ds(done - 16, 16)
                copies.append(
                    pltpu.make_async_copy(
                        spec_ref.at[span], spec_hbm.at[span], sems.at[done // 16 - 1]
                    )
                )
                copies[-1].start()
    at = own_rows + part_rows
    for peer in range(peers):
        rows = rx_ref[peer, at : at + 16, :].astype(F32)
        for shift in range(peers, devices, peers):
            rows += rx_ref[peer + shift, at : at + 16, :].astype(F32)
        value = (rows[0:8] + swap_halves(rows[0:8]) + rows[8:16])[:, 0:WIDTH]
        skip_ref[8 * peer : 8 * peer + 8, :] = value
    for copy in copies:
        copy.wait()


def run(kernel, outs, ins, flops, scratch=(), smem=0, hbm=0, hbm_outs=0, grant=16):
    vmem = pl.BlockSpec(memory_space=pltpu.VMEM)
    far = pl.BlockSpec(memory_space=pltpu.HBM)
    scalar = pl.BlockSpec(memory_space=pltpu.SMEM)
    moved = sum(math.prod(a.shape) * a.dtype.itemsize for a in list(ins) + list(outs))
    return pl.pallas_call(
        kernel,
        out_shape=tuple(outs),
        in_specs=[scalar] * smem + [far] * hbm + [vmem] * (len(ins) - smem - hbm),
        out_specs=tuple([far] * hbm_outs + [vmem] * (len(outs) - hbm_outs)),
        scratch_shapes=list(scratch),
        compiler_params=pltpu.CompilerParams(vmem_limit_bytes=grant * 1024 * 1024),
        cost_estimate=pl.CostEstimate(flops=flops, bytes_accessed=moved, transcendentals=0),
    )(*ins)


def slab_step(
    point_feats,
    pair_point,
    pair_cell,
    kernel,
    counts,
    area,
    normals,
    targets,
    spec_weight,
    skip_weight,
    skip_bias,
    head_weight,
    head_bias,
    out_weight,
):
    n = lax.axis_size("gx")
    points = point_feats.shape[0]
    slots = n * LANES
    slab = GX // n
    low = MODES // n
    depth = ZL * n
    levels = depth * WIDTH // LANES
    rows = MODES * slab
    main = levels * slab * low
    own_rows = low * low * levels
    shape = jax.ShapeDtypeStruct

    by = host_rows(GY, MODES)
    bx = host_rows(GX, MODES)
    by_rows = jnp.asarray(np.repeat(by, slab, axis=0))
    table = np.zeros((MODES, low, n, low, slab), ml_dtypes.bfloat16)
    for index in range(low):
        table[:, index, :, index, :] = bx.reshape(MODES, n, slab)
    table = table.reshape(MODES * low, rows)
    back = jnp.asarray(np.ascontiguousarray(table.T))
    table = jnp.asarray(table)
    peers = 8
    halves = n // peers
    high = MODES // peers
    part_table = np.zeros((halves, MODES, high, peers, high, slab), ml_dtypes.bfloat16)
    for index in range(high):
        part_table[:, :, index, :, index, :] = np.moveaxis(
            bx.reshape(MODES, halves, peers, slab), 1, 0
        )
    part_table = jnp.asarray(part_table.reshape(halves, MODES * high, rows))
    near = [[half * peers + peer for peer in range(peers)] for half in range(halves)]
    half = (lax.axis_index("gx") // peers).astype(jnp.int32).reshape(1)

    def exchange(message):
        return lax.all_to_all(message, "gx", split_axis=0, concat_axis=0, tiled=True)

    group = lax.axis_index("groups").astype(jnp.int32).reshape(1)
    point_rows = pair_point[0]
    cells = pair_cell[:, 0, :]
    area_row = area.reshape(1, points)
    msg, pw = run(
        source_kernel,
        [shape((n, 2 * WIDTH, LANES), BF16), shape((n, LANES), F32)],
        [group, counts, point_rows, kernel[0], area_row, point_feats.T, spec_weight],
        2 * 80 * points * slots,
        scratch=[
            pltpu.VMEM((1, n), jnp.int32),
            pltpu.VMEM((n, LANES), jnp.int32),
            pltpu.VMEM((n, LANES), F32),
            pltpu.VMEM((1, points), F32),
            pltpu.VMEM((WIDTH, points), BF16),
            pltpu.VMEM((MODES, WIDTH, WIDTH), BF16),
            pltpu.SemaphoreType.DMA((6,)),
        ],
        smem=1,
        hbm=6,
        grant=60,
    )
    rx = exchange(msg)
    shared = 512
    lp, zr, rank, same = run(
        functools.partial(place_kernel, depth),
        [
            shape((rows, slots), BF16),
            shape((n, LANES), jnp.int32),
            shape((n, LANES), jnp.int32),
            shape((shared, shared), BF16),
        ],
        [cells, by_rows],
        2 * rows * LANES * slots,
        scratch=[
            pltpu.VMEM((slots, LANES), F32),
            pltpu.VMEM((n, LANES), F32),
            pltpu.VMEM((shared, slots), BF16),
            pltpu.VMEM((16, slots), BF16),
        ],
    )
    sum_scratch = [
        pltpu.VMEM((WIDTH, slots), F32),
        pltpu.VMEM((shared, slots), BF16),
        pltpu.VMEM((slots, LANES), BF16),
        pltpu.VMEM((slots, LANES), F32),
    ]
    own = rx[:, WIDTH : 2 * WIDTH, :]
    other = lax.ppermute(own, "groups", [(0, 1), (1, 0)])
    pair_rows = pltpu.VMEM((WIDTH, slots), BF16)
    deep_rows = pltpu.VMEM((depth * WIDTH, slots), BF16)
    big = 2 * WIDTH * slots * slots + 2 * rows * slots * depth * WIDTH
    msg, lat = run(
        cell_kernel,
        [shape((n, main, LANES), BF16), shape((WIDTH, slots), BF16)],
        [rx, cells, rank, same, zr, lp],
        big,
        scratch=sum_scratch + [pair_rows, deep_rows],
        grant=20,
    )
    columns = exchange(msg)
    msg, spec = run(
        mode_kernel,
        [shape((n, main, LANES), BF16), shape((n, own_rows, LANES), BF16)],
        [group, columns, own, other, table, back],
        4 * MODES * low * rows * depth * WIDTH,
        scratch=[pltpu.VMEM((MODES * low * levels, LANES), F32)] * 2,
        smem=1,
    )
    slabs = exchange(msg)
    msg, pre = run(
        functools.partial(pre_kernel, depth),
        [shape((n, WIDTH, LANES), BF16), shape((WIDTH, slots), F32)],
        [slabs, lp, lat, cells, skip_weight, skip_bias.reshape(WIDTH, 1)],
        2 * rows * slots * depth * WIDTH,
        scratch=[pltpu.VMEM((depth * WIDTH, rows), BF16)],
    )
    returned = exchange(msg)
    (slope,) = run(slope_kernel, [shape(pre.shape, F32)], [pre], 100 * WIDTH * slots)
    out_col = out_weight.reshape(WIDTH, 1)
    pressure, msg = run(
        head_kernel,
        [shape((1, points), F32), shape((n, 2 * WIDTH + 16, LANES), BF16)],
        [returned, point_rows, pw, head_weight, head_bias.reshape(WIDTH, 1), out_col, area_row, normals],
        2 * 3 * WIDTH * points * slots,
        scratch=[pltpu.VMEM((3 * WIDTH, slots), BF16), pltpu.VMEM((points, slots), BF16)],
    )
    grads = exchange(msg)
    scale = 1.0 / math.sqrt(points * n)
    msg, forces, out_grad = run(
        functools.partial(back_kernel, scale),
        [
            shape((peers, halves * main + 16, LANES), BF16),
            shape((1, 2), F32),
            shape((1, WIDTH), F32),
        ],
        [grads, targets.reshape(1, 2), cells, rank, same, zr, lp, lat, slope],
        big,
        scratch=sum_scratch + [pair_rows, pair_rows, deep_rows],
        grant=20,
    )
    grad_columns = lax.all_to_all(
        msg, "gx", split_axis=0, concat_axis=0, tiled=True, axis_index_groups=near
    )
    part_rows = MODES * high * levels // n
    (msg,) = run(
        spec_kernel,
        [shape((n, own_rows + part_rows + 16, LANES), BF16)],
        [half, grad_columns, part_table, spec],
        2 * MODES * high * rows * depth * WIDTH,
        scratch=[pltpu.VMEM((MODES * high * levels, LANES), F32)],
        smem=1,
    )
    finals = exchange(msg)
    spec_grad, skip_grad = run(
        functools.partial(final_kernel, peers),
        [shape((spec_weight.shape[0], WIDTH, WIDTH), F32), shape((WIDTH, WIDTH), F32)],
        [finals],
        2 * NMODE * WIDTH * WIDTH * depth // n,
        scratch=[
            pltpu.VMEM((spec_weight.shape[0], WIDTH, WIDTH), F32),
            pltpu.SemaphoreType.DMA((spec_weight.shape[0] // 16,)),
        ],
        hbm_outs=1,
    )
    return (pressure.reshape(points), forces.reshape(2), spec_grad, skip_grad, out_grad.reshape(WIDTH))


def solution(mesh):
    fits = mesh.shape["gx"] == 16 and mesh.shape["groups"] == 2
    per_device = slab_step if fits else general_step
    in_specs = (
        P(("groups", "gx"), None),
        P(("groups", "gx"), None, None),
        P(None, ("groups", "gx"), None),
        P(("groups", "gx"), None, None),
        P(("groups", "gx"), None),
        P(("groups", "gx")),
        P(None, ("groups", "gx")),
        P("groups"),
        P("gx", None, None),
        P(),
        P(),
        P(),
        P(),
        P(),
    )
    out_specs = (
        P(("groups", "gx")),
        P("groups"),
        P(("groups", "gx"), None, None),
        P("groups", None),
        P("groups"),
    )
    return jax.shard_map(
        per_device, mesh=mesh, in_specs=in_specs, out_specs=out_specs, check_vma=False
    )
```

```python
import functools
import math

import jax
import jax.numpy as jnp
import ml_dtypes
import numpy as np
from jax import lax
from jax.experimental import pallas as pl
from jax.experimental.pallas import tpu as pltpu
from jax.sharding import PartitionSpec as P

GX = 128
GY = 128
MODES = 32
ZL = 1
NMODE = 1024


def fourier_rows(length, number):
    places = jnp.arange(length, dtype=jnp.float32)
    order = jnp.arange(number)
    half = number // 2
    freqs = jnp.where(order < half, order, order - half + 1).astype(jnp.float32)
    angles = 2.0 * math.pi / length * freqs[:, None] * places[None, :]
    table = jnp.where((order < half)[:, None], jnp.cos(angles), jnp.sin(angles))
    return (table * math.sqrt(2.0 / length)).astype(jnp.bfloat16)


def gelu_value(values):
    return 0.5 * values * (1.0 + lax.erf(values * (1.0 / math.sqrt(2.0))))


def gelu_slope(values):
    return 0.5 * (1.0 + lax.erf(values * (1.0 / math.sqrt(2.0)))) + values * jnp.exp(
        -0.5 * values * values
    ) * (1.0 / math.sqrt(2.0 * math.pi))


def general_step(
    point_feats,
    pair_point,
    pair_cell,
    kernel,
    counts,
    area,
    normals,
    targets,
    spec_weight,
    skip_weight,
    skip_bias,
    head_weight,
    head_bias,
    out_weight,
):
    devices = lax.axis_size("gx")
    local_points, width = point_feats.shape
    block_slots = pair_point.shape[2]
    row_count = GX // devices
    depth = ZL * devices
    slab_cells = row_count * GY * depth
    valid_mask = jnp.arange(block_slots)[None, :] < counts[0][:, None]
    point_rows = pair_point[0]
    pair_weight = jnp.where(valid_mask, kernel[0], jnp.float32(0.0))
    sender_weight = pair_weight * area[point_rows]
    contrib = (sender_weight[..., None] * point_feats[point_rows].astype(jnp.float32)).astype(
        jnp.bfloat16
    )
    arrived = lax.all_to_all(contrib, "gx", split_axis=0, concat_axis=0, tiled=True)
    cell_rows = pair_cell[:, 0, :].reshape(-1)
    latent = jax.ops.segment_sum(
        arrived.reshape(-1, width).astype(jnp.float32), cell_rows, num_segments=slab_cells
    ).astype(jnp.bfloat16)
    col_table = fourier_rows(GY, MODES)
    row_table = fourier_rows(GX, MODES)
    volume = latent.reshape(row_count, GY, depth * width)
    along_y = jnp.einsum(
        "by,xyk->xbk", col_table, volume, preferred_element_type=jnp.float32
    ).astype(jnp.bfloat16)
    columns = lax.all_to_all(along_y, "gx", split_axis=2, concat_axis=0, tiled=True)
    spectrum = jnp.einsum(
        "ax,xbk->abk", row_table, columns, preferred_element_type=jnp.float32
    ).astype(jnp.bfloat16)
    mode_rows = lax.all_to_all(
        spectrum.reshape(NMODE, ZL * width), "gx", split_axis=0, concat_axis=1, tiled=True
    )
    own_modes = mode_rows.shape[0]
    mixed_rows = jnp.einsum(
        "mzc,mcd->mzd",
        mode_rows.reshape(own_modes, depth, width),
        spec_weight,
        preferred_element_type=jnp.float32,
    ).astype(jnp.bfloat16)
    mixed = lax.all_to_all(
        mixed_rows.reshape(own_modes, depth * width), "gx", split_axis=1, concat_axis=0, tiled=True
    )
    back_x = jnp.einsum(
        "ax,abk->xbk",
        row_table,
        mixed.reshape(MODES, MODES, ZL * width),
        preferred_element_type=jnp.float32,
    ).astype(jnp.bfloat16)
    slabs = lax.all_to_all(back_x, "gx", split_axis=0, concat_axis=2, tiled=True)
    spatial = jnp.einsum(
        "by,xbk->xyk", col_table, slabs, preferred_element_type=jnp.float32
    ).reshape(slab_cells, width)
    pre = spatial + jnp.dot(latent, skip_weight, preferred_element_type=jnp.float32) + skip_bias
    features = gelu_value(pre).astype(jnp.bfloat16)
    picked = features[cell_rows].reshape(devices, block_slots, width)
    returned = lax.all_to_all(picked, "gx", split_axis=0, concat_axis=0, tiled=True)
    point_latent = jax.ops.segment_sum(
        (pair_weight[..., None] * returned.astype(jnp.float32)).reshape(-1, width),
        point_rows.reshape(-1),
        num_segments=local_points,
    )
    head_matrix = head_weight.astype(jnp.float32)
    head_pre = jnp.dot(point_latent, head_matrix, precision=lax.Precision.HIGHEST) + head_bias
    head = gelu_value(head_pre)
    pressure = jnp.dot(head, out_weight, precision=lax.Precision.HIGHEST)
    weighted = pressure * area
    scale = 1.0 / math.sqrt(local_points * devices)
    totals = lax.psum(
        jnp.stack([jnp.sum(weighted * normals[0]), jnp.sum(weighted * normals[1])]), "gx"
    )
    forces = scale * totals
    misfit = forces - targets
    point_grad = 2.0 * scale * (misfit[0] * normals[0] + misfit[1] * normals[1]) * area
    out_part = jnp.dot(point_grad, head, precision=lax.Precision.HIGHEST)
    head_grad = point_grad[:, None] * out_weight[None, :] * gelu_slope(head_pre)
    latent_grad = jnp.dot(head_grad, head_matrix.T, precision=lax.Precision.HIGHEST).astype(
        jnp.bfloat16
    )
    grad_pairs = (pair_weight[..., None] * latent_grad[point_rows].astype(jnp.float32)).astype(
        jnp.bfloat16
    )
    grad_arrived = lax.all_to_all(grad_pairs, "gx", split_axis=0, concat_axis=0, tiled=True)
    cell_grad = jax.ops.segment_sum(
        grad_arrived.reshape(-1, width).astype(jnp.float32), cell_rows, num_segments=slab_cells
    )
    pre_grad = (cell_grad * gelu_slope(pre)).astype(jnp.bfloat16)
    skip_part = jnp.dot(latent.T, pre_grad, preferred_element_type=jnp.float32)
    grad_y = jnp.einsum(
        "by,xyk->xbk",
        col_table,
        pre_grad.reshape(row_count, GY, depth * width),
        preferred_element_type=jnp.float32,
    ).astype(jnp.bfloat16)
    grad_columns = lax.all_to_all(grad_y, "gx", split_axis=2, concat_axis=0, tiled=True)
    grad_spec = jnp.einsum(
        "ax,xbk->abk", row_table, grad_columns, preferred_element_type=jnp.float32
    ).astype(jnp.bfloat16)
    grad_rows = lax.all_to_all(
        grad_spec.reshape(NMODE, ZL * width), "gx", split_axis=0, concat_axis=1, tiled=True
    )
    own_modes = grad_rows.shape[0]
    spec_grad = jnp.einsum(
        "mzc,mzd->mcd",
        mode_rows.reshape(own_modes, depth, width),
        grad_rows.reshape(own_modes, depth, width),
        preferred_element_type=jnp.float32,
    )
    out_grad, skip_grad = lax.psum((out_part, skip_part), "gx")
    return (pressure, forces, spec_grad, skip_grad, out_grad)


F32 = jnp.float32
BF16 = jnp.bfloat16
LANES = 128
WIDTH = 64


def host_rows(length, number):
    places = np.arange(length, dtype=np.float32)
    order = np.arange(number)
    half = number // 2
    freqs = np.where(order < half, order, order - half + 1).astype(np.float32)
    angles = np.float32(2.0 * math.pi / length) * freqs[:, None] * places[None, :]
    table = np.where((order < half)[:, None], np.cos(angles), np.sin(angles))
    table = table.astype(np.float32) * np.float32(math.sqrt(2.0 / length))
    return table.astype(ml_dtypes.bfloat16)


def three_parts(values):
    first = values.astype(BF16)
    rest = values - first.astype(F32)
    second = rest.astype(BF16)
    third = (rest - second.astype(F32)).astype(BF16)
    return first, second, third


def mm(left, right):
    return jnp.dot(left, right, preferred_element_type=F32)


def mm_nt(left, right):
    return lax.dot_general(left, right, (((1,), (1,)), ((), ())), preferred_element_type=F32)


def mm_tn(left, right):
    return lax.dot_general(left, right, (((0,), (0,)), ((), ())), preferred_element_type=F32)


def two_rows(ref, pair):
    return jnp.concatenate([ref[2 * pair : 2 * pair + 1, :], ref[2 * pair + 1 : 2 * pair + 2, :]], axis=1)


def source_kernel(group_ref, count_hbm, point_hbm, kern_hbm, area_hbm, feat_hbm, weight_hbm, msg_ref, pw_ref, count_ref, point_ref, kern_ref, area_ref, feat_ref, weight_ref, sems):
    devices, points = point_ref.shape[0], feat_ref.shape[1]
    low = MODES // devices
    pieces = (
        (point_hbm, point_ref),
        (area_hbm, area_ref),
        (feat_hbm, feat_ref),
        (kern_hbm, kern_ref),
        (count_hbm, count_ref),
        (weight_hbm.at[pl.ds(group_ref[0] * MODES, MODES)], weight_ref),
    )
    copies = [
        pltpu.make_async_copy(source, place, sems.at[index])
        for index, (source, place) in enumerate(pieces)
    ]
    for copy in copies:
        copy.start()
    for copy in copies[:-1]:
        copy.wait()
    first, second, third = three_parts(area_ref[...])
    place = lax.broadcasted_iota(jnp.int32, (16, points), 0)
    extra = jnp.where(
        place == 0,
        first.astype(F32),
        jnp.where(place == 1, second.astype(F32), jnp.where(place == 2, third.astype(F32), 0.0)),
    ).astype(BF16)
    table = jnp.concatenate([feat_ref[...], extra], axis=0)
    rows = lax.broadcasted_iota(jnp.int32, (points, 2 * LANES), 0)
    lane = lax.broadcasted_iota(jnp.int32, (1, LANES), 1)
    for pair in range(devices // 2):
        hot = jnp.where(rows == two_rows(point_ref, pair), 1.0, 0.0).astype(BF16)
        got = mm(table, hot)
        spread = got[WIDTH : WIDTH + 1] + got[WIDTH + 1 : WIDTH + 2] + got[WIDTH + 2 : WIDTH + 3]
        for half in range(2):
            dest = 2 * pair + half
            cut = slice(half * LANES, (half + 1) * LANES)
            valid = lane < count_ref[0:1, dest : dest + 1]
            weight = jnp.where(valid, kern_ref[dest : dest + 1, :], 0.0)
            pw_ref[dest : dest + 1, :] = weight
            msg_ref[dest, 0:WIDTH, :] = ((weight * spread[:, cut]) * got[0:WIDTH, cut]).astype(BF16)
    copies[-1].wait()
    for dest in range(devices):
        msg_ref[dest, WIDTH : 2 * WIDTH, :] = jnp.concatenate(
            [weight_ref[low * dest], weight_ref[low * dest + 1]], axis=1
        )


def columns_of(row):
    return jnp.broadcast_to(row, (LANES, LANES)).T


def pick_rows(rank_ref, pick_ref):
    rows = lax.broadcasted_iota(jnp.int32, (pick_ref.shape[0], LANES), 0)
    for block in range(rank_ref.shape[0]):
        pick_ref[:, block * LANES : (block + 1) * LANES] = jnp.where(
            rows == rank_ref[block : block + 1, :], 1.0, 0.0
        ).astype(BF16)


def basis_rows(depth, cell_ref, by_ref, lp_ref):
    zbits = depth.bit_length() - 1
    rows = by_ref.shape[0]
    slab = rows // MODES
    wide = 2 * LANES
    yrow = lax.broadcasted_iota(jnp.int32, (GY, wide), 0)
    xrow = jnp.bitwise_and(lax.broadcasted_iota(jnp.int32, (rows, wide), 0), slab - 1)
    for pair in range(cell_ref.shape[0] // 2):
        cells = two_rows(cell_ref, pair)
        ypos = jnp.bitwise_and(jnp.right_shift(cells, zbits), GY - 1)
        xpos = jnp.right_shift(cells, zbits + GY.bit_length() - 1)
        hot = jnp.where(yrow == ypos, 1.0, 0.0).astype(BF16)
        lp_ref[:, pair * wide : (pair + 1) * wide] = jnp.where(
            xrow == xpos, mm(by_ref[...], hot), 0.0
        ).astype(BF16)


def place_kernel(depth, cell_ref, zr_ref, rank_ref, same_ref, col_ref, flag_ref, pick_ref, part_ref):
    devices = cell_ref.shape[0]
    shared = same_ref.shape[0]
    down = lax.broadcasted_iota(jnp.int32, (LANES, LANES), 0)
    along = lax.broadcasted_iota(jnp.int32, (LANES, LANES), 1)
    place = lax.broadcasted_iota(jnp.int32, (16, LANES), 0)
    for block in range(devices):
        cells = cell_ref[block : block + 1, :]
        cut = slice(block * LANES, (block + 1) * LANES)
        col_ref[cut, :] = columns_of(cells.astype(F32))
        high = jnp.right_shift(cells, 7).astype(F32)
        low = jnp.bitwise_and(cells, 127).astype(F32)
        part_ref[:, cut] = jnp.where(place == 0, high, jnp.where(place == 1, low, 0.0)).astype(BF16)
    for block in range(devices):
        cells = cell_ref[block : block + 1, :]
        row = cells.astype(F32)
        cut = slice(block * LANES, (block + 1) * LANES)
        same = jnp.where(col_ref[cut, :] == row, 1.0, 0.0)
        before = jnp.sum(jnp.where(down < along, same, 0.0), axis=0, keepdims=True)
        count = jnp.sum(same, axis=0, keepdims=True)
        if block:
            early = jnp.where(col_ref[0 : block * LANES, :] == row, 1.0, 0.0)
            early = jnp.sum(early, axis=0, keepdims=True)
            before += early
            count += early
        if block < devices - 1:
            late = jnp.where(col_ref[(block + 1) * LANES :, :] == row, 1.0, 0.0)
            count += jnp.sum(late, axis=0, keepdims=True)
        zr_ref[block : block + 1, :] = jnp.where(
            before > 0.0, -1, jnp.bitwise_and(cells, depth - 1)
        )
        flag_ref[block : block + 1, :] = jnp.where(count > 1.0, 1.0, 0.0)
    flags = flag_ref[...]
    marks = flags.astype(BF16)
    inside = mm(marks, jnp.where(down <= along, 1.0, 0.0).astype(BF16))
    above = jnp.where(down < along, 1.0, 0.0)[:, 0:devices][0:devices]
    ahead = jnp.sum(mm_tn(above.astype(BF16), marks), axis=1, keepdims=True)
    rank_ref[...] = jnp.where(flags > 0.0, (inside + ahead - flags).astype(jnp.int32), -1)
    pick_rows(rank_ref, pick_ref)
    found = mm_nt(part_ref[...], pick_ref[...])
    found = found[0:1] * 128.0 + found[1:2]
    for block in range(shared // LANES):
        column = columns_of(found[:, block * LANES : (block + 1) * LANES])
        same_ref[block * LANES : (block + 1) * LANES, :] = jnp.where(
            jnp.concatenate([column] * (shared // LANES), axis=1) == found, 1.0, 0.0
        ).astype(BF16)


def fold_parts(values):
    total = values[0:WIDTH]
    for at in range(WIDTH, values.shape[0], WIDTH):
        total = total + values[at : at + WIDTH]
    return total


def sum_cells(terms, xs_ref, cell_ref, rank_ref, same_ref, sums_ref, pick_ref, full_ref, col_ref):
    devices = cell_ref.shape[0]
    shared = same_ref.shape[0]
    few = jnp.max(rank_ref[...]) < shared

    @pl.when(few)
    def _():
        pick_rows(rank_ref, pick_ref)
        picked = mm_nt(xs_ref[...], pick_ref[...]).astype(BF16)
        total = fold_parts(mm(picked, same_ref[...]))
        parts = jnp.concatenate(three_parts(total)[0 : xs_ref.shape[0] // WIDTH], axis=0)
        for pair in range(devices // 2):
            span = slice(pair * 2 * LANES, (pair + 1) * 2 * LANES)
            got = fold_parts(mm(parts, pick_ref[:, span]))
            sums_ref[:, span] = jnp.where(two_rows(rank_ref, pair) < 0, terms(span), got)

    @pl.when(jnp.logical_not(few))
    def _():
        for block in range(devices):
            col_ref[block * LANES : (block + 1) * LANES, :] = columns_of(
                cell_ref[block : block + 1, :].astype(F32)
            )
        for block in range(devices):
            row = cell_ref[block : block + 1, :].astype(F32)
            full_ref[...] = jnp.where(col_ref[...] == row, 1.0, 0.0).astype(BF16)
            sums_ref[:, block * LANES : (block + 1) * LANES] = fold_parts(
                mm(xs_ref[...], full_ref[...])
            )


def spread_depth(values, zpos, rp_ref, pair):
    cut = slice(pair * 2 * LANES, (pair + 1) * 2 * LANES)
    for level in range(rp_ref.shape[0] // WIDTH):
        rp_ref[level * WIDTH : (level + 1) * WIDTH, cut] = jnp.where(
            zpos == level, values, 0.0
        ).astype(BF16)


def slab_rows(lp_ref, rp_ref, msg_ref):
    devices = msg_ref.shape[0]
    step = lp_ref.shape[0] // devices
    for quad in range(rp_ref.shape[0] // (4 * WIDTH)):
        out = mm_nt(lp_ref[...], rp_ref[quad * 4 * WIDTH : (quad + 1) * 4 * WIDTH, :]).astype(BF16)
        for half in range(2):
            level = 2 * quad + half
            for dest in range(devices):
                msg_ref[dest, level * step : (level + 1) * step, :] = out[
                    dest * step : (dest + 1) * step, half * LANES : (half + 1) * LANES
                ]


def cell_kernel(depth, rx_ref, cell_ref, rank_ref, same_ref, zr_ref, by_ref, msg_ref, lat_ref, sums_ref, pick_ref, full_ref, col_ref, xs_ref, rp_ref, lp_ref):
    devices = rx_ref.shape[0]
    for block in range(devices):
        xs_ref[:, block * LANES : (block + 1) * LANES] = rx_ref[block, 0:WIDTH, :]
    sum_cells(
        lambda span: xs_ref[:, span].astype(F32),
        xs_ref, cell_ref, rank_ref, same_ref, sums_ref, pick_ref, full_ref, col_ref,
    )
    basis_rows(depth, cell_ref, by_ref, lp_ref)
    for pair in range(devices // 2):
        cut = slice(pair * 2 * LANES, (pair + 1) * 2 * LANES)
        latent = sums_ref[:, cut]
        lat_ref[:, cut] = latent.astype(BF16)
        spread_depth(latent, two_rows(zr_ref, pair), rp_ref, pair)
    slab_rows(lp_ref, rp_ref, msg_ref)


def to_modes(rx_ref, table, sp_ref):
    levels = sp_ref.shape[0] // table.shape[0]
    step = table.shape[1] // rx_ref.shape[0]
    for level in range(levels):
        block = rx_ref[:, level * step : (level + 1) * step, :].reshape(table.shape[1], LANES)
        coeffs = mm(table, block).astype(BF16).astype(F32)
        sp_ref[pl.ds(level, table.shape[0], stride=levels), :] = coeffs


def swap_halves(values):
    return pltpu.roll(values, WIDTH, 1)


def mode_kernel(group_ref, rx_ref, own_ref, other_ref, table_ref, back_ref, msg_ref, spec_ref, sp_ref, mx_ref):
    devices = rx_ref.shape[0]
    own_rows = spec_ref.shape[1]
    modes = table_ref.shape[0]
    levels = sp_ref.shape[0] // modes
    step = back_ref.shape[0] // devices
    to_modes(rx_ref, table_ref[...], sp_ref)
    for dest in range(devices):
        spec_ref[dest] = sp_ref[dest * own_rows : (dest + 1) * own_rows, :].astype(BF16)
    left = lax.broadcasted_iota(jnp.int32, (levels, LANES), 1) < WIDTH
    for order in range(MODES):
        source, which = order // 2, order % 2
        mine = jnp.full((WIDTH, LANES), group_ref[0], jnp.int32) == which
        weight = jnp.where(
            mine,
            own_ref[source].astype(F32),
            other_ref[source].astype(F32),
        ).astype(BF16)
        at = order * 2 * levels
        even = sp_ref[at : at + levels, :]
        odd = sp_ref[at + levels : at + 2 * levels, :]
        rows = jnp.concatenate([even, swap_halves(even), odd, swap_halves(odd)], axis=0)
        out = mm(rows[:, 0:WIDTH].astype(BF16), weight)
        mx_ref[at : at + levels, :] = jnp.where(
            left, out[0:levels], swap_halves(out[levels : 2 * levels])
        )
        mx_ref[at + levels : at + 2 * levels, :] = jnp.where(
            left, swap_halves(out[2 * levels : 3 * levels]), out[3 * levels : 4 * levels]
        )
    for level in range(levels):
        mixed = mx_ref[pl.ds(level, modes, stride=levels), :].astype(BF16)
        out = mm(back_ref[...], mixed).astype(BF16)
        for dest in range(devices):
            msg_ref[dest, level * step : (level + 1) * step, :] = out[dest * step : (dest + 1) * step]


def pre_kernel(depth, rx_ref, by_ref, lat_ref, cell_ref, skip_ref, bias_ref, msg_ref, pre_ref, rt_ref, lp_ref):
    devices = rx_ref.shape[0]
    basis_rows(depth, cell_ref, by_ref, lp_ref)
    rows = lp_ref.shape[0]
    step = rows // devices
    for level in range(rt_ref.shape[0] // LANES):
        block = rx_ref[:, level * step : (level + 1) * step, :].reshape(rows, LANES)
        rt_ref[level * LANES : (level + 1) * LANES, :] = block.T
    for pair in range(devices // 2):
        cut = slice(pair * 2 * LANES, (pair + 1) * 2 * LANES)
        zpos = jnp.bitwise_and(two_rows(cell_ref, pair), depth - 1)
        field = mm(rt_ref[...], lp_ref[:, cut])
        total = jnp.where(zpos == 0, field[0:WIDTH], 0.0)
        for level in range(1, depth):
            total += jnp.where(zpos == level, field[level * WIDTH : (level + 1) * WIDTH], 0.0)
        pre = total + mm_tn(skip_ref[...], lat_ref[:, cut]) + bias_ref[...]
        pre_ref[:, cut] = pre
        feats = gelu_value(pre).astype(BF16)
        for half in range(2):
            msg_ref[2 * pair + half] = feats[:, half * LANES : (half + 1) * LANES]


def slope_kernel(pre_ref, slope_ref):
    slope_ref[...] = gelu_slope(pre_ref[...])


def head_kernel(rx_ref, point_ref, pw_ref, head_ref, bias_ref, out_ref, area_ref, normal_ref, pres_ref, msg_ref, value_ref, hot_ref):
    devices = rx_ref.shape[0]
    points = area_ref.shape[1]
    rows = lax.broadcasted_iota(jnp.int32, (points, LANES), 0)
    for block in range(devices):
        cut = slice(block * LANES, (block + 1) * LANES)
        parts = three_parts(pw_ref[block : block + 1, :] * rx_ref[block].astype(F32))
        for index, part in enumerate(parts):
            value_ref[index * WIDTH : (index + 1) * WIDTH, cut] = part
        hot_ref[:, cut] = jnp.where(rows == point_ref[block : block + 1, :], 1.0, 0.0).astype(BF16)
    sums = mm_nt(value_ref[...], hot_ref[...])
    latent = sums[0:WIDTH] + sums[WIDTH : 2 * WIDTH] + sums[2 * WIDTH : 3 * WIDTH]
    first, second, third = three_parts(latent)
    weight = head_ref[...]
    head_pre = mm_tn(weight, first) + mm_tn(weight, second) + mm_tn(weight, third) + bias_ref[...]
    head = gelu_value(head_pre)
    pressure = jnp.sum(head * out_ref[...], axis=0, keepdims=True)
    pres_ref[...] = pressure
    along = [normal_ref[which : which + 1, :] * area_ref[...] for which in range(2)]
    first, second, third = three_parts(out_ref[...] * gelu_slope(head_pre))
    grad = mm(weight, first) + mm(weight, second) + mm(weight, third)
    place = lax.broadcasted_iota(jnp.int32, (16, points), 0)
    extra = jnp.zeros((16, points), F32)
    for which in range(2):
        for index, part in enumerate(three_parts(along[which])):
            extra = jnp.where(place == 3 + 3 * which + index, part.astype(F32), extra)
    table = jnp.concatenate([grad.astype(BF16), extra.astype(BF16)], axis=0)
    lane = lax.broadcasted_iota(jnp.int32, (1, LANES), 1)
    partial = []
    for which in range(2):
        force = jnp.sum(pressure * area_ref[...] * normal_ref[which : which + 1, :], axis=1, keepdims=True)
        partial.append(force)
    force_row = jnp.where(lane == 0, partial[0], jnp.where(lane == 1, partial[1], 0.0))
    out_rows = lax.dot_general(
        jnp.concatenate([along[0], along[1], jnp.zeros((6, points), F32)], axis=0),
        head,
        (((1,), (1,)), ((), ())),
        precision=lax.Precision.HIGHEST,
        preferred_element_type=F32,
    )
    out_row = jnp.concatenate([out_rows[0:1], out_rows[1:2]], axis=1)
    place = lax.broadcasted_iota(jnp.int32, (16, LANES), 0)
    common = jnp.zeros((16, LANES), F32)
    for index, part in enumerate(three_parts(out_row)):
        common = jnp.where(place == 9 + index, part.astype(F32), common)
    for index, part in enumerate(three_parts(force_row)):
        common = jnp.where(place == 12 + index, part.astype(F32), common)
    for pair in range(devices // 2):
        got = mm(table, hot_ref[:, pair * 2 * LANES : (pair + 1) * 2 * LANES])
        for half in range(2):
            block = 2 * pair + half
            cut = slice(half * LANES, (half + 1) * LANES)
            msg_ref[block, 0:WIDTH, :] = got[0:WIDTH, cut].astype(BF16)
            tail = got[WIDTH : WIDTH + 16, cut] + common
            for index, part in enumerate(three_parts(pw_ref[block : block + 1, :])):
                tail = jnp.where(place == index, part.astype(F32), tail)
            msg_ref[block, WIDTH : WIDTH + 16, :] = tail.astype(BF16)


def fold_rows(values):
    first, second, third = three_parts(values)
    upper = jnp.concatenate([first.astype(F32), second.astype(F32)], axis=1)
    lower = jnp.concatenate([third.astype(F32), jnp.zeros_like(values)], axis=1)
    return upper, lower


def back_kernel(depth, scale, rx_ref, target_ref, cell_ref, rank_ref, same_ref, zr_ref, by_ref, lat_ref, slope_ref, msg_ref, force_ref, outg_ref, sums_ref, pick_ref, full_ref, col_ref, xs_ref, pg_ref, rp_ref, lp_ref, gp_ref):
    devices = rx_ref.shape[0]
    main = msg_ref.shape[1] - 16
    extra = slice(WIDTH, WIDTH + 16)
    total = rx_ref[0, extra, :].astype(F32)
    for block in range(1, devices):
        total += rx_ref[block, extra, :].astype(F32)
    forces = scale * (total[12:13] + total[13:14] + total[14:15])
    force_ref[...] = forces[:, 0:2]
    misfit = forces[:, 0:2] - target_ref[...]
    drag, lift = misfit[:, 0:1], misfit[:, 1:2]
    twice = 2.0 * scale
    out_row = total[9:10] + total[10:11] + total[11:12]
    outg_ref[...] = twice * (drag * out_row[:, 0:WIDTH] + lift * out_row[:, WIDTH : 2 * WIDTH])
    for block in range(devices):
        tail = rx_ref[block, extra, :].astype(F32)
        weight, first, second = (
            tail[at : at + 1] + tail[at + 1 : at + 2] + tail[at + 2 : at + 3] for at in (0, 3, 6)
        )
        factor = weight * (twice * (drag * first + lift * second))
        grad = factor * rx_ref[block, 0:WIDTH, :].astype(F32)
        cut = slice(block * LANES, (block + 1) * LANES)
        gp_ref[:, cut] = grad
        upper = grad.astype(BF16)
        xs_ref[0:WIDTH, cut] = upper
        xs_ref[WIDTH : 2 * WIDTH, cut] = (grad - upper.astype(F32)).astype(BF16)
    sum_cells(
        lambda span: gp_ref[:, span],
        xs_ref, cell_ref, rank_ref, same_ref, sums_ref, pick_ref, full_ref, col_ref,
    )
    basis_rows(depth, cell_ref, by_ref, lp_ref)
    for pair in range(devices // 2):
        cut = slice(pair * 2 * LANES, (pair + 1) * 2 * LANES)
        grad = sums_ref[:, cut] * slope_ref[:, cut]
        zpos = two_rows(zr_ref, pair)
        pg_ref[:, cut] = jnp.where(zpos >= 0, grad, 0.0).astype(BF16)
        spread_depth(grad, zpos, rp_ref, pair)
    slab_rows(lp_ref, rp_ref, msg_ref)
    upper, lower = fold_rows(mm_nt(lat_ref[...], pg_ref[...]))
    for dest in range(msg_ref.shape[0]):
        cut = slice(8 * dest, 8 * dest + 8)
        rows = jnp.concatenate([upper[cut], lower[cut]], axis=0)
        msg_ref[dest, main : main + 16, :] = rows.astype(BF16)


def spec_kernel(half_ref, rx_ref, table_ref, spec_ref, msg_ref, sp_ref):
    peers = rx_ref.shape[0]
    devices, own_rows = spec_ref.shape[0], spec_ref.shape[1]
    part_rows = sp_ref.shape[0] // devices
    main = rx_ref.shape[1] - 16
    to_modes(rx_ref, table_ref[half_ref[0]], sp_ref)
    total = rx_ref[0, main : main + 16, :].astype(F32)
    for source in range(1, peers):
        total += rx_ref[source, main : main + 16, :].astype(F32)
    upper, lower = total[0:8], total[8:16]
    left = lax.broadcasted_iota(jnp.int32, (8, LANES), 1) < WIDTH
    value = jnp.where(left, upper + swap_halves(upper) + lower, 0.0)
    first, second, third = three_parts(value)
    upper = first.astype(F32) + swap_halves(second.astype(F32))
    rows = jnp.concatenate([upper, third.astype(F32)], axis=0).astype(BF16)
    for dest in range(devices):
        msg_ref[dest, 0:own_rows, :] = spec_ref[dest]
        msg_ref[dest, own_rows : own_rows + part_rows, :] = sp_ref[
            dest * part_rows : (dest + 1) * part_rows, :
        ].astype(BF16)
        msg_ref[dest, own_rows + part_rows : own_rows + part_rows + 16, :] = rows


def both_halves(values):
    return jnp.concatenate([values, swap_halves(values)], axis=0)[:, 0:WIDTH]


def final_kernel(peers, rx_ref, spec_ref, skip_ref):
    devices = rx_ref.shape[0]
    low = MODES // devices
    high = MODES // peers
    owned = spec_ref.shape[0] // MODES
    part_rows = owned * high * 8
    own_rows = rx_ref.shape[1] - 16 - part_rows
    for which in range(owned):
        for source in range(devices):
            at = which * 8 * low
            coeffs = rx_ref[source, at : at + 8 * low, :].astype(F32)
            peer, inner = divmod(low * source, high)
            at = own_rows + (which * high + inner) * 8
            grads = [
                rx_ref[peer + shift, at : at + 8 * low, :].astype(F32)
                for shift in range(0, devices, peers)
            ]
            for index in range(low):
                cut = slice(8 * index, 8 * index + 8)
                left = both_halves(coeffs[cut])
                left = jnp.concatenate([left] * len(grads), axis=0)
                right = jnp.concatenate([both_halves(part[cut]) for part in grads], axis=0)
                spec_ref[which * MODES + low * source + index] = mm_tn(
                    left.astype(BF16), right.astype(BF16)
                )
    at = own_rows + part_rows
    for peer in range(peers):
        rows = rx_ref[peer, at : at + 16, :].astype(F32)
        for shift in range(peers, devices, peers):
            rows += rx_ref[peer + shift, at : at + 16, :].astype(F32)
        value = (rows[0:8] + swap_halves(rows[0:8]) + rows[8:16])[:, 0:WIDTH]
        skip_ref[8 * peer : 8 * peer + 8, :] = value


def run(kernel, outs, ins, flops, scratch=(), smem=0, hbm=0, hbm_outs=0, grant=16):
    vmem = pl.BlockSpec(memory_space=pltpu.VMEM)
    far = pl.BlockSpec(memory_space=pltpu.HBM)
    scalar = pl.BlockSpec(memory_space=pltpu.SMEM)
    moved = sum(math.prod(a.shape) * a.dtype.itemsize for a in list(ins) + list(outs))
    return pl.pallas_call(
        kernel,
        out_shape=tuple(outs),
        in_specs=[scalar] * smem + [far] * hbm + [vmem] * (len(ins) - smem - hbm),
        out_specs=tuple([far] * hbm_outs + [vmem] * (len(outs) - hbm_outs)),
        scratch_shapes=list(scratch),
        compiler_params=pltpu.CompilerParams(vmem_limit_bytes=grant * 1024 * 1024),
        cost_estimate=pl.CostEstimate(flops=flops, bytes_accessed=moved, transcendentals=0),
    )(*ins)


def slab_step(
    point_feats,
    pair_point,
    pair_cell,
    kernel,
    counts,
    area,
    normals,
    targets,
    spec_weight,
    skip_weight,
    skip_bias,
    head_weight,
    head_bias,
    out_weight,
):
    n = lax.axis_size("gx")
    points = point_feats.shape[0]
    slots = n * LANES
    slab = GX // n
    low = MODES // n
    depth = ZL * n
    levels = depth * WIDTH // LANES
    rows = MODES * slab
    main = levels * slab * low
    own_rows = low * low * levels
    shape = jax.ShapeDtypeStruct

    by = host_rows(GY, MODES)
    bx = host_rows(GX, MODES)
    by_rows = jnp.asarray(np.repeat(by, slab, axis=0))
    table = np.zeros((MODES, low, n, low, slab), ml_dtypes.bfloat16)
    for index in range(low):
        table[:, index, :, index, :] = bx.reshape(MODES, n, slab)
    table = table.reshape(MODES * low, rows)
    back = jnp.asarray(np.ascontiguousarray(table.T))
    table = jnp.asarray(table)
    peers = 8
    halves = n // peers
    high = MODES // peers
    part_table = np.zeros((halves, MODES, high, peers, high, slab), ml_dtypes.bfloat16)
    for index in range(high):
        part_table[:, :, index, :, index, :] = np.moveaxis(
            bx.reshape(MODES, halves, peers, slab), 1, 0
        )
    part_table = jnp.asarray(part_table.reshape(halves, MODES * high, rows))
    near = [[half * peers + peer for peer in range(peers)] for half in range(halves)]
    half = (lax.axis_index("gx") // peers).astype(jnp.int32).reshape(1)

    def exchange(message):
        return lax.all_to_all(message, "gx", split_axis=0, concat_axis=0, tiled=True)

    group = lax.axis_index("groups").astype(jnp.int32).reshape(1)
    point_rows = pair_point[0]
    cells = pair_cell[:, 0, :]
    area_row = area.reshape(1, points)
    msg, pw = run(
        source_kernel,
        [shape((n, 2 * WIDTH, LANES), BF16), shape((n, LANES), F32)],
        [group, counts, point_rows, kernel[0], area_row, point_feats.T, spec_weight],
        2 * 80 * points * slots,
        scratch=[
            pltpu.VMEM((1, n), jnp.int32),
            pltpu.VMEM((n, LANES), jnp.int32),
            pltpu.VMEM((n, LANES), F32),
            pltpu.VMEM((1, points), F32),
            pltpu.VMEM((WIDTH, points), BF16),
            pltpu.VMEM((MODES, WIDTH, WIDTH), BF16),
            pltpu.SemaphoreType.DMA((6,)),
        ],
        smem=1,
        hbm=6,
        grant=60,
    )
    rx = exchange(msg)
    shared = 384
    zr, rank, same = run(
        functools.partial(place_kernel, depth),
        [
            shape((n, LANES), jnp.int32),
            shape((n, LANES), jnp.int32),
            shape((shared, shared), BF16),
        ],
        [cells],
        2 * rows * LANES * slots,
        scratch=[
            pltpu.VMEM((slots, LANES), F32),
            pltpu.VMEM((n, LANES), F32),
            pltpu.VMEM((shared, slots), BF16),
            pltpu.VMEM((16, slots), BF16),
        ],
    )
    sum_scratch = [
        pltpu.VMEM((WIDTH, slots), F32),
        pltpu.VMEM((shared, slots), BF16),
        pltpu.VMEM((slots, LANES), BF16),
        pltpu.VMEM((slots, LANES), F32),
    ]
    own = rx[:, WIDTH : 2 * WIDTH, :]
    other = lax.ppermute(own, "groups", [(0, 1), (1, 0)])
    pair_rows = pltpu.VMEM((WIDTH, slots), BF16)
    basis = pltpu.VMEM((rows, slots), BF16)
    deep_rows = pltpu.VMEM((depth * WIDTH, slots), BF16)
    big = 2 * WIDTH * slots * slots + 2 * rows * slots * depth * WIDTH
    msg, lat = run(
        functools.partial(cell_kernel, depth),
        [shape((n, main, LANES), BF16), shape((WIDTH, slots), BF16)],
        [rx, cells, rank, same, zr, by_rows],
        big,
        scratch=sum_scratch + [pair_rows, deep_rows, basis],
        grant=20,
    )
    columns = exchange(msg)
    msg, spec = run(
        mode_kernel,
        [shape((n, main, LANES), BF16), shape((n, own_rows, LANES), BF16)],
        [group, columns, own, other, table, back],
        4 * MODES * low * rows * depth * WIDTH,
        scratch=[pltpu.VMEM((MODES * low * levels, LANES), F32)] * 2,
        smem=1,
    )
    slabs = exchange(msg)
    msg, pre = run(
        functools.partial(pre_kernel, depth),
        [shape((n, WIDTH, LANES), BF16), shape((WIDTH, slots), F32)],
        [slabs, by_rows, lat, cells, skip_weight, skip_bias.reshape(WIDTH, 1)],
        2 * rows * slots * depth * WIDTH,
        scratch=[pltpu.VMEM((depth * WIDTH, rows), BF16), basis],
    )
    returned = exchange(msg)
    (slope,) = run(slope_kernel, [shape(pre.shape, F32)], [pre], 100 * WIDTH * slots)
    out_col = out_weight.reshape(WIDTH, 1)
    pressure, msg = run(
        head_kernel,
        [shape((1, points), F32), shape((n, WIDTH + 16, LANES), BF16)],
        [returned, point_rows, pw, head_weight, head_bias.reshape(WIDTH, 1), out_col, area_row, normals],
        2 * 3 * WIDTH * points * slots,
        scratch=[pltpu.VMEM((3 * WIDTH, slots), BF16), pltpu.VMEM((points, slots), BF16)],
    )
    grads = exchange(msg)
    scale = 1.0 / math.sqrt(points * n)
    msg, forces, out_grad = run(
        functools.partial(back_kernel, depth, scale),
        [
            shape((peers, halves * main + 16, LANES), BF16),
            shape((1, 2), F32),
            shape((1, WIDTH), F32),
        ],
        [grads, targets.reshape(1, 2), cells, rank, same, zr, by_rows, lat, slope],
        big,
        scratch=sum_scratch
        + [pltpu.VMEM((2 * WIDTH, slots), BF16), pair_rows, deep_rows, basis]
        + [pltpu.VMEM((WIDTH, slots), F32)],
        grant=20,
    )
    grad_columns = lax.all_to_all(
        msg, "gx", split_axis=0, concat_axis=0, tiled=True, axis_index_groups=near
    )
    part_rows = MODES * high * levels // n
    (msg,) = run(
        spec_kernel,
        [shape((n, own_rows + part_rows + 16, LANES), BF16)],
        [half, grad_columns, part_table, spec],
        2 * MODES * high * rows * depth * WIDTH,
        scratch=[pltpu.VMEM((MODES * high * levels, LANES), F32)],
        smem=1,
    )
    finals = exchange(msg)
    spec_grad, skip_grad = run(
        functools.partial(final_kernel, peers),
        [shape((spec_weight.shape[0], WIDTH, WIDTH), F32), shape((WIDTH, WIDTH), F32)],
        [finals],
        2 * NMODE * WIDTH * WIDTH * depth // n,
    )
    return (pressure.reshape(points), forces.reshape(2), spec_grad, skip_grad, out_grad.reshape(WIDTH))


def solution(mesh):
    fits = mesh.shape["gx"] == 16 and mesh.shape["groups"] == 2
    per_device = slab_step if fits else general_step
    in_specs = (
        P(("groups", "gx"), None),
        P(("groups", "gx"), None, None),
        P(None, ("groups", "gx"), None),
        P(("groups", "gx"), None, None),
        P(("groups", "gx"), None),
        P(("groups", "gx")),
        P(None, ("groups", "gx")),
        P("groups"),
        P("gx", None, None),
        P(),
        P(),
        P(),
        P(),
        P(),
    )
    out_specs = (
        P(("groups", "gx")),
        P("groups"),
        P(("groups", "gx"), None, None),
        P("groups", None),
        P("groups"),
    )
    return jax.shard_map(
        per_device, mesh=mesh, in_specs=in_specs, out_specs=out_specs, check_vma=False
    )
```

```python
import functools
import math

import jax
import jax.numpy as jnp
import ml_dtypes
import numpy as np
from jax import lax
from jax.experimental import pallas as pl
from jax.experimental.pallas import tpu as pltpu
from jax.sharding import PartitionSpec as P

GX = 128
GY = 128
MODES = 32
ZL = 1
NMODE = 1024


def fourier_rows(length, number):
    places = jnp.arange(length, dtype=jnp.float32)
    order = jnp.arange(number)
    half = number // 2
    freqs = jnp.where(order < half, order, order - half + 1).astype(jnp.float32)
    angles = 2.0 * math.pi / length * freqs[:, None] * places[None, :]
    table = jnp.where((order < half)[:, None], jnp.cos(angles), jnp.sin(angles))
    return (table * math.sqrt(2.0 / length)).astype(jnp.bfloat16)


def gelu_value(values):
    return 0.5 * values * (1.0 + lax.erf(values * (1.0 / math.sqrt(2.0))))


def gelu_slope(values):
    return 0.5 * (1.0 + lax.erf(values * (1.0 / math.sqrt(2.0)))) + values * jnp.exp(
        -0.5 * values * values
    ) * (1.0 / math.sqrt(2.0 * math.pi))


def general_step(
    point_feats,
    pair_point,
    pair_cell,
    kernel,
    counts,
    area,
    normals,
    targets,
    spec_weight,
    skip_weight,
    skip_bias,
    head_weight,
    head_bias,
    out_weight,
):
    devices = lax.axis_size("gx")
    local_points, width = point_feats.shape
    block_slots = pair_point.shape[2]
    row_count = GX // devices
    depth = ZL * devices
    slab_cells = row_count * GY * depth
    valid_mask = jnp.arange(block_slots)[None, :] < counts[0][:, None]
    point_rows = pair_point[0]
    pair_weight = jnp.where(valid_mask, kernel[0], jnp.float32(0.0))
    sender_weight = pair_weight * area[point_rows]
    contrib = (sender_weight[..., None] * point_feats[point_rows].astype(jnp.float32)).astype(
        jnp.bfloat16
    )
    arrived = lax.all_to_all(contrib, "gx", split_axis=0, concat_axis=0, tiled=True)
    cell_rows = pair_cell[:, 0, :].reshape(-1)
    latent = jax.ops.segment_sum(
        arrived.reshape(-1, width).astype(jnp.float32), cell_rows, num_segments=slab_cells
    ).astype(jnp.bfloat16)
    col_table = fourier_rows(GY, MODES)
    row_table = fourier_rows(GX, MODES)
    volume = latent.reshape(row_count, GY, depth * width)
    along_y = jnp.einsum(
        "by,xyk->xbk", col_table, volume, preferred_element_type=jnp.float32
    ).astype(jnp.bfloat16)
    columns = lax.all_to_all(along_y, "gx", split_axis=2, concat_axis=0, tiled=True)
    spectrum = jnp.einsum(
        "ax,xbk->abk", row_table, columns, preferred_element_type=jnp.float32
    ).astype(jnp.bfloat16)
    mode_rows = lax.all_to_all(
        spectrum.reshape(NMODE, ZL * width), "gx", split_axis=0, concat_axis=1, tiled=True
    )
    own_modes = mode_rows.shape[0]
    mixed_rows = jnp.einsum(
        "mzc,mcd->mzd",
        mode_rows.reshape(own_modes, depth, width),
        spec_weight,
        preferred_element_type=jnp.float32,
    ).astype(jnp.bfloat16)
    mixed = lax.all_to_all(
        mixed_rows.reshape(own_modes, depth * width), "gx", split_axis=1, concat_axis=0, tiled=True
    )
    back_x = jnp.einsum(
        "ax,abk->xbk",
        row_table,
        mixed.reshape(MODES, MODES, ZL * width),
        preferred_element_type=jnp.float32,
    ).astype(jnp.bfloat16)
    slabs = lax.all_to_all(back_x, "gx", split_axis=0, concat_axis=2, tiled=True)
    spatial = jnp.einsum(
        "by,xbk->xyk", col_table, slabs, preferred_element_type=jnp.float32
    ).reshape(slab_cells, width)
    pre = spatial + jnp.dot(latent, skip_weight, preferred_element_type=jnp.float32) + skip_bias
    features = gelu_value(pre).astype(jnp.bfloat16)
    picked = features[cell_rows].reshape(devices, block_slots, width)
    returned = lax.all_to_all(picked, "gx", split_axis=0, concat_axis=0, tiled=True)
    point_latent = jax.ops.segment_sum(
        (pair_weight[..., None] * returned.astype(jnp.float32)).reshape(-1, width),
        point_rows.reshape(-1),
        num_segments=local_points,
    )
    head_matrix = head_weight.astype(jnp.float32)
    head_pre = jnp.dot(point_latent, head_matrix, precision=lax.Precision.HIGHEST) + head_bias
    head = gelu_value(head_pre)
    pressure = jnp.dot(head, out_weight, precision=lax.Precision.HIGHEST)
    weighted = pressure * area
    scale = 1.0 / math.sqrt(local_points * devices)
    totals = lax.psum(
        jnp.stack([jnp.sum(weighted * normals[0]), jnp.sum(weighted * normals[1])]), "gx"
    )
    forces = scale * totals
    misfit = forces - targets
    point_grad = 2.0 * scale * (misfit[0] * normals[0] + misfit[1] * normals[1]) * area
    out_part = jnp.dot(point_grad, head, precision=lax.Precision.HIGHEST)
    head_grad = point_grad[:, None] * out_weight[None, :] * gelu_slope(head_pre)
    latent_grad = jnp.dot(head_grad, head_matrix.T, precision=lax.Precision.HIGHEST).astype(
        jnp.bfloat16
    )
    grad_pairs = (pair_weight[..., None] * latent_grad[point_rows].astype(jnp.float32)).astype(
        jnp.bfloat16
    )
    grad_arrived = lax.all_to_all(grad_pairs, "gx", split_axis=0, concat_axis=0, tiled=True)
    cell_grad = jax.ops.segment_sum(
        grad_arrived.reshape(-1, width).astype(jnp.float32), cell_rows, num_segments=slab_cells
    )
    pre_grad = (cell_grad * gelu_slope(pre)).astype(jnp.bfloat16)
    skip_part = jnp.dot(latent.T, pre_grad, preferred_element_type=jnp.float32)
    grad_y = jnp.einsum(
        "by,xyk->xbk",
        col_table,
        pre_grad.reshape(row_count, GY, depth * width),
        preferred_element_type=jnp.float32,
    ).astype(jnp.bfloat16)
    grad_columns = lax.all_to_all(grad_y, "gx", split_axis=2, concat_axis=0, tiled=True)
    grad_spec = jnp.einsum(
        "ax,xbk->abk", row_table, grad_columns, preferred_element_type=jnp.float32
    ).astype(jnp.bfloat16)
    grad_rows = lax.all_to_all(
        grad_spec.reshape(NMODE, ZL * width), "gx", split_axis=0, concat_axis=1, tiled=True
    )
    own_modes = grad_rows.shape[0]
    spec_grad = jnp.einsum(
        "mzc,mzd->mcd",
        mode_rows.reshape(own_modes, depth, width),
        grad_rows.reshape(own_modes, depth, width),
        preferred_element_type=jnp.float32,
    )
    out_grad, skip_grad = lax.psum((out_part, skip_part), "gx")
    return (pressure, forces, spec_grad, skip_grad, out_grad)


F32 = jnp.float32
BF16 = jnp.bfloat16
LANES = 128
WIDTH = 64


def host_rows(length, number):
    places = np.arange(length, dtype=np.float32)
    order = np.arange(number)
    half = number // 2
    freqs = np.where(order < half, order, order - half + 1).astype(np.float32)
    angles = np.float32(2.0 * math.pi / length) * freqs[:, None] * places[None, :]
    table = np.where((order < half)[:, None], np.cos(angles), np.sin(angles))
    table = table.astype(np.float32) * np.float32(math.sqrt(2.0 / length))
    return table.astype(ml_dtypes.bfloat16)


def three_parts(values):
    first = values.astype(BF16)
    rest = values - first.astype(F32)
    second = rest.astype(BF16)
    third = (rest - second.astype(F32)).astype(BF16)
    return first, second, third


def mm(left, right):
    return jnp.dot(left, right, preferred_element_type=F32)


def mm_nt(left, right):
    return lax.dot_general(left, right, (((1,), (1,)), ((), ())), preferred_element_type=F32)


def mm_tn(left, right):
    return lax.dot_general(left, right, (((0,), (0,)), ((), ())), preferred_element_type=F32)


def two_rows(ref, pair):
    return jnp.concatenate([ref[2 * pair : 2 * pair + 1, :], ref[2 * pair + 1 : 2 * pair + 2, :]], axis=1)


def source_kernel(group_ref, count_hbm, point_hbm, kern_hbm, area_hbm, feat_hbm, weight_hbm, msg_ref, pw_ref, count_ref, point_ref, kern_ref, area_ref, feat_ref, weight_ref, sems):
    devices, points = point_ref.shape[0], feat_ref.shape[1]
    low = MODES // devices
    pieces = (
        (point_hbm, point_ref),
        (area_hbm, area_ref),
        (feat_hbm, feat_ref),
        (kern_hbm, kern_ref),
        (count_hbm, count_ref),
        (weight_hbm.at[pl.ds(group_ref[0] * MODES, MODES)], weight_ref),
    )
    copies = [
        pltpu.make_async_copy(source, place, sems.at[index])
        for index, (source, place) in enumerate(pieces)
    ]
    for copy in copies:
        copy.start()
    for copy in copies[:-1]:
        copy.wait()
    first, second, third = three_parts(area_ref[...])
    place = lax.broadcasted_iota(jnp.int32, (16, points), 0)
    extra = jnp.where(
        place == 0,
        first.astype(F32),
        jnp.where(place == 1, second.astype(F32), jnp.where(place == 2, third.astype(F32), 0.0)),
    ).astype(BF16)
    table = jnp.concatenate([feat_ref[...], extra], axis=0)
    rows = lax.broadcasted_iota(jnp.int32, (points, 2 * LANES), 0)
    lane = lax.broadcasted_iota(jnp.int32, (1, LANES), 1)
    for pair in range(devices // 2):
        hot = jnp.where(rows == two_rows(point_ref, pair), 1.0, 0.0).astype(BF16)
        got = mm(table, hot)
        spread = got[WIDTH : WIDTH + 1] + got[WIDTH + 1 : WIDTH + 2] + got[WIDTH + 2 : WIDTH + 3]
        for half in range(2):
            dest = 2 * pair + half
            cut = slice(half * LANES, (half + 1) * LANES)
            valid = lane < count_ref[0:1, dest : dest + 1]
            weight = jnp.where(valid, kern_ref[dest : dest + 1, :], 0.0)
            pw_ref[dest : dest + 1, :] = weight
            msg_ref[dest, 0:WIDTH, :] = ((weight * spread[:, cut]) * got[0:WIDTH, cut]).astype(BF16)
    copies[-1].wait()
    for dest in range(devices):
        msg_ref[dest, WIDTH : 2 * WIDTH, :] = jnp.concatenate(
            [weight_ref[low * dest], weight_ref[low * dest + 1]], axis=1
        )


def columns_of(row):
    return jnp.broadcast_to(row, (LANES, LANES)).T


def pick_rows(rank_ref, pick_ref):
    rows = lax.broadcasted_iota(jnp.int32, (pick_ref.shape[0], LANES), 0)
    for block in range(rank_ref.shape[0]):
        pick_ref[:, block * LANES : (block + 1) * LANES] = jnp.where(
            rows == rank_ref[block : block + 1, :], 1.0, 0.0
        ).astype(BF16)


def basis_rows(depth, cell_ref, by_ref, lp_ref):
    zbits = depth.bit_length() - 1
    rows = by_ref.shape[0]
    slab = rows // MODES
    wide = 2 * LANES
    yrow = lax.broadcasted_iota(jnp.int32, (GY, wide), 0)
    xrow = jnp.bitwise_and(lax.broadcasted_iota(jnp.int32, (rows, wide), 0), slab - 1)
    for pair in range(cell_ref.shape[0] // 2):
        cells = two_rows(cell_ref, pair)
        ypos = jnp.bitwise_and(jnp.right_shift(cells, zbits), GY - 1)
        xpos = jnp.right_shift(cells, zbits + GY.bit_length() - 1)
        hot = jnp.where(yrow == ypos, 1.0, 0.0).astype(BF16)
        lp_ref[:, pair * wide : (pair + 1) * wide] = jnp.where(
            xrow == xpos, mm(by_ref[...], hot), 0.0
        ).astype(BF16)


def basis_kernel(depth, cell_ref, by_ref, after_ref, lp_ref):
    basis_rows(depth, cell_ref, by_ref, lp_ref)


def place_kernel(depth, cell_ref, by_ref, zr_ref, rank_ref, same_ref, lp_ref, col_ref, flag_ref, pick_ref, part_ref):
    devices = cell_ref.shape[0]
    basis_rows(depth, cell_ref, by_ref, lp_ref)
    shared = same_ref.shape[0]
    down = lax.broadcasted_iota(jnp.int32, (LANES, LANES), 0)
    along = lax.broadcasted_iota(jnp.int32, (LANES, LANES), 1)
    place = lax.broadcasted_iota(jnp.int32, (16, LANES), 0)
    for block in range(devices):
        cells = cell_ref[block : block + 1, :]
        cut = slice(block * LANES, (block + 1) * LANES)
        col_ref[cut, :] = columns_of(cells.astype(F32))
        high = jnp.right_shift(cells, 7).astype(F32)
        low = jnp.bitwise_and(cells, 127).astype(F32)
        part_ref[:, cut] = jnp.where(place == 0, high, jnp.where(place == 1, low, 0.0)).astype(BF16)
    for block in range(devices):
        cells = cell_ref[block : block + 1, :]
        row = cells.astype(F32)
        cut = slice(block * LANES, (block + 1) * LANES)
        same = jnp.where(col_ref[cut, :] == row, 1.0, 0.0)
        before = jnp.sum(jnp.where(down < along, same, 0.0), axis=0, keepdims=True)
        count = jnp.sum(same, axis=0, keepdims=True)
        if block:
            early = jnp.where(col_ref[0 : block * LANES, :] == row, 1.0, 0.0)
            early = jnp.sum(early, axis=0, keepdims=True)
            before += early
            count += early
        if block < devices - 1:
            late = jnp.where(col_ref[(block + 1) * LANES :, :] == row, 1.0, 0.0)
            count += jnp.sum(late, axis=0, keepdims=True)
        zr_ref[block : block + 1, :] = jnp.where(
            before > 0.0, -1, jnp.bitwise_and(cells, depth - 1)
        )
        flag_ref[block : block + 1, :] = jnp.where(count > 1.0, 1.0, 0.0)
    flags = flag_ref[...]
    marks = flags.astype(BF16)
    inside = mm(marks, jnp.where(down <= along, 1.0, 0.0).astype(BF16))
    above = jnp.where(down < along, 1.0, 0.0)[:, 0:devices][0:devices]
    ahead = jnp.sum(mm_tn(above.astype(BF16), marks), axis=1, keepdims=True)
    rank_ref[...] = jnp.where(flags > 0.0, (inside + ahead - flags).astype(jnp.int32), -1)
    pick_rows(rank_ref, pick_ref)
    found = mm_nt(part_ref[...], pick_ref[...])
    found = found[0:1] * 128.0 + found[1:2]
    for block in range(shared // LANES):
        column = columns_of(found[:, block * LANES : (block + 1) * LANES])
        same_ref[block * LANES : (block + 1) * LANES, :] = jnp.where(
            jnp.concatenate([column] * (shared // LANES), axis=1) == found, 1.0, 0.0
        ).astype(BF16)


def fold_parts(values):
    total = values[0:WIDTH]
    for at in range(WIDTH, values.shape[0], WIDTH):
        total = total + values[at : at + WIDTH]
    return total


def sum_cells(terms, xs_ref, cell_ref, rank_ref, same_ref, sums_ref, pick_ref, full_ref, col_ref):
    devices = cell_ref.shape[0]
    shared = same_ref.shape[0]
    few = jnp.max(rank_ref[...]) < shared

    @pl.when(few)
    def _():
        pick_rows(rank_ref, pick_ref)
        picked = mm_nt(pick_ref[...], xs_ref[...]).astype(BF16)
        total = mm(same_ref[...], picked).T
        parts = three_parts(fold_parts(total))[0 : xs_ref.shape[0] // WIDTH]
        parts = jnp.concatenate(parts, axis=0)
        for pair in range(devices // 2):
            span = slice(pair * 2 * LANES, (pair + 1) * 2 * LANES)
            got = fold_parts(mm(parts, pick_ref[:, span]))
            sums_ref[:, span] = jnp.where(two_rows(rank_ref, pair) < 0, terms(span), got)

    @pl.when(jnp.logical_not(few))
    def _():
        for block in range(devices):
            col_ref[block * LANES : (block + 1) * LANES, :] = columns_of(
                cell_ref[block : block + 1, :].astype(F32)
            )
        for block in range(devices):
            row = cell_ref[block : block + 1, :].astype(F32)
            full_ref[...] = jnp.where(col_ref[...] == row, 1.0, 0.0).astype(BF16)
            sums_ref[:, block * LANES : (block + 1) * LANES] = fold_parts(
                mm(xs_ref[...], full_ref[...])
            )


def spread_depth(values, zpos, rp_ref, pair):
    cut = slice(pair * 2 * LANES, (pair + 1) * 2 * LANES)
    for level in range(rp_ref.shape[0] // WIDTH):
        rp_ref[level * WIDTH : (level + 1) * WIDTH, cut] = jnp.where(
            zpos == level, values, 0.0
        ).astype(BF16)


def slab_rows(lp_ref, rp_ref, msg_ref):
    devices = msg_ref.shape[0]
    step = lp_ref.shape[0] // devices
    for quad in range(rp_ref.shape[0] // (4 * WIDTH)):
        out = mm_nt(lp_ref[...], rp_ref[quad * 4 * WIDTH : (quad + 1) * 4 * WIDTH, :]).astype(BF16)
        for half in range(2):
            level = 2 * quad + half
            for dest in range(devices):
                msg_ref[dest, level * step : (level + 1) * step, :] = out[
                    dest * step : (dest + 1) * step, half * LANES : (half + 1) * LANES
                ]


def cell_kernel(rx_ref, cell_ref, rank_ref, same_ref, zr_ref, lp_ref, msg_ref, lat_ref, sums_ref, pick_ref, full_ref, col_ref, xs_ref, rp_ref):
    devices = rx_ref.shape[0]
    for block in range(devices):
        xs_ref[:, block * LANES : (block + 1) * LANES] = rx_ref[block, 0:WIDTH, :]
    sum_cells(
        lambda span: xs_ref[:, span].astype(F32),
        xs_ref, cell_ref, rank_ref, same_ref, sums_ref, pick_ref, full_ref, col_ref,
    )
    for pair in range(devices // 2):
        cut = slice(pair * 2 * LANES, (pair + 1) * 2 * LANES)
        latent = sums_ref[:, cut]
        lat_ref[:, cut] = latent.astype(BF16)
        spread_depth(latent, two_rows(zr_ref, pair), rp_ref, pair)
    slab_rows(lp_ref, rp_ref, msg_ref)


def to_modes(rx_ref, table, sp_ref):
    levels = sp_ref.shape[0] // table.shape[0]
    step = table.shape[1] // rx_ref.shape[0]
    for level in range(levels):
        block = rx_ref[:, level * step : (level + 1) * step, :].reshape(table.shape[1], LANES)
        coeffs = mm(table, block).astype(BF16).astype(F32)
        sp_ref[pl.ds(level, table.shape[0], stride=levels), :] = coeffs


def swap_halves(values):
    return pltpu.roll(values, WIDTH, 1)


def weight_kernel(group_ref, own_ref, other_ref, weight_ref):
    for order in range(MODES):
        source, which = order // 2, order % 2
        mine = jnp.full((WIDTH, LANES), group_ref[0], jnp.int32) == which
        weight_ref[order] = jnp.where(
            mine, own_ref[source].astype(F32), other_ref[source].astype(F32)
        ).astype(BF16)


def mode_kernel(rx_ref, weight_ref, table_ref, back_ref, msg_ref, spec_ref, sp_ref, mx_ref):
    devices = rx_ref.shape[0]
    own_rows = spec_ref.shape[1]
    modes = table_ref.shape[0]
    levels = sp_ref.shape[0] // modes
    step = back_ref.shape[0] // devices
    to_modes(rx_ref, table_ref[...], sp_ref)
    for dest in range(devices):
        spec_ref[dest] = sp_ref[dest * own_rows : (dest + 1) * own_rows, :].astype(BF16)
    left = lax.broadcasted_iota(jnp.int32, (levels, LANES), 1) < WIDTH
    for order in range(MODES):
        at = order * 2 * levels
        even = sp_ref[at : at + levels, :]
        odd = sp_ref[at + levels : at + 2 * levels, :]
        rows = jnp.concatenate([even, swap_halves(even), odd, swap_halves(odd)], axis=0)
        out = mm(rows[:, 0:WIDTH].astype(BF16), weight_ref[order])
        mx_ref[at : at + levels, :] = jnp.where(
            left, out[0:levels], swap_halves(out[levels : 2 * levels])
        )
        mx_ref[at + levels : at + 2 * levels, :] = jnp.where(
            left, swap_halves(out[2 * levels : 3 * levels]), out[3 * levels : 4 * levels]
        )
    for level in range(levels):
        mixed = mx_ref[pl.ds(level, modes, stride=levels), :].astype(BF16)
        out = mm(back_ref[...], mixed).astype(BF16)
        for dest in range(devices):
            msg_ref[dest, level * step : (level + 1) * step, :] = out[dest * step : (dest + 1) * step]


def skip_kernel(depth, cell_ref, by_ref, after_ref, lat_ref, skip_ref, bias_ref, lp_ref, term_ref):
    basis_rows(depth, cell_ref, by_ref, lp_ref)
    term_ref[...] = mm_tn(skip_ref[...], lat_ref[...]) + bias_ref[...]


def pre_kernel(depth, rx_ref, lp_ref, term_ref, cell_ref, spec_ref, msg_ref, pre_ref, rt_ref):
    devices = rx_ref.shape[0]
    rows = lp_ref.shape[0]
    step = rows // devices
    for level in range(rt_ref.shape[0] // LANES):
        block = rx_ref[:, level * step : (level + 1) * step, :].reshape(rows, LANES)
        rt_ref[level * LANES : (level + 1) * LANES, :] = block.T
    for pair in range(devices // 2):
        cut = slice(pair * 2 * LANES, (pair + 1) * 2 * LANES)
        zpos = jnp.bitwise_and(two_rows(cell_ref, pair), depth - 1)
        field = mm(rt_ref[...], lp_ref[:, cut])
        total = jnp.where(zpos == 0, field[0:WIDTH], 0.0)
        for level in range(1, depth):
            total += jnp.where(zpos == level, field[level * WIDTH : (level + 1) * WIDTH], 0.0)
        pre = total + term_ref[:, cut]
        pre_ref[:, cut] = pre
        feats = gelu_value(pre).astype(BF16)
        for half in range(2):
            dest = 2 * pair + half
            msg_ref[dest, 0:WIDTH, :] = feats[:, half * LANES : (half + 1) * LANES]
            msg_ref[dest, WIDTH:, :] = spec_ref[dest]


def slope_kernel(pre_ref, slope_ref):
    slope_ref[...] = gelu_slope(pre_ref[...])


def head_kernel(rx_ref, point_ref, pw_ref, head_ref, bias_ref, out_ref, area_ref, normal_ref, pres_ref, msg_ref, spec_ref, value_ref, hot_ref):
    devices = rx_ref.shape[0]
    points = area_ref.shape[1]
    rows = lax.broadcasted_iota(jnp.int32, (points, LANES), 0)
    for block in range(devices):
        cut = slice(block * LANES, (block + 1) * LANES)
        parts = three_parts(pw_ref[block : block + 1, :] * rx_ref[block, 0:WIDTH, :].astype(F32))
        for index, part in enumerate(parts):
            value_ref[index * WIDTH : (index + 1) * WIDTH, cut] = part
        hot_ref[:, cut] = jnp.where(rows == point_ref[block : block + 1, :], 1.0, 0.0).astype(BF16)
    sums = mm_nt(value_ref[...], hot_ref[...])
    latent = sums[0:WIDTH] + sums[WIDTH : 2 * WIDTH] + sums[2 * WIDTH : 3 * WIDTH]
    first, second, third = three_parts(latent)
    weight = head_ref[...]
    head_pre = mm_tn(weight, first) + mm_tn(weight, second) + mm_tn(weight, third) + bias_ref[...]
    head = gelu_value(head_pre)
    pressure = jnp.sum(head * out_ref[...], axis=0, keepdims=True)
    pres_ref[...] = pressure
    along = [normal_ref[which : which + 1, :] * area_ref[...] for which in range(2)]
    first, second, third = three_parts(out_ref[...] * gelu_slope(head_pre))
    grad = mm(weight, first) + mm(weight, second) + mm(weight, third)
    place = lax.broadcasted_iota(jnp.int32, (16, points), 0)
    extra = jnp.zeros((16, points), F32)
    for which in range(2):
        for index, part in enumerate(three_parts(along[which])):
            extra = jnp.where(place == 3 + 3 * which + index, part.astype(F32), extra)
    table = jnp.concatenate([grad.astype(BF16), extra.astype(BF16)], axis=0)
    lane = lax.broadcasted_iota(jnp.int32, (1, LANES), 1)
    partial = []
    for which in range(2):
        force = jnp.sum(pressure * area_ref[...] * normal_ref[which : which + 1, :], axis=1, keepdims=True)
        partial.append(force)
    force_row = jnp.where(lane == 0, partial[0], jnp.where(lane == 1, partial[1], 0.0))
    out_rows = lax.dot_general(
        jnp.concatenate([along[0], along[1], jnp.zeros((6, points), F32)], axis=0),
        head,
        (((1,), (1,)), ((), ())),
        precision=lax.Precision.HIGHEST,
        preferred_element_type=F32,
    )
    out_row = jnp.concatenate([out_rows[0:1], out_rows[1:2]], axis=1)
    place = lax.broadcasted_iota(jnp.int32, (16, LANES), 0)
    common = jnp.zeros((16, LANES), F32)
    for index, part in enumerate(three_parts(out_row)):
        common = jnp.where(place == 9 + index, part.astype(F32), common)
    for index, part in enumerate(three_parts(force_row)):
        common = jnp.where(place == 12 + index, part.astype(F32), common)
    for pair in range(devices // 2):
        got = mm(table, hot_ref[:, pair * 2 * LANES : (pair + 1) * 2 * LANES])
        for half in range(2):
            block = 2 * pair + half
            cut = slice(half * LANES, (half + 1) * LANES)
            msg_ref[block, 0:WIDTH, :] = got[0:WIDTH, cut].astype(BF16)
            tail = got[WIDTH : WIDTH + 16, cut] + common
            for index, part in enumerate(three_parts(pw_ref[block : block + 1, :])):
                tail = jnp.where(place == index, part.astype(F32), tail)
            msg_ref[block, WIDTH : WIDTH + 16, :] = tail.astype(BF16)
            spec_ref[block] = rx_ref[block, WIDTH:, :]


def fold_rows(values):
    first, second, third = three_parts(values)
    upper = jnp.concatenate([first.astype(F32), second.astype(F32)], axis=1)
    lower = jnp.concatenate([third.astype(F32), jnp.zeros_like(values)], axis=1)
    return upper, lower


def back_kernel(scale, rx_ref, target_ref, cell_ref, rank_ref, same_ref, zr_ref, lp_ref, lat_ref, slope_ref, msg_ref, force_ref, outg_ref, sums_ref, pick_ref, full_ref, col_ref, xs_ref, pg_ref, rp_ref, gp_ref):
    devices = rx_ref.shape[0]
    main = msg_ref.shape[1] - 16
    extra = slice(WIDTH, WIDTH + 16)
    total = rx_ref[0, extra, :].astype(F32)
    for block in range(1, devices):
        total += rx_ref[block, extra, :].astype(F32)
    forces = scale * (total[12:13] + total[13:14] + total[14:15])
    force_ref[...] = forces[:, 0:2]
    misfit = forces[:, 0:2] - target_ref[...]
    drag, lift = misfit[:, 0:1], misfit[:, 1:2]
    twice = 2.0 * scale
    out_row = total[9:10] + total[10:11] + total[11:12]
    outg_ref[...] = twice * (drag * out_row[:, 0:WIDTH] + lift * out_row[:, WIDTH : 2 * WIDTH])
    for block in range(devices):
        tail = rx_ref[block, extra, :].astype(F32)
        weight, first, second = (
            tail[at : at + 1] + tail[at + 1 : at + 2] + tail[at + 2 : at + 3] for at in (0, 3, 6)
        )
        factor = weight * (twice * (drag * first + lift * second))
        grad = factor * rx_ref[block, 0:WIDTH, :].astype(F32)
        cut = slice(block * LANES, (block + 1) * LANES)
        gp_ref[:, cut] = grad
        upper = grad.astype(BF16)
        xs_ref[0:WIDTH, cut] = upper
        xs_ref[WIDTH : 2 * WIDTH, cut] = (grad - upper.astype(F32)).astype(BF16)
    sum_cells(
        lambda span: gp_ref[:, span],
        xs_ref, cell_ref, rank_ref, same_ref, sums_ref, pick_ref, full_ref, col_ref,
    )
    for pair in range(devices // 2):
        cut = slice(pair * 2 * LANES, (pair + 1) * 2 * LANES)
        grad = sums_ref[:, cut] * slope_ref[:, cut]
        zpos = two_rows(zr_ref, pair)
        pg_ref[:, cut] = jnp.where(zpos >= 0, grad, 0.0).astype(BF16)
        spread_depth(grad, zpos, rp_ref, pair)
    slab_rows(lp_ref, rp_ref, msg_ref)
    upper, lower = fold_rows(mm_nt(lat_ref[...], pg_ref[...]))
    for dest in range(msg_ref.shape[0]):
        cut = slice(8 * dest, 8 * dest + 8)
        rows = jnp.concatenate([upper[cut], lower[cut]], axis=0)
        msg_ref[dest, main : main + 16, :] = rows.astype(BF16)


def spec_kernel(half_ref, rx_ref, table_ref, msg_ref, sp_ref):
    peers, devices = rx_ref.shape[0], msg_ref.shape[0]
    part_rows = sp_ref.shape[0] // devices
    main = rx_ref.shape[1] - 16
    to_modes(rx_ref, table_ref[half_ref[0]], sp_ref)
    total = rx_ref[0, main : main + 16, :].astype(F32)
    for source in range(1, peers):
        total += rx_ref[source, main : main + 16, :].astype(F32)
    upper, lower = total[0:8], total[8:16]
    left = lax.broadcasted_iota(jnp.int32, (8, LANES), 1) < WIDTH
    value = jnp.where(left, upper + swap_halves(upper) + lower, 0.0)
    first, second, third = three_parts(value)
    upper = first.astype(F32) + swap_halves(second.astype(F32))
    rows = jnp.concatenate([upper, third.astype(F32)], axis=0).astype(BF16)
    for dest in range(devices):
        msg_ref[dest, 0:part_rows, :] = sp_ref[dest * part_rows : (dest + 1) * part_rows, :].astype(BF16)
        msg_ref[dest, part_rows : part_rows + 16, :] = rows


def final_kernel(peers, rx_ref, own_ref, spec_ref, skip_ref):
    devices = rx_ref.shape[0]
    low = MODES // devices
    high = MODES // peers
    owned = spec_ref.shape[0] // MODES
    part_rows = rx_ref.shape[1] - 16
    left = lax.broadcasted_iota(jnp.int32, (8, LANES), 1) < WIDTH
    for which in range(owned):
        for source in range(devices):
            at = which * 8 * low
            coeffs = own_ref[source, at : at + 8 * low, :].astype(F32)
            first, second = coeffs[0:8], coeffs[8:16]
            block = [
                jnp.where(left, first, 0.0),
                jnp.where(left, swap_halves(first), 0.0),
                jnp.where(left, 0.0, swap_halves(second)),
                jnp.where(left, 0.0, second),
            ]
            peer, inner = divmod(low * source, high)
            at = (which * high + inner) * 8
            grads = []
            for shift in range(0, devices, peers):
                part = rx_ref[peer + shift, at : at + 8 * low, :].astype(F32)
                grads += [part[0:8], swap_halves(part[0:8]), part[8:16], swap_halves(part[8:16])]
            block = jnp.concatenate(block * (devices // peers), axis=0).astype(BF16)
            grads = jnp.concatenate(grads, axis=0)[:, 0:WIDTH].astype(BF16)
            found = mm_tn(block, grads)
            mode = which * MODES + low * source
            spec_ref[mode] = found[0:WIDTH]
            spec_ref[mode + 1] = found[WIDTH : 2 * WIDTH]
    for peer in range(peers):
        rows = rx_ref[peer, part_rows : part_rows + 16, :].astype(F32)
        for shift in range(peers, devices, peers):
            rows += rx_ref[peer + shift, part_rows : part_rows + 16, :].astype(F32)
        value = (rows[0:8] + swap_halves(rows[0:8]) + rows[8:16])[:, 0:WIDTH]
        skip_ref[8 * peer : 8 * peer + 8, :] = value


def run(kernel, outs, ins, flops, scratch=(), smem=0, hbm=0, hbm_outs=0, grant=16):
    vmem = pl.BlockSpec(memory_space=pltpu.VMEM)
    far = pl.BlockSpec(memory_space=pltpu.HBM)
    scalar = pl.BlockSpec(memory_space=pltpu.SMEM)
    moved = sum(math.prod(a.shape) * a.dtype.itemsize for a in list(ins) + list(outs))
    return pl.pallas_call(
        kernel,
        out_shape=tuple(outs),
        in_specs=[scalar] * smem + [far] * hbm + [vmem] * (len(ins) - smem - hbm),
        out_specs=tuple([far] * hbm_outs + [vmem] * (len(outs) - hbm_outs)),
        scratch_shapes=list(scratch),
        compiler_params=pltpu.CompilerParams(vmem_limit_bytes=grant * 1024 * 1024),
        cost_estimate=pl.CostEstimate(flops=flops, bytes_accessed=moved, transcendentals=0),
    )(*ins)


def slab_step(
    point_feats,
    pair_point,
    pair_cell,
    kernel,
    counts,
    area,
    normals,
    targets,
    spec_weight,
    skip_weight,
    skip_bias,
    head_weight,
    head_bias,
    out_weight,
):
    n = lax.axis_size("gx")
    points = point_feats.shape[0]
    slots = n * LANES
    slab = GX // n
    low = MODES // n
    depth = ZL * n
    levels = depth * WIDTH // LANES
    rows = MODES * slab
    main = levels * slab * low
    own_rows = low * low * levels
    shape = jax.ShapeDtypeStruct

    by = host_rows(GY, MODES)
    bx = host_rows(GX, MODES)
    by_rows = jnp.asarray(np.repeat(by, slab, axis=0))
    table = np.zeros((MODES, low, n, low, slab), ml_dtypes.bfloat16)
    for index in range(low):
        table[:, index, :, index, :] = bx.reshape(MODES, n, slab)
    table = table.reshape(MODES * low, rows)
    back = jnp.asarray(np.ascontiguousarray(table.T))
    table = jnp.asarray(table)
    peers = 8
    halves = n // peers
    high = MODES // peers
    part_table = np.zeros((halves, MODES, high, peers, high, slab), ml_dtypes.bfloat16)
    for index in range(high):
        part_table[:, :, index, :, index, :] = np.moveaxis(
            bx.reshape(MODES, halves, peers, slab), 1, 0
        )
    part_table = jnp.asarray(part_table.reshape(halves, MODES * high, rows))
    near = [[half * peers + peer for peer in range(peers)] for half in range(halves)]
    half = (lax.axis_index("gx") // peers).astype(jnp.int32).reshape(1)

    def exchange(message):
        return lax.all_to_all(message, "gx", split_axis=0, concat_axis=0, tiled=True)

    group = lax.axis_index("groups").astype(jnp.int32).reshape(1)
    point_rows = pair_point[0]
    cells = pair_cell[:, 0, :]
    area_row = area.reshape(1, points)
    msg, pw = run(
        source_kernel,
        [shape((n, 2 * WIDTH, LANES), BF16), shape((n, LANES), F32)],
        [group, counts, point_rows, kernel[0], area_row, point_feats.T, spec_weight],
        2 * 80 * points * slots,
        scratch=[
            pltpu.VMEM((1, n), jnp.int32),
            pltpu.VMEM((n, LANES), jnp.int32),
            pltpu.VMEM((n, LANES), F32),
            pltpu.VMEM((1, points), F32),
            pltpu.VMEM((WIDTH, points), BF16),
            pltpu.VMEM((MODES, WIDTH, WIDTH), BF16),
            pltpu.SemaphoreType.DMA((6,)),
        ],
        smem=1,
        hbm=6,
        grant=60,
    )
    rx = exchange(msg)
    shared = 384
    zr, rank, same, lp = run(
        functools.partial(place_kernel, depth),
        [
            shape((n, LANES), jnp.int32),
            shape((n, LANES), jnp.int32),
            shape((shared, shared), BF16),
            shape((rows, slots), BF16),
        ],
        [cells, by_rows],
        2 * rows * LANES * slots,
        scratch=[
            pltpu.VMEM((slots, LANES), F32),
            pltpu.VMEM((n, LANES), F32),
            pltpu.VMEM((shared, slots), BF16),
            pltpu.VMEM((16, slots), BF16),
        ],
    )
    sum_scratch = [
        pltpu.VMEM((WIDTH, slots), F32),
        pltpu.VMEM((shared, slots), BF16),
        pltpu.VMEM((slots, LANES), BF16),
        pltpu.VMEM((slots, LANES), F32),
    ]
    own = rx[:, WIDTH : 2 * WIDTH, :]
    other = lax.ppermute(own, "groups", [(0, 1), (1, 0)])
    pair_rows = pltpu.VMEM((WIDTH, slots), BF16)
    basis = shape((rows, slots), BF16)
    deep_rows = pltpu.VMEM((depth * WIDTH, slots), BF16)
    big = 2 * WIDTH * slots * slots + 2 * rows * slots * depth * WIDTH
    msg, lat = run(
        cell_kernel,
        [shape((n, main, LANES), BF16), shape((WIDTH, slots), BF16)],
        [rx, cells, rank, same, zr, lp],
        big,
        scratch=sum_scratch + [pair_rows, deep_rows],
        grant=20,
    )
    columns = exchange(msg)
    (weights,) = run(
        weight_kernel,
        [shape((MODES, WIDTH, LANES), BF16)],
        [group, own, other],
        MODES * WIDTH * LANES,
        smem=1,
    )
    msg, spec = run(
        mode_kernel,
        [shape((n, main, LANES), BF16), shape((n, own_rows, LANES), BF16)],
        [columns, weights, table, back],
        4 * MODES * low * rows * depth * WIDTH,
        scratch=[pltpu.VMEM((MODES * low * levels, LANES), F32)] * 2,
    )
    slabs = exchange(msg)
    lp, term = run(
        functools.partial(skip_kernel, depth),
        [basis, shape((WIDTH, slots), F32)],
        [cells, by_rows, spec, lat, skip_weight, skip_bias.reshape(WIDTH, 1)],
        2 * rows * LANES * slots,
    )
    msg, pre = run(
        functools.partial(pre_kernel, depth),
        [shape((n, WIDTH + own_rows, LANES), BF16), shape((WIDTH, slots), F32)],
        [slabs, lp, term, cells, spec],
        2 * rows * slots * depth * WIDTH,
        scratch=[pltpu.VMEM((depth * WIDTH, rows), BF16)],
    )
    returned = exchange(msg)
    (slope,) = run(slope_kernel, [shape(pre.shape, F32)], [pre], 100 * WIDTH * slots)
    out_col = out_weight.reshape(WIDTH, 1)
    pressure, msg, own_spec = run(
        head_kernel,
        [
            shape((1, points), F32),
            shape((n, WIDTH + 16, LANES), BF16),
            shape((n, own_rows, LANES), BF16),
        ],
        [returned, point_rows, pw, head_weight, head_bias.reshape(WIDTH, 1), out_col, area_row, normals],
        2 * 3 * WIDTH * points * slots,
        scratch=[pltpu.VMEM((3 * WIDTH, slots), BF16), pltpu.VMEM((points, slots), BF16)],
    )
    grads = exchange(msg)
    (lp,) = run(
        functools.partial(basis_kernel, depth),
        [basis],
        [cells, by_rows, pressure],
        2 * rows * LANES * slots,
    )
    scale = 1.0 / math.sqrt(points * n)
    msg, forces, out_grad = run(
        functools.partial(back_kernel, scale),
        [
            shape((peers, halves * main + 16, LANES), BF16),
            shape((1, 2), F32),
            shape((1, WIDTH), F32),
        ],
        [grads, targets.reshape(1, 2), cells, rank, same, zr, lp, lat, slope],
        big,
        scratch=sum_scratch
        + [pltpu.VMEM((2 * WIDTH, slots), BF16), pair_rows, deep_rows]
        + [pltpu.VMEM((WIDTH, slots), F32)],
        grant=20,
    )
    grad_columns = lax.all_to_all(
        msg, "gx", split_axis=0, concat_axis=0, tiled=True, axis_index_groups=near
    )
    part_rows = MODES * high * levels // n
    (msg,) = run(
        spec_kernel,
        [shape((n, part_rows + 16, LANES), BF16)],
        [half, grad_columns, part_table],
        2 * MODES * high * rows * depth * WIDTH,
        scratch=[pltpu.VMEM((MODES * high * levels, LANES), F32)],
        smem=1,
    )
    finals = exchange(msg)
    spec_grad, skip_grad = run(
        functools.partial(final_kernel, peers),
        [shape((spec_weight.shape[0], WIDTH, WIDTH), F32), shape((WIDTH, WIDTH), F32)],
        [finals, own_spec],
        2 * NMODE * WIDTH * WIDTH * depth // n,
    )
    return (pressure.reshape(points), forces.reshape(2), spec_grad, skip_grad, out_grad.reshape(WIDTH))


def solution(mesh):
    fits = mesh.shape["gx"] == 16 and mesh.shape["groups"] == 2
    per_device = slab_step if fits else general_step
    in_specs = (
        P(("groups", "gx"), None),
        P(("groups", "gx"), None, None),
        P(None, ("groups", "gx"), None),
        P(("groups", "gx"), None, None),
        P(("groups", "gx"), None),
        P(("groups", "gx")),
        P(None, ("groups", "gx")),
        P("groups"),
        P("gx", None, None),
        P(),
        P(),
        P(),
        P(),
        P(),
    )
    out_specs = (
        P(("groups", "gx")),
        P("groups"),
        P(("groups", "gx"), None, None),
        P("groups", None),
        P("groups"),
    )
    return jax.shard_map(
        per_device, mesh=mesh, in_specs=in_specs, out_specs=out_specs, check_vma=False
    )
```

```python
import functools
import math

import jax
import jax.numpy as jnp
import ml_dtypes
import numpy as np
from jax import lax
from jax.experimental import pallas as pl
from jax.experimental.pallas import tpu as pltpu
from jax.sharding import PartitionSpec as P

GX = 128
GY = 128
MODES = 32
ZL = 1
NMODE = 1024


def fourier_rows(length, number):
    places = jnp.arange(length, dtype=jnp.float32)
    order = jnp.arange(number)
    half = number // 2
    freqs = jnp.where(order < half, order, order - half + 1).astype(jnp.float32)
    angles = 2.0 * math.pi / length * freqs[:, None] * places[None, :]
    table = jnp.where((order < half)[:, None], jnp.cos(angles), jnp.sin(angles))
    return (table * math.sqrt(2.0 / length)).astype(jnp.bfloat16)


def gelu_value(values):
    return 0.5 * values * (1.0 + lax.erf(values * (1.0 / math.sqrt(2.0))))


def gelu_slope(values):
    return 0.5 * (1.0 + lax.erf(values * (1.0 / math.sqrt(2.0)))) + values * jnp.exp(
        -0.5 * values * values
    ) * (1.0 / math.sqrt(2.0 * math.pi))


def general_step(
    point_feats,
    pair_point,
    pair_cell,
    kernel,
    counts,
    area,
    normals,
    targets,
    spec_weight,
    skip_weight,
    skip_bias,
    head_weight,
    head_bias,
    out_weight,
):
    devices = lax.axis_size("gx")
    local_points, width = point_feats.shape
    block_slots = pair_point.shape[2]
    row_count = GX // devices
    depth = ZL * devices
    slab_cells = row_count * GY * depth
    valid_mask = jnp.arange(block_slots)[None, :] < counts[0][:, None]
    point_rows = pair_point[0]
    pair_weight = jnp.where(valid_mask, kernel[0], jnp.float32(0.0))
    sender_weight = pair_weight * area[point_rows]
    contrib = (sender_weight[..., None] * point_feats[point_rows].astype(jnp.float32)).astype(
        jnp.bfloat16
    )
    arrived = lax.all_to_all(contrib, "gx", split_axis=0, concat_axis=0, tiled=True)
    cell_rows = pair_cell[:, 0, :].reshape(-1)
    latent = jax.ops.segment_sum(
        arrived.reshape(-1, width).astype(jnp.float32), cell_rows, num_segments=slab_cells
    ).astype(jnp.bfloat16)
    col_table = fourier_rows(GY, MODES)
    row_table = fourier_rows(GX, MODES)
    volume = latent.reshape(row_count, GY, depth * width)
    along_y = jnp.einsum(
        "by,xyk->xbk", col_table, volume, preferred_element_type=jnp.float32
    ).astype(jnp.bfloat16)
    columns = lax.all_to_all(along_y, "gx", split_axis=2, concat_axis=0, tiled=True)
    spectrum = jnp.einsum(
        "ax,xbk->abk", row_table, columns, preferred_element_type=jnp.float32
    ).astype(jnp.bfloat16)
    mode_rows = lax.all_to_all(
        spectrum.reshape(NMODE, ZL * width), "gx", split_axis=0, concat_axis=1, tiled=True
    )
    own_modes = mode_rows.shape[0]
    mixed_rows = jnp.einsum(
        "mzc,mcd->mzd",
        mode_rows.reshape(own_modes, depth, width),
        spec_weight,
        preferred_element_type=jnp.float32,
    ).astype(jnp.bfloat16)
    mixed = lax.all_to_all(
        mixed_rows.reshape(own_modes, depth * width), "gx", split_axis=1, concat_axis=0, tiled=True
    )
    back_x = jnp.einsum(
        "ax,abk->xbk",
        row_table,
        mixed.reshape(MODES, MODES, ZL * width),
        preferred_element_type=jnp.float32,
    ).astype(jnp.bfloat16)
    slabs = lax.all_to_all(back_x, "gx", split_axis=0, concat_axis=2, tiled=True)
    spatial = jnp.einsum(
        "by,xbk->xyk", col_table, slabs, preferred_element_type=jnp.float32
    ).reshape(slab_cells, width)
    pre = spatial + jnp.dot(latent, skip_weight, preferred_element_type=jnp.float32) + skip_bias
    features = gelu_value(pre).astype(jnp.bfloat16)
    picked = features[cell_rows].reshape(devices, block_slots, width)
    returned = lax.all_to_all(picked, "gx", split_axis=0, concat_axis=0, tiled=True)
    point_latent = jax.ops.segment_sum(
        (pair_weight[..., None] * returned.astype(jnp.float32)).reshape(-1, width),
        point_rows.reshape(-1),
        num_segments=local_points,
    )
    head_matrix = head_weight.astype(jnp.float32)
    head_pre = jnp.dot(point_latent, head_matrix, precision=lax.Precision.HIGHEST) + head_bias
    head = gelu_value(head_pre)
    pressure = jnp.dot(head, out_weight, precision=lax.Precision.HIGHEST)
    weighted = pressure * area
    scale = 1.0 / math.sqrt(local_points * devices)
    totals = lax.psum(
        jnp.stack([jnp.sum(weighted * normals[0]), jnp.sum(weighted * normals[1])]), "gx"
    )
    forces = scale * totals
    misfit = forces - targets
    point_grad = 2.0 * scale * (misfit[0] * normals[0] + misfit[1] * normals[1]) * area
    out_part = jnp.dot(point_grad, head, precision=lax.Precision.HIGHEST)
    head_grad = point_grad[:, None] * out_weight[None, :] * gelu_slope(head_pre)
    latent_grad = jnp.dot(head_grad, head_matrix.T, precision=lax.Precision.HIGHEST).astype(
        jnp.bfloat16
    )
    grad_pairs = (pair_weight[..., None] * latent_grad[point_rows].astype(jnp.float32)).astype(
        jnp.bfloat16
    )
    grad_arrived = lax.all_to_all(grad_pairs, "gx", split_axis=0, concat_axis=0, tiled=True)
    cell_grad = jax.ops.segment_sum(
        grad_arrived.reshape(-1, width).astype(jnp.float32), cell_rows, num_segments=slab_cells
    )
    pre_grad = (cell_grad * gelu_slope(pre)).astype(jnp.bfloat16)
    skip_part = jnp.dot(latent.T, pre_grad, preferred_element_type=jnp.float32)
    grad_y = jnp.einsum(
        "by,xyk->xbk",
        col_table,
        pre_grad.reshape(row_count, GY, depth * width),
        preferred_element_type=jnp.float32,
    ).astype(jnp.bfloat16)
    grad_columns = lax.all_to_all(grad_y, "gx", split_axis=2, concat_axis=0, tiled=True)
    grad_spec = jnp.einsum(
        "ax,xbk->abk", row_table, grad_columns, preferred_element_type=jnp.float32
    ).astype(jnp.bfloat16)
    grad_rows = lax.all_to_all(
        grad_spec.reshape(NMODE, ZL * width), "gx", split_axis=0, concat_axis=1, tiled=True
    )
    own_modes = grad_rows.shape[0]
    spec_grad = jnp.einsum(
        "mzc,mzd->mcd",
        mode_rows.reshape(own_modes, depth, width),
        grad_rows.reshape(own_modes, depth, width),
        preferred_element_type=jnp.float32,
    )
    out_grad, skip_grad = lax.psum((out_part, skip_part), "gx")
    return (pressure, forces, spec_grad, skip_grad, out_grad)


F32 = jnp.float32
BF16 = jnp.bfloat16
LANES = 128
WIDTH = 64


def host_rows(length, number):
    places = np.arange(length, dtype=np.float32)
    order = np.arange(number)
    half = number // 2
    freqs = np.where(order < half, order, order - half + 1).astype(np.float32)
    angles = np.float32(2.0 * math.pi / length) * freqs[:, None] * places[None, :]
    table = np.where((order < half)[:, None], np.cos(angles), np.sin(angles))
    table = table.astype(np.float32) * np.float32(math.sqrt(2.0 / length))
    return table.astype(ml_dtypes.bfloat16)


def three_parts(values):
    first = values.astype(BF16)
    rest = values - first.astype(F32)
    second = rest.astype(BF16)
    third = (rest - second.astype(F32)).astype(BF16)
    return first, second, third


def mm(left, right):
    return jnp.dot(left, right, preferred_element_type=F32)


def mm_nt(left, right):
    return lax.dot_general(left, right, (((1,), (1,)), ((), ())), preferred_element_type=F32)


def mm_tn(left, right):
    return lax.dot_general(left, right, (((0,), (0,)), ((), ())), preferred_element_type=F32)


def two_rows(ref, pair):
    return jnp.concatenate([ref[2 * pair : 2 * pair + 1, :], ref[2 * pair + 1 : 2 * pair + 2, :]], axis=1)


def source_kernel(group_ref, count_hbm, point_hbm, kern_hbm, area_hbm, feat_hbm, weight_hbm, msg_ref, pw_ref, count_ref, point_ref, kern_ref, area_ref, feat_ref, weight_ref, sems):
    devices, points = point_ref.shape[0], feat_ref.shape[1]
    low = MODES // devices
    pieces = (
        (point_hbm, point_ref),
        (area_hbm, area_ref),
        (feat_hbm, feat_ref),
        (kern_hbm, kern_ref),
        (count_hbm, count_ref),
        (weight_hbm.at[pl.ds(group_ref[0] * MODES, MODES)], weight_ref),
    )
    copies = [
        pltpu.make_async_copy(source, place, sems.at[index])
        for index, (source, place) in enumerate(pieces)
    ]
    for copy in copies:
        copy.start()
    for copy in copies[:-1]:
        copy.wait()
    first, second, third = three_parts(area_ref[...])
    place = lax.broadcasted_iota(jnp.int32, (16, points), 0)
    extra = jnp.where(
        place == 0,
        first.astype(F32),
        jnp.where(place == 1, second.astype(F32), jnp.where(place == 2, third.astype(F32), 0.0)),
    ).astype(BF16)
    table = jnp.concatenate([feat_ref[...], extra], axis=0)
    rows = lax.broadcasted_iota(jnp.int32, (points, 2 * LANES), 0)
    lane = lax.broadcasted_iota(jnp.int32, (1, LANES), 1)
    for pair in range(devices // 2):
        hot = jnp.where(rows == two_rows(point_ref, pair), 1.0, 0.0).astype(BF16)
        got = mm(table, hot)
        spread = got[WIDTH : WIDTH + 1] + got[WIDTH + 1 : WIDTH + 2] + got[WIDTH + 2 : WIDTH + 3]
        for half in range(2):
            dest = 2 * pair + half
            cut = slice(half * LANES, (half + 1) * LANES)
            valid = lane < count_ref[0:1, dest : dest + 1]
            weight = jnp.where(valid, kern_ref[dest : dest + 1, :], 0.0)
            pw_ref[dest : dest + 1, :] = weight
            msg_ref[dest, 0:WIDTH, :] = ((weight * spread[:, cut]) * got[0:WIDTH, cut]).astype(BF16)
    copies[-1].wait()
    for dest in range(devices):
        msg_ref[dest, WIDTH : 2 * WIDTH, :] = jnp.concatenate(
            [weight_ref[low * dest], weight_ref[low * dest + 1]], axis=1
        )


def columns_of(row):
    return jnp.broadcast_to(row, (LANES, LANES)).T


def pick_rows(rank_ref, pick_ref):
    rows = lax.broadcasted_iota(jnp.int32, (pick_ref.shape[0], LANES), 0)
    for block in range(rank_ref.shape[0]):
        pick_ref[:, block * LANES : (block + 1) * LANES] = jnp.where(
            rows == rank_ref[block : block + 1, :], 1.0, 0.0
        ).astype(BF16)


def basis_rows(depth, cell_ref, by_ref, lp_ref):
    zbits = depth.bit_length() - 1
    rows = by_ref.shape[0]
    slab = rows // MODES
    wide = 2 * LANES
    yrow = lax.broadcasted_iota(jnp.int32, (GY, wide), 0)
    xrow = jnp.bitwise_and(lax.broadcasted_iota(jnp.int32, (rows, wide), 0), slab - 1)
    for pair in range(cell_ref.shape[0] // 2):
        cells = two_rows(cell_ref, pair)
        ypos = jnp.bitwise_and(jnp.right_shift(cells, zbits), GY - 1)
        xpos = jnp.right_shift(cells, zbits + GY.bit_length() - 1)
        hot = jnp.where(yrow == ypos, 1.0, 0.0).astype(BF16)
        lp_ref[:, pair * wide : (pair + 1) * wide] = jnp.where(
            xrow == xpos, mm(by_ref[...], hot), 0.0
        ).astype(BF16)


def basis_kernel(depth, cell_ref, by_ref, after_ref, lp_ref):
    basis_rows(depth, cell_ref, by_ref, lp_ref)


def place_kernel(depth, cell_ref, by_ref, zr_ref, rank_ref, home_ref, lp_ref, col_ref, flag_ref, pick_ref, part_ref):
    devices = cell_ref.shape[0]
    basis_rows(depth, cell_ref, by_ref, lp_ref)
    down = lax.broadcasted_iota(jnp.int32, (LANES, LANES), 0)
    along = lax.broadcasted_iota(jnp.int32, (LANES, LANES), 1)
    place = lax.broadcasted_iota(jnp.int32, (16, LANES), 0)
    for block in range(devices):
        cells = cell_ref[block : block + 1, :]
        row = cells.astype(F32)
        cut = slice(block * LANES, (block + 1) * LANES)
        col_ref[cut, :] = columns_of(row)
        high = jnp.right_shift(cells, 7).astype(F32)
        low = jnp.bitwise_and(cells, 127).astype(F32)
        part_ref[:, cut] = jnp.where(place == 0, high, jnp.where(place == 1, low, 0.0)).astype(BF16)
        same = jnp.logical_and(col_ref[cut, :] == row, down < along)
        before = jnp.max(jnp.where(same, 1.0, 0.0), axis=0, keepdims=True)
        if block:
            early = jnp.where(col_ref[0 : block * LANES, :] == row, 1.0, 0.0)
            before = jnp.maximum(before, jnp.max(early, axis=0, keepdims=True))
        zr_ref[block : block + 1, :] = jnp.where(
            before > 0.0, -1, jnp.bitwise_and(cells, depth - 1)
        )
        flag_ref[block : block + 1, :] = before
    flags = flag_ref[...]
    marks = flags.astype(BF16)
    inside = mm(marks, jnp.where(down <= along, 1.0, 0.0).astype(BF16))
    above = jnp.where(down < along, 1.0, 0.0)[:, 0:devices][0:devices]
    ahead = jnp.sum(mm_tn(above.astype(BF16), marks), axis=1, keepdims=True)
    rank_ref[...] = jnp.where(flags > 0.0, (inside + ahead - flags).astype(jnp.int32), -1)
    pick_rows(rank_ref, pick_ref)
    found = mm_nt(part_ref[...], pick_ref[...])
    found = found[0:1] * 128.0 + found[1:2]
    for block in range(home_ref.shape[0] // LANES):
        cut = slice(block * LANES, (block + 1) * LANES)
        home_ref[cut, :] = columns_of(found[:, cut])


def first_rows(cell_ref, zr_ref, home_ref, first_ref):
    for block in range(cell_ref.shape[0]):
        here = slice(block, block + 1)
        row = jnp.where(zr_ref[here, :] < 0, -1.0, cell_ref[here, :].astype(F32))
        first_ref[:, block * LANES : (block + 1) * LANES] = jnp.where(
            home_ref[...] == row, 1.0, 0.0
        ).astype(BF16)


def fold_parts(values):
    total = values[0:WIDTH]
    for at in range(WIDTH, values.shape[0], WIDTH):
        total = total + values[at : at + WIDTH]
    return total


def sum_cells(terms, xs_ref, cell_ref, rank_ref, zr_ref, home_ref, sums_ref, pick_ref, first_ref, full_ref, col_ref):
    devices = cell_ref.shape[0]
    few = jnp.max(rank_ref[...]) < home_ref.shape[0]

    @pl.when(few)
    def _():
        pick_rows(rank_ref, pick_ref)
        first_rows(cell_ref, zr_ref, home_ref, first_ref)
        moved = mm_nt(xs_ref[...], pick_ref[...]).astype(BF16)
        for pair in range(devices // 2):
            span = slice(pair * 2 * LANES, (pair + 1) * 2 * LANES)
            sums_ref[:, span] = terms(span) + fold_parts(mm(moved, first_ref[:, span]))

    @pl.when(jnp.logical_not(few))
    def _():
        for block in range(devices):
            col_ref[block * LANES : (block + 1) * LANES, :] = columns_of(
                cell_ref[block : block + 1, :].astype(F32)
            )
        for block in range(devices):
            row = cell_ref[block : block + 1, :].astype(F32)
            full_ref[...] = jnp.where(col_ref[...] == row, 1.0, 0.0).astype(BF16)
            sums_ref[:, block * LANES : (block + 1) * LANES] = fold_parts(
                mm(xs_ref[...], full_ref[...])
            )


def spread_depth(values, zpos, rp_ref, pair):
    cut = slice(pair * 2 * LANES, (pair + 1) * 2 * LANES)
    for level in range(rp_ref.shape[0] // WIDTH):
        rp_ref[level * WIDTH : (level + 1) * WIDTH, cut] = jnp.where(
            zpos == level, values, 0.0
        ).astype(BF16)


def slab_rows(lp_ref, rp_ref, msg_ref):
    devices = msg_ref.shape[0]
    step = lp_ref.shape[0] // devices
    for quad in range(rp_ref.shape[0] // (4 * WIDTH)):
        out = mm_nt(lp_ref[...], rp_ref[quad * 4 * WIDTH : (quad + 1) * 4 * WIDTH, :]).astype(BF16)
        for half in range(2):
            level = 2 * quad + half
            for dest in range(devices):
                msg_ref[dest, level * step : (level + 1) * step, :] = out[
                    dest * step : (dest + 1) * step, half * LANES : (half + 1) * LANES
                ]


def cell_kernel(rx_ref, cell_ref, rank_ref, zr_ref, home_ref, lp_ref, msg_ref, lat_ref, sums_ref, pick_ref, first_ref, full_ref, col_ref, xs_ref, rp_ref):
    devices = rx_ref.shape[0]
    for block in range(devices):
        xs_ref[:, block * LANES : (block + 1) * LANES] = rx_ref[block, 0:WIDTH, :]
    sum_cells(
        lambda span: xs_ref[:, span].astype(F32),
        xs_ref, cell_ref, rank_ref, zr_ref, home_ref, sums_ref, pick_ref, first_ref, full_ref, col_ref,
    )
    for pair in range(devices // 2):
        cut = slice(pair * 2 * LANES, (pair + 1) * 2 * LANES)
        latent = sums_ref[:, cut]
        lat_ref[:, cut] = latent.astype(BF16)
        spread_depth(latent, two_rows(zr_ref, pair), rp_ref, pair)
    slab_rows(lp_ref, rp_ref, msg_ref)


def to_modes(rx_ref, table, sp_ref):
    levels = sp_ref.shape[0] // table.shape[0]
    step = table.shape[1] // rx_ref.shape[0]
    for level in range(levels):
        block = rx_ref[:, level * step : (level + 1) * step, :].reshape(table.shape[1], LANES)
        coeffs = mm(table, block).astype(BF16).astype(F32)
        sp_ref[pl.ds(level, table.shape[0], stride=levels), :] = coeffs


def swap_halves(values):
    return pltpu.roll(values, WIDTH, 1)


def weight_kernel(group_ref, own_ref, other_ref, weight_ref):
    for order in range(MODES):
        source, which = order // 2, order % 2
        mine = jnp.full((WIDTH, LANES), group_ref[0], jnp.int32) == which
        weight_ref[order] = jnp.where(
            mine, own_ref[source].astype(F32), other_ref[source].astype(F32)
        ).astype(BF16)


def mode_kernel(rx_ref, weight_ref, table_ref, back_ref, msg_ref, spec_ref, sp_ref, mx_ref):
    devices = rx_ref.shape[0]
    own_rows = spec_ref.shape[1]
    modes = table_ref.shape[0]
    levels = sp_ref.shape[0] // modes
    step = back_ref.shape[0] // devices
    to_modes(rx_ref, table_ref[...], sp_ref)
    for dest in range(devices):
        spec_ref[dest] = sp_ref[dest * own_rows : (dest + 1) * own_rows, :].astype(BF16)
    left = lax.broadcasted_iota(jnp.int32, (levels, LANES), 1) < WIDTH
    for order in range(MODES):
        at = order * 2 * levels
        even = sp_ref[at : at + levels, :]
        odd = sp_ref[at + levels : at + 2 * levels, :]
        rows = jnp.concatenate([even, swap_halves(even), odd, swap_halves(odd)], axis=0)
        out = mm(rows[:, 0:WIDTH].astype(BF16), weight_ref[order])
        mx_ref[at : at + levels, :] = jnp.where(
            left, out[0:levels], swap_halves(out[levels : 2 * levels])
        )
        mx_ref[at + levels : at + 2 * levels, :] = jnp.where(
            left, swap_halves(out[2 * levels : 3 * levels]), out[3 * levels : 4 * levels]
        )
    for level in range(levels):
        mixed = mx_ref[pl.ds(level, modes, stride=levels), :].astype(BF16)
        out = mm(back_ref[...], mixed).astype(BF16)
        for dest in range(devices):
            msg_ref[dest, level * step : (level + 1) * step, :] = out[dest * step : (dest + 1) * step]


def skip_kernel(depth, cell_ref, by_ref, after_ref, rank_ref, zr_ref, home_ref, lat_ref, skip_ref, bias_ref, lp_ref, term_ref, pick_ref, first_ref):
    basis_rows(depth, cell_ref, by_ref, lp_ref)
    few = jnp.max(rank_ref[...]) < home_ref.shape[0]
    pick_rows(rank_ref, pick_ref)
    first_rows(cell_ref, zr_ref, home_ref, first_ref)
    shared = mm_nt(lat_ref[...], first_ref[...]).astype(BF16)
    for pair in range(cell_ref.shape[0] // 2):
        span = slice(pair * 2 * LANES, (pair + 1) * 2 * LANES)
        later = jnp.logical_and(two_rows(rank_ref, pair) >= 0, few)
        latent = jnp.where(later, mm(shared, pick_ref[:, span]), lat_ref[:, span].astype(F32))
        term_ref[:, span] = mm_tn(skip_ref[...], latent.astype(BF16)) + bias_ref[...]


def pre_kernel(depth, rx_ref, lp_ref, term_ref, cell_ref, spec_ref, msg_ref, pre_ref, rt_ref):
    devices = rx_ref.shape[0]
    rows = lp_ref.shape[0]
    step = rows // devices
    for level in range(rt_ref.shape[0] // LANES):
        block = rx_ref[:, level * step : (level + 1) * step, :].reshape(rows, LANES)
        rt_ref[level * LANES : (level + 1) * LANES, :] = block.T
    for pair in range(devices // 2):
        cut = slice(pair * 2 * LANES, (pair + 1) * 2 * LANES)
        zpos = jnp.bitwise_and(two_rows(cell_ref, pair), depth - 1)
        field = mm(rt_ref[...], lp_ref[:, cut])
        total = jnp.where(zpos == 0, field[0:WIDTH], 0.0)
        for level in range(1, depth):
            total += jnp.where(zpos == level, field[level * WIDTH : (level + 1) * WIDTH], 0.0)
        pre = total + term_ref[:, cut]
        pre_ref[:, cut] = pre
        feats = gelu_value(pre).astype(BF16)
        for half in range(2):
            dest = 2 * pair + half
            msg_ref[dest, 0:WIDTH, :] = feats[:, half * LANES : (half + 1) * LANES]
            msg_ref[dest, WIDTH:, :] = spec_ref[dest]


def slope_kernel(pre_ref, slope_ref):
    slope_ref[...] = gelu_slope(pre_ref[...])


def head_kernel(rx_ref, point_ref, pw_ref, head_ref, bias_ref, out_ref, area_ref, normal_ref, pres_ref, msg_ref, spec_ref, value_ref, hot_ref, na_ref):
    devices = rx_ref.shape[0]
    points = area_ref.shape[1]
    rows = lax.broadcasted_iota(jnp.int32, (points, LANES), 0)
    for block in range(devices):
        cut = slice(block * LANES, (block + 1) * LANES)
        parts = three_parts(pw_ref[block : block + 1, :] * rx_ref[block, 0:WIDTH, :].astype(F32))
        for index, part in enumerate(parts):
            value_ref[index * WIDTH : (index + 1) * WIDTH, cut] = part
        hot_ref[:, cut] = jnp.where(rows == point_ref[block : block + 1, :], 1.0, 0.0).astype(BF16)
    sums = mm_nt(value_ref[...], hot_ref[...])
    latent = sums[0:WIDTH] + sums[WIDTH : 2 * WIDTH] + sums[2 * WIDTH : 3 * WIDTH]
    first, second, third = three_parts(latent)
    weight = head_ref[...]
    head_pre = mm_tn(weight, first) + mm_tn(weight, second) + mm_tn(weight, third) + bias_ref[...]
    head = gelu_value(head_pre)
    pressure = jnp.sum(head * out_ref[...], axis=0, keepdims=True)
    pres_ref[...] = pressure
    along = [normal_ref[which : which + 1, :] * area_ref[...] for which in range(2)]
    first, second, third = three_parts(out_ref[...] * gelu_slope(head_pre))
    grad = mm(weight, first) + mm(weight, second) + mm(weight, third)
    place = lax.broadcasted_iota(jnp.int32, (16, points), 0)
    extra = jnp.zeros((16, points), F32)
    for which in range(2):
        for index, part in enumerate(three_parts(along[which])):
            extra = jnp.where(place == 3 * which + index, part.astype(F32), extra)
    table = jnp.concatenate([grad.astype(BF16), extra.astype(BF16)], axis=0)
    lane = lax.broadcasted_iota(jnp.int32, (1, LANES), 1)
    partial = []
    for which in range(2):
        force = jnp.sum(pressure * area_ref[...] * normal_ref[which : which + 1, :], axis=1, keepdims=True)
        partial.append(force)
    force_row = jnp.zeros((1, LANES), F32)
    for which in range(2):
        for index, part in enumerate(three_parts(partial[which])):
            force_row = jnp.where(lane == 3 * which + index, part.astype(F32), force_row)
    out_rows = lax.dot_general(
        jnp.concatenate([along[0], along[1], jnp.zeros((6, points), F32)], axis=0),
        head,
        (((1,), (1,)), ((), ())),
        precision=lax.Precision.HIGHEST,
        preferred_element_type=F32,
    )
    out_row = jnp.concatenate([out_rows[0:1], out_rows[1:2]], axis=1)
    place = lax.broadcasted_iota(jnp.int32, (8, LANES), 0)
    out_parts = three_parts(out_row)
    common = jnp.where(
        place == 4,
        out_parts[0].astype(F32),
        jnp.where(place == 5, out_parts[1].astype(F32), jnp.where(place == 6, force_row, 0.0)),
    )
    for pair in range(devices // 2):
        got = mm(table, hot_ref[:, pair * 2 * LANES : (pair + 1) * 2 * LANES])
        for half in range(2):
            block = 2 * pair + half
            cut = slice(half * LANES, (half + 1) * LANES)
            msg_ref[block, 0:WIDTH, :] = got[0:WIDTH, cut].astype(BF16)
            spec_ref[block] = rx_ref[block, WIDTH:, :]
            for which in range(2):
                at = WIDTH + 3 * which
                na_ref[which, block : block + 1, :] = (
                    got[at : at + 1, cut] + got[at + 1 : at + 2, cut] + got[at + 2 : at + 3, cut]
                )
    scaled = [three_parts(pw_ref[...] * na_ref[which]) for which in range(2)]
    rows = [scaled[which][index].astype(F32) for which in range(2) for index in range(2)]
    for block in range(devices):
        tail = common
        for index, row in enumerate(rows):
            tail = jnp.where(place == index, row[block : block + 1, :], tail)
        msg_ref[block, WIDTH : WIDTH + 8, :] = tail.astype(BF16)


def back_kernel(scale, rx_ref, target_ref, cell_ref, rank_ref, zr_ref, home_ref, lp_ref, lat_ref, slope_ref, msg_ref, skip_ref, force_ref, outg_ref, sums_ref, pick_ref, first_ref, full_ref, col_ref, xs_ref, pg_ref, rp_ref, gp_ref):
    devices = rx_ref.shape[0]
    extra = slice(WIDTH, WIDTH + 8)
    total = rx_ref[0, extra, :].astype(F32)
    for block in range(1, devices):
        total += rx_ref[block, extra, :].astype(F32)
    force = total[6:7]
    lane = lax.broadcasted_iota(jnp.int32, (1, 2), 1)
    forces = scale * jnp.where(
        lane == 0,
        force[:, 0:1] + force[:, 1:2] + force[:, 2:3],
        force[:, 3:4] + force[:, 4:5] + force[:, 5:6],
    )
    force_ref[...] = forces
    misfit = (2.0 * scale) * (forces - target_ref[...])
    drag, lift = misfit[:, 0:1], misfit[:, 1:2]
    out_row = total[4:5] + total[5:6]
    outg_ref[...] = drag * out_row[:, 0:WIDTH] + lift * out_row[:, WIDTH : 2 * WIDTH]
    for block in range(devices):
        tail = rx_ref[block, extra, :].astype(F32)
        factor = drag * (tail[0:1] + tail[1:2]) + lift * (tail[2:3] + tail[3:4])
        grad = factor * rx_ref[block, 0:WIDTH, :].astype(F32)
        cut = slice(block * LANES, (block + 1) * LANES)
        gp_ref[:, cut] = grad
        upper = grad.astype(BF16)
        xs_ref[0:WIDTH, cut] = upper
        xs_ref[WIDTH : 2 * WIDTH, cut] = (grad - upper.astype(F32)).astype(BF16)
    sum_cells(
        lambda span: gp_ref[:, span],
        xs_ref, cell_ref, rank_ref, zr_ref, home_ref, sums_ref, pick_ref, first_ref, full_ref, col_ref,
    )
    for pair in range(devices // 2):
        cut = slice(pair * 2 * LANES, (pair + 1) * 2 * LANES)
        grad = sums_ref[:, cut] * slope_ref[:, cut]
        zpos = two_rows(zr_ref, pair)
        pg_ref[:, cut] = jnp.where(zpos >= 0, grad, 0.0).astype(BF16)
        spread_depth(grad, zpos, rp_ref, pair)
    slab_rows(lp_ref, rp_ref, msg_ref)
    skip_ref[...] = mm_nt(lat_ref[...], pg_ref[...])


def spec_kernel(half_ref, rx_ref, table_ref, msg_ref, sp_ref):
    devices, part_rows = msg_ref.shape[0], msg_ref.shape[1]
    to_modes(rx_ref, table_ref[half_ref[0]], sp_ref)
    for dest in range(devices):
        msg_ref[dest] = sp_ref[dest * part_rows : (dest + 1) * part_rows, :].astype(BF16)


def final_kernel(peers, rx_ref, own_ref, spec_ref):
    devices = rx_ref.shape[0]
    low = MODES // devices
    high = MODES // peers
    owned = spec_ref.shape[0] // MODES
    left = lax.broadcasted_iota(jnp.int32, (8, LANES), 1) < WIDTH
    for which in range(owned):
        for source in range(devices):
            at = which * 8 * low
            coeffs = own_ref[source, at : at + 8 * low, :].astype(F32)
            first, second = coeffs[0:8], coeffs[8:16]
            block = [
                jnp.where(left, first, 0.0),
                jnp.where(left, swap_halves(first), 0.0),
                jnp.where(left, 0.0, swap_halves(second)),
                jnp.where(left, 0.0, second),
            ]
            peer, inner = divmod(low * source, high)
            at = (which * high + inner) * 8
            grads = []
            for shift in range(0, devices, peers):
                part = rx_ref[peer + shift, at : at + 8 * low, :].astype(F32)
                grads += [part[0:8], swap_halves(part[0:8]), part[8:16], swap_halves(part[8:16])]
            block = jnp.concatenate(block * (devices // peers), axis=0).astype(BF16)
            grads = jnp.concatenate(grads, axis=0)[:, 0:WIDTH].astype(BF16)
            found = mm_tn(block, grads)
            mode = which * MODES + low * source
            spec_ref[mode] = found[0:WIDTH]
            spec_ref[mode + 1] = found[WIDTH : 2 * WIDTH]


def run(kernel, outs, ins, flops, scratch=(), smem=0, hbm=0, hbm_outs=0, grant=16):
    vmem = pl.BlockSpec(memory_space=pltpu.VMEM)
    far = pl.BlockSpec(memory_space=pltpu.HBM)
    scalar = pl.BlockSpec(memory_space=pltpu.SMEM)
    moved = sum(math.prod(a.shape) * a.dtype.itemsize for a in list(ins) + list(outs))
    return pl.pallas_call(
        kernel,
        out_shape=tuple(outs),
        in_specs=[scalar] * smem + [far] * hbm + [vmem] * (len(ins) - smem - hbm),
        out_specs=tuple([far] * hbm_outs + [vmem] * (len(outs) - hbm_outs)),
        scratch_shapes=list(scratch),
        compiler_params=pltpu.CompilerParams(vmem_limit_bytes=grant * 1024 * 1024),
        cost_estimate=pl.CostEstimate(flops=flops, bytes_accessed=moved, transcendentals=0),
    )(*ins)


def slab_step(
    point_feats,
    pair_point,
    pair_cell,
    kernel,
    counts,
    area,
    normals,
    targets,
    spec_weight,
    skip_weight,
    skip_bias,
    head_weight,
    head_bias,
    out_weight,
):
    n = lax.axis_size("gx")
    points = point_feats.shape[0]
    slots = n * LANES
    slab = GX // n
    low = MODES // n
    depth = ZL * n
    levels = depth * WIDTH // LANES
    rows = MODES * slab
    main = levels * slab * low
    own_rows = low * low * levels
    shape = jax.ShapeDtypeStruct

    by = host_rows(GY, MODES)
    bx = host_rows(GX, MODES)
    by_rows = jnp.asarray(np.repeat(by, slab, axis=0))
    table = np.zeros((MODES, low, n, low, slab), ml_dtypes.bfloat16)
    for index in range(low):
        table[:, index, :, index, :] = bx.reshape(MODES, n, slab)
    table = table.reshape(MODES * low, rows)
    back = jnp.asarray(np.ascontiguousarray(table.T))
    table = jnp.asarray(table)
    peers = 8
    halves = n // peers
    high = MODES // peers
    part_table = np.zeros((halves, MODES, high, peers, high, slab), ml_dtypes.bfloat16)
    for index in range(high):
        part_table[:, :, index, :, index, :] = np.moveaxis(
            bx.reshape(MODES, halves, peers, slab), 1, 0
        )
    part_table = jnp.asarray(part_table.reshape(halves, MODES * high, rows))
    near = [[half * peers + peer for peer in range(peers)] for half in range(halves)]
    half = (lax.axis_index("gx") // peers).astype(jnp.int32).reshape(1)

    def exchange(message):
        return lax.all_to_all(message, "gx", split_axis=0, concat_axis=0, tiled=True)

    group = lax.axis_index("groups").astype(jnp.int32).reshape(1)
    point_rows = pair_point[0]
    cells = pair_cell[:, 0, :]
    area_row = area.reshape(1, points)
    msg, pw = run(
        source_kernel,
        [shape((n, 2 * WIDTH, LANES), BF16), shape((n, LANES), F32)],
        [group, counts, point_rows, kernel[0], area_row, point_feats.T, spec_weight],
        2 * 80 * points * slots,
        scratch=[
            pltpu.VMEM((1, n), jnp.int32),
            pltpu.VMEM((n, LANES), jnp.int32),
            pltpu.VMEM((n, LANES), F32),
            pltpu.VMEM((1, points), F32),
            pltpu.VMEM((WIDTH, points), BF16),
            pltpu.VMEM((MODES, WIDTH, WIDTH), BF16),
            pltpu.SemaphoreType.DMA((6,)),
        ],
        smem=1,
        hbm=6,
        grant=60,
    )
    rx = exchange(msg)
    shared = 256
    zr, rank, home, lp = run(
        functools.partial(place_kernel, depth),
        [
            shape((n, LANES), jnp.int32),
            shape((n, LANES), jnp.int32),
            shape((shared, LANES), F32),
            shape((rows, slots), BF16),
        ],
        [cells, by_rows],
        2 * rows * LANES * slots,
        scratch=[
            pltpu.VMEM((slots, LANES), F32),
            pltpu.VMEM((n, LANES), F32),
            pltpu.VMEM((shared, slots), BF16),
            pltpu.VMEM((16, slots), BF16),
        ],
    )
    sum_scratch = [
        pltpu.VMEM((WIDTH, slots), F32),
        pltpu.VMEM((shared, slots), BF16),
        pltpu.VMEM((shared, slots), BF16),
        pltpu.VMEM((slots, LANES), BF16),
        pltpu.VMEM((slots, LANES), F32),
    ]
    own = rx[:, WIDTH : 2 * WIDTH, :]
    other = lax.ppermute(own, "groups", [(0, 1), (1, 0)])
    pair_rows = pltpu.VMEM((WIDTH, slots), BF16)
    basis = shape((rows, slots), BF16)
    deep_rows = pltpu.VMEM((depth * WIDTH, slots), BF16)
    big = 2 * WIDTH * slots * slots + 2 * rows * slots * depth * WIDTH
    msg, lat = run(
        cell_kernel,
        [shape((n, main, LANES), BF16), shape((WIDTH, slots), BF16)],
        [rx, cells, rank, zr, home, lp],
        big,
        scratch=sum_scratch + [pair_rows, deep_rows],
        grant=20,
    )
    columns = exchange(msg)
    (weights,) = run(
        weight_kernel,
        [shape((MODES, WIDTH, LANES), BF16)],
        [group, own, other],
        MODES * WIDTH * LANES,
        smem=1,
    )
    msg, spec = run(
        mode_kernel,
        [shape((n, main, LANES), BF16), shape((n, own_rows, LANES), BF16)],
        [columns, weights, table, back],
        4 * MODES * low * rows * depth * WIDTH,
        scratch=[pltpu.VMEM((MODES * low * levels, LANES), F32)] * 2,
    )
    slabs = exchange(msg)
    lp, term = run(
        functools.partial(skip_kernel, depth),
        [basis, shape((WIDTH, slots), F32)],
        [cells, by_rows, spec, rank, zr, home, lat, skip_weight, skip_bias.reshape(WIDTH, 1)],
        2 * rows * LANES * slots,
        scratch=[pltpu.VMEM((shared, slots), BF16)] * 2,
    )
    msg, pre = run(
        functools.partial(pre_kernel, depth),
        [shape((n, WIDTH + own_rows, LANES), BF16), shape((WIDTH, slots), F32)],
        [slabs, lp, term, cells, spec],
        2 * rows * slots * depth * WIDTH,
        scratch=[pltpu.VMEM((depth * WIDTH, rows), BF16)],
    )
    returned = exchange(msg)
    (slope,) = run(slope_kernel, [shape(pre.shape, F32)], [pre], 100 * WIDTH * slots)
    out_col = out_weight.reshape(WIDTH, 1)
    pressure, msg, own_spec = run(
        head_kernel,
        [
            shape((1, points), F32),
            shape((n, WIDTH + 8, LANES), BF16),
            shape((n, own_rows, LANES), BF16),
        ],
        [returned, point_rows, pw, head_weight, head_bias.reshape(WIDTH, 1), out_col, area_row, normals],
        2 * 3 * WIDTH * points * slots,
        scratch=[
            pltpu.VMEM((3 * WIDTH, slots), BF16),
            pltpu.VMEM((points, slots), BF16),
            pltpu.VMEM((2, n, LANES), F32),
        ],
    )
    grads = exchange(msg)
    (lp,) = run(
        functools.partial(basis_kernel, depth),
        [basis],
        [cells, by_rows, pressure],
        2 * rows * LANES * slots,
    )
    scale = 1.0 / math.sqrt(points * n)
    msg, skip_grad, forces, out_grad = run(
        functools.partial(back_kernel, scale),
        [
            shape((peers, halves * main, LANES), BF16),
            shape((WIDTH, WIDTH), F32),
            shape((1, 2), F32),
            shape((1, WIDTH), F32),
        ],
        [grads, targets.reshape(1, 2), cells, rank, zr, home, lp, lat, slope],
        big,
        scratch=sum_scratch
        + [pltpu.VMEM((2 * WIDTH, slots), BF16), pair_rows, deep_rows]
        + [pltpu.VMEM((WIDTH, slots), F32)],
        grant=20,
    )
    grad_columns = lax.all_to_all(
        msg, "gx", split_axis=0, concat_axis=0, tiled=True, axis_index_groups=near
    )
    for bit in (1, 2, 4, 8):
        partner = [(index, index ^ bit) for index in range(n)]
        skip_grad = skip_grad + lax.ppermute(skip_grad, "gx", partner)
    part_rows = MODES * high * levels // n
    (msg,) = run(
        spec_kernel,
        [shape((n, part_rows, LANES), BF16)],
        [half, grad_columns, part_table],
        2 * MODES * high * rows * depth * WIDTH,
        scratch=[pltpu.VMEM((MODES * high * levels, LANES), F32)],
        smem=1,
    )
    finals = exchange(msg)
    (spec_grad,) = run(
        functools.partial(final_kernel, peers),
        [shape((spec_weight.shape[0], WIDTH, WIDTH), F32)],
        [finals, own_spec],
        2 * NMODE * WIDTH * WIDTH * depth // n,
    )
    return (pressure.reshape(points), forces.reshape(2), spec_grad, skip_grad, out_grad.reshape(WIDTH))


def solution(mesh):
    fits = mesh.shape["gx"] == 16 and mesh.shape["groups"] == 2
    per_device = slab_step if fits else general_step
    in_specs = (
        P(("groups", "gx"), None),
        P(("groups", "gx"), None, None),
        P(None, ("groups", "gx"), None),
        P(("groups", "gx"), None, None),
        P(("groups", "gx"), None),
        P(("groups", "gx")),
        P(None, ("groups", "gx")),
        P("groups"),
        P("gx", None, None),
        P(),
        P(),
        P(),
        P(),
        P(),
    )
    out_specs = (
        P(("groups", "gx")),
        P("groups"),
        P(("groups", "gx"), None, None),
        P("groups", None),
        P("groups"),
    )
    return jax.shard_map(
        per_device, mesh=mesh, in_specs=in_specs, out_specs=out_specs, check_vma=False
    )
```

```python
import functools
import math

import jax
import jax.numpy as jnp
import ml_dtypes
import numpy as np
from jax import lax
from jax.experimental import pallas as pl
from jax.experimental.pallas import tpu as pltpu
from jax.sharding import PartitionSpec as P

GX = 128
GY = 128
MODES = 32
ZL = 1
NMODE = 1024


def fourier_rows(length, number):
    places = jnp.arange(length, dtype=jnp.float32)
    order = jnp.arange(number)
    half = number // 2
    freqs = jnp.where(order < half, order, order - half + 1).astype(jnp.float32)
    angles = 2.0 * math.pi / length * freqs[:, None] * places[None, :]
    table = jnp.where((order < half)[:, None], jnp.cos(angles), jnp.sin(angles))
    return (table * math.sqrt(2.0 / length)).astype(jnp.bfloat16)


def gelu_value(values):
    return 0.5 * values * (1.0 + lax.erf(values * (1.0 / math.sqrt(2.0))))


def gelu_slope(values):
    return 0.5 * (1.0 + lax.erf(values * (1.0 / math.sqrt(2.0)))) + values * jnp.exp(
        -0.5 * values * values
    ) * (1.0 / math.sqrt(2.0 * math.pi))


def general_step(
    point_feats,
    pair_point,
    pair_cell,
    kernel,
    counts,
    area,
    normals,
    targets,
    spec_weight,
    skip_weight,
    skip_bias,
    head_weight,
    head_bias,
    out_weight,
):
    devices = lax.axis_size("gx")
    local_points, width = point_feats.shape
    block_slots = pair_point.shape[2]
    row_count = GX // devices
    depth = ZL * devices
    slab_cells = row_count * GY * depth
    valid_mask = jnp.arange(block_slots)[None, :] < counts[0][:, None]
    point_rows = pair_point[0]
    pair_weight = jnp.where(valid_mask, kernel[0], jnp.float32(0.0))
    sender_weight = pair_weight * area[point_rows]
    contrib = (sender_weight[..., None] * point_feats[point_rows].astype(jnp.float32)).astype(
        jnp.bfloat16
    )
    arrived = lax.all_to_all(contrib, "gx", split_axis=0, concat_axis=0, tiled=True)
    cell_rows = pair_cell[:, 0, :].reshape(-1)
    latent = jax.ops.segment_sum(
        arrived.reshape(-1, width).astype(jnp.float32), cell_rows, num_segments=slab_cells
    ).astype(jnp.bfloat16)
    col_table = fourier_rows(GY, MODES)
    row_table = fourier_rows(GX, MODES)
    volume = latent.reshape(row_count, GY, depth * width)
    along_y = jnp.einsum(
        "by,xyk->xbk", col_table, volume, preferred_element_type=jnp.float32
    ).astype(jnp.bfloat16)
    columns = lax.all_to_all(along_y, "gx", split_axis=2, concat_axis=0, tiled=True)
    spectrum = jnp.einsum(
        "ax,xbk->abk", row_table, columns, preferred_element_type=jnp.float32
    ).astype(jnp.bfloat16)
    mode_rows = lax.all_to_all(
        spectrum.reshape(NMODE, ZL * width), "gx", split_axis=0, concat_axis=1, tiled=True
    )
    own_modes = mode_rows.shape[0]
    mixed_rows = jnp.einsum(
        "mzc,mcd->mzd",
        mode_rows.reshape(own_modes, depth, width),
        spec_weight,
        preferred_element_type=jnp.float32,
    ).astype(jnp.bfloat16)
    mixed = lax.all_to_all(
        mixed_rows.reshape(own_modes, depth * width), "gx", split_axis=1, concat_axis=0, tiled=True
    )
    back_x = jnp.einsum(
        "ax,abk->xbk",
        row_table,
        mixed.reshape(MODES, MODES, ZL * width),
        preferred_element_type=jnp.float32,
    ).astype(jnp.bfloat16)
    slabs = lax.all_to_all(back_x, "gx", split_axis=0, concat_axis=2, tiled=True)
    spatial = jnp.einsum(
        "by,xbk->xyk", col_table, slabs, preferred_element_type=jnp.float32
    ).reshape(slab_cells, width)
    pre = spatial + jnp.dot(latent, skip_weight, preferred_element_type=jnp.float32) + skip_bias
    features = gelu_value(pre).astype(jnp.bfloat16)
    picked = features[cell_rows].reshape(devices, block_slots, width)
    returned = lax.all_to_all(picked, "gx", split_axis=0, concat_axis=0, tiled=True)
    point_latent = jax.ops.segment_sum(
        (pair_weight[..., None] * returned.astype(jnp.float32)).reshape(-1, width),
        point_rows.reshape(-1),
        num_segments=local_points,
    )
    head_matrix = head_weight.astype(jnp.float32)
    head_pre = jnp.dot(point_latent, head_matrix, precision=lax.Precision.HIGHEST) + head_bias
    head = gelu_value(head_pre)
    pressure = jnp.dot(head, out_weight, precision=lax.Precision.HIGHEST)
    weighted = pressure * area
    scale = 1.0 / math.sqrt(local_points * devices)
    totals = lax.psum(
        jnp.stack([jnp.sum(weighted * normals[0]), jnp.sum(weighted * normals[1])]), "gx"
    )
    forces = scale * totals
    misfit = forces - targets
    point_grad = 2.0 * scale * (misfit[0] * normals[0] + misfit[1] * normals[1]) * area
    out_part = jnp.dot(point_grad, head, precision=lax.Precision.HIGHEST)
    head_grad = point_grad[:, None] * out_weight[None, :] * gelu_slope(head_pre)
    latent_grad = jnp.dot(head_grad, head_matrix.T, precision=lax.Precision.HIGHEST).astype(
        jnp.bfloat16
    )
    grad_pairs = (pair_weight[..., None] * latent_grad[point_rows].astype(jnp.float32)).astype(
        jnp.bfloat16
    )
    grad_arrived = lax.all_to_all(grad_pairs, "gx", split_axis=0, concat_axis=0, tiled=True)
    cell_grad = jax.ops.segment_sum(
        grad_arrived.reshape(-1, width).astype(jnp.float32), cell_rows, num_segments=slab_cells
    )
    pre_grad = (cell_grad * gelu_slope(pre)).astype(jnp.bfloat16)
    skip_part = jnp.dot(latent.T, pre_grad, preferred_element_type=jnp.float32)
    grad_y = jnp.einsum(
        "by,xyk->xbk",
        col_table,
        pre_grad.reshape(row_count, GY, depth * width),
        preferred_element_type=jnp.float32,
    ).astype(jnp.bfloat16)
    grad_columns = lax.all_to_all(grad_y, "gx", split_axis=2, concat_axis=0, tiled=True)
    grad_spec = jnp.einsum(
        "ax,xbk->abk", row_table, grad_columns, preferred_element_type=jnp.float32
    ).astype(jnp.bfloat16)
    grad_rows = lax.all_to_all(
        grad_spec.reshape(NMODE, ZL * width), "gx", split_axis=0, concat_axis=1, tiled=True
    )
    own_modes = grad_rows.shape[0]
    spec_grad = jnp.einsum(
        "mzc,mzd->mcd",
        mode_rows.reshape(own_modes, depth, width),
        grad_rows.reshape(own_modes, depth, width),
        preferred_element_type=jnp.float32,
    )
    out_grad, skip_grad = lax.psum((out_part, skip_part), "gx")
    return (pressure, forces, spec_grad, skip_grad, out_grad)


F32 = jnp.float32
BF16 = jnp.bfloat16
LANES = 128
WIDTH = 64


def host_rows(length, number):
    places = np.arange(length, dtype=np.float32)
    order = np.arange(number)
    half = number // 2
    freqs = np.where(order < half, order, order - half + 1).astype(np.float32)
    angles = np.float32(2.0 * math.pi / length) * freqs[:, None] * places[None, :]
    table = np.where((order < half)[:, None], np.cos(angles), np.sin(angles))
    table = table.astype(np.float32) * np.float32(math.sqrt(2.0 / length))
    return table.astype(ml_dtypes.bfloat16)


def three_parts(values):
    first = values.astype(BF16)
    rest = values - first.astype(F32)
    second = rest.astype(BF16)
    third = (rest - second.astype(F32)).astype(BF16)
    return first, second, third


def mm(left, right):
    return jnp.dot(left, right, preferred_element_type=F32)


def mm_nt(left, right):
    return lax.dot_general(left, right, (((1,), (1,)), ((), ())), preferred_element_type=F32)


def mm_tn(left, right):
    return lax.dot_general(left, right, (((0,), (0,)), ((), ())), preferred_element_type=F32)


def two_rows(ref, pair):
    return jnp.concatenate([ref[2 * pair : 2 * pair + 1, :], ref[2 * pair + 1 : 2 * pair + 2, :]], axis=1)


def source_kernel(group_ref, count_hbm, point_hbm, kern_hbm, area_hbm, feat_hbm, weight_hbm, msg_ref, pw_ref, count_ref, point_ref, kern_ref, area_ref, feat_ref, weight_ref, sems):
    devices, points = point_ref.shape[0], feat_ref.shape[1]
    low = MODES // devices
    pieces = (
        (point_hbm, point_ref),
        (area_hbm, area_ref),
        (feat_hbm, feat_ref),
        (kern_hbm, kern_ref),
        (count_hbm, count_ref),
        (weight_hbm.at[pl.ds(group_ref[0] * MODES, MODES)], weight_ref),
    )
    copies = [
        pltpu.make_async_copy(source, place, sems.at[index])
        for index, (source, place) in enumerate(pieces)
    ]
    for copy in copies:
        copy.start()
    for copy in copies[:-1]:
        copy.wait()
    first, second, third = three_parts(area_ref[...])
    place = lax.broadcasted_iota(jnp.int32, (16, points), 0)
    extra = jnp.where(
        place == 0,
        first.astype(F32),
        jnp.where(place == 1, second.astype(F32), jnp.where(place == 2, third.astype(F32), 0.0)),
    ).astype(BF16)
    table = jnp.concatenate([feat_ref[...], extra], axis=0)
    rows = lax.broadcasted_iota(jnp.int32, (points, 2 * LANES), 0)
    lane = lax.broadcasted_iota(jnp.int32, (1, LANES), 1)
    for pair in range(devices // 2):
        hot = jnp.where(rows == two_rows(point_ref, pair), 1.0, 0.0).astype(BF16)
        got = mm(table, hot)
        spread = got[WIDTH : WIDTH + 1] + got[WIDTH + 1 : WIDTH + 2] + got[WIDTH + 2 : WIDTH + 3]
        for half in range(2):
            dest = 2 * pair + half
            cut = slice(half * LANES, (half + 1) * LANES)
            valid = lane < count_ref[0:1, dest : dest + 1]
            weight = jnp.where(valid, kern_ref[dest : dest + 1, :], 0.0)
            pw_ref[dest : dest + 1, :] = weight
            msg_ref[dest, 0:WIDTH, :] = ((weight * spread[:, cut]) * got[0:WIDTH, cut]).astype(BF16)
    copies[-1].wait()
    for dest in range(devices):
        msg_ref[dest, WIDTH : 2 * WIDTH, :] = jnp.concatenate(
            [weight_ref[low * dest], weight_ref[low * dest + 1]], axis=1
        )


def columns_of(row):
    return jnp.broadcast_to(row, (LANES, LANES)).T


def pick_rows(rank_ref, pick_ref):
    rows = lax.broadcasted_iota(jnp.int32, (pick_ref.shape[0], LANES), 0)
    for block in range(rank_ref.shape[0]):
        pick_ref[:, block * LANES : (block + 1) * LANES] = jnp.where(
            rows == rank_ref[block : block + 1, :], 1.0, 0.0
        ).astype(BF16)


def basis_rows(depth, cell_ref, by_ref, lp_ref):
    zbits = depth.bit_length() - 1
    rows = by_ref.shape[0]
    slab = rows // MODES
    wide = 2 * LANES
    yrow = lax.broadcasted_iota(jnp.int32, (GY, wide), 0)
    xrow = jnp.bitwise_and(lax.broadcasted_iota(jnp.int32, (16, wide), 0), slab - 1)
    for pair in range(cell_ref.shape[0] // 2):
        cells = two_rows(cell_ref, pair)
        ypos = jnp.bitwise_and(jnp.right_shift(cells, zbits), GY - 1)
        xpos = jnp.right_shift(cells, zbits + GY.bit_length() - 1)
        hot = jnp.where(yrow == ypos, 1.0, 0.0).astype(BF16)
        mask = jnp.where(xrow == xpos, 1.0, 0.0).astype(BF16)
        found = mm(by_ref[...], hot).astype(BF16)
        for at in range(0, rows, 16):
            lp_ref[at : at + 16, pair * wide : (pair + 1) * wide] = found[at : at + 16] * mask


def place_kernel(depth, cell_ref, zr_ref, rank_ref, home_ref, col_ref, flag_ref, pick_ref, part_ref):
    devices = cell_ref.shape[0]
    down = lax.broadcasted_iota(jnp.int32, (LANES, LANES), 0)
    along = lax.broadcasted_iota(jnp.int32, (LANES, LANES), 1)
    place = lax.broadcasted_iota(jnp.int32, (16, LANES), 0)
    for block in range(devices):
        cells = cell_ref[block : block + 1, :]
        row = cells.astype(F32)
        cut = slice(block * LANES, (block + 1) * LANES)
        col_ref[cut, :] = columns_of(row)
        high = jnp.right_shift(cells, 7).astype(F32)
        low = jnp.bitwise_and(cells, 127).astype(F32)
        part_ref[:, cut] = jnp.where(place == 0, high, jnp.where(place == 1, low, 0.0)).astype(BF16)
        same = jnp.logical_and(col_ref[cut, :] == row, down < along)
        before = jnp.max(jnp.where(same, 1.0, 0.0), axis=0, keepdims=True)
        if block:
            early = jnp.where(col_ref[0 : block * LANES, :] == row, 1.0, 0.0)
            before = jnp.maximum(before, jnp.max(early, axis=0, keepdims=True))
        zr_ref[block : block + 1, :] = jnp.where(
            before > 0.0, -1, jnp.bitwise_and(cells, depth - 1)
        )
        flag_ref[block : block + 1, :] = before
    flags = flag_ref[...]
    marks = flags.astype(BF16)
    inside = mm(marks, jnp.where(down <= along, 1.0, 0.0).astype(BF16))
    above = jnp.where(down < along, 1.0, 0.0)[:, 0:devices][0:devices]
    ahead = jnp.sum(mm_tn(above.astype(BF16), marks), axis=1, keepdims=True)
    rank_ref[...] = jnp.where(flags > 0.0, (inside + ahead - flags).astype(jnp.int32), -1)
    pick_rows(rank_ref, pick_ref)
    found = mm_nt(part_ref[...], pick_ref[...])
    found = found[0:1] * 128.0 + found[1:2]
    for block in range(home_ref.shape[0] // LANES):
        cut = slice(block * LANES, (block + 1) * LANES)
        home_ref[cut, :] = columns_of(found[:, cut])


def first_rows(cell_ref, zr_ref, home_ref, first_ref):
    for block in range(cell_ref.shape[0]):
        here = slice(block, block + 1)
        row = jnp.where(zr_ref[here, :] < 0, -1.0, cell_ref[here, :].astype(F32))
        first_ref[:, block * LANES : (block + 1) * LANES] = jnp.where(
            home_ref[...] == row, 1.0, 0.0
        ).astype(BF16)


def fold_parts(values):
    total = values[0:WIDTH]
    for at in range(WIDTH, values.shape[0], WIDTH):
        total = total + values[at : at + WIDTH]
    return total


def sum_cells(terms, xs_ref, cell_ref, rank_ref, zr_ref, home_ref, sums_ref, pick_ref, first_ref, full_ref, col_ref):
    devices = cell_ref.shape[0]
    few = jnp.max(rank_ref[...]) < home_ref.shape[0]

    @pl.when(few)
    def _():
        pick_rows(rank_ref, pick_ref)
        first_rows(cell_ref, zr_ref, home_ref, first_ref)
        moved = mm_nt(xs_ref[...], pick_ref[...]).astype(BF16)
        for pair in range(devices // 2):
            span = slice(pair * 2 * LANES, (pair + 1) * 2 * LANES)
            sums_ref[:, span] = terms(span) + fold_parts(mm(moved, first_ref[:, span]))

    @pl.when(jnp.logical_not(few))
    def _():
        for block in range(devices):
            col_ref[block * LANES : (block + 1) * LANES, :] = columns_of(
                cell_ref[block : block + 1, :].astype(F32)
            )
        for block in range(devices):
            row = cell_ref[block : block + 1, :].astype(F32)
            full_ref[...] = jnp.where(col_ref[...] == row, 1.0, 0.0).astype(BF16)
            sums_ref[:, block * LANES : (block + 1) * LANES] = fold_parts(
                mm(xs_ref[...], full_ref[...])
            )


def spread_depth(values, zpos, rp_ref, pair):
    cut = slice(pair * 2 * LANES, (pair + 1) * 2 * LANES)
    for level in range(rp_ref.shape[0] // WIDTH):
        rp_ref[level * WIDTH : (level + 1) * WIDTH, cut] = jnp.where(
            zpos == level, values, 0.0
        ).astype(BF16)


def slab_rows(lp_ref, rp_ref, msg_ref):
    devices = msg_ref.shape[0]
    step = lp_ref.shape[0] // devices
    for quad in range(rp_ref.shape[0] // (4 * WIDTH)):
        out = mm_nt(lp_ref[...], rp_ref[quad * 4 * WIDTH : (quad + 1) * 4 * WIDTH, :]).astype(BF16)
        for half in range(2):
            level = 2 * quad + half
            for dest in range(devices):
                msg_ref[dest, level * step : (level + 1) * step, :] = out[
                    dest * step : (dest + 1) * step, half * LANES : (half + 1) * LANES
                ]


def cell_kernel(depth, rx_ref, cell_ref, rank_ref, zr_ref, home_ref, by_ref, msg_ref, lat_ref, sums_ref, pick_ref, first_ref, full_ref, col_ref, xs_ref, rp_ref, lp_ref):
    devices = rx_ref.shape[0]
    for block in range(devices):
        xs_ref[:, block * LANES : (block + 1) * LANES] = rx_ref[block, 0:WIDTH, :]
    sum_cells(
        lambda span: xs_ref[:, span].astype(F32),
        xs_ref, cell_ref, rank_ref, zr_ref, home_ref, sums_ref, pick_ref, first_ref, full_ref, col_ref,
    )
    basis_rows(depth, cell_ref, by_ref, lp_ref)
    for pair in range(devices // 2):
        cut = slice(pair * 2 * LANES, (pair + 1) * 2 * LANES)
        latent = sums_ref[:, cut]
        lat_ref[:, cut] = latent.astype(BF16)
        spread_depth(latent, two_rows(zr_ref, pair), rp_ref, pair)
    slab_rows(lp_ref, rp_ref, msg_ref)


def to_modes(rx_ref, table, sp_ref):
    levels = sp_ref.shape[0] // table.shape[0]
    step = table.shape[1] // rx_ref.shape[0]
    for level in range(levels):
        block = rx_ref[:, level * step : (level + 1) * step, :].reshape(table.shape[1], LANES)
        coeffs = mm(table, block).astype(BF16).astype(F32)
        sp_ref[pl.ds(level, table.shape[0], stride=levels), :] = coeffs


def swap_halves(values):
    return pltpu.roll(values, WIDTH, 1)


def weight_kernel(group_ref, own_ref, other_ref, weight_ref):
    for order in range(MODES):
        source, which = order // 2, order % 2
        mine = jnp.full((WIDTH, LANES), group_ref[0], jnp.int32) == which
        weight_ref[order] = jnp.where(
            mine, own_ref[source].astype(F32), other_ref[source].astype(F32)
        ).astype(BF16)


def mode_kernel(rx_ref, weight_ref, table_ref, back_ref, msg_ref, spec_ref, sp_ref, mx_ref):
    devices = rx_ref.shape[0]
    own_rows = spec_ref.shape[1]
    modes = table_ref.shape[0]
    levels = sp_ref.shape[0] // modes
    step = back_ref.shape[0] // devices
    to_modes(rx_ref, table_ref[...], sp_ref)
    for dest in range(devices):
        spec_ref[dest] = sp_ref[dest * own_rows : (dest + 1) * own_rows, :].astype(BF16)
    left = lax.broadcasted_iota(jnp.int32, (levels, LANES), 1) < WIDTH
    for order in range(MODES):
        at = order * 2 * levels
        even = sp_ref[at : at + levels, :]
        odd = sp_ref[at + levels : at + 2 * levels, :]
        rows = jnp.concatenate([even, swap_halves(even), odd, swap_halves(odd)], axis=0)
        out = mm(rows[:, 0:WIDTH].astype(BF16), weight_ref[order])
        mx_ref[at : at + levels, :] = jnp.where(
            left, out[0:levels], swap_halves(out[levels : 2 * levels])
        )
        mx_ref[at + levels : at + 2 * levels, :] = jnp.where(
            left, swap_halves(out[2 * levels : 3 * levels]), out[3 * levels : 4 * levels]
        )
    for level in range(levels):
        mixed = mx_ref[pl.ds(level, modes, stride=levels), :].astype(BF16)
        out = mm(back_ref[...], mixed).astype(BF16)
        for dest in range(devices):
            msg_ref[dest, level * step : (level + 1) * step, :] = out[dest * step : (dest + 1) * step]


def skip_kernel(cell_ref, rank_ref, zr_ref, home_ref, lat_ref, skip_ref, bias_ref, term_ref, pick_ref, first_ref):
    few = jnp.max(rank_ref[...]) < home_ref.shape[0]
    pick_rows(rank_ref, pick_ref)
    first_rows(cell_ref, zr_ref, home_ref, first_ref)
    shared = mm_nt(lat_ref[...], first_ref[...]).astype(BF16)
    for pair in range(cell_ref.shape[0] // 2):
        span = slice(pair * 2 * LANES, (pair + 1) * 2 * LANES)
        later = jnp.logical_and(two_rows(rank_ref, pair) >= 0, few)
        latent = jnp.where(later, mm(shared, pick_ref[:, span]), lat_ref[:, span].astype(F32))
        term_ref[:, span] = mm_tn(skip_ref[...], latent.astype(BF16)) + bias_ref[...]


def pre_kernel(depth, rx_ref, by_ref, term_ref, cell_ref, spec_ref, msg_ref, pre_ref, rt_ref, lp_ref):
    devices = rx_ref.shape[0]
    basis_rows(depth, cell_ref, by_ref, lp_ref)
    rows = lp_ref.shape[0]
    step = rows // devices
    for level in range(rt_ref.shape[0] // LANES):
        block = rx_ref[:, level * step : (level + 1) * step, :].reshape(rows, LANES)
        rt_ref[level * LANES : (level + 1) * LANES, :] = block.T
    for pair in range(devices // 2):
        cut = slice(pair * 2 * LANES, (pair + 1) * 2 * LANES)
        zpos = jnp.bitwise_and(two_rows(cell_ref, pair), depth - 1)
        field = mm(rt_ref[...], lp_ref[:, cut])
        total = jnp.where(zpos == 0, field[0:WIDTH], 0.0)
        for level in range(1, depth):
            total += jnp.where(zpos == level, field[level * WIDTH : (level + 1) * WIDTH], 0.0)
        pre = total + term_ref[:, cut]
        pre_ref[:, cut] = pre
        feats = gelu_value(pre).astype(BF16)
        for half in range(2):
            dest = 2 * pair + half
            msg_ref[dest, 0:WIDTH, :] = feats[:, half * LANES : (half + 1) * LANES]
            msg_ref[dest, WIDTH:, :] = spec_ref[dest]


def head_kernel(rx_ref, point_ref, pw_ref, head_ref, bias_ref, out_ref, area_ref, normal_ref, pres_ref, msg_ref, spec_ref, value_ref, hot_ref, na_ref):
    devices = rx_ref.shape[0]
    points = area_ref.shape[1]
    rows = lax.broadcasted_iota(jnp.int32, (points, LANES), 0)
    for block in range(devices):
        cut = slice(block * LANES, (block + 1) * LANES)
        parts = three_parts(pw_ref[block : block + 1, :] * rx_ref[block, 0:WIDTH, :].astype(F32))
        for index, part in enumerate(parts):
            value_ref[index * WIDTH : (index + 1) * WIDTH, cut] = part
        hot_ref[:, cut] = jnp.where(rows == point_ref[block : block + 1, :], 1.0, 0.0).astype(BF16)
    sums = mm_nt(value_ref[...], hot_ref[...])
    latent = sums[0:WIDTH] + sums[WIDTH : 2 * WIDTH] + sums[2 * WIDTH : 3 * WIDTH]
    first, second, third = three_parts(latent)
    weight = head_ref[...]
    head_pre = mm_tn(weight, first) + mm_tn(weight, second) + mm_tn(weight, third) + bias_ref[...]
    head = gelu_value(head_pre)
    pressure = jnp.sum(head * out_ref[...], axis=0, keepdims=True)
    pres_ref[...] = pressure
    along = [normal_ref[which : which + 1, :] * area_ref[...] for which in range(2)]
    first, second, third = three_parts(out_ref[...] * gelu_slope(head_pre))
    grad = mm(weight, first) + mm(weight, second) + mm(weight, third)
    place = lax.broadcasted_iota(jnp.int32, (16, points), 0)
    extra = jnp.zeros((16, points), F32)
    for which in range(2):
        for index, part in enumerate(three_parts(along[which])):
            extra = jnp.where(place == 3 * which + index, part.astype(F32), extra)
    table = jnp.concatenate([grad.astype(BF16), extra.astype(BF16)], axis=0)
    lane = lax.broadcasted_iota(jnp.int32, (1, LANES), 1)
    partial = []
    for which in range(2):
        force = jnp.sum(pressure * area_ref[...] * normal_ref[which : which + 1, :], axis=1, keepdims=True)
        partial.append(force)
    force_row = jnp.zeros((1, LANES), F32)
    for which in range(2):
        for index, part in enumerate(three_parts(partial[which])):
            force_row = jnp.where(lane == 3 * which + index, part.astype(F32), force_row)
    out_rows = lax.dot_general(
        jnp.concatenate([along[0], along[1], jnp.zeros((6, points), F32)], axis=0),
        head,
        (((1,), (1,)), ((), ())),
        precision=lax.Precision.HIGHEST,
        preferred_element_type=F32,
    )
    out_row = jnp.concatenate([out_rows[0:1], out_rows[1:2]], axis=1)
    place = lax.broadcasted_iota(jnp.int32, (8, LANES), 0)
    out_parts = three_parts(out_row)
    common = jnp.where(
        place == 4,
        out_parts[0].astype(F32),
        jnp.where(place == 5, out_parts[1].astype(F32), jnp.where(place == 6, force_row, 0.0)),
    )
    for pair in range(devices // 2):
        got = mm(table, hot_ref[:, pair * 2 * LANES : (pair + 1) * 2 * LANES])
        for half in range(2):
            block = 2 * pair + half
            cut = slice(half * LANES, (half + 1) * LANES)
            msg_ref[block, 0:WIDTH, :] = got[0:WIDTH, cut].astype(BF16)
            spec_ref[block] = rx_ref[block, WIDTH:, :]
            for which in range(2):
                at = WIDTH + 3 * which
                na_ref[which, block : block + 1, :] = (
                    got[at : at + 1, cut] + got[at + 1 : at + 2, cut] + got[at + 2 : at + 3, cut]
                )
    scaled = [three_parts(pw_ref[...] * na_ref[which]) for which in range(2)]
    rows = [scaled[which][index].astype(F32) for which in range(2) for index in range(2)]
    for block in range(devices):
        tail = common
        for index, row in enumerate(rows):
            tail = jnp.where(place == index, row[block : block + 1, :], tail)
        msg_ref[block, WIDTH : WIDTH + 8, :] = tail.astype(BF16)


def back_kernel(depth, scale, rx_ref, target_ref, cell_ref, rank_ref, zr_ref, home_ref, by_ref, lat_ref, pre_ref, msg_ref, force_ref, outg_ref, sums_ref, pick_ref, first_ref, full_ref, col_ref, xs_ref, pg_ref, rp_ref, gp_ref, lp_ref):
    devices = rx_ref.shape[0]
    main = msg_ref.shape[1] - 8
    basis_rows(depth, cell_ref, by_ref, lp_ref)
    extra = slice(WIDTH, WIDTH + 8)
    total = rx_ref[0, extra, :].astype(F32)
    for block in range(1, devices):
        total += rx_ref[block, extra, :].astype(F32)
    force = total[6:7]
    lane = lax.broadcasted_iota(jnp.int32, (1, 2), 1)
    forces = scale * jnp.where(
        lane == 0,
        force[:, 0:1] + force[:, 1:2] + force[:, 2:3],
        force[:, 3:4] + force[:, 4:5] + force[:, 5:6],
    )
    force_ref[...] = forces
    misfit = (2.0 * scale) * (forces - target_ref[...])
    drag, lift = misfit[:, 0:1], misfit[:, 1:2]
    out_row = total[4:5] + total[5:6]
    outg_ref[...] = drag * out_row[:, 0:WIDTH] + lift * out_row[:, WIDTH : 2 * WIDTH]
    for block in range(devices):
        tail = rx_ref[block, extra, :].astype(F32)
        factor = drag * (tail[0:1] + tail[1:2]) + lift * (tail[2:3] + tail[3:4])
        grad = factor * rx_ref[block, 0:WIDTH, :].astype(F32)
        cut = slice(block * LANES, (block + 1) * LANES)
        gp_ref[:, cut] = grad
        upper = grad.astype(BF16)
        xs_ref[0:WIDTH, cut] = upper
        xs_ref[WIDTH : 2 * WIDTH, cut] = (grad - upper.astype(F32)).astype(BF16)
    sum_cells(
        lambda span: gp_ref[:, span],
        xs_ref, cell_ref, rank_ref, zr_ref, home_ref, sums_ref, pick_ref, first_ref, full_ref, col_ref,
    )
    for pair in range(devices // 2):
        cut = slice(pair * 2 * LANES, (pair + 1) * 2 * LANES)
        grad = sums_ref[:, cut] * gelu_slope(pre_ref[:, cut])
        zpos = two_rows(zr_ref, pair)
        pg_ref[:, cut] = jnp.where(zpos >= 0, grad, 0.0).astype(BF16)
        spread_depth(grad, zpos, rp_ref, pair)
    slab_rows(lp_ref, rp_ref, msg_ref)
    skip = mm_nt(lat_ref[...], pg_ref[...])
    for dest in range(msg_ref.shape[0]):
        msg_ref[dest, main : main + 8, :] = two_parts(skip[8 * dest : 8 * dest + 8]).astype(BF16)


def two_parts(values):
    first, second, _ = three_parts(values)
    return jnp.concatenate([first.astype(F32), second.astype(F32)], axis=1)


def spec_kernel(half_ref, rx_ref, table_ref, msg_ref, sp_ref):
    peers, devices = rx_ref.shape[0], msg_ref.shape[0]
    part_rows = sp_ref.shape[0] // devices
    main = rx_ref.shape[1] - 8
    to_modes(rx_ref, table_ref[half_ref[0]], sp_ref)
    total = rx_ref[0, main : main + 8, :].astype(F32)
    for source in range(1, peers):
        total += rx_ref[source, main : main + 8, :].astype(F32)
    total = two_parts((total + swap_halves(total))[:, 0:WIDTH]).astype(BF16)
    for dest in range(devices):
        msg_ref[dest, 0:part_rows, :] = sp_ref[dest * part_rows : (dest + 1) * part_rows, :].astype(BF16)
        msg_ref[dest, part_rows : part_rows + 8, :] = total


def final_kernel(peers, rx_ref, own_ref, spec_ref, skip_ref):
    devices = rx_ref.shape[0]
    low = MODES // devices
    high = MODES // peers
    owned = spec_ref.shape[0] // MODES
    left = lax.broadcasted_iota(jnp.int32, (8, LANES), 1) < WIDTH
    for which in range(owned):
        for source in range(devices):
            at = which * 8 * low
            coeffs = own_ref[source, at : at + 8 * low, :].astype(F32)
            first, second = coeffs[0:8], coeffs[8:16]
            block = [
                jnp.where(left, first, 0.0),
                jnp.where(left, swap_halves(first), 0.0),
                jnp.where(left, 0.0, swap_halves(second)),
                jnp.where(left, 0.0, second),
            ]
            peer, inner = divmod(low * source, high)
            at = (which * high + inner) * 8
            grads = []
            for shift in range(0, devices, peers):
                part = rx_ref[peer + shift, at : at + 8 * low, :].astype(F32)
                grads += [part[0:8], swap_halves(part[0:8]), part[8:16], swap_halves(part[8:16])]
            block = jnp.concatenate(block * (devices // peers), axis=0).astype(BF16)
            grads = jnp.concatenate(grads, axis=0)[:, 0:WIDTH].astype(BF16)
            found = mm_tn(block, grads)
            mode = which * MODES + low * source
            spec_ref[mode] = found[0:WIDTH]
            spec_ref[mode + 1] = found[WIDTH : 2 * WIDTH]
    main = rx_ref.shape[1] - 8
    for peer in range(peers):
        rows = rx_ref[peer, main : main + 8, :].astype(F32)
        for shift in range(peers, devices, peers):
            rows += rx_ref[peer + shift, main : main + 8, :].astype(F32)
        skip_ref[8 * peer : 8 * peer + 8, :] = (rows + swap_halves(rows))[:, 0:WIDTH]


def run(kernel, outs, ins, flops, scratch=(), smem=0, hbm=0, hbm_outs=0, grant=16):
    vmem = pl.BlockSpec(memory_space=pltpu.VMEM)
    far = pl.BlockSpec(memory_space=pltpu.HBM)
    scalar = pl.BlockSpec(memory_space=pltpu.SMEM)
    moved = sum(math.prod(a.shape) * a.dtype.itemsize for a in list(ins) + list(outs))
    return pl.pallas_call(
        kernel,
        out_shape=tuple(outs),
        in_specs=[scalar] * smem + [far] * hbm + [vmem] * (len(ins) - smem - hbm),
        out_specs=tuple([far] * hbm_outs + [vmem] * (len(outs) - hbm_outs)),
        scratch_shapes=list(scratch),
        compiler_params=pltpu.CompilerParams(vmem_limit_bytes=grant * 1024 * 1024),
        cost_estimate=pl.CostEstimate(flops=flops, bytes_accessed=moved, transcendentals=0),
    )(*ins)


def slab_step(
    point_feats,
    pair_point,
    pair_cell,
    kernel,
    counts,
    area,
    normals,
    targets,
    spec_weight,
    skip_weight,
    skip_bias,
    head_weight,
    head_bias,
    out_weight,
):
    n = lax.axis_size("gx")
    points = point_feats.shape[0]
    slots = n * LANES
    slab = GX // n
    low = MODES // n
    depth = ZL * n
    levels = depth * WIDTH // LANES
    rows = MODES * slab
    main = levels * slab * low
    own_rows = low * low * levels
    shape = jax.ShapeDtypeStruct

    by = host_rows(GY, MODES)
    bx = host_rows(GX, MODES)
    by_rows = jnp.asarray(np.repeat(by, slab, axis=0))
    table = np.zeros((MODES, low, n, low, slab), ml_dtypes.bfloat16)
    for index in range(low):
        table[:, index, :, index, :] = bx.reshape(MODES, n, slab)
    table = table.reshape(MODES * low, rows)
    back = jnp.asarray(np.ascontiguousarray(table.T))
    table = jnp.asarray(table)
    peers = 8
    halves = n // peers
    high = MODES // peers
    part_table = np.zeros((halves, MODES, high, peers, high, slab), ml_dtypes.bfloat16)
    for index in range(high):
        part_table[:, :, index, :, index, :] = np.moveaxis(
            bx.reshape(MODES, halves, peers, slab), 1, 0
        )
    part_table = jnp.asarray(part_table.reshape(halves, MODES * high, rows))
    near = [[half * peers + peer for peer in range(peers)] for half in range(halves)]
    half = (lax.axis_index("gx") // peers).astype(jnp.int32).reshape(1)

    def exchange(message):
        return lax.all_to_all(message, "gx", split_axis=0, concat_axis=0, tiled=True)

    def exchange_alone(message, *others):
        return lax.optimization_barrier((exchange(message),) + others)

    group = lax.axis_index("groups").astype(jnp.int32).reshape(1)
    point_rows = pair_point[0]
    cells = pair_cell[:, 0, :]
    area_row = area.reshape(1, points)
    msg, pw = run(
        source_kernel,
        [shape((n, 2 * WIDTH, LANES), BF16), shape((n, LANES), F32)],
        [group, counts, point_rows, kernel[0], area_row, point_feats.T, spec_weight],
        2 * 80 * points * slots,
        scratch=[
            pltpu.VMEM((1, n), jnp.int32),
            pltpu.VMEM((n, LANES), jnp.int32),
            pltpu.VMEM((n, LANES), F32),
            pltpu.VMEM((1, points), F32),
            pltpu.VMEM((WIDTH, points), BF16),
            pltpu.VMEM((MODES, WIDTH, WIDTH), BF16),
            pltpu.SemaphoreType.DMA((6,)),
        ],
        smem=1,
        hbm=6,
        grant=60,
    )
    rx = exchange(msg)
    shared = 256
    zr, rank, home = run(
        functools.partial(place_kernel, depth),
        [
            shape((n, LANES), jnp.int32),
            shape((n, LANES), jnp.int32),
            shape((shared, LANES), F32),
        ],
        [cells],
        2 * rows * LANES * slots,
        scratch=[
            pltpu.VMEM((slots, LANES), F32),
            pltpu.VMEM((n, LANES), F32),
            pltpu.VMEM((shared, slots), BF16),
            pltpu.VMEM((16, slots), BF16),
        ],
    )
    sum_scratch = [
        pltpu.VMEM((WIDTH, slots), F32),
        pltpu.VMEM((shared, slots), BF16),
        pltpu.VMEM((shared, slots), BF16),
        pltpu.VMEM((slots, LANES), BF16),
        pltpu.VMEM((slots, LANES), F32),
    ]
    own = rx[:, WIDTH : 2 * WIDTH, :]
    other = lax.ppermute(own, "groups", [(0, 1), (1, 0)])
    pair_rows = pltpu.VMEM((WIDTH, slots), BF16)
    basis = pltpu.VMEM((rows, slots), BF16)
    deep_rows = pltpu.VMEM((depth * WIDTH, slots), BF16)
    big = 2 * WIDTH * slots * slots + 2 * rows * slots * depth * WIDTH
    msg, lat = run(
        functools.partial(cell_kernel, depth),
        [shape((n, main, LANES), BF16), shape((WIDTH, slots), BF16)],
        [rx, cells, rank, zr, home, by_rows],
        big,
        scratch=sum_scratch + [pair_rows, deep_rows, basis],
        grant=20,
    )
    columns = exchange(msg)
    (term,) = run(
        skip_kernel,
        [shape((WIDTH, slots), F32)],
        [cells, rank, zr, home, lat, skip_weight, skip_bias.reshape(WIDTH, 1)],
        2 * shared * WIDTH * slots,
        scratch=[pltpu.VMEM((shared, slots), BF16)] * 2,
    )
    (weights,) = run(
        weight_kernel,
        [shape((MODES, WIDTH, LANES), BF16)],
        [group, own, other],
        MODES * WIDTH * LANES,
        smem=1,
    )
    msg, spec = run(
        mode_kernel,
        [shape((n, main, LANES), BF16), shape((n, own_rows, LANES), BF16)],
        [columns, weights, table, back],
        4 * MODES * low * rows * depth * WIDTH,
        scratch=[pltpu.VMEM((MODES * low * levels, LANES), F32)] * 2,
    )
    slabs, spec, lat, term, cells, zr, rank, home, pw = exchange_alone(
        msg, spec, lat, term, cells, zr, rank, home, pw
    )
    msg, pre = run(
        functools.partial(pre_kernel, depth),
        [shape((n, WIDTH + own_rows, LANES), BF16), shape((WIDTH, slots), F32)],
        [slabs, by_rows, term, cells, spec],
        2 * rows * slots * depth * WIDTH,
        scratch=[pltpu.VMEM((depth * WIDTH, rows), BF16), basis],
    )
    returned, pre, lat, cells, zr, rank, home, pw = exchange_alone(
        msg, pre, lat, cells, zr, rank, home, pw
    )
    out_col = out_weight.reshape(WIDTH, 1)
    pressure, msg, own_spec = run(
        head_kernel,
        [
            shape((1, points), F32),
            shape((n, WIDTH + 8, LANES), BF16),
            shape((n, own_rows, LANES), BF16),
        ],
        [returned, point_rows, pw, head_weight, head_bias.reshape(WIDTH, 1), out_col, area_row, normals],
        2 * 3 * WIDTH * points * slots,
        scratch=[
            pltpu.VMEM((3 * WIDTH, slots), BF16),
            pltpu.VMEM((points, slots), BF16),
            pltpu.VMEM((2, n, LANES), F32),
        ],
    )
    grads, pressure, own_spec, pre, lat, cells, zr, rank, home = exchange_alone(
        msg, pressure, own_spec, pre, lat, cells, zr, rank, home
    )
    scale = 1.0 / math.sqrt(points * n)
    msg, forces, out_grad = run(
        functools.partial(back_kernel, depth, scale),
        [
            shape((peers, halves * main + 8, LANES), BF16),
            shape((1, 2), F32),
            shape((1, WIDTH), F32),
        ],
        [grads, targets.reshape(1, 2), cells, rank, zr, home, by_rows, lat, pre],
        big,
        scratch=sum_scratch
        + [pltpu.VMEM((2 * WIDTH, slots), BF16), pair_rows, deep_rows]
        + [pltpu.VMEM((WIDTH, slots), F32), basis],
        grant=20,
    )
    grad_columns, forces, out_grad, own_spec = lax.optimization_barrier(
        (
            lax.all_to_all(
                msg, "gx", split_axis=0, concat_axis=0, tiled=True, axis_index_groups=near
            ),
            forces,
            out_grad,
            own_spec,
        )
    )
    part_rows = MODES * high * levels // n
    (msg,) = run(
        spec_kernel,
        [shape((n, part_rows + 8, LANES), BF16)],
        [half, grad_columns, part_table],
        2 * MODES * high * rows * depth * WIDTH,
        scratch=[pltpu.VMEM((MODES * high * levels, LANES), F32)],
        smem=1,
    )
    finals, own_spec, forces, out_grad = exchange_alone(msg, own_spec, forces, out_grad)
    spec_grad, skip_grad = run(
        functools.partial(final_kernel, peers),
        [shape((spec_weight.shape[0], WIDTH, WIDTH), F32), shape((WIDTH, WIDTH), F32)],
        [finals, own_spec],
        2 * NMODE * WIDTH * WIDTH * depth // n,
    )
    return (pressure.reshape(points), forces.reshape(2), spec_grad, skip_grad, out_grad.reshape(WIDTH))


def solution(mesh):
    fits = mesh.shape["gx"] == 16 and mesh.shape["groups"] == 2
    per_device = slab_step if fits else general_step
    in_specs = (
        P(("groups", "gx"), None),
        P(("groups", "gx"), None, None),
        P(None, ("groups", "gx"), None),
        P(("groups", "gx"), None, None),
        P(("groups", "gx"), None),
        P(("groups", "gx")),
        P(None, ("groups", "gx")),
        P("groups"),
        P("gx", None, None),
        P(),
        P(),
        P(),
        P(),
        P(),
    )
    out_specs = (
        P(("groups", "gx")),
        P("groups"),
        P(("groups", "gx"), None, None),
        P("groups", None),
        P("groups"),
    )
    return jax.shard_map(
        per_device, mesh=mesh, in_specs=in_specs, out_specs=out_specs, check_vma=False
    )
```

```python
import functools
import math

import jax
import jax.numpy as jnp
import ml_dtypes
import numpy as np
from jax import lax
from jax.experimental import pallas as pl
from jax.experimental.pallas import tpu as pltpu
from jax.sharding import PartitionSpec as P

GX = 128
GY = 128
MODES = 32
ZL = 1
NMODE = 1024


def fourier_rows(length, number):
    places = jnp.arange(length, dtype=jnp.float32)
    order = jnp.arange(number)
    half = number // 2
    freqs = jnp.where(order < half, order, order - half + 1).astype(jnp.float32)
    angles = 2.0 * math.pi / length * freqs[:, None] * places[None, :]
    table = jnp.where((order < half)[:, None], jnp.cos(angles), jnp.sin(angles))
    return (table * math.sqrt(2.0 / length)).astype(jnp.bfloat16)


def gelu_value(values):
    return 0.5 * values * (1.0 + lax.erf(values * (1.0 / math.sqrt(2.0))))


def gelu_slope(values):
    return 0.5 * (1.0 + lax.erf(values * (1.0 / math.sqrt(2.0)))) + values * jnp.exp(
        -0.5 * values * values
    ) * (1.0 / math.sqrt(2.0 * math.pi))


def general_step(
    point_feats,
    pair_point,
    pair_cell,
    kernel,
    counts,
    area,
    normals,
    targets,
    spec_weight,
    skip_weight,
    skip_bias,
    head_weight,
    head_bias,
    out_weight,
):
    devices = lax.axis_size("gx")
    local_points, width = point_feats.shape
    block_slots = pair_point.shape[2]
    row_count = GX // devices
    depth = ZL * devices
    slab_cells = row_count * GY * depth
    valid_mask = jnp.arange(block_slots)[None, :] < counts[0][:, None]
    point_rows = pair_point[0]
    pair_weight = jnp.where(valid_mask, kernel[0], jnp.float32(0.0))
    sender_weight = pair_weight * area[point_rows]
    contrib = (sender_weight[..., None] * point_feats[point_rows].astype(jnp.float32)).astype(
        jnp.bfloat16
    )
    arrived = lax.all_to_all(contrib, "gx", split_axis=0, concat_axis=0, tiled=True)
    cell_rows = pair_cell[:, 0, :].reshape(-1)
    latent = jax.ops.segment_sum(
        arrived.reshape(-1, width).astype(jnp.float32), cell_rows, num_segments=slab_cells
    ).astype(jnp.bfloat16)
    col_table = fourier_rows(GY, MODES)
    row_table = fourier_rows(GX, MODES)
    volume = latent.reshape(row_count, GY, depth * width)
    along_y = jnp.einsum(
        "by,xyk->xbk", col_table, volume, preferred_element_type=jnp.float32
    ).astype(jnp.bfloat16)
    columns = lax.all_to_all(along_y, "gx", split_axis=2, concat_axis=0, tiled=True)
    spectrum = jnp.einsum(
        "ax,xbk->abk", row_table, columns, preferred_element_type=jnp.float32
    ).astype(jnp.bfloat16)
    mode_rows = lax.all_to_all(
        spectrum.reshape(NMODE, ZL * width), "gx", split_axis=0, concat_axis=1, tiled=True
    )
    own_modes = mode_rows.shape[0]
    mixed_rows = jnp.einsum(
        "mzc,mcd->mzd",
        mode_rows.reshape(own_modes, depth, width),
        spec_weight,
        preferred_element_type=jnp.float32,
    ).astype(jnp.bfloat16)
    mixed = lax.all_to_all(
        mixed_rows.reshape(own_modes, depth * width), "gx", split_axis=1, concat_axis=0, tiled=True
    )
    back_x = jnp.einsum(
        "ax,abk->xbk",
        row_table,
        mixed.reshape(MODES, MODES, ZL * width),
        preferred_element_type=jnp.float32,
    ).astype(jnp.bfloat16)
    slabs = lax.all_to_all(back_x, "gx", split_axis=0, concat_axis=2, tiled=True)
    spatial = jnp.einsum(
        "by,xbk->xyk", col_table, slabs, preferred_element_type=jnp.float32
    ).reshape(slab_cells, width)
    pre = spatial + jnp.dot(latent, skip_weight, preferred_element_type=jnp.float32) + skip_bias
    features = gelu_value(pre).astype(jnp.bfloat16)
    picked = features[cell_rows].reshape(devices, block_slots, width)
    returned = lax.all_to_all(picked, "gx", split_axis=0, concat_axis=0, tiled=True)
    point_latent = jax.ops.segment_sum(
        (pair_weight[..., None] * returned.astype(jnp.float32)).reshape(-1, width),
        point_rows.reshape(-1),
        num_segments=local_points,
    )
    head_matrix = head_weight.astype(jnp.float32)
    head_pre = jnp.dot(point_latent, head_matrix, precision=lax.Precision.HIGHEST) + head_bias
    head = gelu_value(head_pre)
    pressure = jnp.dot(head, out_weight, precision=lax.Precision.HIGHEST)
    weighted = pressure * area
    scale = 1.0 / math.sqrt(local_points * devices)
    totals = lax.psum(
        jnp.stack([jnp.sum(weighted * normals[0]), jnp.sum(weighted * normals[1])]), "gx"
    )
    forces = scale * totals
    misfit = forces - targets
    point_grad = 2.0 * scale * (misfit[0] * normals[0] + misfit[1] * normals[1]) * area
    out_part = jnp.dot(point_grad, head, precision=lax.Precision.HIGHEST)
    head_grad = point_grad[:, None] * out_weight[None, :] * gelu_slope(head_pre)
    latent_grad = jnp.dot(head_grad, head_matrix.T, precision=lax.Precision.HIGHEST).astype(
        jnp.bfloat16
    )
    grad_pairs = (pair_weight[..., None] * latent_grad[point_rows].astype(jnp.float32)).astype(
        jnp.bfloat16
    )
    grad_arrived = lax.all_to_all(grad_pairs, "gx", split_axis=0, concat_axis=0, tiled=True)
    cell_grad = jax.ops.segment_sum(
        grad_arrived.reshape(-1, width).astype(jnp.float32), cell_rows, num_segments=slab_cells
    )
    pre_grad = (cell_grad * gelu_slope(pre)).astype(jnp.bfloat16)
    skip_part = jnp.dot(latent.T, pre_grad, preferred_element_type=jnp.float32)
    grad_y = jnp.einsum(
        "by,xyk->xbk",
        col_table,
        pre_grad.reshape(row_count, GY, depth * width),
        preferred_element_type=jnp.float32,
    ).astype(jnp.bfloat16)
    grad_columns = lax.all_to_all(grad_y, "gx", split_axis=2, concat_axis=0, tiled=True)
    grad_spec = jnp.einsum(
        "ax,xbk->abk", row_table, grad_columns, preferred_element_type=jnp.float32
    ).astype(jnp.bfloat16)
    grad_rows = lax.all_to_all(
        grad_spec.reshape(NMODE, ZL * width), "gx", split_axis=0, concat_axis=1, tiled=True
    )
    own_modes = grad_rows.shape[0]
    spec_grad = jnp.einsum(
        "mzc,mzd->mcd",
        mode_rows.reshape(own_modes, depth, width),
        grad_rows.reshape(own_modes, depth, width),
        preferred_element_type=jnp.float32,
    )
    out_grad, skip_grad = lax.psum((out_part, skip_part), "gx")
    return (pressure, forces, spec_grad, skip_grad, out_grad)


F32 = jnp.float32
BF16 = jnp.bfloat16
LANES = 128
WIDTH = 64


def host_rows(length, number):
    places = np.arange(length, dtype=np.float32)
    order = np.arange(number)
    half = number // 2
    freqs = np.where(order < half, order, order - half + 1).astype(np.float32)
    angles = np.float32(2.0 * math.pi / length) * freqs[:, None] * places[None, :]
    table = np.where((order < half)[:, None], np.cos(angles), np.sin(angles))
    table = table.astype(np.float32) * np.float32(math.sqrt(2.0 / length))
    return table.astype(ml_dtypes.bfloat16)


def three_parts(values):
    first = values.astype(BF16)
    rest = values - first.astype(F32)
    second = rest.astype(BF16)
    third = (rest - second.astype(F32)).astype(BF16)
    return first, second, third


def mm(left, right):
    return jnp.dot(left, right, preferred_element_type=F32)


def mm_nt(left, right):
    return lax.dot_general(left, right, (((1,), (1,)), ((), ())), preferred_element_type=F32)


def mm_tn(left, right):
    return lax.dot_general(left, right, (((0,), (0,)), ((), ())), preferred_element_type=F32)


def two_rows(ref, pair):
    return jnp.concatenate([ref[2 * pair : 2 * pair + 1, :], ref[2 * pair + 1 : 2 * pair + 2, :]], axis=1)


def source_kernel(group_ref, half_ref, count_hbm, point_hbm, kern_hbm, area_hbm, feat_hbm, weight_hbm, msg_ref, pw_ref, count_ref, point_ref, kern_ref, area_ref, feat_ref, weight_ref, sems):
    devices, points = point_ref.shape[0], feat_ref.shape[1]
    low = MODES // devices
    pieces = (
        (point_hbm, point_ref),
        (area_hbm, area_ref),
        (feat_hbm, feat_ref),
        (kern_hbm, kern_ref),
        (count_hbm, count_ref),
        (weight_hbm.at[pl.ds(group_ref[0] * MODES, MODES)], weight_ref),
    )
    copies = [
        pltpu.make_async_copy(source, place, sems.at[index])
        for index, (source, place) in enumerate(pieces)
    ]
    for copy in copies:
        copy.start()
    for copy in copies[:-1]:
        copy.wait()
    first, second, third = three_parts(area_ref[...])
    place = lax.broadcasted_iota(jnp.int32, (16, points), 0)
    extra = jnp.where(
        place == 0,
        first.astype(F32),
        jnp.where(place == 1, second.astype(F32), jnp.where(place == 2, third.astype(F32), 0.0)),
    ).astype(BF16)
    table = jnp.concatenate([feat_ref[...], extra], axis=0)
    rows = lax.broadcasted_iota(jnp.int32, (points, 2 * LANES), 0)
    lane = lax.broadcasted_iota(jnp.int32, (1, LANES), 1)
    for pair in range(devices // 2):
        hot = jnp.where(rows == two_rows(point_ref, pair), 1.0, 0.0).astype(BF16)
        got = mm(table, hot)
        spread = got[WIDTH : WIDTH + 1] + got[WIDTH + 1 : WIDTH + 2] + got[WIDTH + 2 : WIDTH + 3]
        for half in range(2):
            dest = 2 * pair + half
            cut = slice(half * LANES, (half + 1) * LANES)
            valid = lane < count_ref[0:1, dest : dest + 1]
            weight = jnp.where(valid, kern_ref[dest : dest + 1, :], 0.0)
            pw_ref[dest : dest + 1, :] = weight
            msg_ref[dest, 0:WIDTH, :] = ((weight * spread[:, cut]) * got[0:WIDTH, cut]).astype(BF16)
    copies[-1].wait()
    for dest in range(devices):
        msg_ref[dest, WIDTH : 2 * WIDTH, :] = jnp.concatenate(
            [weight_ref[low * dest], weight_ref[low * dest + 1]], axis=1
        )


def columns_of(row):
    return jnp.broadcast_to(row, (LANES, LANES)).T


def column_of(row):
    down = lax.broadcasted_iota(jnp.int32, (WIDTH, WIDTH), 0)
    along = lax.broadcasted_iota(jnp.int32, (WIDTH, WIDTH), 1)
    return jnp.sum(jnp.where(down == along, row, 0.0), axis=1, keepdims=True)


def pick_rows(rank_ref, pick_ref):
    rows = lax.broadcasted_iota(jnp.int32, (pick_ref.shape[0], LANES), 0)
    for block in range(rank_ref.shape[0]):
        pick_ref[:, block * LANES : (block + 1) * LANES] = jnp.where(
            rows == rank_ref[block : block + 1, :], 1.0, 0.0
        ).astype(BF16)


def basis_rows(depth, cell_ref, by_ref, lp_ref):
    zbits = depth.bit_length() - 1
    rows = by_ref.shape[0]
    slab = rows // MODES
    wide = 2 * LANES
    yrow = lax.broadcasted_iota(jnp.int32, (GY, wide), 0)
    xrow = jnp.bitwise_and(lax.broadcasted_iota(jnp.int32, (16, wide), 0), slab - 1)
    for pair in range(cell_ref.shape[0] // 2):
        cells = two_rows(cell_ref, pair)
        ypos = jnp.bitwise_and(jnp.right_shift(cells, zbits), GY - 1)
        xpos = jnp.right_shift(cells, zbits + GY.bit_length() - 1)
        hot = jnp.where(yrow == ypos, 1.0, 0.0).astype(BF16)
        mask = jnp.where(xrow == xpos, 1.0, 0.0).astype(BF16)
        found = mm(by_ref[...], hot).astype(BF16)
        for at in range(0, rows, 16):
            lp_ref[at : at + 16, pair * wide : (pair + 1) * wide] = found[at : at + 16] * mask


def place_kernel(depth, cell_ref, zr_ref, rank_ref, home_ref, col_ref, flag_ref, pick_ref, part_ref):
    devices = cell_ref.shape[0]
    down = lax.broadcasted_iota(jnp.int32, (LANES, LANES), 0)
    along = lax.broadcasted_iota(jnp.int32, (LANES, LANES), 1)
    place = lax.broadcasted_iota(jnp.int32, (16, LANES), 0)
    for block in range(devices):
        cells = cell_ref[block : block + 1, :]
        row = cells.astype(F32)
        cut = slice(block * LANES, (block + 1) * LANES)
        col_ref[cut, :] = columns_of(row)
        high = jnp.right_shift(cells, 7).astype(F32)
        low = jnp.bitwise_and(cells, 127).astype(F32)
        part_ref[:, cut] = jnp.where(place == 0, high, jnp.where(place == 1, low, 0.0)).astype(BF16)
        same = jnp.logical_and(col_ref[cut, :] == row, down < along)
        before = jnp.max(jnp.where(same, 1.0, 0.0), axis=0, keepdims=True)
        if block:
            early = jnp.where(col_ref[0 : block * LANES, :] == row, 1.0, 0.0)
            before = jnp.maximum(before, jnp.max(early, axis=0, keepdims=True))
        zr_ref[block : block + 1, :] = jnp.where(
            before > 0.0, -1, jnp.bitwise_and(cells, depth - 1)
        )
        flag_ref[block : block + 1, :] = before
    flags = flag_ref[...]
    marks = flags.astype(BF16)
    inside = mm(marks, jnp.where(down <= along, 1.0, 0.0).astype(BF16))
    above = jnp.where(down < along, 1.0, 0.0)[:, 0:devices][0:devices]
    ahead = jnp.sum(mm_tn(above.astype(BF16), marks), axis=1, keepdims=True)
    rank_ref[...] = jnp.where(flags > 0.0, (inside + ahead - flags).astype(jnp.int32), -1)
    pick_rows(rank_ref, pick_ref)
    found = mm_nt(part_ref[...], pick_ref[...])
    found = found[0:1] * 128.0 + found[1:2]
    for block in range(home_ref.shape[0] // LANES):
        cut = slice(block * LANES, (block + 1) * LANES)
        home_ref[cut, :] = columns_of(found[:, cut])


def first_rows(cell_ref, zr_ref, home_ref, first_ref):
    for block in range(cell_ref.shape[0]):
        here = slice(block, block + 1)
        row = jnp.where(zr_ref[here, :] < 0, -1.0, cell_ref[here, :].astype(F32))
        first_ref[:, block * LANES : (block + 1) * LANES] = jnp.where(
            home_ref[...] == row, 1.0, 0.0
        ).astype(BF16)


def fold_parts(values):
    total = values[0:WIDTH]
    for at in range(WIDTH, values.shape[0], WIDTH):
        total = total + values[at : at + WIDTH]
    return total


def sum_cells(terms, xs_ref, cell_ref, rank_ref, zr_ref, home_ref, sums_ref, pick_ref, first_ref, full_ref, col_ref):
    devices = cell_ref.shape[0]
    few = jnp.max(rank_ref[...]) < home_ref.shape[0]

    @pl.when(few)
    def _():
        pick_rows(rank_ref, pick_ref)
        first_rows(cell_ref, zr_ref, home_ref, first_ref)
        moved = mm_nt(xs_ref[...], pick_ref[...]).astype(BF16)
        for pair in range(devices // 2):
            span = slice(pair * 2 * LANES, (pair + 1) * 2 * LANES)
            sums_ref[:, span] = terms(span) + fold_parts(mm(moved, first_ref[:, span]))

    @pl.when(jnp.logical_not(few))
    def _():
        for block in range(devices):
            col_ref[block * LANES : (block + 1) * LANES, :] = columns_of(
                cell_ref[block : block + 1, :].astype(F32)
            )
        for block in range(devices):
            row = cell_ref[block : block + 1, :].astype(F32)
            full_ref[...] = jnp.where(col_ref[...] == row, 1.0, 0.0).astype(BF16)
            sums_ref[:, block * LANES : (block + 1) * LANES] = fold_parts(
                mm(xs_ref[...], full_ref[...])
            )


def spread_depth(values, zpos, rp_ref, pair):
    cut = slice(pair * 2 * LANES, (pair + 1) * 2 * LANES)
    for level in range(rp_ref.shape[0] // WIDTH):
        rp_ref[level * WIDTH : (level + 1) * WIDTH, cut] = jnp.where(
            zpos == level, values, 0.0
        ).astype(BF16)


def slab_rows(lp_ref, rp_ref, msg_ref):
    devices = msg_ref.shape[0]
    step = lp_ref.shape[0] // devices
    for quad in range(rp_ref.shape[0] // (4 * WIDTH)):
        out = mm_nt(lp_ref[...], rp_ref[quad * 4 * WIDTH : (quad + 1) * 4 * WIDTH, :]).astype(BF16)
        for half in range(2):
            level = 2 * quad + half
            for dest in range(devices):
                msg_ref[dest, level * step : (level + 1) * step, :] = out[
                    dest * step : (dest + 1) * step, half * LANES : (half + 1) * LANES
                ]


def cell_kernel(depth, rx_ref, cell_ref, rank_ref, zr_ref, home_ref, by_ref, msg_ref, lat_ref, sums_ref, pick_ref, first_ref, full_ref, col_ref, xs_ref, rp_ref, lp_ref):
    devices = rx_ref.shape[0]
    for block in range(devices):
        xs_ref[:, block * LANES : (block + 1) * LANES] = rx_ref[block, 0:WIDTH, :]
    sum_cells(
        lambda span: xs_ref[:, span].astype(F32),
        xs_ref, cell_ref, rank_ref, zr_ref, home_ref, sums_ref, pick_ref, first_ref, full_ref, col_ref,
    )
    basis_rows(depth, cell_ref, by_ref, lp_ref)
    for pair in range(devices // 2):
        cut = slice(pair * 2 * LANES, (pair + 1) * 2 * LANES)
        latent = sums_ref[:, cut]
        lat_ref[:, cut] = latent.astype(BF16)
        spread_depth(latent, two_rows(zr_ref, pair), rp_ref, pair)
    slab_rows(lp_ref, rp_ref, msg_ref)


def to_modes(rx_ref, table, sp_ref):
    levels = sp_ref.shape[0] // table.shape[0]
    step = table.shape[1] // rx_ref.shape[0]
    for level in range(levels):
        block = rx_ref[:, level * step : (level + 1) * step, :].reshape(table.shape[1], LANES)
        coeffs = mm(table, block).astype(BF16).astype(F32)
        sp_ref[pl.ds(level, table.shape[0], stride=levels), :] = coeffs


def swap_halves(values):
    return pltpu.roll(values, WIDTH, 1)


def weight_kernel(group_ref, own_ref, other_ref, weight_ref):
    for order in range(MODES):
        source, which = order // 2, order % 2
        mine = jnp.full((WIDTH, LANES), group_ref[0], jnp.int32) == which
        weight_ref[order] = jnp.where(
            mine, own_ref[source].astype(F32), other_ref[source].astype(F32)
        ).astype(BF16)


def mode_kernel(rx_ref, weight_ref, table_ref, back_ref, term_ref, msg_ref, spec_ref, sp_ref, mx_ref):
    devices = rx_ref.shape[0]
    own_rows = spec_ref.shape[1]
    modes = table_ref.shape[0]
    levels = sp_ref.shape[0] // modes
    step = back_ref.shape[0] // devices
    to_modes(rx_ref, table_ref[...], sp_ref)
    for dest in range(devices):
        spec_ref[dest] = sp_ref[dest * own_rows : (dest + 1) * own_rows, :].astype(BF16)
    left = lax.broadcasted_iota(jnp.int32, (levels, LANES), 1) < WIDTH
    for order in range(MODES):
        at = order * 2 * levels
        even = sp_ref[at : at + levels, :]
        odd = sp_ref[at + levels : at + 2 * levels, :]
        rows = jnp.concatenate([even, swap_halves(even), odd, swap_halves(odd)], axis=0)
        out = mm(rows[:, 0:WIDTH].astype(BF16), weight_ref[order])
        mx_ref[at : at + levels, :] = jnp.where(
            left, out[0:levels], swap_halves(out[levels : 2 * levels])
        )
        mx_ref[at + levels : at + 2 * levels, :] = jnp.where(
            left, swap_halves(out[2 * levels : 3 * levels]), out[3 * levels : 4 * levels]
        )
    for level in range(levels):
        mixed = mx_ref[pl.ds(level, modes, stride=levels), :].astype(BF16)
        out = mm(back_ref[...], mixed).astype(BF16)
        for dest in range(devices):
            msg_ref[dest, level * step : (level + 1) * step, :] = out[dest * step : (dest + 1) * step]


def skip_kernel(cell_ref, rank_ref, zr_ref, home_ref, lat_ref, skip_ref, bias_ref, term_ref, pick_ref, first_ref):
    few = jnp.max(rank_ref[...]) < home_ref.shape[0]
    bias = column_of(bias_ref[...])
    pick_rows(rank_ref, pick_ref)
    first_rows(cell_ref, zr_ref, home_ref, first_ref)
    shared = mm_nt(lat_ref[...], first_ref[...]).astype(BF16)
    for pair in range(cell_ref.shape[0] // 2):
        span = slice(pair * 2 * LANES, (pair + 1) * 2 * LANES)
        later = jnp.logical_and(two_rows(rank_ref, pair) >= 0, few)
        latent = jnp.where(later, mm(shared, pick_ref[:, span]), lat_ref[:, span].astype(F32))
        term_ref[:, span] = mm_tn(skip_ref[...], latent.astype(BF16)) + bias


def pre_kernel(depth, rx_ref, by_ref, term_ref, cell_ref, spec_ref, msg_ref, pre_ref, rt_ref, lp_ref):
    devices = rx_ref.shape[0]
    basis_rows(depth, cell_ref, by_ref, lp_ref)
    rows = lp_ref.shape[0]
    step = rows // devices
    for level in range(rt_ref.shape[0] // LANES):
        block = rx_ref[:, level * step : (level + 1) * step, :].reshape(rows, LANES)
        rt_ref[level * LANES : (level + 1) * LANES, :] = block.T
    for pair in range(devices // 2):
        cut = slice(pair * 2 * LANES, (pair + 1) * 2 * LANES)
        zpos = jnp.bitwise_and(two_rows(cell_ref, pair), depth - 1)
        field = mm(rt_ref[...], lp_ref[:, cut])
        total = jnp.where(zpos == 0, field[0:WIDTH], 0.0)
        for level in range(1, depth):
            total += jnp.where(zpos == level, field[level * WIDTH : (level + 1) * WIDTH], 0.0)
        pre = total + term_ref[:, cut]
        pre_ref[:, cut] = pre
        feats = gelu_value(pre).astype(BF16)
        for half in range(2):
            dest = 2 * pair + half
            msg_ref[dest, 0:WIDTH, :] = feats[:, half * LANES : (half + 1) * LANES]
            msg_ref[dest, WIDTH:, :] = spec_ref[dest]


def head_kernel(rx_ref, point_ref, pw_ref, head_ref, bias_ref, out_ref, area_ref, normal_ref, pres_ref, msg_ref, spec_ref, value_ref, hot_ref, na_ref):
    devices = rx_ref.shape[0]
    points = area_ref.shape[1]
    rows = lax.broadcasted_iota(jnp.int32, (points, LANES), 0)
    for block in range(devices):
        cut = slice(block * LANES, (block + 1) * LANES)
        parts = three_parts(pw_ref[block : block + 1, :] * rx_ref[block, 0:WIDTH, :].astype(F32))
        for index, part in enumerate(parts):
            value_ref[index * WIDTH : (index + 1) * WIDTH, cut] = part
        hot_ref[:, cut] = jnp.where(rows == point_ref[block : block + 1, :], 1.0, 0.0).astype(BF16)
    sums = mm_nt(value_ref[...], hot_ref[...])
    latent = sums[0:WIDTH] + sums[WIDTH : 2 * WIDTH] + sums[2 * WIDTH : 3 * WIDTH]
    first, second, third = three_parts(latent)
    weight = head_ref[...]
    head_pre = mm_tn(weight, first) + mm_tn(weight, second) + mm_tn(weight, third) + column_of(bias_ref[...])
    out_column = column_of(out_ref[...])
    head = gelu_value(head_pre)
    pressure = jnp.sum(head * out_column, axis=0, keepdims=True)
    pres_ref[...] = pressure
    along = [normal_ref[which : which + 1, :] * area_ref[...] for which in range(2)]
    first, second, third = three_parts(out_column * gelu_slope(head_pre))
    grad = mm(weight, first) + mm(weight, second) + mm(weight, third)
    place = lax.broadcasted_iota(jnp.int32, (16, points), 0)
    extra = jnp.zeros((16, points), F32)
    for which in range(2):
        for index, part in enumerate(three_parts(along[which])):
            extra = jnp.where(place == 3 * which + index, part.astype(F32), extra)
    table = jnp.concatenate([grad.astype(BF16), extra.astype(BF16)], axis=0)
    lane = lax.broadcasted_iota(jnp.int32, (1, LANES), 1)
    partial = []
    for which in range(2):
        force = jnp.sum(pressure * area_ref[...] * normal_ref[which : which + 1, :], axis=1, keepdims=True)
        partial.append(force)
    force_row = jnp.zeros((1, LANES), F32)
    for which in range(2):
        for index, part in enumerate(three_parts(partial[which])):
            force_row = jnp.where(lane == 3 * which + index, part.astype(F32), force_row)
    out_rows = lax.dot_general(
        jnp.concatenate([along[0], along[1], jnp.zeros((6, points), F32)], axis=0),
        head,
        (((1,), (1,)), ((), ())),
        precision=lax.Precision.HIGHEST,
        preferred_element_type=F32,
    )
    out_row = jnp.concatenate([out_rows[0:1], out_rows[1:2]], axis=1)
    place = lax.broadcasted_iota(jnp.int32, (8, LANES), 0)
    out_parts = three_parts(out_row)
    common = jnp.where(
        place == 4,
        out_parts[0].astype(F32),
        jnp.where(place == 5, out_parts[1].astype(F32), jnp.where(place == 6, force_row, 0.0)),
    )
    for pair in range(devices // 2):
        got = mm(table, hot_ref[:, pair * 2 * LANES : (pair + 1) * 2 * LANES])
        for half in range(2):
            block = 2 * pair + half
            cut = slice(half * LANES, (half + 1) * LANES)
            msg_ref[block, 0:WIDTH, :] = got[0:WIDTH, cut].astype(BF16)
            spec_ref[block] = rx_ref[block, WIDTH:, :]
            for which in range(2):
                at = WIDTH + 3 * which
                na_ref[which, block : block + 1, :] = (
                    got[at : at + 1, cut] + got[at + 1 : at + 2, cut] + got[at + 2 : at + 3, cut]
                )
    scaled = [three_parts(pw_ref[...] * na_ref[which]) for which in range(2)]
    rows = [scaled[which][index].astype(F32) for which in range(2) for index in range(2)]
    for block in range(devices):
        tail = common
        for index, row in enumerate(rows):
            tail = jnp.where(place == index, row[block : block + 1, :], tail)
        msg_ref[block, WIDTH : WIDTH + 8, :] = tail.astype(BF16)


def back_kernel(depth, scale, rx_ref, target_ref, cell_ref, rank_ref, zr_ref, home_ref, by_ref, lat_ref, pre_ref, msg_ref, force_ref, outg_ref, sums_ref, pick_ref, first_ref, full_ref, col_ref, xs_ref, pg_ref, rp_ref, gp_ref, lp_ref):
    devices = rx_ref.shape[0]
    main = msg_ref.shape[1] - 8
    basis_rows(depth, cell_ref, by_ref, lp_ref)
    extra = slice(WIDTH, WIDTH + 8)
    total = rx_ref[0, extra, :].astype(F32)
    for block in range(1, devices):
        total += rx_ref[block, extra, :].astype(F32)
    force = total[6:7]
    lane = lax.broadcasted_iota(jnp.int32, (1, 2), 1)
    forces = scale * jnp.where(
        lane == 0,
        force[:, 0:1] + force[:, 1:2] + force[:, 2:3],
        force[:, 3:4] + force[:, 4:5] + force[:, 5:6],
    )
    force_ref[...] = forces
    misfit = (2.0 * scale) * (forces - target_ref[...])
    drag, lift = misfit[:, 0:1], misfit[:, 1:2]
    out_row = total[4:5] + total[5:6]
    outg_ref[...] = drag * out_row[:, 0:WIDTH] + lift * out_row[:, WIDTH : 2 * WIDTH]
    for block in range(devices):
        tail = rx_ref[block, extra, :].astype(F32)
        factor = drag * (tail[0:1] + tail[1:2]) + lift * (tail[2:3] + tail[3:4])
        grad = factor * rx_ref[block, 0:WIDTH, :].astype(F32)
        cut = slice(block * LANES, (block + 1) * LANES)
        gp_ref[:, cut] = grad
        upper = grad.astype(BF16)
        xs_ref[0:WIDTH, cut] = upper
        xs_ref[WIDTH : 2 * WIDTH, cut] = (grad - upper.astype(F32)).astype(BF16)
    sum_cells(
        lambda span: gp_ref[:, span],
        xs_ref, cell_ref, rank_ref, zr_ref, home_ref, sums_ref, pick_ref, first_ref, full_ref, col_ref,
    )
    for pair in range(devices // 2):
        cut = slice(pair * 2 * LANES, (pair + 1) * 2 * LANES)
        grad = sums_ref[:, cut] * gelu_slope(pre_ref[:, cut])
        zpos = two_rows(zr_ref, pair)
        pg_ref[:, cut] = jnp.where(zpos >= 0, grad, 0.0).astype(BF16)
        spread_depth(grad, zpos, rp_ref, pair)
    slab_rows(lp_ref, rp_ref, msg_ref)
    skip = mm_nt(lat_ref[...], pg_ref[...])
    for dest in range(msg_ref.shape[0]):
        msg_ref[dest, main : main + 8, :] = two_parts(skip[8 * dest : 8 * dest + 8]).astype(BF16)


def two_parts(values):
    first, second, _ = three_parts(values)
    return jnp.concatenate([first.astype(F32), second.astype(F32)], axis=1)


def spec_kernel(half_ref, rx_ref, table_ref, msg_ref, sp_ref):
    peers, devices = rx_ref.shape[0], msg_ref.shape[0]
    part_rows = sp_ref.shape[0] // devices
    main = rx_ref.shape[1] - 8
    to_modes(rx_ref, table_ref[half_ref[0]], sp_ref)
    total = rx_ref[0, main : main + 8, :].astype(F32)
    for source in range(1, peers):
        total += rx_ref[source, main : main + 8, :].astype(F32)
    total = two_parts((total + swap_halves(total))[:, 0:WIDTH]).astype(BF16)
    for dest in range(devices):
        msg_ref[dest, 0:part_rows, :] = sp_ref[dest * part_rows : (dest + 1) * part_rows, :].astype(BF16)
        msg_ref[dest, part_rows : part_rows + 8, :] = total


def final_kernel(peers, rx_ref, own_ref, spec_ref, skip_ref):
    devices = rx_ref.shape[0]
    low = MODES // devices
    high = MODES // peers
    owned = spec_ref.shape[0] // MODES
    left = lax.broadcasted_iota(jnp.int32, (8, LANES), 1) < WIDTH
    for which in range(owned):
        for source in range(devices):
            at = which * 8 * low
            coeffs = own_ref[source, at : at + 8 * low, :].astype(F32)
            first, second = coeffs[0:8], coeffs[8:16]
            block = [
                jnp.where(left, first, 0.0),
                jnp.where(left, swap_halves(first), 0.0),
                jnp.where(left, 0.0, swap_halves(second)),
                jnp.where(left, 0.0, second),
            ]
            peer, inner = divmod(low * source, high)
            at = (which * high + inner) * 8
            grads = []
            for shift in range(0, devices, peers):
                part = rx_ref[peer + shift, at : at + 8 * low, :].astype(F32)
                grads += [part[0:8], swap_halves(part[0:8]), part[8:16], swap_halves(part[8:16])]
            block = jnp.concatenate(block * (devices // peers), axis=0).astype(BF16)
            grads = jnp.concatenate(grads, axis=0)[:, 0:WIDTH].astype(BF16)
            found = mm_tn(block, grads)
            mode = which * MODES + low * source
            spec_ref[mode] = found[0:WIDTH]
            spec_ref[mode + 1] = found[WIDTH : 2 * WIDTH]
    main = rx_ref.shape[1] - 8
    for peer in range(peers):
        rows = rx_ref[peer, main : main + 8, :].astype(F32)
        for shift in range(peers, devices, peers):
            rows += rx_ref[peer + shift, main : main + 8, :].astype(F32)
        skip_ref[8 * peer : 8 * peer + 8, :] = (rows + swap_halves(rows))[:, 0:WIDTH]


def run(kernel, outs, ins, flops, scratch=(), smem=0, hbm=0, hbm_outs=0, grant=16):
    vmem = pl.BlockSpec(memory_space=pltpu.VMEM)
    far = pl.BlockSpec(memory_space=pltpu.HBM)
    scalar = pl.BlockSpec(memory_space=pltpu.SMEM)
    moved = sum(math.prod(a.shape) * a.dtype.itemsize for a in list(ins) + list(outs))
    return pl.pallas_call(
        kernel,
        out_shape=tuple(outs),
        in_specs=[scalar] * smem + [far] * hbm + [vmem] * (len(ins) - smem - hbm),
        out_specs=tuple([far] * hbm_outs + [vmem] * (len(outs) - hbm_outs)),
        scratch_shapes=list(scratch),
        compiler_params=pltpu.CompilerParams(vmem_limit_bytes=grant * 1024 * 1024),
        cost_estimate=pl.CostEstimate(flops=flops, bytes_accessed=moved, transcendentals=0),
    )(*ins)


def slab_step(
    point_feats,
    pair_point,
    pair_cell,
    kernel,
    counts,
    area,
    normals,
    targets,
    spec_weight,
    skip_weight,
    skip_bias,
    head_weight,
    head_bias,
    out_weight,
):
    n = lax.axis_size("gx")
    points = point_feats.shape[0]
    slots = n * LANES
    slab = GX // n
    low = MODES // n
    depth = ZL * n
    levels = depth * WIDTH // LANES
    rows = MODES * slab
    main = levels * slab * low
    own_rows = low * low * levels
    shape = jax.ShapeDtypeStruct

    by = host_rows(GY, MODES)
    bx = host_rows(GX, MODES)
    by_rows = jnp.asarray(np.repeat(by, slab, axis=0))
    table = np.zeros((MODES, low, n, low, slab), ml_dtypes.bfloat16)
    for index in range(low):
        table[:, index, :, index, :] = bx.reshape(MODES, n, slab)
    table = table.reshape(MODES * low, rows)
    back = jnp.asarray(np.ascontiguousarray(table.T))
    table = jnp.asarray(table)
    peers = 8
    halves = n // peers
    high = MODES // peers
    part_table = np.zeros((halves, MODES, high, peers, high, slab), ml_dtypes.bfloat16)
    for index in range(high):
        part_table[:, :, index, :, index, :] = np.moveaxis(
            bx.reshape(MODES, halves, peers, slab), 1, 0
        )
    part_table = jnp.asarray(part_table.reshape(halves, MODES * high, rows))
    near = [[half * peers + peer for peer in range(peers)] for half in range(halves)]
    half = lax.shift_right_logical(lax.axis_index("gx"), peers.bit_length() - 1)
    half = half.astype(jnp.int32).reshape(1)

    def exchange(message):
        return lax.all_to_all(message, "gx", split_axis=0, concat_axis=0, tiled=True)

    def exchange_alone(message, *others):
        return lax.optimization_barrier((exchange(message),) + others)

    group = lax.axis_index("groups").astype(jnp.int32).reshape(1)
    point_rows = pair_point[0]
    cells = pair_cell[:, 0, :]
    area_row = area.reshape(1, points)
    msg, pw = run(
        source_kernel,
        [shape((n, 2 * WIDTH, LANES), BF16), shape((n, LANES), F32)],
        [group, half, counts, point_rows, kernel[0], area_row, point_feats.T, spec_weight],
        2 * 80 * points * slots,
        scratch=[
            pltpu.VMEM((1, n), jnp.int32),
            pltpu.VMEM((n, LANES), jnp.int32),
            pltpu.VMEM((n, LANES), F32),
            pltpu.VMEM((1, points), F32),
            pltpu.VMEM((WIDTH, points), BF16),
            pltpu.VMEM((MODES, WIDTH, WIDTH), BF16),
            pltpu.SemaphoreType.DMA((6,)),
        ],
        smem=2,
        hbm=6,
        grant=60,
    )
    rx = exchange(msg)
    shared = 256
    zr, rank, home = run(
        functools.partial(place_kernel, depth),
        [
            shape((n, LANES), jnp.int32),
            shape((n, LANES), jnp.int32),
            shape((shared, LANES), F32),
        ],
        [cells],
        2 * rows * LANES * slots,
        scratch=[
            pltpu.VMEM((slots, LANES), F32),
            pltpu.VMEM((n, LANES), F32),
            pltpu.VMEM((shared, slots), BF16),
            pltpu.VMEM((16, slots), BF16),
        ],
    )
    sum_scratch = [
        pltpu.VMEM((WIDTH, slots), F32),
        pltpu.VMEM((shared, slots), BF16),
        pltpu.VMEM((shared, slots), BF16),
        pltpu.VMEM((slots, LANES), BF16),
        pltpu.VMEM((slots, LANES), F32),
    ]
    own = rx[:, WIDTH : 2 * WIDTH, :]
    other = lax.ppermute(own, "groups", [(0, 1), (1, 0)])
    pair_rows = pltpu.VMEM((WIDTH, slots), BF16)
    basis = pltpu.VMEM((rows, slots), BF16)
    deep_rows = pltpu.VMEM((depth * WIDTH, slots), BF16)
    big = 2 * WIDTH * slots * slots + 2 * rows * slots * depth * WIDTH
    msg, lat = run(
        functools.partial(cell_kernel, depth),
        [shape((n, main, LANES), BF16), shape((WIDTH, slots), BF16)],
        [rx, cells, rank, zr, home, by_rows],
        big,
        scratch=sum_scratch + [pair_rows, deep_rows, basis],
        grant=20,
    )
    columns = exchange(msg)
    (term,) = run(
        skip_kernel,
        [shape((WIDTH, slots), F32)],
        [cells, rank, zr, home, lat, skip_weight, skip_bias.reshape(1, WIDTH)],
        2 * shared * WIDTH * slots,
        scratch=[pltpu.VMEM((shared, slots), BF16)] * 2,
    )
    (weights,) = run(
        weight_kernel,
        [shape((MODES, WIDTH, LANES), BF16)],
        [group, own, other],
        MODES * WIDTH * LANES,
        smem=1,
    )
    msg, spec = run(
        mode_kernel,
        [shape((n, main, LANES), BF16), shape((n, own_rows, LANES), BF16)],
        [columns, weights, table, back, term],
        4 * MODES * low * rows * depth * WIDTH,
        scratch=[pltpu.VMEM((MODES * low * levels, LANES), F32)] * 2,
    )
    slabs, spec, lat, term, cells, zr, rank, home, pw = exchange_alone(
        msg, spec, lat, term, cells, zr, rank, home, pw
    )
    msg, pre = run(
        functools.partial(pre_kernel, depth),
        [shape((n, WIDTH + own_rows, LANES), BF16), shape((WIDTH, slots), F32)],
        [slabs, by_rows, term, cells, spec],
        2 * rows * slots * depth * WIDTH,
        scratch=[pltpu.VMEM((depth * WIDTH, rows), BF16), basis],
    )
    returned, pre, lat, cells, zr, rank, home, pw = exchange_alone(
        msg, pre, lat, cells, zr, rank, home, pw
    )
    out_row = out_weight.reshape(1, WIDTH)
    pressure, msg, own_spec = run(
        head_kernel,
        [
            shape((1, points), F32),
            shape((n, WIDTH + 8, LANES), BF16),
            shape((n, own_rows, LANES), BF16),
        ],
        [returned, point_rows, pw, head_weight, head_bias.reshape(1, WIDTH), out_row, area_row, normals],
        2 * 3 * WIDTH * points * slots,
        scratch=[
            pltpu.VMEM((3 * WIDTH, slots), BF16),
            pltpu.VMEM((points, slots), BF16),
            pltpu.VMEM((2, n, LANES), F32),
        ],
    )
    grads, pressure, own_spec, pre, lat, cells, zr, rank, home = exchange_alone(
        msg, pressure, own_spec, pre, lat, cells, zr, rank, home
    )
    scale = 1.0 / math.sqrt(points * n)
    msg, forces, out_grad = run(
        functools.partial(back_kernel, depth, scale),
        [
            shape((peers, halves * main + 8, LANES), BF16),
            shape((1, 2), F32),
            shape((1, WIDTH), F32),
        ],
        [grads, targets.reshape(1, 2), cells, rank, zr, home, by_rows, lat, pre],
        big,
        scratch=sum_scratch
        + [pltpu.VMEM((2 * WIDTH, slots), BF16), pair_rows, deep_rows]
        + [pltpu.VMEM((WIDTH, slots), F32), basis],
        grant=20,
    )
    grad_columns, forces, out_grad, own_spec = lax.optimization_barrier(
        (
            lax.all_to_all(
                msg, "gx", split_axis=0, concat_axis=0, tiled=True, axis_index_groups=near
            ),
            forces,
            out_grad,
            own_spec,
        )
    )
    part_rows = MODES * high * levels // n
    (msg,) = run(
        spec_kernel,
        [shape((n, part_rows + 8, LANES), BF16)],
        [half, grad_columns, part_table],
        2 * MODES * high * rows * depth * WIDTH,
        scratch=[pltpu.VMEM((MODES * high * levels, LANES), F32)],
        smem=1,
    )
    finals, own_spec, forces, out_grad = exchange_alone(msg, own_spec, forces, out_grad)
    spec_grad, skip_grad = run(
        functools.partial(final_kernel, peers),
        [shape((spec_weight.shape[0], WIDTH, WIDTH), F32), shape((WIDTH, WIDTH), F32)],
        [finals, own_spec],
        2 * NMODE * WIDTH * WIDTH * depth // n,
    )
    return (pressure.reshape(points), forces.reshape(2), spec_grad, skip_grad, out_grad.reshape(WIDTH))


def solution(mesh):
    fits = mesh.shape["gx"] == 16 and mesh.shape["groups"] == 2
    per_device = slab_step if fits else general_step
    in_specs = (
        P(("groups", "gx"), None),
        P(("groups", "gx"), None, None),
        P(None, ("groups", "gx"), None),
        P(("groups", "gx"), None, None),
        P(("groups", "gx"), None),
        P(("groups", "gx")),
        P(None, ("groups", "gx")),
        P("groups"),
        P("gx", None, None),
        P(),
        P(),
        P(),
        P(),
        P(),
    )
    out_specs = (
        P(("groups", "gx")),
        P("groups"),
        P(("groups", "gx"), None, None),
        P("groups", None),
        P("groups"),
    )
    return jax.shard_map(
        per_device, mesh=mesh, in_specs=in_specs, out_specs=out_specs, check_vma=False
    )
```

```python
import functools
import math

import jax
import jax.numpy as jnp
import ml_dtypes
import numpy as np
from jax import lax
from jax.experimental import pallas as pl
from jax.experimental.pallas import tpu as pltpu
from jax.sharding import PartitionSpec as P

GX = 128
GY = 128
MODES = 32
ZL = 1
NMODE = 1024


def fourier_rows(length, number):
    places = jnp.arange(length, dtype=jnp.float32)
    order = jnp.arange(number)
    half = number // 2
    freqs = jnp.where(order < half, order, order - half + 1).astype(jnp.float32)
    angles = 2.0 * math.pi / length * freqs[:, None] * places[None, :]
    table = jnp.where((order < half)[:, None], jnp.cos(angles), jnp.sin(angles))
    return (table * math.sqrt(2.0 / length)).astype(jnp.bfloat16)


def gelu_value(values):
    return 0.5 * values * (1.0 + lax.erf(values * (1.0 / math.sqrt(2.0))))


def gelu_slope(values):
    return 0.5 * (1.0 + lax.erf(values * (1.0 / math.sqrt(2.0)))) + values * jnp.exp(
        -0.5 * values * values
    ) * (1.0 / math.sqrt(2.0 * math.pi))


def general_step(
    point_feats,
    pair_point,
    pair_cell,
    kernel,
    counts,
    area,
    normals,
    targets,
    spec_weight,
    skip_weight,
    skip_bias,
    head_weight,
    head_bias,
    out_weight,
):
    devices = lax.axis_size("gx")
    local_points, width = point_feats.shape
    block_slots = pair_point.shape[2]
    row_count = GX // devices
    depth = ZL * devices
    slab_cells = row_count * GY * depth
    valid_mask = jnp.arange(block_slots)[None, :] < counts[0][:, None]
    point_rows = pair_point[0]
    pair_weight = jnp.where(valid_mask, kernel[0], jnp.float32(0.0))
    sender_weight = pair_weight * area[point_rows]
    contrib = (sender_weight[..., None] * point_feats[point_rows].astype(jnp.float32)).astype(
        jnp.bfloat16
    )
    arrived = lax.all_to_all(contrib, "gx", split_axis=0, concat_axis=0, tiled=True)
    cell_rows = pair_cell[:, 0, :].reshape(-1)
    latent = jax.ops.segment_sum(
        arrived.reshape(-1, width).astype(jnp.float32), cell_rows, num_segments=slab_cells
    ).astype(jnp.bfloat16)
    col_table = fourier_rows(GY, MODES)
    row_table = fourier_rows(GX, MODES)
    volume = latent.reshape(row_count, GY, depth * width)
    along_y = jnp.einsum(
        "by,xyk->xbk", col_table, volume, preferred_element_type=jnp.float32
    ).astype(jnp.bfloat16)
    columns = lax.all_to_all(along_y, "gx", split_axis=2, concat_axis=0, tiled=True)
    spectrum = jnp.einsum(
        "ax,xbk->abk", row_table, columns, preferred_element_type=jnp.float32
    ).astype(jnp.bfloat16)
    mode_rows = lax.all_to_all(
        spectrum.reshape(NMODE, ZL * width), "gx", split_axis=0, concat_axis=1, tiled=True
    )
    own_modes = mode_rows.shape[0]
    mixed_rows = jnp.einsum(
        "mzc,mcd->mzd",
        mode_rows.reshape(own_modes, depth, width),
        spec_weight,
        preferred_element_type=jnp.float32,
    ).astype(jnp.bfloat16)
    mixed = lax.all_to_all(
        mixed_rows.reshape(own_modes, depth * width), "gx", split_axis=1, concat_axis=0, tiled=True
    )
    back_x = jnp.einsum(
        "ax,abk->xbk",
        row_table,
        mixed.reshape(MODES, MODES, ZL * width),
        preferred_element_type=jnp.float32,
    ).astype(jnp.bfloat16)
    slabs = lax.all_to_all(back_x, "gx", split_axis=0, concat_axis=2, tiled=True)
    spatial = jnp.einsum(
        "by,xbk->xyk", col_table, slabs, preferred_element_type=jnp.float32
    ).reshape(slab_cells, width)
    pre = spatial + jnp.dot(latent, skip_weight, preferred_element_type=jnp.float32) + skip_bias
    features = gelu_value(pre).astype(jnp.bfloat16)
    picked = features[cell_rows].reshape(devices, block_slots, width)
    returned = lax.all_to_all(picked, "gx", split_axis=0, concat_axis=0, tiled=True)
    point_latent = jax.ops.segment_sum(
        (pair_weight[..., None] * returned.astype(jnp.float32)).reshape(-1, width),
        point_rows.reshape(-1),
        num_segments=local_points,
    )
    head_matrix = head_weight.astype(jnp.float32)
    head_pre = jnp.dot(point_latent, head_matrix, precision=lax.Precision.HIGHEST) + head_bias
    head = gelu_value(head_pre)
    pressure = jnp.dot(head, out_weight, precision=lax.Precision.HIGHEST)
    weighted = pressure * area
    scale = 1.0 / math.sqrt(local_points * devices)
    totals = lax.psum(
        jnp.stack([jnp.sum(weighted * normals[0]), jnp.sum(weighted * normals[1])]), "gx"
    )
    forces = scale * totals
    misfit = forces - targets
    point_grad = 2.0 * scale * (misfit[0] * normals[0] + misfit[1] * normals[1]) * area
    out_part = jnp.dot(point_grad, head, precision=lax.Precision.HIGHEST)
    head_grad = point_grad[:, None] * out_weight[None, :] * gelu_slope(head_pre)
    latent_grad = jnp.dot(head_grad, head_matrix.T, precision=lax.Precision.HIGHEST).astype(
        jnp.bfloat16
    )
    grad_pairs = (pair_weight[..., None] * latent_grad[point_rows].astype(jnp.float32)).astype(
        jnp.bfloat16
    )
    grad_arrived = lax.all_to_all(grad_pairs, "gx", split_axis=0, concat_axis=0, tiled=True)
    cell_grad = jax.ops.segment_sum(
        grad_arrived.reshape(-1, width).astype(jnp.float32), cell_rows, num_segments=slab_cells
    )
    pre_grad = (cell_grad * gelu_slope(pre)).astype(jnp.bfloat16)
    skip_part = jnp.dot(latent.T, pre_grad, preferred_element_type=jnp.float32)
    grad_y = jnp.einsum(
        "by,xyk->xbk",
        col_table,
        pre_grad.reshape(row_count, GY, depth * width),
        preferred_element_type=jnp.float32,
    ).astype(jnp.bfloat16)
    grad_columns = lax.all_to_all(grad_y, "gx", split_axis=2, concat_axis=0, tiled=True)
    grad_spec = jnp.einsum(
        "ax,xbk->abk", row_table, grad_columns, preferred_element_type=jnp.float32
    ).astype(jnp.bfloat16)
    grad_rows = lax.all_to_all(
        grad_spec.reshape(NMODE, ZL * width), "gx", split_axis=0, concat_axis=1, tiled=True
    )
    own_modes = grad_rows.shape[0]
    spec_grad = jnp.einsum(
        "mzc,mzd->mcd",
        mode_rows.reshape(own_modes, depth, width),
        grad_rows.reshape(own_modes, depth, width),
        preferred_element_type=jnp.float32,
    )
    out_grad, skip_grad = lax.psum((out_part, skip_part), "gx")
    return (pressure, forces, spec_grad, skip_grad, out_grad)


F32 = jnp.float32
BF16 = jnp.bfloat16
LANES = 128
WIDTH = 64


def host_rows(length, number):
    places = np.arange(length, dtype=np.float32)
    order = np.arange(number)
    half = number // 2
    freqs = np.where(order < half, order, order - half + 1).astype(np.float32)
    angles = np.float32(2.0 * math.pi / length) * freqs[:, None] * places[None, :]
    table = np.where((order < half)[:, None], np.cos(angles), np.sin(angles))
    table = table.astype(np.float32) * np.float32(math.sqrt(2.0 / length))
    return table.astype(ml_dtypes.bfloat16)


def three_parts(values):
    first = values.astype(BF16)
    rest = values - first.astype(F32)
    second = rest.astype(BF16)
    third = (rest - second.astype(F32)).astype(BF16)
    return first, second, third


def mm(left, right):
    return jnp.dot(left, right, preferred_element_type=F32)


def mm_nt(left, right):
    return lax.dot_general(left, right, (((1,), (1,)), ((), ())), preferred_element_type=F32)


def mm_tn(left, right):
    return lax.dot_general(left, right, (((0,), (0,)), ((), ())), preferred_element_type=F32)


def two_rows(ref, pair):
    return jnp.concatenate([ref[2 * pair : 2 * pair + 1, :], ref[2 * pair + 1 : 2 * pair + 2, :]], axis=1)


def source_kernel(group_ref, half_ref, count_hbm, point_hbm, kern_hbm, area_hbm, feat_hbm, weight_hbm, msg_ref, pw_ref, count_ref, point_ref, kern_ref, area_ref, feat_ref, weight_ref, sems):
    devices, points = point_ref.shape[0], feat_ref.shape[1]
    low = MODES // devices
    pieces = (
        (point_hbm, point_ref),
        (area_hbm, area_ref),
        (feat_hbm, feat_ref),
        (kern_hbm, kern_ref),
        (count_hbm, count_ref),
        (weight_hbm.at[pl.ds(group_ref[0] * MODES, MODES)], weight_ref),
    )
    copies = [
        pltpu.make_async_copy(source, place, sems.at[index])
        for index, (source, place) in enumerate(pieces)
    ]
    for copy in copies:
        copy.start()
    for copy in copies[:-1]:
        copy.wait()
    first, second, third = three_parts(area_ref[...])
    place = lax.broadcasted_iota(jnp.int32, (16, points), 0)
    extra = jnp.where(
        place == 0,
        first.astype(F32),
        jnp.where(place == 1, second.astype(F32), jnp.where(place == 2, third.astype(F32), 0.0)),
    ).astype(BF16)
    table = jnp.concatenate([feat_ref[...], extra], axis=0)
    rows = lax.broadcasted_iota(jnp.int32, (points, 2 * LANES), 0)
    lane = lax.broadcasted_iota(jnp.int32, (1, LANES), 1)
    for pair in range(devices // 2):
        hot = jnp.where(rows == two_rows(point_ref, pair), 1.0, 0.0).astype(BF16)
        got = mm(table, hot)
        spread = got[WIDTH : WIDTH + 1] + got[WIDTH + 1 : WIDTH + 2] + got[WIDTH + 2 : WIDTH + 3]
        for half in range(2):
            dest = 2 * pair + half
            cut = slice(half * LANES, (half + 1) * LANES)
            valid = lane < count_ref[0:1, dest : dest + 1]
            weight = jnp.where(valid, kern_ref[dest : dest + 1, :], 0.0)
            pw_ref[dest : dest + 1, :] = weight
            msg_ref[dest, 0:WIDTH, :] = ((weight * spread[:, cut]) * got[0:WIDTH, cut]).astype(BF16)
    copies[-1].wait()
    for dest in range(devices):
        msg_ref[dest, WIDTH : 2 * WIDTH, :] = jnp.concatenate(
            [weight_ref[low * dest], weight_ref[low * dest + 1]], axis=1
        )


def columns_of(row):
    return jnp.broadcast_to(row, (LANES, LANES)).T


def column_of(row):
    down = lax.broadcasted_iota(jnp.int32, (WIDTH, WIDTH), 0)
    along = lax.broadcasted_iota(jnp.int32, (WIDTH, WIDTH), 1)
    return jnp.sum(jnp.where(down == along, row, 0.0), axis=1, keepdims=True)


def pick_rows(rank_ref, pick_ref):
    rows = lax.broadcasted_iota(jnp.int32, (pick_ref.shape[0], LANES), 0)
    for block in range(rank_ref.shape[0]):
        pick_ref[:, block * LANES : (block + 1) * LANES] = jnp.where(
            rows == rank_ref[block : block + 1, :], 1.0, 0.0
        ).astype(BF16)


def basis_rows(depth, cell_ref, by_ref, lp_ref):
    zbits = depth.bit_length() - 1
    rows = by_ref.shape[0]
    slab = rows // MODES
    wide = 2 * LANES
    yrow = lax.broadcasted_iota(jnp.int32, (GY, wide), 0)
    xrow = jnp.bitwise_and(lax.broadcasted_iota(jnp.int32, (16, wide), 0), slab - 1)
    for pair in range(cell_ref.shape[0] // 2):
        cells = two_rows(cell_ref, pair)
        ypos = jnp.bitwise_and(jnp.right_shift(cells, zbits), GY - 1)
        xpos = jnp.right_shift(cells, zbits + GY.bit_length() - 1)
        hot = jnp.where(yrow == ypos, 1.0, 0.0).astype(BF16)
        mask = jnp.where(xrow == xpos, 1.0, 0.0).astype(BF16)
        found = mm(by_ref[...], hot).astype(BF16)
        for at in range(0, rows, 16):
            lp_ref[at : at + 16, pair * wide : (pair + 1) * wide] = found[at : at + 16] * mask


def place_kernel(depth, cell_ref, by_ref, zr_ref, rank_ref, home_ref, lp_ref, col_ref, flag_ref, pick_ref, part_ref):
    devices = cell_ref.shape[0]
    basis_rows(depth, cell_ref, by_ref, lp_ref)
    down = lax.broadcasted_iota(jnp.int32, (LANES, LANES), 0)
    along = lax.broadcasted_iota(jnp.int32, (LANES, LANES), 1)
    place = lax.broadcasted_iota(jnp.int32, (16, LANES), 0)
    for block in range(devices):
        cells = cell_ref[block : block + 1, :]
        row = cells.astype(F32)
        cut = slice(block * LANES, (block + 1) * LANES)
        col_ref[cut, :] = columns_of(row)
        high = jnp.right_shift(cells, 7).astype(F32)
        low = jnp.bitwise_and(cells, 127).astype(F32)
        part_ref[:, cut] = jnp.where(place == 0, high, jnp.where(place == 1, low, 0.0)).astype(BF16)
        same = jnp.logical_and(col_ref[cut, :] == row, down < along)
        before = jnp.max(jnp.where(same, 1.0, 0.0), axis=0, keepdims=True)
        if block:
            early = jnp.where(col_ref[0 : block * LANES, :] == row, 1.0, 0.0)
            before = jnp.maximum(before, jnp.max(early, axis=0, keepdims=True))
        zr_ref[block : block + 1, :] = jnp.where(
            before > 0.0, -1, jnp.bitwise_and(cells, depth - 1)
        )
        flag_ref[block : block + 1, :] = before
    flags = flag_ref[...]
    marks = flags.astype(BF16)
    inside = mm(marks, jnp.where(down <= along, 1.0, 0.0).astype(BF16))
    above = jnp.where(down < along, 1.0, 0.0)[:, 0:devices][0:devices]
    ahead = jnp.sum(mm_tn(above.astype(BF16), marks), axis=1, keepdims=True)
    rank_ref[...] = jnp.where(flags > 0.0, (inside + ahead - flags).astype(jnp.int32), -1)
    pick_rows(rank_ref, pick_ref)
    found = mm_nt(part_ref[...], pick_ref[...])
    found = found[0:1] * 128.0 + found[1:2]
    for block in range(home_ref.shape[0] // LANES):
        cut = slice(block * LANES, (block + 1) * LANES)
        home_ref[cut, :] = columns_of(found[:, cut])


def first_rows(cell_ref, zr_ref, home_ref, first_ref):
    for block in range(cell_ref.shape[0]):
        here = slice(block, block + 1)
        row = jnp.where(zr_ref[here, :] < 0, -1.0, cell_ref[here, :].astype(F32))
        first_ref[:, block * LANES : (block + 1) * LANES] = jnp.where(
            home_ref[...] == row, 1.0, 0.0
        ).astype(BF16)


def fold_parts(values):
    total = values[0:WIDTH]
    for at in range(WIDTH, values.shape[0], WIDTH):
        total = total + values[at : at + WIDTH]
    return total


def sum_cells(terms, xs_ref, cell_ref, rank_ref, zr_ref, home_ref, sums_ref, pick_ref, first_ref, full_ref, col_ref):
    devices = cell_ref.shape[0]
    few = jnp.max(rank_ref[...]) < home_ref.shape[0]

    @pl.when(few)
    def _():
        pick_rows(rank_ref, pick_ref)
        first_rows(cell_ref, zr_ref, home_ref, first_ref)
        moved = mm_nt(xs_ref[...], pick_ref[...]).astype(BF16)
        for pair in range(devices // 2):
            span = slice(pair * 2 * LANES, (pair + 1) * 2 * LANES)
            sums_ref[:, span] = terms(span) + fold_parts(mm(moved, first_ref[:, span]))

    @pl.when(jnp.logical_not(few))
    def _():
        for block in range(devices):
            col_ref[block * LANES : (block + 1) * LANES, :] = columns_of(
                cell_ref[block : block + 1, :].astype(F32)
            )
        for block in range(devices):
            row = cell_ref[block : block + 1, :].astype(F32)
            full_ref[...] = jnp.where(col_ref[...] == row, 1.0, 0.0).astype(BF16)
            sums_ref[:, block * LANES : (block + 1) * LANES] = fold_parts(
                mm(xs_ref[...], full_ref[...])
            )


def slab_rows(value_ref, zr_ref, lp_ref, rp_ref, msg_ref):
    devices = msg_ref.shape[0]
    step = lp_ref.shape[0] // devices
    for quad in range(rp_ref.shape[0] // (4 * WIDTH)):
        for pair in range(zr_ref.shape[0] // 2):
            cut = slice(pair * 2 * LANES, (pair + 1) * 2 * LANES)
            zpos = two_rows(zr_ref, pair)
            values = value_ref[:, cut].astype(F32)
            for level in range(4 * quad, 4 * quad + 4):
                rp_ref[level * WIDTH : (level + 1) * WIDTH, cut] = jnp.where(
                    zpos == level, values, 0.0
                ).astype(BF16)
        out = mm_nt(lp_ref[...], rp_ref[quad * 4 * WIDTH : (quad + 1) * 4 * WIDTH, :]).astype(BF16)
        for half in range(2):
            level = 2 * quad + half
            for dest in range(devices):
                msg_ref[dest, level * step : (level + 1) * step, :] = out[
                    dest * step : (dest + 1) * step, half * LANES : (half + 1) * LANES
                ]


def cell_kernel(rx_ref, cell_ref, rank_ref, zr_ref, home_ref, lp_ref, msg_ref, lat_ref, sums_ref, pick_ref, first_ref, full_ref, col_ref, xs_ref, rp_ref):
    devices = rx_ref.shape[0]
    for block in range(devices):
        xs_ref[:, block * LANES : (block + 1) * LANES] = rx_ref[block, 0:WIDTH, :]
    sum_cells(
        lambda span: xs_ref[:, span].astype(F32),
        xs_ref, cell_ref, rank_ref, zr_ref, home_ref, sums_ref, pick_ref, first_ref, full_ref, col_ref,
    )
    for pair in range(devices // 2):
        cut = slice(pair * 2 * LANES, (pair + 1) * 2 * LANES)
        latent = sums_ref[:, cut]
        lat_ref[:, cut] = latent.astype(BF16)
    slab_rows(lat_ref, zr_ref, lp_ref, rp_ref, msg_ref)


def to_modes(rx_ref, table, sp_ref):
    levels = sp_ref.shape[0] // table.shape[0]
    step = table.shape[1] // rx_ref.shape[0]
    for level in range(levels):
        block = rx_ref[:, level * step : (level + 1) * step, :].reshape(table.shape[1], LANES)
        coeffs = mm(table, block).astype(BF16).astype(F32)
        sp_ref[pl.ds(level, table.shape[0], stride=levels), :] = coeffs


def swap_halves(values):
    return pltpu.roll(values, WIDTH, 1)


def weight_kernel(group_ref, own_ref, other_ref, weight_ref):
    for order in range(MODES):
        source, which = order // 2, order % 2
        mine = jnp.full((WIDTH, LANES), group_ref[0], jnp.int32) == which
        weight_ref[order] = jnp.where(
            mine, own_ref[source].astype(F32), other_ref[source].astype(F32)
        ).astype(BF16)


def mode_kernel(rx_ref, weight_ref, table_ref, back_ref, term_ref, msg_ref, spec_ref, sp_ref, mx_ref):
    devices = rx_ref.shape[0]
    own_rows = spec_ref.shape[1]
    modes = table_ref.shape[0]
    levels = sp_ref.shape[0] // modes
    step = back_ref.shape[0] // devices
    to_modes(rx_ref, table_ref[...], sp_ref)
    for dest in range(devices):
        spec_ref[dest] = sp_ref[dest * own_rows : (dest + 1) * own_rows, :].astype(BF16)
    left = lax.broadcasted_iota(jnp.int32, (levels, LANES), 1) < WIDTH
    for order in range(MODES):
        at = order * 2 * levels
        even = sp_ref[at : at + levels, :]
        odd = sp_ref[at + levels : at + 2 * levels, :]
        rows = jnp.concatenate([even, swap_halves(even), odd, swap_halves(odd)], axis=0)
        out = mm(rows[:, 0:WIDTH].astype(BF16), weight_ref[order])
        mx_ref[at : at + levels, :] = jnp.where(
            left, out[0:levels], swap_halves(out[levels : 2 * levels])
        )
        mx_ref[at + levels : at + 2 * levels, :] = jnp.where(
            left, swap_halves(out[2 * levels : 3 * levels]), out[3 * levels : 4 * levels]
        )
    for level in range(levels):
        mixed = mx_ref[pl.ds(level, modes, stride=levels), :].astype(BF16)
        out = mm(back_ref[...], mixed).astype(BF16)
        for dest in range(devices):
            msg_ref[dest, level * step : (level + 1) * step, :] = out[dest * step : (dest + 1) * step]


def skip_kernel(cell_ref, rank_ref, zr_ref, home_ref, lat_ref, skip_ref, bias_ref, term_ref, pick_ref, first_ref):
    few = jnp.max(rank_ref[...]) < home_ref.shape[0]
    bias = column_of(bias_ref[...])
    pick_rows(rank_ref, pick_ref)
    first_rows(cell_ref, zr_ref, home_ref, first_ref)
    shared = mm_nt(lat_ref[...], first_ref[...]).astype(BF16)
    for pair in range(cell_ref.shape[0] // 2):
        span = slice(pair * 2 * LANES, (pair + 1) * 2 * LANES)
        later = jnp.logical_and(two_rows(rank_ref, pair) >= 0, few)
        latent = jnp.where(later, mm(shared, pick_ref[:, span]), lat_ref[:, span].astype(F32))
        term_ref[:, span] = mm_tn(skip_ref[...], latent.astype(BF16)) + bias


def pre_kernel(depth, rx_ref, lp_ref, term_ref, cell_ref, spec_ref, msg_ref, pre_ref, rt_ref):
    devices = rx_ref.shape[0]
    rows = lp_ref.shape[0]
    step = rows // devices
    for level in range(rt_ref.shape[0] // LANES):
        block = rx_ref[:, level * step : (level + 1) * step, :].reshape(rows, LANES)
        rt_ref[level * LANES : (level + 1) * LANES, :] = block.T
    for pair in range(devices // 2):
        cut = slice(pair * 2 * LANES, (pair + 1) * 2 * LANES)
        zpos = jnp.bitwise_and(two_rows(cell_ref, pair), depth - 1)
        field = mm(rt_ref[...], lp_ref[:, cut])
        total = jnp.where(zpos == 0, field[0:WIDTH], 0.0)
        for level in range(1, depth):
            total += jnp.where(zpos == level, field[level * WIDTH : (level + 1) * WIDTH], 0.0)
        pre = total + term_ref[:, cut]
        pre_ref[:, cut] = pre
        feats = gelu_value(pre).astype(BF16)
        for half in range(2):
            dest = 2 * pair + half
            msg_ref[dest, 0:WIDTH, :] = feats[:, half * LANES : (half + 1) * LANES]
            msg_ref[dest, WIDTH:, :] = spec_ref[dest]


def head_kernel(rx_ref, point_ref, pw_ref, head_ref, bias_ref, out_ref, area_ref, normal_ref, pres_ref, msg_ref, spec_ref, value_ref, hot_ref, na_ref):
    devices = rx_ref.shape[0]
    points = area_ref.shape[1]
    rows = lax.broadcasted_iota(jnp.int32, (points, LANES), 0)
    for block in range(devices):
        cut = slice(block * LANES, (block + 1) * LANES)
        parts = three_parts(pw_ref[block : block + 1, :] * rx_ref[block, 0:WIDTH, :].astype(F32))
        for index, part in enumerate(parts):
            value_ref[index * WIDTH : (index + 1) * WIDTH, cut] = part
        hot_ref[:, cut] = jnp.where(rows == point_ref[block : block + 1, :], 1.0, 0.0).astype(BF16)
    sums = mm_nt(value_ref[...], hot_ref[...])
    latent = sums[0:WIDTH] + sums[WIDTH : 2 * WIDTH] + sums[2 * WIDTH : 3 * WIDTH]
    first, second, third = three_parts(latent)
    weight = head_ref[...]
    head_pre = mm_tn(weight, first) + mm_tn(weight, second) + mm_tn(weight, third) + column_of(bias_ref[...])
    out_column = column_of(out_ref[...])
    head = gelu_value(head_pre)
    pressure = jnp.sum(head * out_column, axis=0, keepdims=True)
    pres_ref[...] = pressure
    along = [normal_ref[which : which + 1, :] * area_ref[...] for which in range(2)]
    first, second, third = three_parts(out_column * gelu_slope(head_pre))
    grad = mm(weight, first) + mm(weight, second) + mm(weight, third)
    place = lax.broadcasted_iota(jnp.int32, (16, points), 0)
    extra = jnp.zeros((16, points), F32)
    for which in range(2):
        for index, part in enumerate(three_parts(along[which])):
            extra = jnp.where(place == 3 * which + index, part.astype(F32), extra)
    table = jnp.concatenate([grad.astype(BF16), extra.astype(BF16)], axis=0)
    lane = lax.broadcasted_iota(jnp.int32, (1, LANES), 1)
    partial = []
    for which in range(2):
        force = jnp.sum(pressure * area_ref[...] * normal_ref[which : which + 1, :], axis=1, keepdims=True)
        partial.append(force)
    force_row = jnp.zeros((1, LANES), F32)
    for which in range(2):
        for index, part in enumerate(three_parts(partial[which])):
            force_row = jnp.where(lane == 3 * which + index, part.astype(F32), force_row)
    out_rows = lax.dot_general(
        jnp.concatenate([along[0], along[1], jnp.zeros((6, points), F32)], axis=0),
        head,
        (((1,), (1,)), ((), ())),
        precision=lax.Precision.HIGHEST,
        preferred_element_type=F32,
    )
    out_row = jnp.concatenate([out_rows[0:1], out_rows[1:2]], axis=1)
    place = lax.broadcasted_iota(jnp.int32, (8, LANES), 0)
    out_parts = three_parts(out_row)
    common = jnp.where(
        place == 4,
        out_parts[0].astype(F32),
        jnp.where(place == 5, out_parts[1].astype(F32), jnp.where(place == 6, force_row, 0.0)),
    )
    for pair in range(devices // 2):
        got = mm(table, hot_ref[:, pair * 2 * LANES : (pair + 1) * 2 * LANES])
        for half in range(2):
            block = 2 * pair + half
            cut = slice(half * LANES, (half + 1) * LANES)
            msg_ref[block, 0:WIDTH, :] = got[0:WIDTH, cut].astype(BF16)
            spec_ref[block] = rx_ref[block, WIDTH:, :]
            for which in range(2):
                at = WIDTH + 3 * which
                na_ref[which, block : block + 1, :] = (
                    got[at : at + 1, cut] + got[at + 1 : at + 2, cut] + got[at + 2 : at + 3, cut]
                )
    scaled = [three_parts(pw_ref[...] * na_ref[which]) for which in range(2)]
    rows = [scaled[which][index].astype(F32) for which in range(2) for index in range(2)]
    for block in range(devices):
        tail = common
        for index, row in enumerate(rows):
            tail = jnp.where(place == index, row[block : block + 1, :], tail)
        msg_ref[block, WIDTH : WIDTH + 8, :] = tail.astype(BF16)


def back_kernel(depth, scale, rx_ref, target_ref, cell_ref, rank_ref, zr_ref, home_ref, lp_ref, lat_ref, pre_ref, msg_ref, force_ref, outg_ref, sums_ref, pick_ref, first_ref, full_ref, col_ref, xs_ref, pg_ref, rp_ref, gp_ref):
    devices = rx_ref.shape[0]
    main = msg_ref.shape[1] - 8
    extra = slice(WIDTH, WIDTH + 8)
    total = rx_ref[0, extra, :].astype(F32)
    for block in range(1, devices):
        total += rx_ref[block, extra, :].astype(F32)
    force = total[6:7]
    lane = lax.broadcasted_iota(jnp.int32, (1, 2), 1)
    forces = scale * jnp.where(
        lane == 0,
        force[:, 0:1] + force[:, 1:2] + force[:, 2:3],
        force[:, 3:4] + force[:, 4:5] + force[:, 5:6],
    )
    force_ref[...] = forces
    misfit = (2.0 * scale) * (forces - target_ref[...])
    drag, lift = misfit[:, 0:1], misfit[:, 1:2]
    out_row = total[4:5] + total[5:6]
    outg_ref[...] = drag * out_row[:, 0:WIDTH] + lift * out_row[:, WIDTH : 2 * WIDTH]
    for block in range(devices):
        tail = rx_ref[block, extra, :].astype(F32)
        factor = drag * (tail[0:1] + tail[1:2]) + lift * (tail[2:3] + tail[3:4])
        grad = factor * rx_ref[block, 0:WIDTH, :].astype(F32)
        cut = slice(block * LANES, (block + 1) * LANES)
        gp_ref[:, cut] = grad
        upper = grad.astype(BF16)
        xs_ref[0:WIDTH, cut] = upper
        xs_ref[WIDTH : 2 * WIDTH, cut] = (grad - upper.astype(F32)).astype(BF16)
    sum_cells(
        lambda span: gp_ref[:, span],
        xs_ref, cell_ref, rank_ref, zr_ref, home_ref, sums_ref, pick_ref, first_ref, full_ref, col_ref,
    )
    for pair in range(devices // 2):
        cut = slice(pair * 2 * LANES, (pair + 1) * 2 * LANES)
        grad = sums_ref[:, cut] * gelu_slope(pre_ref[:, cut])
        zpos = two_rows(zr_ref, pair)
        pg_ref[:, cut] = jnp.where(zpos >= 0, grad, 0.0).astype(BF16)
    slab_rows(pg_ref, zr_ref, lp_ref, rp_ref, msg_ref)
    skip = mm_nt(lat_ref[...], pg_ref[...])
    for dest in range(msg_ref.shape[0]):
        msg_ref[dest, main : main + 8, :] = two_parts(skip[8 * dest : 8 * dest + 8]).astype(BF16)


def two_parts(values):
    first, second, _ = three_parts(values)
    return jnp.concatenate([first.astype(F32), second.astype(F32)], axis=1)


def spec_kernel(half_ref, rx_ref, table_ref, msg_ref, sp_ref):
    peers, devices = rx_ref.shape[0], msg_ref.shape[0]
    part_rows = sp_ref.shape[0] // devices
    main = rx_ref.shape[1] - 8
    to_modes(rx_ref, table_ref[half_ref[0]], sp_ref)
    total = rx_ref[0, main : main + 8, :].astype(F32)
    for source in range(1, peers):
        total += rx_ref[source, main : main + 8, :].astype(F32)
    total = two_parts((total + swap_halves(total))[:, 0:WIDTH]).astype(BF16)
    for dest in range(devices):
        msg_ref[dest, 0:part_rows, :] = sp_ref[dest * part_rows : (dest + 1) * part_rows, :].astype(BF16)
        msg_ref[dest, part_rows : part_rows + 8, :] = total


def final_kernel(peers, rx_ref, own_ref, spec_ref, skip_ref):
    devices = rx_ref.shape[0]
    low = MODES // devices
    high = MODES // peers
    owned = spec_ref.shape[0] // MODES
    left = lax.broadcasted_iota(jnp.int32, (8, LANES), 1) < WIDTH
    for which in range(owned):
        for source in range(devices):
            at = which * 8 * low
            coeffs = own_ref[source, at : at + 8 * low, :].astype(F32)
            first, second = coeffs[0:8], coeffs[8:16]
            block = [
                jnp.where(left, first, 0.0),
                jnp.where(left, swap_halves(first), 0.0),
                jnp.where(left, 0.0, swap_halves(second)),
                jnp.where(left, 0.0, second),
            ]
            peer, inner = divmod(low * source, high)
            at = (which * high + inner) * 8
            grads = []
            for shift in range(0, devices, peers):
                part = rx_ref[peer + shift, at : at + 8 * low, :].astype(F32)
                grads += [part[0:8], swap_halves(part[0:8]), part[8:16], swap_halves(part[8:16])]
            block = jnp.concatenate(block * (devices // peers), axis=0).astype(BF16)
            grads = jnp.concatenate(grads, axis=0)[:, 0:WIDTH].astype(BF16)
            found = mm_tn(block, grads)
            mode = which * MODES + low * source
            spec_ref[mode] = found[0:WIDTH]
            spec_ref[mode + 1] = found[WIDTH : 2 * WIDTH]
    main = rx_ref.shape[1] - 8
    for peer in range(peers):
        rows = rx_ref[peer, main : main + 8, :].astype(F32)
        for shift in range(peers, devices, peers):
            rows += rx_ref[peer + shift, main : main + 8, :].astype(F32)
        skip_ref[8 * peer : 8 * peer + 8, :] = (rows + swap_halves(rows))[:, 0:WIDTH]


def run(kernel, outs, ins, flops, scratch=(), smem=0, hbm=0, hbm_outs=0, grant=16):
    vmem = pl.BlockSpec(memory_space=pltpu.VMEM)
    far = pl.BlockSpec(memory_space=pltpu.HBM)
    scalar = pl.BlockSpec(memory_space=pltpu.SMEM)
    moved = sum(math.prod(a.shape) * a.dtype.itemsize for a in list(ins) + list(outs))
    return pl.pallas_call(
        kernel,
        out_shape=tuple(outs),
        in_specs=[scalar] * smem + [far] * hbm + [vmem] * (len(ins) - smem - hbm),
        out_specs=tuple([far] * hbm_outs + [vmem] * (len(outs) - hbm_outs)),
        scratch_shapes=list(scratch),
        compiler_params=pltpu.CompilerParams(vmem_limit_bytes=grant * 1024 * 1024),
        cost_estimate=pl.CostEstimate(flops=flops, bytes_accessed=moved, transcendentals=0),
    )(*ins)


def slab_step(
    point_feats,
    pair_point,
    pair_cell,
    kernel,
    counts,
    area,
    normals,
    targets,
    spec_weight,
    skip_weight,
    skip_bias,
    head_weight,
    head_bias,
    out_weight,
):
    n = lax.axis_size("gx")
    points = point_feats.shape[0]
    slots = n * LANES
    slab = GX // n
    low = MODES // n
    depth = ZL * n
    levels = depth * WIDTH // LANES
    rows = MODES * slab
    main = levels * slab * low
    own_rows = low * low * levels
    shape = jax.ShapeDtypeStruct

    by = host_rows(GY, MODES)
    bx = host_rows(GX, MODES)
    by_rows = jnp.asarray(np.repeat(by, slab, axis=0))
    table = np.zeros((MODES, low, n, low, slab), ml_dtypes.bfloat16)
    for index in range(low):
        table[:, index, :, index, :] = bx.reshape(MODES, n, slab)
    table = table.reshape(MODES * low, rows)
    back = jnp.asarray(np.ascontiguousarray(table.T))
    table = jnp.asarray(table)
    peers = 8
    halves = n // peers
    high = MODES // peers
    part_table = np.zeros((halves, MODES, high, peers, high, slab), ml_dtypes.bfloat16)
    for index in range(high):
        part_table[:, :, index, :, index, :] = np.moveaxis(
            bx.reshape(MODES, halves, peers, slab), 1, 0
        )
    part_table = jnp.asarray(part_table.reshape(halves, MODES * high, rows))
    near = [[half * peers + peer for peer in range(peers)] for half in range(halves)]
    half = lax.shift_right_logical(lax.axis_index("gx"), peers.bit_length() - 1)
    half = half.astype(jnp.int32).reshape(1)

    def exchange(message):
        return lax.all_to_all(message, "gx", split_axis=0, concat_axis=0, tiled=True)

    def exchange_alone(message, *others):
        return lax.optimization_barrier((exchange(message),) + others)

    group = lax.axis_index("groups").astype(jnp.int32).reshape(1)
    point_rows = pair_point[0]
    cells = pair_cell[:, 0, :]
    area_row = area.reshape(1, points)
    msg, pw = run(
        source_kernel,
        [shape((n, 2 * WIDTH, LANES), BF16), shape((n, LANES), F32)],
        [group, half, counts, point_rows, kernel[0], area_row, point_feats.T, spec_weight],
        2 * 80 * points * slots,
        scratch=[
            pltpu.VMEM((1, n), jnp.int32),
            pltpu.VMEM((n, LANES), jnp.int32),
            pltpu.VMEM((n, LANES), F32),
            pltpu.VMEM((1, points), F32),
            pltpu.VMEM((WIDTH, points), BF16),
            pltpu.VMEM((MODES, WIDTH, WIDTH), BF16),
            pltpu.SemaphoreType.DMA((6,)),
        ],
        smem=2,
        hbm=6,
        grant=60,
    )
    rx = exchange(msg)
    shared = 256
    zr, rank, home, lp = run(
        functools.partial(place_kernel, depth),
        [
            shape((n, LANES), jnp.int32),
            shape((n, LANES), jnp.int32),
            shape((shared, LANES), F32),
            shape((rows, slots), BF16),
        ],
        [cells, by_rows],
        2 * rows * LANES * slots,
        scratch=[
            pltpu.VMEM((slots, LANES), F32),
            pltpu.VMEM((n, LANES), F32),
            pltpu.VMEM((shared, slots), BF16),
            pltpu.VMEM((16, slots), BF16),
        ],
    )
    sum_scratch = [
        pltpu.VMEM((WIDTH, slots), F32),
        pltpu.VMEM((shared, slots), BF16),
        pltpu.VMEM((shared, slots), BF16),
        pltpu.VMEM((slots, LANES), BF16),
        pltpu.VMEM((slots, LANES), F32),
    ]
    own = rx[:, WIDTH : 2 * WIDTH, :]
    other = lax.ppermute(own, "groups", [(0, 1), (1, 0)])
    pair_rows = pltpu.VMEM((WIDTH, slots), BF16)
    basis = pltpu.VMEM((rows, slots), BF16)
    deep_rows = pltpu.VMEM((depth * WIDTH, slots), BF16)
    big = 2 * WIDTH * slots * slots + 2 * rows * slots * depth * WIDTH
    msg, lat = run(
        cell_kernel,
        [shape((n, main, LANES), BF16), shape((WIDTH, slots), BF16)],
        [rx, cells, rank, zr, home, lp],
        big,
        scratch=sum_scratch + [pair_rows, deep_rows],
        grant=20,
    )
    columns = exchange(msg)
    (term,) = run(
        skip_kernel,
        [shape((WIDTH, slots), F32)],
        [cells, rank, zr, home, lat, skip_weight, skip_bias.reshape(1, WIDTH)],
        2 * shared * WIDTH * slots,
        scratch=[pltpu.VMEM((shared, slots), BF16)] * 2,
    )
    (weights,) = run(
        weight_kernel,
        [shape((MODES, WIDTH, LANES), BF16)],
        [group, own, other],
        MODES * WIDTH * LANES,
        smem=1,
    )
    msg, spec = run(
        mode_kernel,
        [shape((n, main, LANES), BF16), shape((n, own_rows, LANES), BF16)],
        [columns, weights, table, back, term],
        4 * MODES * low * rows * depth * WIDTH,
        scratch=[pltpu.VMEM((MODES * low * levels, LANES), F32)] * 2,
    )
    slabs, spec, lat, term, cells, zr, rank, home, pw = exchange_alone(
        msg, spec, lat, term, cells, zr, rank, home, pw
    )
    msg, pre = run(
        functools.partial(pre_kernel, depth),
        [shape((n, WIDTH + own_rows, LANES), BF16), shape((WIDTH, slots), F32)],
        [slabs, lp, term, cells, spec],
        2 * rows * slots * depth * WIDTH,
        scratch=[pltpu.VMEM((depth * WIDTH, rows), BF16)],
    )
    returned, pre, lat, cells, zr, rank, home, pw = exchange_alone(
        msg, pre, lat, cells, zr, rank, home, pw
    )
    out_row = out_weight.reshape(1, WIDTH)
    pressure, msg, own_spec = run(
        head_kernel,
        [
            shape((1, points), F32),
            shape((n, WIDTH + 8, LANES), BF16),
            shape((n, own_rows, LANES), BF16),
        ],
        [returned, point_rows, pw, head_weight, head_bias.reshape(1, WIDTH), out_row, area_row, normals],
        2 * 3 * WIDTH * points * slots,
        scratch=[
            pltpu.VMEM((3 * WIDTH, slots), BF16),
            pltpu.VMEM((points, slots), BF16),
            pltpu.VMEM((2, n, LANES), F32),
        ],
    )
    grads, pressure, own_spec, pre, lat, cells, zr, rank, home = exchange_alone(
        msg, pressure, own_spec, pre, lat, cells, zr, rank, home
    )
    scale = 1.0 / math.sqrt(points * n)
    msg, forces, out_grad = run(
        functools.partial(back_kernel, depth, scale),
        [
            shape((peers, halves * main + 8, LANES), BF16),
            shape((1, 2), F32),
            shape((1, WIDTH), F32),
        ],
        [grads, targets.reshape(1, 2), cells, rank, zr, home, lp, lat, pre],
        big,
        scratch=sum_scratch
        + [pltpu.VMEM((2 * WIDTH, slots), BF16), pair_rows, deep_rows]
        + [pltpu.VMEM((WIDTH, slots), F32)],
        grant=20,
    )
    grad_columns, forces, out_grad, own_spec = lax.optimization_barrier(
        (
            lax.all_to_all(
                msg, "gx", split_axis=0, concat_axis=0, tiled=True, axis_index_groups=near
            ),
            forces,
            out_grad,
            own_spec,
        )
    )
    part_rows = MODES * high * levels // n
    (msg,) = run(
        spec_kernel,
        [shape((n, part_rows + 8, LANES), BF16)],
        [half, grad_columns, part_table],
        2 * MODES * high * rows * depth * WIDTH,
        scratch=[pltpu.VMEM((MODES * high * levels, LANES), F32)],
        smem=1,
    )
    finals, own_spec, forces, out_grad = exchange_alone(msg, own_spec, forces, out_grad)
    spec_grad, skip_grad = run(
        functools.partial(final_kernel, peers),
        [shape((spec_weight.shape[0], WIDTH, WIDTH), F32), shape((WIDTH, WIDTH), F32)],
        [finals, own_spec],
        2 * NMODE * WIDTH * WIDTH * depth // n,
    )
    return (pressure.reshape(points), forces.reshape(2), spec_grad, skip_grad, out_grad.reshape(WIDTH))


def solution(mesh):
    fits = mesh.shape["gx"] == 16 and mesh.shape["groups"] == 2
    per_device = slab_step if fits else general_step
    in_specs = (
        P(("groups", "gx"), None),
        P(("groups", "gx"), None, None),
        P(None, ("groups", "gx"), None),
        P(("groups", "gx"), None, None),
        P(("groups", "gx"), None),
        P(("groups", "gx")),
        P(None, ("groups", "gx")),
        P("groups"),
        P("gx", None, None),
        P(),
        P(),
        P(),
        P(),
        P(),
    )
    out_specs = (
        P(("groups", "gx")),
        P("groups"),
        P(("groups", "gx"), None, None),
        P("groups", None),
        P("groups"),
    )
    return jax.shard_map(
        per_device, mesh=mesh, in_specs=in_specs, out_specs=out_specs, check_vma=False
    )
```

```python
import functools
import math

import jax
import jax.numpy as jnp
import ml_dtypes
import numpy as np
from jax import lax
from jax.experimental import pallas as pl
from jax.experimental.pallas import tpu as pltpu
from jax.sharding import PartitionSpec as P

GX = 128
GY = 128
MODES = 32
ZL = 1
NMODE = 1024


def fourier_rows(length, number):
    places = jnp.arange(length, dtype=jnp.float32)
    order = jnp.arange(number)
    half = number // 2
    freqs = jnp.where(order < half, order, order - half + 1).astype(jnp.float32)
    angles = 2.0 * math.pi / length * freqs[:, None] * places[None, :]
    table = jnp.where((order < half)[:, None], jnp.cos(angles), jnp.sin(angles))
    return (table * math.sqrt(2.0 / length)).astype(jnp.bfloat16)


def gelu_value(values):
    return 0.5 * values * (1.0 + lax.erf(values * (1.0 / math.sqrt(2.0))))


def gelu_slope(values):
    return 0.5 * (1.0 + lax.erf(values * (1.0 / math.sqrt(2.0)))) + values * jnp.exp(
        -0.5 * values * values
    ) * (1.0 / math.sqrt(2.0 * math.pi))


def general_step(
    point_feats,
    pair_point,
    pair_cell,
    kernel,
    counts,
    area,
    normals,
    targets,
    spec_weight,
    skip_weight,
    skip_bias,
    head_weight,
    head_bias,
    out_weight,
):
    devices = lax.axis_size("gx")
    local_points, width = point_feats.shape
    block_slots = pair_point.shape[2]
    row_count = GX // devices
    depth = ZL * devices
    slab_cells = row_count * GY * depth
    valid_mask = jnp.arange(block_slots)[None, :] < counts[0][:, None]
    point_rows = pair_point[0]
    pair_weight = jnp.where(valid_mask, kernel[0], jnp.float32(0.0))
    sender_weight = pair_weight * area[point_rows]
    contrib = (sender_weight[..., None] * point_feats[point_rows].astype(jnp.float32)).astype(
        jnp.bfloat16
    )
    arrived = lax.all_to_all(contrib, "gx", split_axis=0, concat_axis=0, tiled=True)
    cell_rows = pair_cell[:, 0, :].reshape(-1)
    latent = jax.ops.segment_sum(
        arrived.reshape(-1, width).astype(jnp.float32), cell_rows, num_segments=slab_cells
    ).astype(jnp.bfloat16)
    col_table = fourier_rows(GY, MODES)
    row_table = fourier_rows(GX, MODES)
    volume = latent.reshape(row_count, GY, depth * width)
    along_y = jnp.einsum(
        "by,xyk->xbk", col_table, volume, preferred_element_type=jnp.float32
    ).astype(jnp.bfloat16)
    columns = lax.all_to_all(along_y, "gx", split_axis=2, concat_axis=0, tiled=True)
    spectrum = jnp.einsum(
        "ax,xbk->abk", row_table, columns, preferred_element_type=jnp.float32
    ).astype(jnp.bfloat16)
    mode_rows = lax.all_to_all(
        spectrum.reshape(NMODE, ZL * width), "gx", split_axis=0, concat_axis=1, tiled=True
    )
    own_modes = mode_rows.shape[0]
    mixed_rows = jnp.einsum(
        "mzc,mcd->mzd",
        mode_rows.reshape(own_modes, depth, width),
        spec_weight,
        preferred_element_type=jnp.float32,
    ).astype(jnp.bfloat16)
    mixed = lax.all_to_all(
        mixed_rows.reshape(own_modes, depth * width), "gx", split_axis=1, concat_axis=0, tiled=True
    )
    back_x = jnp.einsum(
        "ax,abk->xbk",
        row_table,
        mixed.reshape(MODES, MODES, ZL * width),
        preferred_element_type=jnp.float32,
    ).astype(jnp.bfloat16)
    slabs = lax.all_to_all(back_x, "gx", split_axis=0, concat_axis=2, tiled=True)
    spatial = jnp.einsum(
        "by,xbk->xyk", col_table, slabs, preferred_element_type=jnp.float32
    ).reshape(slab_cells, width)
    pre = spatial + jnp.dot(latent, skip_weight, preferred_element_type=jnp.float32) + skip_bias
    features = gelu_value(pre).astype(jnp.bfloat16)
    picked = features[cell_rows].reshape(devices, block_slots, width)
    returned = lax.all_to_all(picked, "gx", split_axis=0, concat_axis=0, tiled=True)
    point_latent = jax.ops.segment_sum(
        (pair_weight[..., None] * returned.astype(jnp.float32)).reshape(-1, width),
        point_rows.reshape(-1),
        num_segments=local_points,
    )
    head_matrix = head_weight.astype(jnp.float32)
    head_pre = jnp.dot(point_latent, head_matrix, precision=lax.Precision.HIGHEST) + head_bias
    head = gelu_value(head_pre)
    pressure = jnp.dot(head, out_weight, precision=lax.Precision.HIGHEST)
    weighted = pressure * area
    scale = 1.0 / math.sqrt(local_points * devices)
    totals = lax.psum(
        jnp.stack([jnp.sum(weighted * normals[0]), jnp.sum(weighted * normals[1])]), "gx"
    )
    forces = scale * totals
    misfit = forces - targets
    point_grad = 2.0 * scale * (misfit[0] * normals[0] + misfit[1] * normals[1]) * area
    out_part = jnp.dot(point_grad, head, precision=lax.Precision.HIGHEST)
    head_grad = point_grad[:, None] * out_weight[None, :] * gelu_slope(head_pre)
    latent_grad = jnp.dot(head_grad, head_matrix.T, precision=lax.Precision.HIGHEST).astype(
        jnp.bfloat16
    )
    grad_pairs = (pair_weight[..., None] * latent_grad[point_rows].astype(jnp.float32)).astype(
        jnp.bfloat16
    )
    grad_arrived = lax.all_to_all(grad_pairs, "gx", split_axis=0, concat_axis=0, tiled=True)
    cell_grad = jax.ops.segment_sum(
        grad_arrived.reshape(-1, width).astype(jnp.float32), cell_rows, num_segments=slab_cells
    )
    pre_grad = (cell_grad * gelu_slope(pre)).astype(jnp.bfloat16)
    skip_part = jnp.dot(latent.T, pre_grad, preferred_element_type=jnp.float32)
    grad_y = jnp.einsum(
        "by,xyk->xbk",
        col_table,
        pre_grad.reshape(row_count, GY, depth * width),
        preferred_element_type=jnp.float32,
    ).astype(jnp.bfloat16)
    grad_columns = lax.all_to_all(grad_y, "gx", split_axis=2, concat_axis=0, tiled=True)
    grad_spec = jnp.einsum(
        "ax,xbk->abk", row_table, grad_columns, preferred_element_type=jnp.float32
    ).astype(jnp.bfloat16)
    grad_rows = lax.all_to_all(
        grad_spec.reshape(NMODE, ZL * width), "gx", split_axis=0, concat_axis=1, tiled=True
    )
    own_modes = grad_rows.shape[0]
    spec_grad = jnp.einsum(
        "mzc,mzd->mcd",
        mode_rows.reshape(own_modes, depth, width),
        grad_rows.reshape(own_modes, depth, width),
        preferred_element_type=jnp.float32,
    )
    out_grad, skip_grad = lax.psum((out_part, skip_part), "gx")
    return (pressure, forces, spec_grad, skip_grad, out_grad)


F32 = jnp.float32
BF16 = jnp.bfloat16
LANES = 128
WIDTH = 64


def host_rows(length, number):
    places = np.arange(length, dtype=np.float32)
    order = np.arange(number)
    half = number // 2
    freqs = np.where(order < half, order, order - half + 1).astype(np.float32)
    angles = np.float32(2.0 * math.pi / length) * freqs[:, None] * places[None, :]
    table = np.where((order < half)[:, None], np.cos(angles), np.sin(angles))
    table = table.astype(np.float32) * np.float32(math.sqrt(2.0 / length))
    return table.astype(ml_dtypes.bfloat16)


def three_parts(values):
    first = values.astype(BF16)
    rest = values - first.astype(F32)
    second = rest.astype(BF16)
    third = (rest - second.astype(F32)).astype(BF16)
    return first, second, third


def mm(left, right):
    return jnp.dot(left, right, preferred_element_type=F32)


def mm_nt(left, right):
    return lax.dot_general(left, right, (((1,), (1,)), ((), ())), preferred_element_type=F32)


def mm_tn(left, right):
    return lax.dot_general(left, right, (((0,), (0,)), ((), ())), preferred_element_type=F32)


def short_rows(count):
    return lax.broadcasted_iota(jnp.int32, (count, LANES), 0).astype(jnp.int16)


def matches(rows, row):
    short = jnp.broadcast_to(row, (16, LANES)).astype(jnp.int16)
    tall = jnp.broadcast_to(short[None], (rows.shape[0] // 16, 16, LANES)).reshape(rows.shape)
    return jnp.where(rows == tall, jnp.ones((), BF16), jnp.zeros((), BF16))


def two_rows(ref, pair):
    return jnp.concatenate([ref[2 * pair : 2 * pair + 1, :], ref[2 * pair + 1 : 2 * pair + 2, :]], axis=1)


def source_kernel(group_ref, half_ref, count_hbm, point_hbm, kern_hbm, area_hbm, feat_hbm, weight_hbm, msg_ref, pw_ref, count_ref, point_ref, kern_ref, area_ref, feat_ref, weight_ref, sems):
    devices, points = point_ref.shape[0], feat_ref.shape[1]
    low = MODES // devices
    pieces = (
        (point_hbm, point_ref),
        (area_hbm, area_ref),
        (feat_hbm, feat_ref),
        (kern_hbm, kern_ref),
        (count_hbm, count_ref),
        (weight_hbm.at[pl.ds(group_ref[0] * MODES, MODES)], weight_ref),
    )
    copies = [
        pltpu.make_async_copy(source, place, sems.at[index])
        for index, (source, place) in enumerate(pieces)
    ]
    for copy in copies:
        copy.start()
    for copy in copies[:-1]:
        copy.wait()
    first, second, third = three_parts(area_ref[...])
    place = lax.broadcasted_iota(jnp.int32, (16, points), 0)
    extra = jnp.where(
        place == 0,
        first.astype(F32),
        jnp.where(place == 1, second.astype(F32), jnp.where(place == 2, third.astype(F32), 0.0)),
    ).astype(BF16)
    table = jnp.concatenate([feat_ref[...], extra], axis=0)
    rows = short_rows(points)
    lane = lax.broadcasted_iota(jnp.int32, (1, LANES), 1)
    for pair in range(devices // 2):
        hot = jnp.concatenate(
            [matches(rows, point_ref[at : at + 1, :]) for at in (2 * pair, 2 * pair + 1)], axis=1
        )
        got = mm(table, hot)
        spread = got[WIDTH : WIDTH + 1] + got[WIDTH + 1 : WIDTH + 2] + got[WIDTH + 2 : WIDTH + 3]
        for half in range(2):
            dest = 2 * pair + half
            cut = slice(half * LANES, (half + 1) * LANES)
            valid = lane < count_ref[0:1, dest : dest + 1]
            weight = jnp.where(valid, kern_ref[dest : dest + 1, :], 0.0)
            pw_ref[dest : dest + 1, :] = weight
            msg_ref[dest, 0:WIDTH, :] = ((weight * spread[:, cut]) * got[0:WIDTH, cut]).astype(BF16)
    copies[-1].wait()
    for dest in range(devices):
        msg_ref[dest, WIDTH : 2 * WIDTH, :] = jnp.concatenate(
            [weight_ref[low * dest], weight_ref[low * dest + 1]], axis=1
        )


def columns_of(row):
    return jnp.broadcast_to(row, (LANES, LANES)).T


def column_of(row):
    down = lax.broadcasted_iota(jnp.int32, (WIDTH, WIDTH), 0)
    along = lax.broadcasted_iota(jnp.int32, (WIDTH, WIDTH), 1)
    return jnp.sum(jnp.where(down == along, row, 0.0), axis=1, keepdims=True)


def pick_rows(rank_ref, pick_ref):
    rows = short_rows(pick_ref.shape[0])
    for block in range(rank_ref.shape[0]):
        pick_ref[:, block * LANES : (block + 1) * LANES] = matches(
            rows, rank_ref[block : block + 1, :]
        )


def basis_rows(depth, cell_ref, by_ref, lp_ref):
    zbits = depth.bit_length() - 1
    rows = by_ref.shape[0]
    slab = rows // MODES
    wide = 2 * LANES
    yrow = lax.broadcasted_iota(jnp.int32, (GY, wide), 0)
    xrow = jnp.bitwise_and(lax.broadcasted_iota(jnp.int32, (16, wide), 0), slab - 1)
    for pair in range(cell_ref.shape[0] // 2):
        cells = two_rows(cell_ref, pair)
        ypos = jnp.bitwise_and(jnp.right_shift(cells, zbits), GY - 1)
        xpos = jnp.right_shift(cells, zbits + GY.bit_length() - 1)
        hot = jnp.where(yrow == ypos, 1.0, 0.0).astype(BF16)
        mask = jnp.where(xrow == xpos, 1.0, 0.0).astype(BF16)
        found = mm(by_ref[...], hot).astype(BF16)
        for at in range(0, rows, 16):
            lp_ref[at : at + 16, pair * wide : (pair + 1) * wide] = found[at : at + 16] * mask


def place_kernel(depth, cell_ref, by_ref, zr_ref, rank_ref, home_ref, lp_ref, col_ref, flag_ref, pick_ref, part_ref):
    devices = cell_ref.shape[0]
    basis_rows(depth, cell_ref, by_ref, lp_ref)
    down = lax.broadcasted_iota(jnp.int32, (LANES, LANES), 0)
    along = lax.broadcasted_iota(jnp.int32, (LANES, LANES), 1)
    place = lax.broadcasted_iota(jnp.int32, (16, LANES), 0)
    for block in range(devices):
        cells = cell_ref[block : block + 1, :]
        row = cells.astype(F32)
        cut = slice(block * LANES, (block + 1) * LANES)
        col_ref[cut, :] = columns_of(row)
        high = jnp.right_shift(cells, 7).astype(F32)
        low = jnp.bitwise_and(cells, 127).astype(F32)
        part_ref[:, cut] = jnp.where(place == 0, high, jnp.where(place == 1, low, 0.0)).astype(BF16)
        same = jnp.logical_and(col_ref[cut, :] == row, down < along)
        before = jnp.max(jnp.where(same, 1.0, 0.0), axis=0, keepdims=True)
        if block:
            early = jnp.where(col_ref[0 : block * LANES, :] == row, 1.0, 0.0)
            before = jnp.maximum(before, jnp.max(early, axis=0, keepdims=True))
        zr_ref[block : block + 1, :] = jnp.where(
            before > 0.0, -1, jnp.bitwise_and(cells, depth - 1)
        )
        flag_ref[block : block + 1, :] = before
    flags = flag_ref[...]
    marks = flags.astype(BF16)
    inside = mm(marks, jnp.where(down <= along, 1.0, 0.0).astype(BF16))
    above = jnp.where(down < along, 1.0, 0.0)[:, 0:devices][0:devices]
    ahead = jnp.sum(mm_tn(above.astype(BF16), marks), axis=1, keepdims=True)
    rank_ref[...] = jnp.where(flags > 0.0, (inside + ahead - flags).astype(jnp.int32), -1)
    pick_rows(rank_ref, pick_ref)
    found = mm_nt(part_ref[...], pick_ref[...])
    found = found[0:1] * 128.0 + found[1:2]
    for block in range(home_ref.shape[0] // LANES):
        cut = slice(block * LANES, (block + 1) * LANES)
        home_ref[cut, :] = columns_of(found[:, cut])


def first_rows(cell_ref, zr_ref, home_ref, first_ref):
    homes = home_ref[...].astype(jnp.int32).astype(jnp.int16)
    for block in range(cell_ref.shape[0]):
        here = slice(block, block + 1)
        row = jnp.where(zr_ref[here, :] < 0, -1, cell_ref[here, :])
        first_ref[:, block * LANES : (block + 1) * LANES] = matches(homes, row)


def fold_parts(values):
    total = values[0:WIDTH]
    for at in range(WIDTH, values.shape[0], WIDTH):
        total = total + values[at : at + WIDTH]
    return total


def sum_cells(terms, xs_ref, cell_ref, rank_ref, zr_ref, home_ref, sums_ref, pick_ref, first_ref, full_ref, col_ref):
    devices = cell_ref.shape[0]
    few = jnp.max(rank_ref[...]) < home_ref.shape[0]

    @pl.when(few)
    def _():
        pick_rows(rank_ref, pick_ref)
        first_rows(cell_ref, zr_ref, home_ref, first_ref)
        moved = mm_nt(xs_ref[...], pick_ref[...]).astype(BF16)
        for pair in range(devices // 2):
            span = slice(pair * 2 * LANES, (pair + 1) * 2 * LANES)
            sums_ref[:, span] = terms(span) + fold_parts(mm(moved, first_ref[:, span]))

    @pl.when(jnp.logical_not(few))
    def _():
        for block in range(devices):
            col_ref[block * LANES : (block + 1) * LANES, :] = columns_of(
                cell_ref[block : block + 1, :].astype(F32)
            )
        for block in range(devices):
            row = cell_ref[block : block + 1, :].astype(F32)
            full_ref[...] = jnp.where(col_ref[...] == row, 1.0, 0.0).astype(BF16)
            sums_ref[:, block * LANES : (block + 1) * LANES] = fold_parts(
                mm(xs_ref[...], full_ref[...])
            )


def slab_rows(value_ref, zpos_of, lp_ref, rp_ref, msg_ref):
    devices = msg_ref.shape[0]
    step = lp_ref.shape[0] // devices
    for quad in range(rp_ref.shape[0] // (4 * WIDTH)):
        for pair in range(value_ref.shape[1] // (2 * LANES)):
            cut = slice(pair * 2 * LANES, (pair + 1) * 2 * LANES)
            zpos = zpos_of(pair)
            values = value_ref[:, cut].astype(F32)
            for level in range(4 * quad, 4 * quad + 4):
                rp_ref[level * WIDTH : (level + 1) * WIDTH, cut] = jnp.where(
                    zpos == level, values, 0.0
                ).astype(BF16)
        out = mm_nt(lp_ref[...], rp_ref[quad * 4 * WIDTH : (quad + 1) * 4 * WIDTH, :]).astype(BF16)
        for half in range(2):
            level = 2 * quad + half
            for dest in range(devices):
                msg_ref[dest, level * step : (level + 1) * step, :] = out[
                    dest * step : (dest + 1) * step, half * LANES : (half + 1) * LANES
                ]


def cell_kernel(rx_ref, cell_ref, rank_ref, zr_ref, home_ref, lp_ref, msg_ref, lat_ref, sums_ref, pick_ref, first_ref, full_ref, col_ref, xs_ref, rp_ref):
    devices = rx_ref.shape[0]
    for block in range(devices):
        xs_ref[:, block * LANES : (block + 1) * LANES] = rx_ref[block, 0:WIDTH, :]
    sum_cells(
        lambda span: xs_ref[:, span].astype(F32),
        xs_ref, cell_ref, rank_ref, zr_ref, home_ref, sums_ref, pick_ref, first_ref, full_ref, col_ref,
    )
    for pair in range(devices // 2):
        cut = slice(pair * 2 * LANES, (pair + 1) * 2 * LANES)
        latent = sums_ref[:, cut]
        lat_ref[:, cut] = latent.astype(BF16)
    slab_rows(lat_ref, lambda pair: two_rows(zr_ref, pair), lp_ref, rp_ref, msg_ref)


def to_modes(rx_ref, table, sp_ref):
    levels = sp_ref.shape[0] // table.shape[0]
    step = table.shape[1] // rx_ref.shape[0]
    for level in range(levels):
        block = rx_ref[:, level * step : (level + 1) * step, :].reshape(table.shape[1], LANES)
        coeffs = mm(table, block).astype(BF16).astype(F32)
        sp_ref[pl.ds(level, table.shape[0], stride=levels), :] = coeffs


def swap_halves(values):
    return pltpu.roll(values, WIDTH, 1)


def weight_kernel(group_ref, own_ref, other_ref, weight_ref):
    for order in range(MODES):
        source, which = order // 2, order % 2
        mine = jnp.full((WIDTH, LANES), group_ref[0], jnp.int32) == which
        weight_ref[order] = jnp.where(
            mine, own_ref[source].astype(F32), other_ref[source].astype(F32)
        ).astype(BF16)


def mode_kernel(rx_ref, weight_ref, table_ref, back_ref, term_ref, msg_ref, spec_ref, sp_ref, mx_ref):
    devices = rx_ref.shape[0]
    own_rows = spec_ref.shape[1]
    modes = table_ref.shape[0]
    levels = sp_ref.shape[0] // modes
    step = back_ref.shape[0] // devices
    to_modes(rx_ref, table_ref[...], sp_ref)
    for dest in range(devices):
        spec_ref[dest] = sp_ref[dest * own_rows : (dest + 1) * own_rows, :].astype(BF16)
    left = lax.broadcasted_iota(jnp.int32, (levels, LANES), 1) < WIDTH
    for order in range(MODES):
        at = order * 2 * levels
        even = sp_ref[at : at + levels, :]
        odd = sp_ref[at + levels : at + 2 * levels, :]
        rows = jnp.concatenate([even, swap_halves(even), odd, swap_halves(odd)], axis=0)
        out = mm(rows[:, 0:WIDTH].astype(BF16), weight_ref[order])
        mx_ref[at : at + levels, :] = jnp.where(
            left, out[0:levels], swap_halves(out[levels : 2 * levels])
        )
        mx_ref[at + levels : at + 2 * levels, :] = jnp.where(
            left, swap_halves(out[2 * levels : 3 * levels]), out[3 * levels : 4 * levels]
        )
    for level in range(levels):
        mixed = mx_ref[pl.ds(level, modes, stride=levels), :].astype(BF16)
        out = mm(back_ref[...], mixed).astype(BF16)
        for dest in range(devices):
            msg_ref[dest, level * step : (level + 1) * step, :] = out[dest * step : (dest + 1) * step]


def skip_kernel(cell_ref, rank_ref, zr_ref, home_ref, lat_ref, skip_ref, bias_ref, term_ref, full_ref, pick_ref, first_ref):
    few = jnp.max(rank_ref[...]) < home_ref.shape[0]
    bias = column_of(bias_ref[...])
    pick_rows(rank_ref, pick_ref)
    first_rows(cell_ref, zr_ref, home_ref, first_ref)
    shared = mm_nt(lat_ref[...], first_ref[...]).astype(BF16)
    for pair in range(cell_ref.shape[0] // 2):
        span = slice(pair * 2 * LANES, (pair + 1) * 2 * LANES)
        later = jnp.logical_and(two_rows(rank_ref, pair) >= 0, few)
        latent = jnp.where(later, mm(shared, pick_ref[:, span]), lat_ref[:, span].astype(F32))
        full_ref[:, span] = latent.astype(BF16)
        term_ref[:, span] = mm_tn(skip_ref[...], latent.astype(BF16)) + bias


def pre_kernel(depth, rx_ref, lp_ref, term_ref, cell_ref, spec_ref, msg_ref, pre_ref, rt_ref):
    devices = rx_ref.shape[0]
    rows = lp_ref.shape[0]
    step = rows // devices
    for level in range(rt_ref.shape[0] // LANES):
        block = rx_ref[:, level * step : (level + 1) * step, :].reshape(rows, LANES)
        rt_ref[level * LANES : (level + 1) * LANES, :] = block.T
    for pair in range(devices // 2):
        cut = slice(pair * 2 * LANES, (pair + 1) * 2 * LANES)
        zpos = jnp.bitwise_and(two_rows(cell_ref, pair), depth - 1)
        field = mm(rt_ref[...], lp_ref[:, cut])
        total = jnp.where(zpos == 0, field[0:WIDTH], 0.0)
        for level in range(1, depth):
            total += jnp.where(zpos == level, field[level * WIDTH : (level + 1) * WIDTH], 0.0)
        pre = total + term_ref[:, cut]
        pre_ref[:, cut] = pre
        feats = gelu_value(pre).astype(BF16)
        for half in range(2):
            dest = 2 * pair + half
            msg_ref[dest, 0:WIDTH, :] = feats[:, half * LANES : (half + 1) * LANES]
            msg_ref[dest, WIDTH:, :] = spec_ref[dest]


def head_kernel(rx_ref, point_ref, pw_ref, head_ref, bias_ref, out_ref, area_ref, normal_ref, pres_ref, msg_ref, spec_ref, value_ref, hot_ref, na_ref):
    devices = rx_ref.shape[0]
    points = area_ref.shape[1]
    rows = short_rows(points)
    for block in range(devices):
        cut = slice(block * LANES, (block + 1) * LANES)
        parts = three_parts(pw_ref[block : block + 1, :] * rx_ref[block, 0:WIDTH, :].astype(F32))[0:2]
        for index, part in enumerate(parts):
            value_ref[index * WIDTH : (index + 1) * WIDTH, cut] = part
        hot_ref[:, cut] = matches(rows, point_ref[block : block + 1, :])
    sums = mm_nt(value_ref[...], hot_ref[...])
    latent = sums[0:WIDTH] + sums[WIDTH : 2 * WIDTH]
    first, second, third = three_parts(latent)
    weight = head_ref[...]
    head_pre = mm_tn(weight, first) + mm_tn(weight, second) + mm_tn(weight, third) + column_of(bias_ref[...])
    out_column = column_of(out_ref[...])
    head = gelu_value(head_pre)
    pressure = jnp.sum(head * out_column, axis=0, keepdims=True)
    pres_ref[...] = pressure
    along = [normal_ref[which : which + 1, :] * area_ref[...] for which in range(2)]
    first, second, third = three_parts(out_column * gelu_slope(head_pre))
    grad = mm(weight, first) + mm(weight, second) + mm(weight, third)
    place = lax.broadcasted_iota(jnp.int32, (16, points), 0)
    extra = jnp.zeros((16, points), F32)
    for which in range(2):
        for index, part in enumerate(three_parts(along[which])):
            extra = jnp.where(place == 3 * which + index, part.astype(F32), extra)
    table = jnp.concatenate([grad.astype(BF16), extra.astype(BF16)], axis=0)
    lane = lax.broadcasted_iota(jnp.int32, (1, LANES), 1)
    partial = []
    for which in range(2):
        force = jnp.sum(pressure * area_ref[...] * normal_ref[which : which + 1, :], axis=1, keepdims=True)
        partial.append(force)
    force_row = jnp.zeros((1, LANES), F32)
    for which in range(2):
        for index, part in enumerate(three_parts(partial[which])):
            force_row = jnp.where(lane == 3 * which + index, part.astype(F32), force_row)
    out_rows = lax.dot_general(
        jnp.concatenate([along[0], along[1], jnp.zeros((6, points), F32)], axis=0),
        head,
        (((1,), (1,)), ((), ())),
        precision=lax.Precision.HIGHEST,
        preferred_element_type=F32,
    )
    out_row = jnp.concatenate([out_rows[0:1], out_rows[1:2]], axis=1)
    place = lax.broadcasted_iota(jnp.int32, (8, LANES), 0)
    out_parts = three_parts(out_row)
    common = jnp.where(
        place == 4,
        out_parts[0].astype(F32),
        jnp.where(place == 5, out_parts[1].astype(F32), jnp.where(place == 6, force_row, 0.0)),
    )
    for pair in range(devices // 2):
        got = mm(table, hot_ref[:, pair * 2 * LANES : (pair + 1) * 2 * LANES])
        for half in range(2):
            block = 2 * pair + half
            cut = slice(half * LANES, (half + 1) * LANES)
            msg_ref[block, 0:WIDTH, :] = got[0:WIDTH, cut].astype(BF16)
            spec_ref[block] = rx_ref[block, WIDTH:, :]
            for which in range(2):
                at = WIDTH + 3 * which
                na_ref[which, block : block + 1, :] = (
                    got[at : at + 1, cut] + got[at + 1 : at + 2, cut] + got[at + 2 : at + 3, cut]
                )
    scaled = [three_parts(pw_ref[...] * na_ref[which]) for which in range(2)]
    rows = [scaled[which][index].astype(F32) for which in range(2) for index in range(2)]
    for block in range(devices):
        tail = common
        for index, row in enumerate(rows):
            tail = jnp.where(place == index, row[block : block + 1, :], tail)
        msg_ref[block, WIDTH : WIDTH + 8, :] = tail.astype(BF16)


def back_kernel(depth, scale, rx_ref, target_ref, cell_ref, lp_ref, lat_ref, pre_ref, msg_ref, force_ref, outg_ref, pg_ref, rp_ref):
    devices = rx_ref.shape[0]
    main = msg_ref.shape[1] - 8
    extra = slice(WIDTH, WIDTH + 8)
    total = rx_ref[0, extra, :].astype(F32)
    for block in range(1, devices):
        total += rx_ref[block, extra, :].astype(F32)
    force = total[6:7]
    lane = lax.broadcasted_iota(jnp.int32, (1, 2), 1)
    forces = scale * jnp.where(
        lane == 0,
        force[:, 0:1] + force[:, 1:2] + force[:, 2:3],
        force[:, 3:4] + force[:, 4:5] + force[:, 5:6],
    )
    force_ref[...] = forces
    misfit = (2.0 * scale) * (forces - target_ref[...])
    drag, lift = misfit[:, 0:1], misfit[:, 1:2]
    out_row = total[4:5] + total[5:6]
    outg_ref[...] = drag * out_row[:, 0:WIDTH] + lift * out_row[:, WIDTH : 2 * WIDTH]
    for block in range(devices):
        tail = rx_ref[block, extra, :].astype(F32)
        factor = drag * (tail[0:1] + tail[1:2]) + lift * (tail[2:3] + tail[3:4])
        cut = slice(block * LANES, (block + 1) * LANES)
        slope = gelu_slope(pre_ref[:, cut])
        grad = factor * rx_ref[block, 0:WIDTH, :].astype(F32) * slope
        pg_ref[:, cut] = grad.astype(BF16)
    slab_rows(
        pg_ref,
        lambda pair: jnp.bitwise_and(two_rows(cell_ref, pair), depth - 1),
        lp_ref, rp_ref, msg_ref,
    )
    skip = mm_nt(lat_ref[...], pg_ref[...])
    for dest in range(msg_ref.shape[0]):
        msg_ref[dest, main : main + 8, :] = two_parts(skip[8 * dest : 8 * dest + 8]).astype(BF16)


def two_parts(values):
    first, second, _ = three_parts(values)
    return jnp.concatenate([first.astype(F32), second.astype(F32)], axis=1)


def spec_kernel(half_ref, rx_ref, table_ref, msg_ref, sp_ref):
    peers, devices = rx_ref.shape[0], msg_ref.shape[0]
    part_rows = sp_ref.shape[0] // devices
    main = rx_ref.shape[1] - 8
    to_modes(rx_ref, table_ref[half_ref[0]], sp_ref)
    total = rx_ref[0, main : main + 8, :].astype(F32)
    for source in range(1, peers):
        total += rx_ref[source, main : main + 8, :].astype(F32)
    total = two_parts((total + swap_halves(total))[:, 0:WIDTH]).astype(BF16)
    for dest in range(devices):
        msg_ref[dest, 0:part_rows, :] = sp_ref[dest * part_rows : (dest + 1) * part_rows, :].astype(BF16)
        msg_ref[dest, part_rows : part_rows + 8, :] = total


def final_kernel(peers, rx_ref, own_ref, spec_ref, skip_ref):
    devices = rx_ref.shape[0]
    low = MODES // devices
    high = MODES // peers
    owned = spec_ref.shape[0] // MODES
    left = lax.broadcasted_iota(jnp.int32, (8, LANES), 1) < WIDTH
    for which in range(owned):
        for source in range(devices):
            at = which * 8 * low
            coeffs = own_ref[source, at : at + 8 * low, :].astype(F32)
            first, second = coeffs[0:8], coeffs[8:16]
            block = [
                jnp.where(left, first, 0.0),
                jnp.where(left, swap_halves(first), 0.0),
                jnp.where(left, 0.0, swap_halves(second)),
                jnp.where(left, 0.0, second),
            ]
            peer, inner = divmod(low * source, high)
            at = (which * high + inner) * 8
            grads = []
            for shift in range(0, devices, peers):
                part = rx_ref[peer + shift, at : at + 8 * low, :].astype(F32)
                grads += [part[0:8], swap_halves(part[0:8]), part[8:16], swap_halves(part[8:16])]
            block = jnp.concatenate(block * (devices // peers), axis=0).astype(BF16)
            grads = jnp.concatenate(grads, axis=0)[:, 0:WIDTH].astype(BF16)
            found = mm_tn(block, grads)
            mode = which * MODES + low * source
            spec_ref[mode] = found[0:WIDTH]
            spec_ref[mode + 1] = found[WIDTH : 2 * WIDTH]
    main = rx_ref.shape[1] - 8
    for peer in range(peers):
        rows = rx_ref[peer, main : main + 8, :].astype(F32)
        for shift in range(peers, devices, peers):
            rows += rx_ref[peer + shift, main : main + 8, :].astype(F32)
        skip_ref[8 * peer : 8 * peer + 8, :] = (rows + swap_halves(rows))[:, 0:WIDTH]


def run(kernel, outs, ins, flops, scratch=(), smem=0, hbm=0, hbm_outs=0, grant=16):
    vmem = pl.BlockSpec(memory_space=pltpu.VMEM)
    far = pl.BlockSpec(memory_space=pltpu.HBM)
    scalar = pl.BlockSpec(memory_space=pltpu.SMEM)
    moved = sum(math.prod(a.shape) * a.dtype.itemsize for a in list(ins) + list(outs))
    return pl.pallas_call(
        kernel,
        out_shape=tuple(outs),
        in_specs=[scalar] * smem + [far] * hbm + [vmem] * (len(ins) - smem - hbm),
        out_specs=tuple([far] * hbm_outs + [vmem] * (len(outs) - hbm_outs)),
        scratch_shapes=list(scratch),
        compiler_params=pltpu.CompilerParams(vmem_limit_bytes=grant * 1024 * 1024),
        cost_estimate=pl.CostEstimate(flops=flops, bytes_accessed=moved, transcendentals=0),
    )(*ins)


def slab_step(
    point_feats,
    pair_point,
    pair_cell,
    kernel,
    counts,
    area,
    normals,
    targets,
    spec_weight,
    skip_weight,
    skip_bias,
    head_weight,
    head_bias,
    out_weight,
):
    n = lax.axis_size("gx")
    points = point_feats.shape[0]
    slots = n * LANES
    slab = GX // n
    low = MODES // n
    depth = ZL * n
    levels = depth * WIDTH // LANES
    rows = MODES * slab
    main = levels * slab * low
    own_rows = low * low * levels
    shape = jax.ShapeDtypeStruct

    by = host_rows(GY, MODES)
    bx = host_rows(GX, MODES)
    by_rows = jnp.asarray(np.repeat(by, slab, axis=0))
    table = np.zeros((MODES, low, n, low, slab), ml_dtypes.bfloat16)
    for index in range(low):
        table[:, index, :, index, :] = bx.reshape(MODES, n, slab)
    table = table.reshape(MODES * low, rows)
    back = jnp.asarray(np.ascontiguousarray(table.T))
    table = jnp.asarray(table)
    peers = 8
    halves = n // peers
    high = MODES // peers
    part_table = np.zeros((halves, MODES, high, peers, high, slab), ml_dtypes.bfloat16)
    for index in range(high):
        part_table[:, :, index, :, index, :] = np.moveaxis(
            bx.reshape(MODES, halves, peers, slab), 1, 0
        )
    part_table = jnp.asarray(part_table.reshape(halves, MODES * high, rows))
    near = [[half * peers + peer for peer in range(peers)] for half in range(halves)]
    half = lax.shift_right_logical(lax.axis_index("gx"), peers.bit_length() - 1)
    half = half.astype(jnp.int32).reshape(1)

    def exchange(message):
        return lax.all_to_all(message, "gx", split_axis=0, concat_axis=0, tiled=True)

    def exchange_alone(message, *others):
        return lax.optimization_barrier((exchange(message),) + others)

    group = lax.axis_index("groups").astype(jnp.int32).reshape(1)
    point_rows = pair_point[0]
    cells = pair_cell[:, 0, :]
    area_row = area.reshape(1, points)
    msg, pw = run(
        source_kernel,
        [shape((n, 2 * WIDTH, LANES), BF16), shape((n, LANES), F32)],
        [group, half, counts, point_rows, kernel[0], area_row, point_feats.T, spec_weight],
        2 * 80 * points * slots,
        scratch=[
            pltpu.VMEM((1, n), jnp.int32),
            pltpu.VMEM((n, LANES), jnp.int32),
            pltpu.VMEM((n, LANES), F32),
            pltpu.VMEM((1, points), F32),
            pltpu.VMEM((WIDTH, points), BF16),
            pltpu.VMEM((MODES, WIDTH, WIDTH), BF16),
            pltpu.SemaphoreType.DMA((6,)),
        ],
        smem=2,
        hbm=6,
        grant=60,
    )
    rx = exchange(msg)
    shared = 256
    zr, rank, home, lp = run(
        functools.partial(place_kernel, depth),
        [
            shape((n, LANES), jnp.int32),
            shape((n, LANES), jnp.int32),
            shape((shared, LANES), F32),
            shape((rows, slots), BF16),
        ],
        [cells, by_rows],
        2 * rows * LANES * slots,
        scratch=[
            pltpu.VMEM((slots, LANES), F32),
            pltpu.VMEM((n, LANES), F32),
            pltpu.VMEM((shared, slots), BF16),
            pltpu.VMEM((16, slots), BF16),
        ],
    )
    sum_scratch = [
        pltpu.VMEM((WIDTH, slots), F32),
        pltpu.VMEM((shared, slots), BF16),
        pltpu.VMEM((shared, slots), BF16),
        pltpu.VMEM((slots, LANES), BF16),
        pltpu.VMEM((slots, LANES), F32),
    ]
    own = rx[:, WIDTH : 2 * WIDTH, :]
    other = lax.ppermute(own, "groups", [(0, 1), (1, 0)])
    pair_rows = pltpu.VMEM((WIDTH, slots), BF16)
    basis = pltpu.VMEM((rows, slots), BF16)
    deep_rows = pltpu.VMEM((depth * WIDTH, slots), BF16)
    big = 2 * WIDTH * slots * slots + 2 * rows * slots * depth * WIDTH
    msg, lat = run(
        cell_kernel,
        [shape((n, main, LANES), BF16), shape((WIDTH, slots), BF16)],
        [rx, cells, rank, zr, home, lp],
        big,
        scratch=sum_scratch + [pair_rows, deep_rows],
        grant=20,
    )
    columns = exchange(msg)
    term, lat = run(
        skip_kernel,
        [shape((WIDTH, slots), F32), shape((WIDTH, slots), BF16)],
        [cells, rank, zr, home, lat, skip_weight, skip_bias.reshape(1, WIDTH)],
        2 * shared * WIDTH * slots,
        scratch=[pltpu.VMEM((shared, slots), BF16)] * 2,
    )
    (weights,) = run(
        weight_kernel,
        [shape((MODES, WIDTH, LANES), BF16)],
        [group, own, other],
        MODES * WIDTH * LANES,
        smem=1,
    )
    msg, spec = run(
        mode_kernel,
        [shape((n, main, LANES), BF16), shape((n, own_rows, LANES), BF16)],
        [columns, weights, table, back, term],
        4 * MODES * low * rows * depth * WIDTH,
        scratch=[pltpu.VMEM((MODES * low * levels, LANES), F32)] * 2,
    )
    slabs, spec, lat, term, cells, pw = exchange_alone(
        msg, spec, lat, term, cells, pw
    )
    msg, pre = run(
        functools.partial(pre_kernel, depth),
        [shape((n, WIDTH + own_rows, LANES), BF16), shape((WIDTH, slots), F32)],
        [slabs, lp, term, cells, spec],
        2 * rows * slots * depth * WIDTH,
        scratch=[pltpu.VMEM((depth * WIDTH, rows), BF16)],
    )
    returned, pre, lat, cells, pw = exchange_alone(
        msg, pre, lat, cells, pw
    )
    out_row = out_weight.reshape(1, WIDTH)
    pressure, msg, own_spec = run(
        head_kernel,
        [
            shape((1, points), F32),
            shape((n, WIDTH + 8, LANES), BF16),
            shape((n, own_rows, LANES), BF16),
        ],
        [returned, point_rows, pw, head_weight, head_bias.reshape(1, WIDTH), out_row, area_row, normals],
        2 * 3 * WIDTH * points * slots,
        scratch=[
            pltpu.VMEM((2 * WIDTH, slots), BF16),
            pltpu.VMEM((points, slots), BF16),
            pltpu.VMEM((2, n, LANES), F32),
        ],
    )
    grads, pressure, own_spec, pre, lat, cells = exchange_alone(
        msg, pressure, own_spec, pre, lat, cells
    )
    scale = 1.0 / math.sqrt(points * n)
    msg, forces, out_grad = run(
        functools.partial(back_kernel, depth, scale),
        [
            shape((peers, halves * main + 8, LANES), BF16),
            shape((1, 2), F32),
            shape((1, WIDTH), F32),
        ],
        [grads, targets.reshape(1, 2), cells, lp, lat, pre],
        2 * rows * slots * depth * WIDTH,
        scratch=[pair_rows, deep_rows],
        grant=20,
    )
    grad_columns, forces, out_grad, own_spec = lax.optimization_barrier(
        (
            lax.all_to_all(
                msg, "gx", split_axis=0, concat_axis=0, tiled=True, axis_index_groups=near
            ),
            forces,
            out_grad,
            own_spec,
        )
    )
    part_rows = MODES * high * levels // n
    (msg,) = run(
        spec_kernel,
        [shape((n, part_rows + 8, LANES), BF16)],
        [half, grad_columns, part_table],
        2 * MODES * high * rows * depth * WIDTH,
        scratch=[pltpu.VMEM((MODES * high * levels, LANES), F32)],
        smem=1,
    )
    finals, own_spec, forces, out_grad = exchange_alone(msg, own_spec, forces, out_grad)
    spec_grad, skip_grad = run(
        functools.partial(final_kernel, peers),
        [shape((spec_weight.shape[0], WIDTH, WIDTH), F32), shape((WIDTH, WIDTH), F32)],
        [finals, own_spec],
        2 * NMODE * WIDTH * WIDTH * depth // n,
    )
    return (pressure.reshape(points), forces.reshape(2), spec_grad, skip_grad, out_grad.reshape(WIDTH))


def solution(mesh):
    fits = mesh.shape["gx"] == 16 and mesh.shape["groups"] == 2
    per_device = slab_step if fits else general_step
    in_specs = (
        P(("groups", "gx"), None),
        P(("groups", "gx"), None, None),
        P(None, ("groups", "gx"), None),
        P(("groups", "gx"), None, None),
        P(("groups", "gx"), None),
        P(("groups", "gx")),
        P(None, ("groups", "gx")),
        P("groups"),
        P("gx", None, None),
        P(),
        P(),
        P(),
        P(),
        P(),
    )
    out_specs = (
        P(("groups", "gx")),
        P("groups"),
        P(("groups", "gx"), None, None),
        P("groups", None),
        P("groups"),
    )
    return jax.shard_map(
        per_device, mesh=mesh, in_specs=in_specs, out_specs=out_specs, check_vma=False
    )
```

```python
import functools
import math

import jax
import jax.numpy as jnp
import ml_dtypes
import numpy as np
from jax import lax
from jax.experimental import pallas as pl
from jax.experimental.pallas import tpu as pltpu
from jax.sharding import PartitionSpec as P

GX = 128
GY = 128
MODES = 32
ZL = 1
NMODE = 1024


def fourier_rows(length, number):
    places = jnp.arange(length, dtype=jnp.float32)
    order = jnp.arange(number)
    half = number // 2
    freqs = jnp.where(order < half, order, order - half + 1).astype(jnp.float32)
    angles = 2.0 * math.pi / length * freqs[:, None] * places[None, :]
    table = jnp.where((order < half)[:, None], jnp.cos(angles), jnp.sin(angles))
    return (table * math.sqrt(2.0 / length)).astype(jnp.bfloat16)


def gelu_value(values):
    return 0.5 * values * (1.0 + lax.erf(values * (1.0 / math.sqrt(2.0))))


def gelu_slope(values):
    return 0.5 * (1.0 + lax.erf(values * (1.0 / math.sqrt(2.0)))) + values * jnp.exp(
        -0.5 * values * values
    ) * (1.0 / math.sqrt(2.0 * math.pi))


def general_step(
    point_feats,
    pair_point,
    pair_cell,
    kernel,
    counts,
    area,
    normals,
    targets,
    spec_weight,
    skip_weight,
    skip_bias,
    head_weight,
    head_bias,
    out_weight,
):
    devices = lax.axis_size("gx")
    local_points, width = point_feats.shape
    block_slots = pair_point.shape[2]
    row_count = GX // devices
    depth = ZL * devices
    slab_cells = row_count * GY * depth
    valid_mask = jnp.arange(block_slots)[None, :] < counts[0][:, None]
    point_rows = pair_point[0]
    pair_weight = jnp.where(valid_mask, kernel[0], jnp.float32(0.0))
    sender_weight = pair_weight * area[point_rows]
    contrib = (sender_weight[..., None] * point_feats[point_rows].astype(jnp.float32)).astype(
        jnp.bfloat16
    )
    arrived = lax.all_to_all(contrib, "gx", split_axis=0, concat_axis=0, tiled=True)
    cell_rows = pair_cell[:, 0, :].reshape(-1)
    latent = jax.ops.segment_sum(
        arrived.reshape(-1, width).astype(jnp.float32), cell_rows, num_segments=slab_cells
    ).astype(jnp.bfloat16)
    col_table = fourier_rows(GY, MODES)
    row_table = fourier_rows(GX, MODES)
    volume = latent.reshape(row_count, GY, depth * width)
    along_y = jnp.einsum(
        "by,xyk->xbk", col_table, volume, preferred_element_type=jnp.float32
    ).astype(jnp.bfloat16)
    columns = lax.all_to_all(along_y, "gx", split_axis=2, concat_axis=0, tiled=True)
    spectrum = jnp.einsum(
        "ax,xbk->abk", row_table, columns, preferred_element_type=jnp.float32
    ).astype(jnp.bfloat16)
    mode_rows = lax.all_to_all(
        spectrum.reshape(NMODE, ZL * width), "gx", split_axis=0, concat_axis=1, tiled=True
    )
    own_modes = mode_rows.shape[0]
    mixed_rows = jnp.einsum(
        "mzc,mcd->mzd",
        mode_rows.reshape(own_modes, depth, width),
        spec_weight,
        preferred_element_type=jnp.float32,
    ).astype(jnp.bfloat16)
    mixed = lax.all_to_all(
        mixed_rows.reshape(own_modes, depth * width), "gx", split_axis=1, concat_axis=0, tiled=True
    )
    back_x = jnp.einsum(
        "ax,abk->xbk",
        row_table,
        mixed.reshape(MODES, MODES, ZL * width),
        preferred_element_type=jnp.float32,
    ).astype(jnp.bfloat16)
    slabs = lax.all_to_all(back_x, "gx", split_axis=0, concat_axis=2, tiled=True)
    spatial = jnp.einsum(
        "by,xbk->xyk", col_table, slabs, preferred_element_type=jnp.float32
    ).reshape(slab_cells, width)
    pre = spatial + jnp.dot(latent, skip_weight, preferred_element_type=jnp.float32) + skip_bias
    features = gelu_value(pre).astype(jnp.bfloat16)
    picked = features[cell_rows].reshape(devices, block_slots, width)
    returned = lax.all_to_all(picked, "gx", split_axis=0, concat_axis=0, tiled=True)
    point_latent = jax.ops.segment_sum(
        (pair_weight[..., None] * returned.astype(jnp.float32)).reshape(-1, width),
        point_rows.reshape(-1),
        num_segments=local_points,
    )
    head_matrix = head_weight.astype(jnp.float32)
    head_pre = jnp.dot(point_latent, head_matrix, precision=lax.Precision.HIGHEST) + head_bias
    head = gelu_value(head_pre)
    pressure = jnp.dot(head, out_weight, precision=lax.Precision.HIGHEST)
    weighted = pressure * area
    scale = 1.0 / math.sqrt(local_points * devices)
    totals = lax.psum(
        jnp.stack([jnp.sum(weighted * normals[0]), jnp.sum(weighted * normals[1])]), "gx"
    )
    forces = scale * totals
    misfit = forces - targets
    point_grad = 2.0 * scale * (misfit[0] * normals[0] + misfit[1] * normals[1]) * area
    out_part = jnp.dot(point_grad, head, precision=lax.Precision.HIGHEST)
    head_grad = point_grad[:, None] * out_weight[None, :] * gelu_slope(head_pre)
    latent_grad = jnp.dot(head_grad, head_matrix.T, precision=lax.Precision.HIGHEST).astype(
        jnp.bfloat16
    )
    grad_pairs = (pair_weight[..., None] * latent_grad[point_rows].astype(jnp.float32)).astype(
        jnp.bfloat16
    )
    grad_arrived = lax.all_to_all(grad_pairs, "gx", split_axis=0, concat_axis=0, tiled=True)
    cell_grad = jax.ops.segment_sum(
        grad_arrived.reshape(-1, width).astype(jnp.float32), cell_rows, num_segments=slab_cells
    )
    pre_grad = (cell_grad * gelu_slope(pre)).astype(jnp.bfloat16)
    skip_part = jnp.dot(latent.T, pre_grad, preferred_element_type=jnp.float32)
    grad_y = jnp.einsum(
        "by,xyk->xbk",
        col_table,
        pre_grad.reshape(row_count, GY, depth * width),
        preferred_element_type=jnp.float32,
    ).astype(jnp.bfloat16)
    grad_columns = lax.all_to_all(grad_y, "gx", split_axis=2, concat_axis=0, tiled=True)
    grad_spec = jnp.einsum(
        "ax,xbk->abk", row_table, grad_columns, preferred_element_type=jnp.float32
    ).astype(jnp.bfloat16)
    grad_rows = lax.all_to_all(
        grad_spec.reshape(NMODE, ZL * width), "gx", split_axis=0, concat_axis=1, tiled=True
    )
    own_modes = grad_rows.shape[0]
    spec_grad = jnp.einsum(
        "mzc,mzd->mcd",
        mode_rows.reshape(own_modes, depth, width),
        grad_rows.reshape(own_modes, depth, width),
        preferred_element_type=jnp.float32,
    )
    out_grad, skip_grad = lax.psum((out_part, skip_part), "gx")
    return (pressure, forces, spec_grad, skip_grad, out_grad)


F32 = jnp.float32
BF16 = jnp.bfloat16
LANES = 128
WIDTH = 64


def host_rows(length, number):
    places = np.arange(length, dtype=np.float32)
    order = np.arange(number)
    half = number // 2
    freqs = np.where(order < half, order, order - half + 1).astype(np.float32)
    angles = np.float32(2.0 * math.pi / length) * freqs[:, None] * places[None, :]
    table = np.where((order < half)[:, None], np.cos(angles), np.sin(angles))
    table = table.astype(np.float32) * np.float32(math.sqrt(2.0 / length))
    return table.astype(ml_dtypes.bfloat16)


def gelu_both(values):
    half = 0.5 * (1.0 + lax.erf(values * (1.0 / math.sqrt(2.0))))
    bell = jnp.exp(-0.5 * values * values) * (1.0 / math.sqrt(2.0 * math.pi))
    return values * half, half + values * bell


def three_parts(values):
    first = values.astype(BF16)
    rest = values - first.astype(F32)
    second = rest.astype(BF16)
    third = (rest - second.astype(F32)).astype(BF16)
    return first, second, third


def mm(left, right):
    return jnp.dot(left, right, preferred_element_type=F32)


def mm_nt(left, right):
    return lax.dot_general(left, right, (((1,), (1,)), ((), ())), preferred_element_type=F32)


def mm_tn(left, right):
    return lax.dot_general(left, right, (((0,), (0,)), ((), ())), preferred_element_type=F32)


def short_rows(count):
    return lax.broadcasted_iota(jnp.int32, (count, LANES), 0).astype(jnp.int16)


def matches(rows, row):
    short = jnp.broadcast_to(row, (16, LANES)).astype(jnp.int16)
    tall = jnp.broadcast_to(short[None], (rows.shape[0] // 16, 16, LANES)).reshape(rows.shape)
    return jnp.where(rows == tall, jnp.ones((), BF16), jnp.zeros((), BF16))


def two_rows(ref, pair):
    return jnp.concatenate([ref[2 * pair : 2 * pair + 1, :], ref[2 * pair + 1 : 2 * pair + 2, :]], axis=1)


def source_kernel(group_ref, half_ref, count_hbm, point_hbm, kern_hbm, area_hbm, feat_hbm, weight_hbm, msg_ref, pw_ref, count_ref, point_ref, kern_ref, area_ref, feat_ref, weight_ref, sems):
    devices, points = point_ref.shape[0], feat_ref.shape[1]
    low = MODES // devices
    pieces = (
        (point_hbm, point_ref),
        (area_hbm, area_ref),
        (feat_hbm, feat_ref),
        (kern_hbm, kern_ref),
        (count_hbm, count_ref),
        (weight_hbm.at[pl.ds(group_ref[0] * MODES, MODES)], weight_ref),
    )
    copies = [
        pltpu.make_async_copy(source, place, sems.at[index])
        for index, (source, place) in enumerate(pieces)
    ]
    for copy in copies:
        copy.start()
    for copy in copies[:-1]:
        copy.wait()
    first, second, third = three_parts(area_ref[...])
    place = lax.broadcasted_iota(jnp.int32, (16, points), 0)
    extra = jnp.where(
        place == 0,
        first.astype(F32),
        jnp.where(place == 1, second.astype(F32), jnp.where(place == 2, third.astype(F32), 0.0)),
    ).astype(BF16)
    table = jnp.concatenate([feat_ref[...], extra], axis=0)
    rows = short_rows(points)
    lane = lax.broadcasted_iota(jnp.int32, (1, LANES), 1)
    kept = []
    for pair in range(devices // 2):
        hot = jnp.concatenate(
            [matches(rows, point_ref[at : at + 1, :]) for at in (2 * pair, 2 * pair + 1)], axis=1
        )
        got = mm(table, hot)
        spread = got[WIDTH : WIDTH + 1] + got[WIDTH + 1 : WIDTH + 2] + got[WIDTH + 2 : WIDTH + 3]
        for half in range(2):
            dest = 2 * pair + half
            cut = slice(half * LANES, (half + 1) * LANES)
            valid = lane < count_ref[0:1, dest : dest + 1]
            weight = jnp.where(valid, kern_ref[dest : dest + 1, :], 0.0)
            kept.append(weight)
            msg_ref[dest, 0:WIDTH, :] = ((weight * spread[:, cut]) * got[0:WIDTH, cut]).astype(BF16)
    pw_ref[...] = jnp.concatenate(kept, axis=0)
    copies[-1].wait()
    for dest in range(devices):
        msg_ref[dest, WIDTH : 2 * WIDTH, :] = jnp.concatenate(
            [weight_ref[low * dest], weight_ref[low * dest + 1]], axis=1
        )


def columns_of(row):
    return jnp.broadcast_to(row, (LANES, LANES)).T


def column_of(row):
    down = lax.broadcasted_iota(jnp.int32, (WIDTH, WIDTH), 0)
    along = lax.broadcasted_iota(jnp.int32, (WIDTH, WIDTH), 1)
    return jnp.sum(jnp.where(down == along, row, 0.0), axis=1, keepdims=True)


def pick_rows(rank_ref, pick_ref):
    rows = short_rows(pick_ref.shape[0])
    for block in range(rank_ref.shape[0]):
        pick_ref[:, block * LANES : (block + 1) * LANES] = matches(
            rows, rank_ref[block : block + 1, :]
        )


def basis_rows(depth, cell_ref, by_ref, lp_ref):
    zbits = depth.bit_length() - 1
    rows = by_ref.shape[0]
    slab = rows // MODES
    wide = 2 * LANES
    yrow = lax.broadcasted_iota(jnp.int32, (GY, wide), 0)
    xrow = jnp.bitwise_and(lax.broadcasted_iota(jnp.int32, (16, wide), 0), slab - 1)
    for pair in range(cell_ref.shape[0] // 2):
        cells = two_rows(cell_ref, pair)
        ypos = jnp.bitwise_and(jnp.right_shift(cells, zbits), GY - 1)
        xpos = jnp.right_shift(cells, zbits + GY.bit_length() - 1)
        hot = jnp.where(yrow == ypos, 1.0, 0.0).astype(BF16)
        mask = jnp.where(xrow == xpos, 1.0, 0.0).astype(BF16)
        found = mm(by_ref[...], hot).astype(BF16)
        for at in range(0, rows, 16):
            lp_ref[at : at + 16, pair * wide : (pair + 1) * wide] = found[at : at + 16] * mask


def place_kernel(depth, cell_ref, by_ref, zr_ref, rank_ref, home_ref, lp_ref, col_ref, pick_ref, part_ref):
    devices = cell_ref.shape[0]
    basis_rows(depth, cell_ref, by_ref, lp_ref)
    down = lax.broadcasted_iota(jnp.int32, (LANES, LANES), 0)
    along = lax.broadcasted_iota(jnp.int32, (LANES, LANES), 1)
    place = lax.broadcasted_iota(jnp.int32, (16, LANES), 0)
    seen = []
    for block in range(devices):
        cells = cell_ref[block : block + 1, :]
        row = cells.astype(F32)
        cut = slice(block * LANES, (block + 1) * LANES)
        col_ref[cut, :] = columns_of(row)
        high = jnp.right_shift(cells, 7).astype(F32)
        low = jnp.bitwise_and(cells, 127).astype(F32)
        part_ref[:, cut] = jnp.where(place == 0, high, jnp.where(place == 1, low, 0.0)).astype(BF16)
        same = jnp.logical_and(col_ref[cut, :] == row, down < along)
        before = jnp.max(jnp.where(same, 1.0, 0.0), axis=0, keepdims=True)
        if block:
            early = jnp.where(col_ref[0 : block * LANES, :] == row, 1.0, 0.0)
            before = jnp.maximum(before, jnp.max(early, axis=0, keepdims=True))
        seen.append(before)
    flags = jnp.concatenate(seen, axis=0)
    zr_ref[...] = jnp.where(flags > 0.0, -1, jnp.bitwise_and(cell_ref[...], depth - 1))
    marks = flags.astype(BF16)
    inside = mm(marks, jnp.where(down <= along, 1.0, 0.0).astype(BF16))
    above = jnp.where(down < along, 1.0, 0.0)[:, 0:devices][0:devices]
    ahead = jnp.sum(mm_tn(above.astype(BF16), marks), axis=1, keepdims=True)
    rank_ref[...] = jnp.where(flags > 0.0, (inside + ahead - flags).astype(jnp.int32), -1)
    pick_rows(rank_ref, pick_ref)
    found = mm_nt(part_ref[...], pick_ref[...])
    found = found[0:1] * 128.0 + found[1:2]
    for block in range(home_ref.shape[0] // LANES):
        cut = slice(block * LANES, (block + 1) * LANES)
        home_ref[cut, :] = columns_of(found[:, cut])


def first_rows(cell_ref, zr_ref, home_ref, first_ref):
    homes = home_ref[...].astype(jnp.int32).astype(jnp.int16)
    for block in range(cell_ref.shape[0]):
        here = slice(block, block + 1)
        row = jnp.where(zr_ref[here, :] < 0, -1, cell_ref[here, :])
        first_ref[:, block * LANES : (block + 1) * LANES] = matches(homes, row)


def fold_parts(values):
    total = values[0:WIDTH]
    for at in range(WIDTH, values.shape[0], WIDTH):
        total = total + values[at : at + WIDTH]
    return total


def sum_cells(terms, xs_ref, cell_ref, rank_ref, zr_ref, home_ref, sums_ref, pick_ref, first_ref, full_ref, col_ref):
    devices = cell_ref.shape[0]
    few = jnp.max(rank_ref[...]) < home_ref.shape[0]

    @pl.when(few)
    def _():
        pick_rows(rank_ref, pick_ref)
        first_rows(cell_ref, zr_ref, home_ref, first_ref)
        moved = mm_nt(xs_ref[...], pick_ref[...]).astype(BF16)
        for pair in range(devices // 2):
            span = slice(pair * 2 * LANES, (pair + 1) * 2 * LANES)
            sums_ref[:, span] = terms(span) + fold_parts(mm(moved, first_ref[:, span]))

    @pl.when(jnp.logical_not(few))
    def _():
        for block in range(devices):
            col_ref[block * LANES : (block + 1) * LANES, :] = columns_of(
                cell_ref[block : block + 1, :].astype(F32)
            )
        for block in range(devices):
            row = cell_ref[block : block + 1, :].astype(F32)
            full_ref[...] = jnp.where(col_ref[...] == row, 1.0, 0.0).astype(BF16)
            sums_ref[:, block * LANES : (block + 1) * LANES] = fold_parts(
                mm(xs_ref[...], full_ref[...])
            )


def slab_rows(value_ref, zpos_of, lp_ref, rp_ref, msg_ref):
    devices = msg_ref.shape[0]
    step = lp_ref.shape[0] // devices
    for quad in range(rp_ref.shape[0] // (4 * WIDTH)):
        for pair in range(value_ref.shape[1] // (2 * LANES)):
            cut = slice(pair * 2 * LANES, (pair + 1) * 2 * LANES)
            zpos = zpos_of(pair)
            values = value_ref[:, cut].astype(F32)
            for level in range(4 * quad, 4 * quad + 4):
                rp_ref[level * WIDTH : (level + 1) * WIDTH, cut] = jnp.where(
                    zpos == level, values, 0.0
                ).astype(BF16)
        out = mm_nt(lp_ref[...], rp_ref[quad * 4 * WIDTH : (quad + 1) * 4 * WIDTH, :]).astype(BF16)
        for half in range(2):
            level = 2 * quad + half
            for dest in range(devices):
                msg_ref[dest, level * step : (level + 1) * step, :] = out[
                    dest * step : (dest + 1) * step, half * LANES : (half + 1) * LANES
                ]


def cell_kernel(rx_ref, cell_ref, rank_ref, zr_ref, home_ref, lp_ref, msg_ref, lat_ref, sums_ref, pick_ref, first_ref, full_ref, col_ref, xs_ref, rp_ref):
    devices = rx_ref.shape[0]
    for block in range(devices):
        xs_ref[:, block * LANES : (block + 1) * LANES] = rx_ref[block, 0:WIDTH, :]
    sum_cells(
        lambda span: xs_ref[:, span].astype(F32),
        xs_ref, cell_ref, rank_ref, zr_ref, home_ref, sums_ref, pick_ref, first_ref, full_ref, col_ref,
    )
    for pair in range(devices // 2):
        cut = slice(pair * 2 * LANES, (pair + 1) * 2 * LANES)
        latent = sums_ref[:, cut]
        lat_ref[:, cut] = latent.astype(BF16)
    slab_rows(lat_ref, lambda pair: two_rows(zr_ref, pair), lp_ref, rp_ref, msg_ref)


def to_modes(rx_ref, table, sp_ref):
    levels = sp_ref.shape[0] // table.shape[0]
    step = table.shape[1] // rx_ref.shape[0]
    for level in range(levels):
        block = rx_ref[:, level * step : (level + 1) * step, :].reshape(table.shape[1], LANES)
        coeffs = mm(table, block).astype(BF16).astype(F32)
        sp_ref[pl.ds(level, table.shape[0], stride=levels), :] = coeffs


def swap_halves(values):
    return pltpu.roll(values, WIDTH, 1)


def weight_kernel(group_ref, own_ref, other_ref, weight_ref):
    for order in range(MODES):
        source, which = order // 2, order % 2
        mine = jnp.full((WIDTH, LANES), group_ref[0], jnp.int32) == which
        weight_ref[order] = jnp.where(
            mine, own_ref[source].astype(F32), other_ref[source].astype(F32)
        ).astype(BF16)


def mode_kernel(rx_ref, weight_ref, table_ref, back_ref, term_ref, msg_ref, spec_ref, sp_ref, mx_ref):
    devices = rx_ref.shape[0]
    own_rows = spec_ref.shape[1]
    modes = table_ref.shape[0]
    levels = sp_ref.shape[0] // modes
    step = back_ref.shape[0] // devices
    to_modes(rx_ref, table_ref[...], sp_ref)
    for dest in range(devices):
        spec_ref[dest] = sp_ref[dest * own_rows : (dest + 1) * own_rows, :].astype(BF16)
    left = lax.broadcasted_iota(jnp.int32, (levels, LANES), 1) < WIDTH
    for order in range(MODES):
        at = order * 2 * levels
        even = sp_ref[at : at + levels, :]
        odd = sp_ref[at + levels : at + 2 * levels, :]
        rows = jnp.concatenate([even, swap_halves(even), odd, swap_halves(odd)], axis=0)
        out = mm(rows[:, 0:WIDTH].astype(BF16), weight_ref[order])
        mx_ref[at : at + levels, :] = jnp.where(
            left, out[0:levels], swap_halves(out[levels : 2 * levels])
        )
        mx_ref[at + levels : at + 2 * levels, :] = jnp.where(
            left, swap_halves(out[2 * levels : 3 * levels]), out[3 * levels : 4 * levels]
        )
    for level in range(levels):
        mixed = mx_ref[pl.ds(level, modes, stride=levels), :].astype(BF16)
        out = mm(back_ref[...], mixed).astype(BF16)
        for dest in range(devices):
            msg_ref[dest, level * step : (level + 1) * step, :] = out[dest * step : (dest + 1) * step]


def skip_kernel(cell_ref, rank_ref, zr_ref, home_ref, lat_ref, skip_ref, bias_ref, term_ref, full_ref, pick_ref, first_ref):
    few = jnp.max(rank_ref[...]) < home_ref.shape[0]
    bias = column_of(bias_ref[...])
    pick_rows(rank_ref, pick_ref)
    first_rows(cell_ref, zr_ref, home_ref, first_ref)
    shared = mm_nt(lat_ref[...], first_ref[...]).astype(BF16)
    for pair in range(cell_ref.shape[0] // 2):
        span = slice(pair * 2 * LANES, (pair + 1) * 2 * LANES)
        later = jnp.logical_and(two_rows(rank_ref, pair) >= 0, few)
        latent = jnp.where(later, mm(shared, pick_ref[:, span]), lat_ref[:, span].astype(F32))
        full_ref[:, span] = latent.astype(BF16)
        term_ref[:, span] = mm_tn(skip_ref[...], latent.astype(BF16)) + bias


def pre_kernel(depth, rx_ref, lp_ref, term_ref, cell_ref, spec_ref, msg_ref, slope_ref, rt_ref):
    devices = rx_ref.shape[0]
    rows = lp_ref.shape[0]
    step = rows // devices
    for level in range(rt_ref.shape[0] // LANES):
        block = rx_ref[:, level * step : (level + 1) * step, :].reshape(rows, LANES)
        rt_ref[level * LANES : (level + 1) * LANES, :] = block.T
    for pair in range(devices // 2):
        cut = slice(pair * 2 * LANES, (pair + 1) * 2 * LANES)
        zpos = jnp.bitwise_and(two_rows(cell_ref, pair), depth - 1)
        field = mm(rt_ref[...], lp_ref[:, cut])
        total = jnp.where(zpos == 0, field[0:WIDTH], 0.0)
        for level in range(1, depth):
            total += jnp.where(zpos == level, field[level * WIDTH : (level + 1) * WIDTH], 0.0)
        pre = total + term_ref[:, cut]
        feats, slope = gelu_both(pre)
        slope_ref[:, cut] = slope
        feats = feats.astype(BF16)
        for half in range(2):
            dest = 2 * pair + half
            msg_ref[dest, 0:WIDTH, :] = feats[:, half * LANES : (half + 1) * LANES]
            msg_ref[dest, WIDTH : WIDTH + 16, :] = spec_ref[dest, 0:16, :]


def head_kernel(rx_ref, point_ref, pw_ref, head_ref, bias_ref, out_ref, area_ref, normal_ref, own_ref, pres_ref, msg_ref, spec_ref, value_ref, hot_ref):
    devices = rx_ref.shape[0]
    points = area_ref.shape[1]
    rows = short_rows(points)
    for block in range(devices):
        cut = slice(block * LANES, (block + 1) * LANES)
        parts = three_parts(pw_ref[block : block + 1, :] * rx_ref[block, 0:WIDTH, :].astype(F32))[0:2]
        for index, part in enumerate(parts):
            value_ref[index * WIDTH : (index + 1) * WIDTH, cut] = part
        hot_ref[:, cut] = matches(rows, point_ref[block : block + 1, :])
    sums = mm_nt(value_ref[...], hot_ref[...])
    latent = sums[0:WIDTH] + sums[WIDTH : 2 * WIDTH]
    first, second, third = three_parts(latent)
    weight = head_ref[...]
    head_pre = mm_tn(weight, first) + mm_tn(weight, second) + mm_tn(weight, third) + column_of(bias_ref[...])
    out_column = column_of(out_ref[...])
    head, head_slope = gelu_both(head_pre)
    pressure = jnp.sum(head * out_column, axis=0, keepdims=True)
    pres_ref[...] = pressure
    along = [normal_ref[which : which + 1, :] * area_ref[...] for which in range(2)]
    first, second, third = three_parts(out_column * head_slope)
    grad = mm(weight, first) + mm(weight, second) + mm(weight, third)
    place = lax.broadcasted_iota(jnp.int32, (16, points), 0)
    extra = jnp.zeros((16, points), F32)
    for which in range(2):
        for index, part in enumerate(three_parts(along[which])):
            extra = jnp.where(place == 3 * which + index, part.astype(F32), extra)
    table = jnp.concatenate([grad.astype(BF16), extra.astype(BF16)], axis=0)
    lane = lax.broadcasted_iota(jnp.int32, (1, LANES), 1)
    partial = []
    for which in range(2):
        force = jnp.sum(pressure * area_ref[...] * normal_ref[which : which + 1, :], axis=1, keepdims=True)
        partial.append(force)
    force_row = jnp.zeros((1, LANES), F32)
    for which in range(2):
        for index, part in enumerate(three_parts(partial[which])):
            force_row = jnp.where(lane == 3 * which + index, part.astype(F32), force_row)
    out_rows = lax.dot_general(
        jnp.concatenate([along[0], along[1], jnp.zeros((6, points), F32)], axis=0),
        head,
        (((1,), (1,)), ((), ())),
        precision=lax.Precision.HIGHEST,
        preferred_element_type=F32,
    )
    out_row = jnp.concatenate([out_rows[0:1], out_rows[1:2]], axis=1)
    place = lax.broadcasted_iota(jnp.int32, (8, LANES), 0)
    out_parts = three_parts(out_row)
    common = jnp.where(
        place == 4,
        out_parts[0].astype(F32),
        jnp.where(place == 5, out_parts[1].astype(F32), jnp.where(place == 6, force_row, 0.0)),
    )
    found = ([], [])
    for pair in range(devices // 2):
        got = mm(table, hot_ref[:, pair * 2 * LANES : (pair + 1) * 2 * LANES])
        for half in range(2):
            block = 2 * pair + half
            cut = slice(half * LANES, (half + 1) * LANES)
            msg_ref[block, 0:WIDTH, :] = got[0:WIDTH, cut].astype(BF16)
            spec_ref[block] = rx_ref[block, WIDTH : WIDTH + 16, :]
            for which in range(2):
                at = WIDTH + 3 * which
                found[which].append(
                    got[at : at + 1, cut] + got[at + 1 : at + 2, cut] + got[at + 2 : at + 3, cut]
                )
    scaled = [
        three_parts(pw_ref[...] * jnp.concatenate(found[which], axis=0)) for which in range(2)
    ]
    rows = [scaled[which][index].astype(F32) for which in range(2) for index in range(2)]
    for block in range(devices):
        tail = common
        for index, row in enumerate(rows):
            tail = jnp.where(place == index, row[block : block + 1, :], tail)
        tail = jnp.concatenate([tail, own_ref[block, 16:32, :].astype(F32)[0:8]], axis=0)
        msg_ref[block, WIDTH : WIDTH + 16, :] = tail.astype(BF16)


def back_kernel(depth, scale, rx_ref, target_ref, cell_ref, lp_ref, lat_ref, slope_ref, msg_ref, force_ref, outg_ref, spec_ref, pg_ref, rp_ref):
    devices = rx_ref.shape[0]
    main = msg_ref.shape[1] - 16
    extra = slice(WIDTH, WIDTH + 16)
    total = rx_ref[0, extra, :].astype(F32)
    for block in range(1, devices):
        total += rx_ref[block, extra, :].astype(F32)
    force = total[6:7]
    lane = lax.broadcasted_iota(jnp.int32, (1, 2), 1)
    forces = scale * jnp.where(
        lane == 0,
        force[:, 0:1] + force[:, 1:2] + force[:, 2:3],
        force[:, 3:4] + force[:, 4:5] + force[:, 5:6],
    )
    force_ref[...] = forces
    misfit = (2.0 * scale) * (forces - target_ref[...])
    drag, lift = misfit[:, 0:1], misfit[:, 1:2]
    out_row = total[4:5] + total[5:6]
    outg_ref[...] = drag * out_row[:, 0:WIDTH] + lift * out_row[:, WIDTH : 2 * WIDTH]
    for block in range(devices):
        tail = rx_ref[block, extra, :].astype(F32)
        spec_ref[block] = tail[8:16]
        factor = drag * (tail[0:1] + tail[1:2]) + lift * (tail[2:3] + tail[3:4])
        cut = slice(block * LANES, (block + 1) * LANES)
        grad = factor * rx_ref[block, 0:WIDTH, :].astype(F32) * slope_ref[:, cut]
        pg_ref[:, cut] = grad.astype(BF16)
    slab_rows(
        pg_ref,
        lambda pair: jnp.bitwise_and(two_rows(cell_ref, pair), depth - 1),
        lp_ref, rp_ref, msg_ref,
    )
    skip = mm_nt(lat_ref[...], pg_ref[...])
    for dest in range(msg_ref.shape[0]):
        rows = two_parts(skip[8 * dest : 8 * dest + 8])
        rows = jnp.concatenate([rows, jnp.zeros_like(rows)], axis=0)
        msg_ref[dest, main : main + 16, :] = rows.astype(BF16)


def two_parts(values):
    first, second, _ = three_parts(values)
    return jnp.concatenate([first.astype(F32), second.astype(F32)], axis=1)


def spec_kernel(half_ref, rx_ref, table_ref, own_ref, msg_ref, sp_ref):
    peers, devices = rx_ref.shape[0], msg_ref.shape[0]
    part_rows = sp_ref.shape[0] // devices
    main = rx_ref.shape[1] - 16
    to_modes(rx_ref, table_ref[half_ref[0]], sp_ref)
    total = rx_ref[0, main : main + 16, :].astype(F32)
    for source in range(1, peers):
        total += rx_ref[source, main : main + 16, :].astype(F32)
    total = total[0:8]
    total = two_parts((total + swap_halves(total))[:, 0:WIDTH])
    for dest in range(devices):
        msg_ref[dest, 0:part_rows, :] = sp_ref[dest * part_rows : (dest + 1) * part_rows, :].astype(BF16)
        rows = jnp.concatenate([total, own_ref[dest, 16:32, :].astype(F32)[8:16]], axis=0)
        msg_ref[dest, part_rows : part_rows + 16, :] = rows.astype(BF16)


def final_kernel(peers, rx_ref, own_ref, next_ref, spec_ref, skip_ref):
    devices = rx_ref.shape[0]
    low = MODES // devices
    high = MODES // peers
    owned = spec_ref.shape[0] // MODES
    left = lax.broadcasted_iota(jnp.int32, (8, LANES), 1) < WIDTH
    main = rx_ref.shape[1] - 16
    for which in range(owned):
        for source in range(devices):
            if which == 0:
                coeffs = own_ref[source].astype(F32)
                first, second = coeffs[0:8], coeffs[8:16]
            else:
                first = next_ref[source]
                second = rx_ref[source, main : main + 16, :].astype(F32)[8:16]
            block = [
                jnp.where(left, first, 0.0),
                jnp.where(left, swap_halves(first), 0.0),
                jnp.where(left, 0.0, swap_halves(second)),
                jnp.where(left, 0.0, second),
            ]
            peer, inner = divmod(low * source, high)
            at = (which * high + inner) * 8
            grads = []
            for shift in range(0, devices, peers):
                part = rx_ref[peer + shift, at : at + 8 * low, :].astype(F32)
                grads += [part[0:8], swap_halves(part[0:8]), part[8:16], swap_halves(part[8:16])]
            block = jnp.concatenate(block * (devices // peers), axis=0).astype(BF16)
            grads = jnp.concatenate(grads, axis=0)[:, 0:WIDTH].astype(BF16)
            found = mm_tn(block, grads)
            mode = which * MODES + low * source
            spec_ref[mode] = found[0:WIDTH]
            spec_ref[mode + 1] = found[WIDTH : 2 * WIDTH]
    for peer in range(peers):
        rows = rx_ref[peer, main : main + 16, :].astype(F32)
        for shift in range(peers, devices, peers):
            rows += rx_ref[peer + shift, main : main + 16, :].astype(F32)
        rows = rows[0:8]
        skip_ref[8 * peer : 8 * peer + 8, :] = (rows + swap_halves(rows))[:, 0:WIDTH]


def run(kernel, outs, ins, flops, scratch=(), smem=0, hbm=0, hbm_outs=0, grant=16):
    vmem = pl.BlockSpec(memory_space=pltpu.VMEM)
    far = pl.BlockSpec(memory_space=pltpu.HBM)
    scalar = pl.BlockSpec(memory_space=pltpu.SMEM)
    moved = sum(math.prod(a.shape) * a.dtype.itemsize for a in list(ins) + list(outs))
    return pl.pallas_call(
        kernel,
        out_shape=tuple(outs),
        in_specs=[scalar] * smem + [far] * hbm + [vmem] * (len(ins) - smem - hbm),
        out_specs=tuple([far] * hbm_outs + [vmem] * (len(outs) - hbm_outs)),
        scratch_shapes=list(scratch),
        compiler_params=pltpu.CompilerParams(vmem_limit_bytes=grant * 1024 * 1024),
        cost_estimate=pl.CostEstimate(flops=flops, bytes_accessed=moved, transcendentals=0),
    )(*ins)


def slab_step(
    point_feats,
    pair_point,
    pair_cell,
    kernel,
    counts,
    area,
    normals,
    targets,
    spec_weight,
    skip_weight,
    skip_bias,
    head_weight,
    head_bias,
    out_weight,
):
    n = lax.axis_size("gx")
    points = point_feats.shape[0]
    slots = n * LANES
    slab = GX // n
    low = MODES // n
    depth = ZL * n
    levels = depth * WIDTH // LANES
    rows = MODES * slab
    main = levels * slab * low
    own_rows = low * low * levels
    shape = jax.ShapeDtypeStruct

    by = host_rows(GY, MODES)
    bx = host_rows(GX, MODES)
    by_rows = jnp.asarray(np.repeat(by, slab, axis=0))
    table = np.zeros((MODES, low, n, low, slab), ml_dtypes.bfloat16)
    for index in range(low):
        table[:, index, :, index, :] = bx.reshape(MODES, n, slab)
    table = table.reshape(MODES * low, rows)
    back = jnp.asarray(np.ascontiguousarray(table.T))
    table = jnp.asarray(table)
    peers = 8
    halves = n // peers
    high = MODES // peers
    part_table = np.zeros((halves, MODES, high, peers, high, slab), ml_dtypes.bfloat16)
    for index in range(high):
        part_table[:, :, index, :, index, :] = np.moveaxis(
            bx.reshape(MODES, halves, peers, slab), 1, 0
        )
    part_table = jnp.asarray(part_table.reshape(halves, MODES * high, rows))
    near = [[half * peers + peer for peer in range(peers)] for half in range(halves)]
    half = lax.shift_right_logical(lax.axis_index("gx"), peers.bit_length() - 1)
    half = half.astype(jnp.int32).reshape(1)

    def exchange(message):
        return lax.all_to_all(message, "gx", split_axis=0, concat_axis=0, tiled=True)

    def exchange_alone(message, *others):
        return lax.optimization_barrier((exchange(message),) + others)

    group = lax.axis_index("groups").astype(jnp.int32).reshape(1)
    point_rows = pair_point[0]
    cells = pair_cell[:, 0, :]
    area_row = area.reshape(1, points)
    msg, pw = run(
        source_kernel,
        [shape((n, 2 * WIDTH, LANES), BF16), shape((n, LANES), F32)],
        [group, half, counts, point_rows, kernel[0], area_row, point_feats.T, spec_weight],
        2 * 80 * points * slots,
        scratch=[
            pltpu.VMEM((1, n), jnp.int32),
            pltpu.VMEM((n, LANES), jnp.int32),
            pltpu.VMEM((n, LANES), F32),
            pltpu.VMEM((1, points), F32),
            pltpu.VMEM((WIDTH, points), BF16),
            pltpu.VMEM((MODES, WIDTH, WIDTH), BF16),
            pltpu.SemaphoreType.DMA((6,)),
        ],
        smem=2,
        hbm=6,
        grant=60,
    )
    rx = exchange(msg)
    shared = 256
    zr, rank, home, lp = run(
        functools.partial(place_kernel, depth),
        [
            shape((n, LANES), jnp.int32),
            shape((n, LANES), jnp.int32),
            shape((shared, LANES), F32),
            shape((rows, slots), BF16),
        ],
        [cells, by_rows],
        2 * rows * LANES * slots,
        scratch=[
            pltpu.VMEM((slots, LANES), F32),
            pltpu.VMEM((shared, slots), BF16),
            pltpu.VMEM((16, slots), BF16),
        ],
    )
    sum_scratch = [
        pltpu.VMEM((WIDTH, slots), F32),
        pltpu.VMEM((shared, slots), BF16),
        pltpu.VMEM((shared, slots), BF16),
        pltpu.VMEM((slots, LANES), BF16),
        pltpu.VMEM((slots, LANES), F32),
    ]
    own = rx[:, WIDTH : 2 * WIDTH, :]
    other = lax.ppermute(own, "groups", [(0, 1), (1, 0)])
    pair_rows = pltpu.VMEM((WIDTH, slots), BF16)
    basis = pltpu.VMEM((rows, slots), BF16)
    deep_rows = pltpu.VMEM((depth * WIDTH, slots), BF16)
    big = 2 * WIDTH * slots * slots + 2 * rows * slots * depth * WIDTH
    msg, lat = run(
        cell_kernel,
        [shape((n, main, LANES), BF16), shape((WIDTH, slots), BF16)],
        [rx, cells, rank, zr, home, lp],
        big,
        scratch=sum_scratch + [pair_rows, deep_rows],
        grant=20,
    )
    columns = exchange(msg)
    term, lat = run(
        skip_kernel,
        [shape((WIDTH, slots), F32), shape((WIDTH, slots), BF16)],
        [cells, rank, zr, home, lat, skip_weight, skip_bias.reshape(1, WIDTH)],
        2 * shared * WIDTH * slots,
        scratch=[pltpu.VMEM((shared, slots), BF16)] * 2,
    )
    (weights,) = run(
        weight_kernel,
        [shape((MODES, WIDTH, LANES), BF16)],
        [group, own, other],
        MODES * WIDTH * LANES,
        smem=1,
    )
    msg, spec = run(
        mode_kernel,
        [shape((n, main, LANES), BF16), shape((n, own_rows, LANES), BF16)],
        [columns, weights, table, back, term],
        4 * MODES * low * rows * depth * WIDTH,
        scratch=[pltpu.VMEM((MODES * low * levels, LANES), F32)] * 2,
    )
    slabs, spec, lat, term, cells, pw = exchange_alone(
        msg, spec, lat, term, cells, pw
    )
    msg, pre = run(
        functools.partial(pre_kernel, depth),
        [shape((n, WIDTH + 16, LANES), BF16), shape((WIDTH, slots), F32)],
        [slabs, lp, term, cells, spec],
        2 * rows * slots * depth * WIDTH,
        scratch=[pltpu.VMEM((depth * WIDTH, rows), BF16)],
    )
    returned, pre, lat, cells, pw, spec = exchange_alone(
        msg, pre, lat, cells, pw, spec
    )
    out_row = out_weight.reshape(1, WIDTH)
    pressure, msg, own_spec = run(
        head_kernel,
        [
            shape((1, points), F32),
            shape((n, WIDTH + 16, LANES), BF16),
            shape((n, 16, LANES), BF16),
        ],
        [returned, point_rows, pw, head_weight, head_bias.reshape(1, WIDTH), out_row, area_row, normals, spec],
        2 * 3 * WIDTH * points * slots,
        scratch=[
            pltpu.VMEM((2 * WIDTH, slots), BF16),
            pltpu.VMEM((points, slots), BF16),
        ],
    )
    grads, pressure, own_spec, pre, lat, cells, spec = exchange_alone(
        msg, pressure, own_spec, pre, lat, cells, spec
    )
    scale = 1.0 / math.sqrt(points * n)
    msg, forces, out_grad, next_spec = run(
        functools.partial(back_kernel, depth, scale),
        [
            shape((peers, halves * main + 16, LANES), BF16),
            shape((1, 2), F32),
            shape((1, WIDTH), F32),
            shape((n, 8, LANES), F32),
        ],
        [grads, targets.reshape(1, 2), cells, lp, lat, pre],
        2 * rows * slots * depth * WIDTH,
        scratch=[pair_rows, deep_rows],
        grant=20,
    )
    grad_columns, forces, out_grad, own_spec = lax.optimization_barrier(
        (
            lax.all_to_all(
                msg, "gx", split_axis=0, concat_axis=0, tiled=True, axis_index_groups=near
            ),
            forces,
            out_grad,
            own_spec,
        )
    )
    part_rows = MODES * high * levels // n
    (msg,) = run(
        spec_kernel,
        [shape((n, part_rows + 16, LANES), BF16)],
        [half, grad_columns, part_table, spec],
        2 * MODES * high * rows * depth * WIDTH,
        scratch=[pltpu.VMEM((MODES * high * levels, LANES), F32)],
        smem=1,
    )
    finals, own_spec, forces, out_grad = exchange_alone(msg, own_spec, forces, out_grad)
    spec_grad, skip_grad = run(
        functools.partial(final_kernel, peers),
        [shape((spec_weight.shape[0], WIDTH, WIDTH), F32), shape((WIDTH, WIDTH), F32)],
        [finals, own_spec, next_spec],
        2 * NMODE * WIDTH * WIDTH * depth // n,
    )
    return (pressure.reshape(points), forces.reshape(2), spec_grad, skip_grad, out_grad.reshape(WIDTH))


def solution(mesh):
    fits = mesh.shape["gx"] == 16 and mesh.shape["groups"] == 2
    per_device = slab_step if fits else general_step
    in_specs = (
        P(("groups", "gx"), None),
        P(("groups", "gx"), None, None),
        P(None, ("groups", "gx"), None),
        P(("groups", "gx"), None, None),
        P(("groups", "gx"), None),
        P(("groups", "gx")),
        P(None, ("groups", "gx")),
        P("groups"),
        P("gx", None, None),
        P(),
        P(),
        P(),
        P(),
        P(),
    )
    out_specs = (
        P(("groups", "gx")),
        P("groups"),
        P(("groups", "gx"), None, None),
        P("groups", None),
        P("groups"),
    )
    return jax.shard_map(
        per_device, mesh=mesh, in_specs=in_specs, out_specs=out_specs, check_vma=False
    )
```

```python
import functools
import math

import jax
import jax.numpy as jnp
import ml_dtypes
import numpy as np
from jax import lax
from jax.experimental import pallas as pl
from jax.experimental.pallas import tpu as pltpu
from jax.sharding import PartitionSpec as P

GX = 128
GY = 128
MODES = 32
ZL = 1
NMODE = 1024


def fourier_rows(length, number):
    places = jnp.arange(length, dtype=jnp.float32)
    order = jnp.arange(number)
    half = number // 2
    freqs = jnp.where(order < half, order, order - half + 1).astype(jnp.float32)
    angles = 2.0 * math.pi / length * freqs[:, None] * places[None, :]
    table = jnp.where((order < half)[:, None], jnp.cos(angles), jnp.sin(angles))
    return (table * math.sqrt(2.0 / length)).astype(jnp.bfloat16)


def gelu_value(values):
    return 0.5 * values * (1.0 + lax.erf(values * (1.0 / math.sqrt(2.0))))


def gelu_slope(values):
    return 0.5 * (1.0 + lax.erf(values * (1.0 / math.sqrt(2.0)))) + values * jnp.exp(
        -0.5 * values * values
    ) * (1.0 / math.sqrt(2.0 * math.pi))


def general_step(
    point_feats,
    pair_point,
    pair_cell,
    kernel,
    counts,
    area,
    normals,
    targets,
    spec_weight,
    skip_weight,
    skip_bias,
    head_weight,
    head_bias,
    out_weight,
):
    devices = lax.axis_size("gx")
    local_points, width = point_feats.shape
    block_slots = pair_point.shape[2]
    row_count = GX // devices
    depth = ZL * devices
    slab_cells = row_count * GY * depth
    valid_mask = jnp.arange(block_slots)[None, :] < counts[0][:, None]
    point_rows = pair_point[0]
    pair_weight = jnp.where(valid_mask, kernel[0], jnp.float32(0.0))
    sender_weight = pair_weight * area[point_rows]
    contrib = (sender_weight[..., None] * point_feats[point_rows].astype(jnp.float32)).astype(
        jnp.bfloat16
    )
    arrived = lax.all_to_all(contrib, "gx", split_axis=0, concat_axis=0, tiled=True)
    cell_rows = pair_cell[:, 0, :].reshape(-1)
    latent = jax.ops.segment_sum(
        arrived.reshape(-1, width).astype(jnp.float32), cell_rows, num_segments=slab_cells
    ).astype(jnp.bfloat16)
    col_table = fourier_rows(GY, MODES)
    row_table = fourier_rows(GX, MODES)
    volume = latent.reshape(row_count, GY, depth * width)
    along_y = jnp.einsum(
        "by,xyk->xbk", col_table, volume, preferred_element_type=jnp.float32
    ).astype(jnp.bfloat16)
    columns = lax.all_to_all(along_y, "gx", split_axis=2, concat_axis=0, tiled=True)
    spectrum = jnp.einsum(
        "ax,xbk->abk", row_table, columns, preferred_element_type=jnp.float32
    ).astype(jnp.bfloat16)
    mode_rows = lax.all_to_all(
        spectrum.reshape(NMODE, ZL * width), "gx", split_axis=0, concat_axis=1, tiled=True
    )
    own_modes = mode_rows.shape[0]
    mixed_rows = jnp.einsum(
        "mzc,mcd->mzd",
        mode_rows.reshape(own_modes, depth, width),
        spec_weight,
        preferred_element_type=jnp.float32,
    ).astype(jnp.bfloat16)
    mixed = lax.all_to_all(
        mixed_rows.reshape(own_modes, depth * width), "gx", split_axis=1, concat_axis=0, tiled=True
    )
    back_x = jnp.einsum(
        "ax,abk->xbk",
        row_table,
        mixed.reshape(MODES, MODES, ZL * width),
        preferred_element_type=jnp.float32,
    ).astype(jnp.bfloat16)
    slabs = lax.all_to_all(back_x, "gx", split_axis=0, concat_axis=2, tiled=True)
    spatial = jnp.einsum(
        "by,xbk->xyk", col_table, slabs, preferred_element_type=jnp.float32
    ).reshape(slab_cells, width)
    pre = spatial + jnp.dot(latent, skip_weight, preferred_element_type=jnp.float32) + skip_bias
    features = gelu_value(pre).astype(jnp.bfloat16)
    picked = features[cell_rows].reshape(devices, block_slots, width)
    returned = lax.all_to_all(picked, "gx", split_axis=0, concat_axis=0, tiled=True)
    point_latent = jax.ops.segment_sum(
        (pair_weight[..., None] * returned.astype(jnp.float32)).reshape(-1, width),
        point_rows.reshape(-1),
        num_segments=local_points,
    )
    head_matrix = head_weight.astype(jnp.float32)
    head_pre = jnp.dot(point_latent, head_matrix, precision=lax.Precision.HIGHEST) + head_bias
    head = gelu_value(head_pre)
    pressure = jnp.dot(head, out_weight, precision=lax.Precision.HIGHEST)
    weighted = pressure * area
    scale = 1.0 / math.sqrt(local_points * devices)
    totals = lax.psum(
        jnp.stack([jnp.sum(weighted * normals[0]), jnp.sum(weighted * normals[1])]), "gx"
    )
    forces = scale * totals
    misfit = forces - targets
    point_grad = 2.0 * scale * (misfit[0] * normals[0] + misfit[1] * normals[1]) * area
    out_part = jnp.dot(point_grad, head, precision=lax.Precision.HIGHEST)
    head_grad = point_grad[:, None] * out_weight[None, :] * gelu_slope(head_pre)
    latent_grad = jnp.dot(head_grad, head_matrix.T, precision=lax.Precision.HIGHEST).astype(
        jnp.bfloat16
    )
    grad_pairs = (pair_weight[..., None] * latent_grad[point_rows].astype(jnp.float32)).astype(
        jnp.bfloat16
    )
    grad_arrived = lax.all_to_all(grad_pairs, "gx", split_axis=0, concat_axis=0, tiled=True)
    cell_grad = jax.ops.segment_sum(
        grad_arrived.reshape(-1, width).astype(jnp.float32), cell_rows, num_segments=slab_cells
    )
    pre_grad = (cell_grad * gelu_slope(pre)).astype(jnp.bfloat16)
    skip_part = jnp.dot(latent.T, pre_grad, preferred_element_type=jnp.float32)
    grad_y = jnp.einsum(
        "by,xyk->xbk",
        col_table,
        pre_grad.reshape(row_count, GY, depth * width),
        preferred_element_type=jnp.float32,
    ).astype(jnp.bfloat16)
    grad_columns = lax.all_to_all(grad_y, "gx", split_axis=2, concat_axis=0, tiled=True)
    grad_spec = jnp.einsum(
        "ax,xbk->abk", row_table, grad_columns, preferred_element_type=jnp.float32
    ).astype(jnp.bfloat16)
    grad_rows = lax.all_to_all(
        grad_spec.reshape(NMODE, ZL * width), "gx", split_axis=0, concat_axis=1, tiled=True
    )
    own_modes = grad_rows.shape[0]
    spec_grad = jnp.einsum(
        "mzc,mzd->mcd",
        mode_rows.reshape(own_modes, depth, width),
        grad_rows.reshape(own_modes, depth, width),
        preferred_element_type=jnp.float32,
    )
    out_grad, skip_grad = lax.psum((out_part, skip_part), "gx")
    return (pressure, forces, spec_grad, skip_grad, out_grad)


F32 = jnp.float32
BF16 = jnp.bfloat16
LANES = 128
WIDTH = 64


def host_rows(length, number):
    places = np.arange(length, dtype=np.float32)
    order = np.arange(number)
    half = number // 2
    freqs = np.where(order < half, order, order - half + 1).astype(np.float32)
    angles = np.float32(2.0 * math.pi / length) * freqs[:, None] * places[None, :]
    table = np.where((order < half)[:, None], np.cos(angles), np.sin(angles))
    table = table.astype(np.float32) * np.float32(math.sqrt(2.0 / length))
    return table.astype(ml_dtypes.bfloat16)


def gelu_both(values):
    half = 0.5 * (1.0 + lax.erf(values * (1.0 / math.sqrt(2.0))))
    bell = jnp.exp(-0.5 * values * values) * (1.0 / math.sqrt(2.0 * math.pi))
    return values * half, half + values * bell


def three_parts(values):
    first = values.astype(BF16)
    rest = values - first.astype(F32)
    second = rest.astype(BF16)
    third = (rest - second.astype(F32)).astype(BF16)
    return first, second, third


def mm(left, right):
    return jnp.dot(left, right, preferred_element_type=F32)


def mm_nt(left, right):
    return lax.dot_general(left, right, (((1,), (1,)), ((), ())), preferred_element_type=F32)


def mm_tn(left, right):
    return lax.dot_general(left, right, (((0,), (0,)), ((), ())), preferred_element_type=F32)


def short_rows(count):
    return lax.broadcasted_iota(jnp.int32, (count, LANES), 0).astype(jnp.int16)


def matches(rows, row):
    short = jnp.broadcast_to(row, (16, LANES)).astype(jnp.int16)
    tall = jnp.broadcast_to(short[None], (rows.shape[0] // 16, 16, LANES)).reshape(rows.shape)
    return jnp.where(rows == tall, jnp.ones((), BF16), jnp.zeros((), BF16))


def two_rows(ref, pair):
    return jnp.concatenate([ref[2 * pair : 2 * pair + 1, :], ref[2 * pair + 1 : 2 * pair + 2, :]], axis=1)


def source_kernel(group_ref, half_ref, count_hbm, point_hbm, kern_hbm, area_hbm, feat_hbm, weight_hbm, msg_ref, pw_ref, count_ref, point_ref, kern_ref, area_ref, feat_ref, weight_ref, sems):
    devices, points = point_ref.shape[0], feat_ref.shape[1]
    low = MODES // devices
    pieces = (
        (point_hbm, point_ref),
        (area_hbm, area_ref),
        (feat_hbm, feat_ref),
        (kern_hbm, kern_ref),
        (count_hbm, count_ref),
        (weight_hbm.at[pl.ds(group_ref[0] * MODES, MODES)], weight_ref),
    )
    copies = [
        pltpu.make_async_copy(source, place, sems.at[index])
        for index, (source, place) in enumerate(pieces)
    ]
    for copy in copies:
        copy.start()
    for copy in copies[:-1]:
        copy.wait()
    first, second, third = three_parts(area_ref[...])
    place = lax.broadcasted_iota(jnp.int32, (16, points), 0)
    extra = jnp.where(
        place == 0,
        first.astype(F32),
        jnp.where(place == 1, second.astype(F32), jnp.where(place == 2, third.astype(F32), 0.0)),
    ).astype(BF16)
    table = jnp.concatenate([feat_ref[...], extra], axis=0)
    rows = short_rows(points)
    lane = lax.broadcasted_iota(jnp.int32, (1, LANES), 1)
    kept = []
    for pair in range(devices // 2):
        hot = jnp.concatenate(
            [matches(rows, point_ref[at : at + 1, :]) for at in (2 * pair, 2 * pair + 1)], axis=1
        )
        got = mm(table, hot)
        spread = got[WIDTH : WIDTH + 1] + got[WIDTH + 1 : WIDTH + 2] + got[WIDTH + 2 : WIDTH + 3]
        for half in range(2):
            dest = 2 * pair + half
            cut = slice(half * LANES, (half + 1) * LANES)
            valid = lane < count_ref[0:1, dest : dest + 1]
            weight = jnp.where(valid, kern_ref[dest : dest + 1, :], 0.0)
            kept.append(weight)
            msg_ref[dest, 0:WIDTH, :] = ((weight * spread[:, cut]) * got[0:WIDTH, cut]).astype(BF16)
    pw_ref[...] = jnp.concatenate(kept, axis=0)
    copies[-1].wait()
    for dest in range(devices):
        msg_ref[dest, WIDTH : 2 * WIDTH, :] = jnp.concatenate(
            [weight_ref[low * dest], weight_ref[low * dest + 1]], axis=1
        )


def columns_of(row):
    return jnp.broadcast_to(row, (LANES, LANES)).T


def column_of(row):
    down = lax.broadcasted_iota(jnp.int32, (WIDTH, WIDTH), 0)
    along = lax.broadcasted_iota(jnp.int32, (WIDTH, WIDTH), 1)
    return jnp.sum(jnp.where(down == along, row, 0.0), axis=1, keepdims=True)


def pick_rows(rank_ref, pick_ref):
    rows = short_rows(pick_ref.shape[0])
    for block in range(rank_ref.shape[0]):
        pick_ref[:, block * LANES : (block + 1) * LANES] = matches(
            rows, rank_ref[block : block + 1, :]
        )


def basis_rows(depth, cell_ref, by_ref, lp_ref):
    zbits = depth.bit_length() - 1
    rows = by_ref.shape[0]
    slab = rows // MODES
    wide = 2 * LANES
    yrow = lax.broadcasted_iota(jnp.int32, (GY, wide), 0)
    xrow = jnp.bitwise_and(lax.broadcasted_iota(jnp.int32, (16, wide), 0), slab - 1)
    for pair in range(cell_ref.shape[0] // 2):
        cells = two_rows(cell_ref, pair)
        ypos = jnp.bitwise_and(jnp.right_shift(cells, zbits), GY - 1)
        xpos = jnp.right_shift(cells, zbits + GY.bit_length() - 1)
        hot = jnp.where(yrow == ypos, 1.0, 0.0).astype(BF16)
        mask = jnp.where(xrow == xpos, 1.0, 0.0).astype(BF16)
        found = mm(by_ref[...], hot).astype(BF16)
        for at in range(0, rows, 16):
            lp_ref[at : at + 16, pair * wide : (pair + 1) * wide] = found[at : at + 16] * mask


def place_kernel(depth, cell_ref, by_ref, zr_ref, rank_ref, home_ref, lp_ref, col_ref, pick_ref, part_ref):
    devices = cell_ref.shape[0]
    basis_rows(depth, cell_ref, by_ref, lp_ref)
    down = lax.broadcasted_iota(jnp.int32, (LANES, LANES), 0)
    along = lax.broadcasted_iota(jnp.int32, (LANES, LANES), 1)
    place = lax.broadcasted_iota(jnp.int32, (16, LANES), 0)
    seen = []
    for block in range(devices):
        cells = cell_ref[block : block + 1, :]
        row = cells.astype(F32)
        cut = slice(block * LANES, (block + 1) * LANES)
        col_ref[cut, :] = columns_of(row)
        high = jnp.right_shift(cells, 7).astype(F32)
        low = jnp.bitwise_and(cells, 127).astype(F32)
        part_ref[:, cut] = jnp.where(place == 0, high, jnp.where(place == 1, low, 0.0)).astype(BF16)
        same = jnp.logical_and(col_ref[cut, :] == row, down < along)
        before = jnp.max(jnp.where(same, 1.0, 0.0), axis=0, keepdims=True)
        if block:
            early = jnp.where(col_ref[0 : block * LANES, :] == row, 1.0, 0.0)
            before = jnp.maximum(before, jnp.max(early, axis=0, keepdims=True))
        seen.append(before)
    flags = jnp.concatenate(seen, axis=0)
    zr_ref[...] = jnp.where(flags > 0.0, -1, jnp.bitwise_and(cell_ref[...], depth - 1))
    marks = flags.astype(BF16)
    inside = mm(marks, jnp.where(down <= along, 1.0, 0.0).astype(BF16))
    above = jnp.where(down < along, 1.0, 0.0)[:, 0:devices][0:devices]
    ahead = jnp.sum(mm_tn(above.astype(BF16), marks), axis=1, keepdims=True)
    rank_ref[...] = jnp.where(flags > 0.0, (inside + ahead - flags).astype(jnp.int32), -1)
    pick_rows(rank_ref, pick_ref)
    found = mm_nt(part_ref[...], pick_ref[...])
    found = found[0:1] * 128.0 + found[1:2]
    shared = home_ref.shape[0]
    found = jnp.concatenate([found, jnp.zeros((1, -shared % LANES), F32)], axis=1)
    for at in range(0, shared, LANES):
        rows = min(LANES, shared - at)
        home_ref[at : at + rows, :] = columns_of(found[:, at : at + LANES])[0:rows]


def first_rows(cell_ref, zr_ref, home_ref, first_ref):
    homes = home_ref[...].astype(jnp.int32).astype(jnp.int16)
    for block in range(cell_ref.shape[0]):
        here = slice(block, block + 1)
        row = jnp.where(zr_ref[here, :] < 0, -1, cell_ref[here, :])
        first_ref[:, block * LANES : (block + 1) * LANES] = matches(homes, row)


def fold_parts(values):
    total = values[0:WIDTH]
    for at in range(WIDTH, values.shape[0], WIDTH):
        total = total + values[at : at + WIDTH]
    return total


def sum_cells(terms, xs_ref, cell_ref, rank_ref, zr_ref, home_ref, sums_ref, pick_ref, first_ref, full_ref, col_ref):
    devices = cell_ref.shape[0]
    few = jnp.max(rank_ref[...]) < home_ref.shape[0]

    @pl.when(few)
    def _():
        pick_rows(rank_ref, pick_ref)
        first_rows(cell_ref, zr_ref, home_ref, first_ref)
        moved = mm_nt(xs_ref[...], pick_ref[...]).astype(BF16)
        for pair in range(devices // 2):
            span = slice(pair * 2 * LANES, (pair + 1) * 2 * LANES)
            sums_ref[:, span] = terms(span) + fold_parts(mm(moved, first_ref[:, span]))

    @pl.when(jnp.logical_not(few))
    def _():
        for block in range(devices):
            col_ref[block * LANES : (block + 1) * LANES, :] = columns_of(
                cell_ref[block : block + 1, :].astype(F32)
            )
        for block in range(devices):
            row = cell_ref[block : block + 1, :].astype(F32)
            full_ref[...] = jnp.where(col_ref[...] == row, 1.0, 0.0).astype(BF16)
            sums_ref[:, block * LANES : (block + 1) * LANES] = fold_parts(
                mm(xs_ref[...], full_ref[...])
            )


def slab_rows(value_ref, zpos_of, lp_ref, rp_ref, msg_ref):
    devices = msg_ref.shape[0]
    step = lp_ref.shape[0] // devices
    for quad in range(rp_ref.shape[0] // (4 * WIDTH)):
        for pair in range(value_ref.shape[1] // (2 * LANES)):
            cut = slice(pair * 2 * LANES, (pair + 1) * 2 * LANES)
            zpos = zpos_of(pair)
            values = value_ref[:, cut].astype(F32)
            for level in range(4 * quad, 4 * quad + 4):
                rp_ref[level * WIDTH : (level + 1) * WIDTH, cut] = jnp.where(
                    zpos == level, values, 0.0
                ).astype(BF16)
        out = mm_nt(lp_ref[...], rp_ref[quad * 4 * WIDTH : (quad + 1) * 4 * WIDTH, :]).astype(BF16)
        for half in range(2):
            level = 2 * quad + half
            for dest in range(devices):
                msg_ref[dest, level * step : (level + 1) * step, :] = out[
                    dest * step : (dest + 1) * step, half * LANES : (half + 1) * LANES
                ]


def cell_kernel(rx_ref, cell_ref, rank_ref, zr_ref, home_ref, lp_ref, msg_ref, lat_ref, sums_ref, pick_ref, first_ref, full_ref, col_ref, xs_ref, rp_ref):
    devices = rx_ref.shape[0]
    for block in range(devices):
        xs_ref[:, block * LANES : (block + 1) * LANES] = rx_ref[block, 0:WIDTH, :]
    sum_cells(
        lambda span: xs_ref[:, span].astype(F32),
        xs_ref, cell_ref, rank_ref, zr_ref, home_ref, sums_ref, pick_ref, first_ref, full_ref, col_ref,
    )
    for pair in range(devices // 2):
        cut = slice(pair * 2 * LANES, (pair + 1) * 2 * LANES)
        latent = sums_ref[:, cut]
        lat_ref[:, cut] = latent.astype(BF16)
    slab_rows(lat_ref, lambda pair: two_rows(zr_ref, pair), lp_ref, rp_ref, msg_ref)


def to_modes(rx_ref, table, sp_ref):
    levels = sp_ref.shape[0] // table.shape[0]
    step = table.shape[1] // rx_ref.shape[0]
    for level in range(levels):
        block = rx_ref[:, level * step : (level + 1) * step, :].reshape(table.shape[1], LANES)
        coeffs = mm(table, block).astype(BF16).astype(F32)
        sp_ref[pl.ds(level, table.shape[0], stride=levels), :] = coeffs


def swap_halves(values):
    return pltpu.roll(values, WIDTH, 1)


def weight_kernel(group_ref, own_ref, other_ref, weight_ref):
    for order in range(MODES):
        source, which = order // 2, order % 2
        mine = jnp.full((WIDTH, LANES), group_ref[0], jnp.int32) == which
        weight_ref[order] = jnp.where(
            mine, own_ref[source].astype(F32), other_ref[source].astype(F32)
        ).astype(BF16)


def mode_kernel(rx_ref, weight_ref, table_ref, back_ref, term_ref, msg_ref, spec_ref, sp_ref, mx_ref):
    devices = rx_ref.shape[0]
    own_rows = spec_ref.shape[1]
    modes = table_ref.shape[0]
    levels = sp_ref.shape[0] // modes
    step = back_ref.shape[0] // devices
    to_modes(rx_ref, table_ref[...], sp_ref)
    for dest in range(devices):
        spec_ref[dest] = sp_ref[dest * own_rows : (dest + 1) * own_rows, :].astype(BF16)
    left = lax.broadcasted_iota(jnp.int32, (levels, LANES), 1) < WIDTH
    for order in range(MODES):
        at = order * 2 * levels
        even = sp_ref[at : at + levels, :]
        odd = sp_ref[at + levels : at + 2 * levels, :]
        rows = jnp.concatenate([even, swap_halves(even), odd, swap_halves(odd)], axis=0)
        out = mm(rows[:, 0:WIDTH].astype(BF16), weight_ref[order])
        mx_ref[at : at + levels, :] = jnp.where(
            left, out[0:levels], swap_halves(out[levels : 2 * levels])
        )
        mx_ref[at + levels : at + 2 * levels, :] = jnp.where(
            left, swap_halves(out[2 * levels : 3 * levels]), out[3 * levels : 4 * levels]
        )
    for level in range(levels):
        mixed = mx_ref[pl.ds(level, modes, stride=levels), :].astype(BF16)
        out = mm(back_ref[...], mixed).astype(BF16)
        for dest in range(devices):
            msg_ref[dest, level * step : (level + 1) * step, :] = out[dest * step : (dest + 1) * step]


def skip_kernel(cell_ref, rank_ref, zr_ref, home_ref, lat_ref, skip_ref, bias_ref, term_ref, full_ref, pick_ref, first_ref):
    few = jnp.max(rank_ref[...]) < home_ref.shape[0]
    bias = column_of(bias_ref[...])
    pick_rows(rank_ref, pick_ref)
    first_rows(cell_ref, zr_ref, home_ref, first_ref)
    shared = mm_nt(lat_ref[...], first_ref[...]).astype(BF16)
    for pair in range(cell_ref.shape[0] // 2):
        span = slice(pair * 2 * LANES, (pair + 1) * 2 * LANES)
        later = jnp.logical_and(two_rows(rank_ref, pair) >= 0, few)
        latent = jnp.where(later, mm(shared, pick_ref[:, span]), lat_ref[:, span].astype(F32))
        full_ref[:, span] = latent.astype(BF16)
        term_ref[:, span] = mm_tn(skip_ref[...], latent.astype(BF16)) + bias


def pre_kernel(depth, rx_ref, lp_ref, term_ref, cell_ref, spec_ref, msg_ref, slope_ref, rt_ref):
    devices = rx_ref.shape[0]
    rows = lp_ref.shape[0]
    step = rows // devices
    for level in range(rt_ref.shape[0] // LANES):
        block = rx_ref[:, level * step : (level + 1) * step, :].reshape(rows, LANES)
        rt_ref[level * LANES : (level + 1) * LANES, :] = block.T
    for pair in range(devices // 2):
        cut = slice(pair * 2 * LANES, (pair + 1) * 2 * LANES)
        zpos = jnp.bitwise_and(two_rows(cell_ref, pair), depth - 1)
        field = mm(rt_ref[...], lp_ref[:, cut])
        total = jnp.where(zpos == 0, field[0:WIDTH], 0.0)
        for level in range(1, depth):
            total += jnp.where(zpos == level, field[level * WIDTH : (level + 1) * WIDTH], 0.0)
        pre = total + term_ref[:, cut]
        feats, slope = gelu_both(pre)
        slope_ref[:, cut] = slope
        feats = feats.astype(BF16)
        for half in range(2):
            dest = 2 * pair + half
            msg_ref[dest, 0:WIDTH, :] = feats[:, half * LANES : (half + 1) * LANES]
            msg_ref[dest, WIDTH : WIDTH + 16, :] = spec_ref[dest, 0:16, :]


def head_kernel(rx_ref, point_ref, pw_ref, head_ref, bias_ref, out_ref, area_ref, normal_ref, own_ref, pres_ref, msg_ref, spec_ref, value_ref, hot_ref):
    devices = rx_ref.shape[0]
    points = area_ref.shape[1]
    rows = short_rows(points)
    for block in range(devices):
        cut = slice(block * LANES, (block + 1) * LANES)
        parts = three_parts(pw_ref[block : block + 1, :] * rx_ref[block, 0:WIDTH, :].astype(F32))[0:2]
        for index, part in enumerate(parts):
            value_ref[index * WIDTH : (index + 1) * WIDTH, cut] = part
        hot_ref[:, cut] = matches(rows, point_ref[block : block + 1, :])
    sums = mm_nt(value_ref[...], hot_ref[...])
    latent = sums[0:WIDTH] + sums[WIDTH : 2 * WIDTH]
    first, second, third = three_parts(latent)
    weight = head_ref[...]
    head_pre = mm_tn(weight, first) + mm_tn(weight, second) + mm_tn(weight, third) + column_of(bias_ref[...])
    out_column = column_of(out_ref[...])
    head, head_slope = gelu_both(head_pre)
    pressure = jnp.sum(head * out_column, axis=0, keepdims=True)
    pres_ref[...] = pressure
    along = [normal_ref[which : which + 1, :] * area_ref[...] for which in range(2)]
    first, second, third = three_parts(out_column * head_slope)
    grad = mm(weight, first) + mm(weight, second) + mm(weight, third)
    place = lax.broadcasted_iota(jnp.int32, (16, points), 0)
    extra = jnp.zeros((16, points), F32)
    for which in range(2):
        for index, part in enumerate(three_parts(along[which])):
            extra = jnp.where(place == 3 * which + index, part.astype(F32), extra)
    table = jnp.concatenate([grad.astype(BF16), extra.astype(BF16)], axis=0)
    lane = lax.broadcasted_iota(jnp.int32, (1, LANES), 1)
    partial = []
    for which in range(2):
        force = jnp.sum(pressure * area_ref[...] * normal_ref[which : which + 1, :], axis=1, keepdims=True)
        partial.append(force)
    force_row = jnp.zeros((1, LANES), F32)
    for which in range(2):
        for index, part in enumerate(three_parts(partial[which])):
            force_row = jnp.where(lane == 3 * which + index, part.astype(F32), force_row)
    out_rows = lax.dot_general(
        jnp.concatenate([along[0], along[1], jnp.zeros((6, points), F32)], axis=0),
        head,
        (((1,), (1,)), ((), ())),
        precision=lax.Precision.HIGHEST,
        preferred_element_type=F32,
    )
    out_row = jnp.concatenate([out_rows[0:1], out_rows[1:2]], axis=1)
    place = lax.broadcasted_iota(jnp.int32, (8, LANES), 0)
    out_parts = three_parts(out_row)
    common = jnp.where(
        place == 4,
        out_parts[0].astype(F32),
        jnp.where(place == 5, out_parts[1].astype(F32), jnp.where(place == 6, force_row, 0.0)),
    )
    found = ([], [])
    for pair in range(devices // 2):
        got = mm(table, hot_ref[:, pair * 2 * LANES : (pair + 1) * 2 * LANES])
        for half in range(2):
            block = 2 * pair + half
            cut = slice(half * LANES, (half + 1) * LANES)
            msg_ref[block, 0:WIDTH, :] = got[0:WIDTH, cut].astype(BF16)
            spec_ref[block] = rx_ref[block, WIDTH : WIDTH + 16, :]
            for which in range(2):
                at = WIDTH + 3 * which
                found[which].append(
                    got[at : at + 1, cut] + got[at + 1 : at + 2, cut] + got[at + 2 : at + 3, cut]
                )
    scaled = [
        three_parts(pw_ref[...] * jnp.concatenate(found[which], axis=0)) for which in range(2)
    ]
    rows = [scaled[which][index].astype(F32) for which in range(2) for index in range(2)]
    for block in range(devices):
        tail = common
        for index, row in enumerate(rows):
            tail = jnp.where(place == index, row[block : block + 1, :], tail)
        tail = jnp.concatenate([tail, own_ref[block, 16:32, :].astype(F32)[0:8]], axis=0)
        msg_ref[block, WIDTH : WIDTH + 16, :] = tail.astype(BF16)


def back_kernel(depth, scale, rx_ref, target_ref, cell_ref, lp_ref, lat_ref, slope_ref, msg_ref, force_ref, outg_ref, spec_ref, pg_ref, rp_ref):
    devices = rx_ref.shape[0]
    main = msg_ref.shape[1] - 16
    extra = slice(WIDTH, WIDTH + 16)
    total = rx_ref[0, extra, :].astype(F32)
    for block in range(1, devices):
        total += rx_ref[block, extra, :].astype(F32)
    force = total[6:7]
    lane = lax.broadcasted_iota(jnp.int32, (1, 2), 1)
    forces = scale * jnp.where(
        lane == 0,
        force[:, 0:1] + force[:, 1:2] + force[:, 2:3],
        force[:, 3:4] + force[:, 4:5] + force[:, 5:6],
    )
    force_ref[...] = forces
    misfit = (2.0 * scale) * (forces - target_ref[...])
    drag, lift = misfit[:, 0:1], misfit[:, 1:2]
    out_row = total[4:5] + total[5:6]
    outg_ref[...] = drag * out_row[:, 0:WIDTH] + lift * out_row[:, WIDTH : 2 * WIDTH]
    for block in range(devices):
        tail = rx_ref[block, extra, :].astype(F32)
        spec_ref[block] = tail[8:16]
        factor = drag * (tail[0:1] + tail[1:2]) + lift * (tail[2:3] + tail[3:4])
        cut = slice(block * LANES, (block + 1) * LANES)
        grad = factor * rx_ref[block, 0:WIDTH, :].astype(F32) * slope_ref[:, cut]
        pg_ref[:, cut] = grad.astype(BF16)
    slab_rows(
        pg_ref,
        lambda pair: jnp.bitwise_and(two_rows(cell_ref, pair), depth - 1),
        lp_ref, rp_ref, msg_ref,
    )
    skip = mm_nt(lat_ref[...], pg_ref[...])
    for dest in range(msg_ref.shape[0]):
        rows = two_parts(skip[8 * dest : 8 * dest + 8])
        rows = jnp.concatenate([rows, jnp.zeros_like(rows)], axis=0)
        msg_ref[dest, main : main + 16, :] = rows.astype(BF16)


def two_parts(values):
    first, second, _ = three_parts(values)
    return jnp.concatenate([first.astype(F32), second.astype(F32)], axis=1)


def spec_kernel(half_ref, rx_ref, table_ref, own_ref, msg_ref, sp_ref):
    peers, devices = rx_ref.shape[0], msg_ref.shape[0]
    part_rows = sp_ref.shape[0] // devices
    main = rx_ref.shape[1] - 16
    to_modes(rx_ref, table_ref[half_ref[0]], sp_ref)
    total = rx_ref[0, main : main + 16, :].astype(F32)
    for source in range(1, peers):
        total += rx_ref[source, main : main + 16, :].astype(F32)
    total = total[0:8]
    total = two_parts((total + swap_halves(total))[:, 0:WIDTH])
    for dest in range(devices):
        msg_ref[dest, 0:part_rows, :] = sp_ref[dest * part_rows : (dest + 1) * part_rows, :].astype(BF16)
        rows = jnp.concatenate([total, own_ref[dest, 16:32, :].astype(F32)[8:16]], axis=0)
        msg_ref[dest, part_rows : part_rows + 16, :] = rows.astype(BF16)


def final_kernel(peers, rx_ref, own_ref, next_ref, spec_ref, skip_ref):
    devices = rx_ref.shape[0]
    low = MODES // devices
    high = MODES // peers
    owned = spec_ref.shape[0] // MODES
    left = lax.broadcasted_iota(jnp.int32, (8, LANES), 1) < WIDTH
    main = rx_ref.shape[1] - 16
    for which in range(owned):
        for source in range(devices):
            if which == 0:
                coeffs = own_ref[source].astype(F32)
                first, second = coeffs[0:8], coeffs[8:16]
            else:
                first = next_ref[source]
                second = rx_ref[source, main : main + 16, :].astype(F32)[8:16]
            block = [
                jnp.where(left, first, 0.0),
                jnp.where(left, swap_halves(first), 0.0),
                jnp.where(left, 0.0, swap_halves(second)),
                jnp.where(left, 0.0, second),
            ]
            peer, inner = divmod(low * source, high)
            at = (which * high + inner) * 8
            grads = []
            for shift in range(0, devices, peers):
                part = rx_ref[peer + shift, at : at + 8 * low, :].astype(F32)
                grads += [part[0:8], swap_halves(part[0:8]), part[8:16], swap_halves(part[8:16])]
            block = jnp.concatenate(block * (devices // peers), axis=0).astype(BF16)
            grads = jnp.concatenate(grads, axis=0)[:, 0:WIDTH].astype(BF16)
            found = mm_tn(block, grads)
            mode = which * MODES + low * source
            spec_ref[mode] = found[0:WIDTH]
            spec_ref[mode + 1] = found[WIDTH : 2 * WIDTH]
    for peer in range(peers):
        rows = rx_ref[peer, main : main + 16, :].astype(F32)
        for shift in range(peers, devices, peers):
            rows += rx_ref[peer + shift, main : main + 16, :].astype(F32)
        rows = rows[0:8]
        skip_ref[8 * peer : 8 * peer + 8, :] = (rows + swap_halves(rows))[:, 0:WIDTH]


def run(kernel, outs, ins, flops, scratch=(), smem=0, hbm=0, hbm_outs=0, grant=16):
    vmem = pl.BlockSpec(memory_space=pltpu.VMEM)
    far = pl.BlockSpec(memory_space=pltpu.HBM)
    scalar = pl.BlockSpec(memory_space=pltpu.SMEM)
    moved = sum(math.prod(a.shape) * a.dtype.itemsize for a in list(ins) + list(outs))
    return pl.pallas_call(
        kernel,
        out_shape=tuple(outs),
        in_specs=[scalar] * smem + [far] * hbm + [vmem] * (len(ins) - smem - hbm),
        out_specs=tuple([far] * hbm_outs + [vmem] * (len(outs) - hbm_outs)),
        scratch_shapes=list(scratch),
        compiler_params=pltpu.CompilerParams(vmem_limit_bytes=grant * 1024 * 1024),
        cost_estimate=pl.CostEstimate(flops=flops, bytes_accessed=moved, transcendentals=0),
    )(*ins)


def slab_step(
    point_feats,
    pair_point,
    pair_cell,
    kernel,
    counts,
    area,
    normals,
    targets,
    spec_weight,
    skip_weight,
    skip_bias,
    head_weight,
    head_bias,
    out_weight,
):
    n = lax.axis_size("gx")
    points = point_feats.shape[0]
    slots = n * LANES
    slab = GX // n
    low = MODES // n
    depth = ZL * n
    levels = depth * WIDTH // LANES
    rows = MODES * slab
    main = levels * slab * low
    own_rows = low * low * levels
    shape = jax.ShapeDtypeStruct

    by = host_rows(GY, MODES)
    bx = host_rows(GX, MODES)
    by_rows = jnp.asarray(np.repeat(by, slab, axis=0))
    table = np.zeros((MODES, low, n, low, slab), ml_dtypes.bfloat16)
    for index in range(low):
        table[:, index, :, index, :] = bx.reshape(MODES, n, slab)
    table = table.reshape(MODES * low, rows)
    back = jnp.asarray(np.ascontiguousarray(table.T))
    table = jnp.asarray(table)
    peers = 8
    halves = n // peers
    high = MODES // peers
    part_table = np.zeros((halves, MODES, high, peers, high, slab), ml_dtypes.bfloat16)
    for index in range(high):
        part_table[:, :, index, :, index, :] = np.moveaxis(
            bx.reshape(MODES, halves, peers, slab), 1, 0
        )
    part_table = jnp.asarray(part_table.reshape(halves, MODES * high, rows))
    near = [[half * peers + peer for peer in range(peers)] for half in range(halves)]
    half = lax.shift_right_logical(lax.axis_index("gx"), peers.bit_length() - 1)
    half = half.astype(jnp.int32).reshape(1)

    def exchange(message):
        return lax.all_to_all(message, "gx", split_axis=0, concat_axis=0, tiled=True)

    def exchange_alone(message, *others):
        return lax.optimization_barrier((exchange(message),) + others)

    group = lax.axis_index("groups").astype(jnp.int32).reshape(1)
    point_rows = pair_point[0]
    cells = pair_cell[:, 0, :]
    area_row = area.reshape(1, points)
    msg, pw = run(
        source_kernel,
        [shape((n, 2 * WIDTH, LANES), BF16), shape((n, LANES), F32)],
        [group, half, counts, point_rows, kernel[0], area_row, point_feats.T, spec_weight],
        2 * 80 * points * slots,
        scratch=[
            pltpu.VMEM((1, n), jnp.int32),
            pltpu.VMEM((n, LANES), jnp.int32),
            pltpu.VMEM((n, LANES), F32),
            pltpu.VMEM((1, points), F32),
            pltpu.VMEM((WIDTH, points), BF16),
            pltpu.VMEM((MODES, WIDTH, WIDTH), BF16),
            pltpu.SemaphoreType.DMA((6,)),
        ],
        smem=2,
        hbm=6,
        grant=60,
    )
    rx = exchange(msg)
    shared = 192
    zr, rank, home, lp = run(
        functools.partial(place_kernel, depth),
        [
            shape((n, LANES), jnp.int32),
            shape((n, LANES), jnp.int32),
            shape((shared, LANES), F32),
            shape((rows, slots), BF16),
        ],
        [cells, by_rows],
        2 * rows * LANES * slots,
        scratch=[
            pltpu.VMEM((slots, LANES), F32),
            pltpu.VMEM((shared, slots), BF16),
            pltpu.VMEM((16, slots), BF16),
        ],
    )
    sum_scratch = [
        pltpu.VMEM((WIDTH, slots), F32),
        pltpu.VMEM((shared, slots), BF16),
        pltpu.VMEM((shared, slots), BF16),
        pltpu.VMEM((slots, LANES), BF16),
        pltpu.VMEM((slots, LANES), F32),
    ]
    own = rx[:, WIDTH : 2 * WIDTH, :]
    other = lax.ppermute(own, "groups", [(0, 1), (1, 0)])
    pair_rows = pltpu.VMEM((WIDTH, slots), BF16)
    basis = pltpu.VMEM((rows, slots), BF16)
    deep_rows = pltpu.VMEM((depth * WIDTH, slots), BF16)
    big = 2 * WIDTH * slots * slots + 2 * rows * slots * depth * WIDTH
    msg, lat = run(
        cell_kernel,
        [shape((n, main, LANES), BF16), shape((WIDTH, slots), BF16)],
        [rx, cells, rank, zr, home, lp],
        big,
        scratch=sum_scratch + [pair_rows, deep_rows],
        grant=20,
    )
    columns = exchange(msg)
    term, lat = run(
        skip_kernel,
        [shape((WIDTH, slots), F32), shape((WIDTH, slots), BF16)],
        [cells, rank, zr, home, lat, skip_weight, skip_bias.reshape(1, WIDTH)],
        2 * shared * WIDTH * slots,
        scratch=[pltpu.VMEM((shared, slots), BF16)] * 2,
    )
    (weights,) = run(
        weight_kernel,
        [shape((MODES, WIDTH, LANES), BF16)],
        [group, own, other],
        MODES * WIDTH * LANES,
        smem=1,
    )
    msg, spec = run(
        mode_kernel,
        [shape((n, main, LANES), BF16), shape((n, own_rows, LANES), BF16)],
        [columns, weights, table, back, term],
        4 * MODES * low * rows * depth * WIDTH,
        scratch=[pltpu.VMEM((MODES * low * levels, LANES), F32)] * 2,
    )
    slabs, spec, lat, term, cells, pw = exchange_alone(
        msg, spec, lat, term, cells, pw
    )
    msg, pre = run(
        functools.partial(pre_kernel, depth),
        [shape((n, WIDTH + 16, LANES), BF16), shape((WIDTH, slots), F32)],
        [slabs, lp, term, cells, spec],
        2 * rows * slots * depth * WIDTH,
        scratch=[pltpu.VMEM((depth * WIDTH, rows), BF16)],
    )
    returned, pre, lat, cells, pw, spec = exchange_alone(
        msg, pre, lat, cells, pw, spec
    )
    out_row = out_weight.reshape(1, WIDTH)
    pressure, msg, own_spec = run(
        head_kernel,
        [
            shape((1, points), F32),
            shape((n, WIDTH + 16, LANES), BF16),
            shape((n, 16, LANES), BF16),
        ],
        [returned, point_rows, pw, head_weight, head_bias.reshape(1, WIDTH), out_row, area_row, normals, spec],
        2 * 3 * WIDTH * points * slots,
        scratch=[
            pltpu.VMEM((2 * WIDTH, slots), BF16),
            pltpu.VMEM((points, slots), BF16),
        ],
    )
    grads, pressure, own_spec, pre, lat, cells, spec = exchange_alone(
        msg, pressure, own_spec, pre, lat, cells, spec
    )
    scale = 1.0 / math.sqrt(points * n)
    msg, forces, out_grad, next_spec = run(
        functools.partial(back_kernel, depth, scale),
        [
            shape((peers, halves * main + 16, LANES), BF16),
            shape((1, 2), F32),
            shape((1, WIDTH), F32),
            shape((n, 8, LANES), F32),
        ],
        [grads, targets.reshape(1, 2), cells, lp, lat, pre],
        2 * rows * slots * depth * WIDTH,
        scratch=[pair_rows, deep_rows],
        grant=20,
    )
    grad_columns, forces, out_grad, own_spec = lax.optimization_barrier(
        (
            lax.all_to_all(
                msg, "gx", split_axis=0, concat_axis=0, tiled=True, axis_index_groups=near
            ),
            forces,
            out_grad,
            own_spec,
        )
    )
    part_rows = MODES * high * levels // n
    (msg,) = run(
        spec_kernel,
        [shape((n, part_rows + 16, LANES), BF16)],
        [half, grad_columns, part_table, spec],
        2 * MODES * high * rows * depth * WIDTH,
        scratch=[pltpu.VMEM((MODES * high * levels, LANES), F32)],
        smem=1,
    )
    finals, own_spec, forces, out_grad = exchange_alone(msg, own_spec, forces, out_grad)
    spec_grad, skip_grad = run(
        functools.partial(final_kernel, peers),
        [shape((spec_weight.shape[0], WIDTH, WIDTH), F32), shape((WIDTH, WIDTH), F32)],
        [finals, own_spec, next_spec],
        2 * NMODE * WIDTH * WIDTH * depth // n,
    )
    return (pressure.reshape(points), forces.reshape(2), spec_grad, skip_grad, out_grad.reshape(WIDTH))


def solution(mesh):
    fits = mesh.shape["gx"] == 16 and mesh.shape["groups"] == 2
    per_device = slab_step if fits else general_step
    in_specs = (
        P(("groups", "gx"), None),
        P(("groups", "gx"), None, None),
        P(None, ("groups", "gx"), None),
        P(("groups", "gx"), None, None),
        P(("groups", "gx"), None),
        P(("groups", "gx")),
        P(None, ("groups", "gx")),
        P("groups"),
        P("gx", None, None),
        P(),
        P(),
        P(),
        P(),
        P(),
    )
    out_specs = (
        P(("groups", "gx")),
        P("groups"),
        P(("groups", "gx"), None, None),
        P("groups", None),
        P("groups"),
    )
    return jax.shard_map(
        per_device, mesh=mesh, in_specs=in_specs, out_specs=out_specs, check_vma=False
    )
```
